32 devices in a mesh: row: 2 (over x), seq: 16 (over z, y, core).
Axes of the slice: x: 2, y: 2, z: 4, core: 2. Of those that a mesh axis runs over, the one named last changes fastest.
Arguments:
- tokens: bfloat16 [2, 2048, 1600], P('row', 'seq'), may hold values from -6 to 6
- doc_ids: int32 [2, 2048], P('row', 'seq'), may hold values from 0 to 8, as said below
- meta_tokens: bfloat16 [128, 1600], P(('row', 'seq')), may hold values from -6 to 6
- mixer_params: bfloat16 [22246400], P(('row', 'seq'))
- small_params: bfloat16 [81600], P(('row', 'seq'))
- ffn_params: bfloat16 [26419200], P(('row', 'seq'))
- cotangent: bfloat16 [2, 2048, 1600], P('row', 'seq'), may hold values from -6 to 6
Outputs:
- block_out: bfloat16 [2, 2048, 1600], P('row', 'seq')
- grad_tokens: float32 [2, 2048, 1600], P('row', 'seq')
- grad_meta: float32 [128, 1600], P(('row', 'seq'))
- grad_mixer: float32 [22246400], P(('row', 'seq'))
- grad_small: float32 [81600], P(('row', 'seq'))
- grad_ffn: float32 [26419200], P(('row', 'seq'))
The draws below stay inside these ranges and needn't reach their ends.
Inputs may be any that keep to these rules, and one draw needn't show every extreme that they name: `doc_ids`: ids never fall along a row, rise by one at each document start, start at 0 and end at 8 in every row (each row holds exactly 9 documents); in one row, chosen by the seed, no document starts at positions 128 to 1920.
All inputs are finite; a program needn't handle non-finite values.
Results may differ from the reference program's by a relative error of at most 0.015.
Values may be sent and summed in bfloat16 or wider, within the bound.
A program may use at most 960 MiB of HBM per device.

```python
import math
from functools import partial
import jax
import jax.numpy as jnp
from jax import lax

D = 1600
HEADS = 25
GROUPS = 5
HEAD = 64
INNER = 3200
STATE = 16
CONV = 4
DT_RANK = 100
FF = 5504
META = 128
TOK_SEQ = 128
WINDOW = 1024
ROWS = 2
LENGTH = 2048
FINE_SIZE = 81600


def normal_pieces(base_key, layout, factors):
    pieces = []
    for piece_idx in range(len(layout)):
        piece_len = math.prod(layout[piece_idx])
        pieces.append(jax.random.normal(jax.random.fold_in(base_key, piece_idx), (piece_len,), jnp.float32) * factors[piece_idx])
    return jnp.concatenate(pieces)


def draw_mixer_params(key, part):
    key = jax.random.fold_in(key, 11)
    layout = [(D, HEADS * HEAD), (D, 2 * GROUPS * HEAD), (D, 2 * INNER), (INNER, DT_RANK + 2 * STATE), (DT_RANK, INNER), (HEADS * HEAD + INNER, D)]
    factors = [D ** (-0.5), D ** (-0.5), D ** (-0.5), 2.0 * INNER ** (-0.5), DT_RANK ** (-0.5), 2.0 * (HEADS * HEAD + INNER) ** (-0.5)]
    return normal_pieces(key, layout, factors).astype(jnp.bfloat16)


def draw_ffn_params(key, part):
    key = jax.random.fold_in(key, 13)
    layout = [(D, FF), (D, FF), (FF, D)]
    factors = [D ** (-0.5), D ** (-0.5), 1.5 * FF ** (-0.5)]
    return normal_pieces(key, layout, factors).astype(jnp.bfloat16)


def uniform_piece(base_key, piece_idx, piece_len, lower, upper):
    return jax.random.uniform(jax.random.fold_in(base_key, piece_idx), (piece_len,), jnp.float32, lower, upper)


def draw_small_params(key, part):
    key = jax.random.fold_in(key, 17)
    g_one = uniform_piece(key, 0, D, 0.7, 1.3)
    g_attn = uniform_piece(key, 1, HEADS * HEAD, 0.7, 1.3)
    g_ssm = uniform_piece(key, 2, INNER, 0.7, 1.3)
    g_two = uniform_piece(key, 3, D, 0.7, 1.3)
    conv_w = (jax.random.normal(jax.random.fold_in(key, 4), (CONV * INNER,), jnp.float32) * 0.5).reshape(CONV, INNER)
    conv_b = jax.random.normal(jax.random.fold_in(key, 5), (INNER,), jnp.float32) * 0.3
    dt_bias = uniform_piece(key, 6, INNER, -6.0, -1.0)
    a_log = uniform_piece(key, 7, INNER * STATE, -6.0, 1.5).reshape(INNER, STATE)
    d_skip = uniform_piece(key, 8, INNER, 0.5, 1.5)
    channel_part = jnp.concatenate([g_ssm[:, None], conv_w.T, conv_b[:, None], dt_bias[:, None], a_log, d_skip[:, None]], axis=1)
    packed_rows = jnp.concatenate([g_one[:, None], g_attn[:, None], g_two[:, None], channel_part.reshape(D, -1)], axis=1).reshape(-1)
    used = D * (3 + 2 * (CONV + STATE + 4))
    tail = uniform_piece(key, 9, FINE_SIZE - used, -1.0, 1.0)
    return jnp.concatenate([packed_rows, tail]).astype(jnp.bfloat16)


def draw_doc_ids(key, part):
    key = jax.random.fold_in(key, 5)
    starts_count = 8
    positions = jnp.arange(LENGTH, dtype=jnp.int32)
    picked = jax.random.randint(jax.random.fold_in(key, 1), (ROWS, LENGTH), 0, 2 ** 30 // LENGTH)
    chosen = jax.random.randint(jax.random.fold_in(key, 2), (), 0, ROWS)
    middle = (positions >= TOK_SEQ) & (positions <= LENGTH - TOK_SEQ)
    blocked = (jnp.arange(ROWS, dtype=jnp.int32)[:, None] == chosen) & middle[None, :] | (positions[None, :] == 0)
    scores = jnp.where(blocked, -1, picked * LENGTH + positions[None, :])
    _, start_pos = lax.top_k(scores, starts_count)
    doc_flags = jnp.sum((positions[None, None, :] == start_pos[:, :, None]).astype(jnp.int32), axis=1)
    return jnp.cumsum(doc_flags, axis=1).astype(jnp.int32)


def levels(rng, extent, split, smallest, top_value):
    loudness, own = 1.0, jax.random.fold_in(rng, 6)
    for dim, shards_of in split:
        heights = jnp.exp(jax.random.uniform(jax.random.fold_in(own, dim), (shards_of,), jnp.float32, smallest / len(split), top_value / len(split)))
        loudness = loudness * jnp.repeat(heights, extent[dim] // shards_of).reshape([-1 if axis == dim else 1 for axis in range(len(extent))])
    return loudness


def normal_values(rng, shape, deviation, reach, cuts=(), kind=jnp.bfloat16):
    values = deviation * jax.random.normal(rng, shape, jnp.float32)
    if cuts:
        values = values * levels(rng, shape, cuts, -0.22, 0.18)
    return jnp.clip(values, -reach, reach).astype(kind)


def setup_inputs(seed: int = 0) -> dict:
    arg_keys = jax.random.split(jax.random.key(seed), 8)
    return {
        "tokens": normal_values(arg_keys[0], (ROWS, LENGTH, D), 1.0, 6.0, ((0, 2), (1, 16))),
        "doc_ids": draw_doc_ids(jax.random.fold_in(arg_keys[7], 71), 0),
        "meta_tokens": normal_values(arg_keys[2], (META, D), 1.0, 6.0, ((0, 32),)),
        "mixer_params": draw_mixer_params(jax.random.fold_in(arg_keys[7], 71), 0),
        "small_params": draw_small_params(jax.random.fold_in(arg_keys[7], 71), 0),
        "ffn_params": draw_ffn_params(jax.random.fold_in(arg_keys[7], 71), 0),
        "cotangent": normal_values(arg_keys[6], (ROWS, LENGTH, D), 1.0, 6.0, ((0, 2), (1, 16))),
    }


norm_eps = 1e-05

@jax.custom_vjp
def low(v):
    return lax.optimization_barrier(v.astype(jnp.bfloat16)).astype(jnp.float32)

@jax.custom_vjp
def low_back(v):
    return v

def low_keep(v):
    return (low(v), None)

def low_pass(kept, grad):
    return (grad,)

def back_keep(v):
    return (v, None)

def back_low(kept, grad):
    return (low(grad),)
low.defvjp(low_keep, low_pass)
low_back.defvjp(back_keep, back_low)

def split_flat(flat_vec, layout):
    pieces = []
    offset = 0
    for piece_shape in layout:
        piece_len = math.prod(piece_shape)
        pieces.append(flat_vec[offset:offset + piece_len].reshape(piece_shape))
        offset += piece_len
    return pieces

def mixer_layout():
    return [(D, HEADS * HEAD), (D, 2 * GROUPS * HEAD), (D, 2 * INNER), (INNER, DT_RANK + 2 * STATE), (DT_RANK, INNER), (HEADS * HEAD + INNER, D)]

def small_split(flat_vec):
    width = CONV + STATE + 4
    packed_rows = flat_vec[:D * (3 + 2 * width)].reshape(D, 3 + 2 * width)
    channel_part = packed_rows[:, 3:].reshape(INNER, width)
    return (packed_rows[:, 0], packed_rows[:, 1], channel_part[:, 0], packed_rows[:, 2], channel_part[:, 1:1 + CONV].T, channel_part[:, 1 + CONV], channel_part[:, 2 + CONV], channel_part[:, 3 + CONV:3 + CONV + STATE], channel_part[:, 3 + CONV + STATE])

def ffn_layout():
    return [(D, FF), (D, FF), (FF, D)]

def rms_norm(values, gain_vec):
    return values * lax.rsqrt(lax.optimization_barrier(jnp.mean(values * values, axis=-1, keepdims=True)) + norm_eps) * gain_vec

def silu_fn(values):
    return values / (1.0 + jnp.exp(-values))

def softplus_fn(values):
    return jnp.maximum(values, 0.0) + jnp.log1p(jnp.exp(-jnp.abs(values)))

def matmul_hi(left, right):
    return jnp.einsum('...k,kn->...n', left, right, precision=lax.Precision.HIGHEST)

def conv_piece(extended, conv_w, conv_b, lag_masks):
    shard_len = extended.shape[1] - (CONV - 1)
    summed = conv_b
    for j in range(CONV):
        summed = summed + conv_w[j] * extended[:, CONV - 1 - j:CONV - 1 - j + shard_len] * lag_masks[j]
    return silu_fn(summed)

def mix_piece(attn_out, ssm_out, g_attn, g_ssm):
    return 0.5 * jnp.concatenate([rms_norm(attn_out, g_attn), rms_norm(ssm_out, g_ssm)], axis=-1)

def attend_rows(queries, kv_rows, meta_kv, doc_first):
    q_block = min(512, LENGTH)
    blocks = LENGTH // q_block
    key_width = GROUPS * HEAD

    def one_row(row_inputs):
        q_row, kv_row, first_row = row_inputs
        padded = jnp.concatenate([jnp.zeros((WINDOW, kv_row.shape[1]), kv_row.dtype), kv_row], axis=0)

        def one_block(block_idx):
            anchor = block_idx * q_block
            q_part = lax.dynamic_slice_in_dim(q_row, anchor, q_block, 0).reshape(q_block, GROUPS, HEADS // GROUPS, HEAD)
            key_part = jnp.concatenate([meta_kv, lax.dynamic_slice_in_dim(padded, anchor, WINDOW + q_block, 0)], axis=0)
            key_four = key_part[:, :key_width].reshape(-1, GROUPS, HEAD)
            val_four = key_part[:, key_width:].reshape(-1, GROUPS, HEAD)
            q_pos = anchor + jnp.arange(q_block, dtype=jnp.int32)
            k_pos = anchor - WINDOW + jnp.arange(WINDOW + q_block, dtype=jnp.int32)
            first_part = lax.dynamic_slice_in_dim(first_row, anchor, q_block, 0)
            allowed = (k_pos[None] >= first_part[:, None]) & (k_pos[None] <= q_pos[:, None]) & (k_pos[None] > q_pos[:, None] - WINDOW)
            allowed = jnp.concatenate([jnp.ones((q_block, meta_kv.shape[0]), bool), allowed], axis=1)
            raw_dot = low_back(jnp.einsum('qghd,kgd->ghqk', q_part, key_four, precision=lax.Precision.HIGHEST))
            scores = jnp.where(allowed[None, None], raw_dot * HEAD ** (-0.5), -1e+30)
            exp_scores = jnp.exp(scores - lax.optimization_barrier(jnp.max(scores, axis=-1, keepdims=True)))
            prob_half = low(exp_scores / lax.optimization_barrier(jnp.sum(exp_scores, axis=-1, keepdims=True)))
            attended = jnp.einsum('ghqk,kgd->qghd', prob_half, val_four, precision=lax.Precision.HIGHEST)
            return attended.reshape(q_block, HEADS * HEAD)
        outputs = lax.map(jax.checkpoint(one_block), jnp.arange(blocks, dtype=jnp.int32))
        return outputs.reshape(LENGTH, HEADS * HEAD)
    return lax.map(one_row, (queries, kv_rows, doc_first))

def ssm_rows(conv_out, pre_dt, b_in, c_read, z_in, keep_mask, dt_bias, a_log, d_skip):
    delta_t = softplus_fn(pre_dt + dt_bias)
    a_mat = -jnp.exp(a_log)

    def token_step(ssm_state, inputs):
        c_t, dt_t, b_t, read_t, keep_t = inputs
        decay_now = jnp.exp(dt_t[:, None] * a_mat) * keep_t
        ssm_state = decay_now * ssm_state + (dt_t * c_t)[:, None] * b_t[None, :]
        return (ssm_state, lax.optimization_barrier(jnp.sum(ssm_state * read_t[None, :], axis=1)))

    @jax.checkpoint
    def block_step(ssm_state, blocked):
        return lax.scan(token_step, ssm_state, blocked)

    def one_row(c_row, dt_row, b_row, read_row, keep_row):
        blocked = tuple((v.reshape((LENGTH // TOK_SEQ, TOK_SEQ) + v.shape[1:]) for v in (c_row, dt_row, b_row, read_row, keep_row)))
        _, outputs = lax.scan(block_step, jnp.zeros((INNER, STATE), jnp.float32), blocked)
        return outputs.reshape(LENGTH, INNER)
    y_ssm = jax.vmap(one_row)(conv_out, delta_t, b_in, c_read, keep_mask) + d_skip * conv_out
    return y_ssm * silu_fn(z_in)

def forward(tokens, meta_tokens, mixer_params, small_params, ffn_params, doc_first):
    w_q, w_kv, w_in, w_x, w_dt, w_out = split_flat(mixer_params, mixer_layout())
    g_one, g_attn, g_ssm, g_two, conv_w, conv_b, dt_bias, a_log, d_skip = small_split(small_params)
    w_gate, w_up, w_down = split_flat(ffn_params, ffn_layout())
    positions = jnp.arange(LENGTH, dtype=jnp.int32)
    keep_mask = (positions[None] != doc_first).astype(jnp.float32)
    lag_masks = jnp.stack([(positions[None] - j >= doc_first).astype(jnp.float32)[..., None] for j in range(CONV)])
    normed = low(rms_norm(tokens, g_one))
    queries = low_back(low(matmul_hi(normed, w_q)))
    kv_rows = low_back(low(matmul_hi(normed, w_kv)))
    meta_kv = low_back(low(matmul_hi(low(rms_norm(meta_tokens, g_one)), w_kv)))
    xz_rows = low_back(low(matmul_hi(normed, w_in)))
    attn_out = low_back(attend_rows(queries, kv_rows, meta_kv, doc_first))
    padded = jnp.pad(xz_rows[..., :INNER], ((0, 0), (CONV - 1, 0), (0, 0)))
    conv_out = low(conv_piece(padded, conv_w, conv_b, lag_masks))
    projected = low_back(matmul_hi(conv_out, w_x))
    rank_low = low(projected[..., :DT_RANK])
    pre_dt = low_back(matmul_hi(rank_low, w_dt))
    ssm_out = ssm_rows(conv_out, pre_dt, projected[..., DT_RANK:DT_RANK + STATE], projected[..., DT_RANK + STATE:], xz_rows[..., INNER:], keep_mask, dt_bias, a_log, d_skip)
    mixed = low(mix_piece(attn_out, ssm_out, g_attn, g_ssm))
    hidden = tokens + low_back(matmul_hi(mixed, w_out))
    second = low(rms_norm(hidden, g_two))
    gate_pre = low_back(matmul_hi(second, w_gate))
    up_pre = low_back(matmul_hi(second, w_up))
    act_low = low(silu_fn(gate_pre) * up_pre)
    return hidden + matmul_hi(act_low, w_down)

def reference(tokens, doc_ids, meta_tokens, mixer_params, small_params, ffn_params, cotangent):
    positions = jnp.arange(LENGTH, dtype=jnp.int32)
    doc_flags = jnp.concatenate([jnp.ones((ROWS, 1), bool), doc_ids[:, 1:] != doc_ids[:, :-1]], axis=1)
    doc_first = lax.cummax(jnp.where(doc_flags, positions[None, :], 0), axis=1).astype(jnp.int32)
    inputs = (tokens.astype(jnp.float32), meta_tokens.astype(jnp.float32), mixer_params.astype(jnp.float32), small_params.astype(jnp.float32), ffn_params.astype(jnp.float32))
    result, pullback = jax.vjp(partial(forward, doc_first=doc_first), *inputs)
    grads = pullback(cotangent.astype(jnp.float32))
    return (result.astype(jnp.bfloat16), grads[0], grads[1], grads[2], grads[3], grads[4])
```

```python
import functools
from functools import partial
import math

import jax
import jax.numpy as jnp
from jax import lax
from jax.experimental import pallas as pl
from jax.experimental.pallas import tpu as pltpu
from jax.sharding import PartitionSpec as P

D = 1600
HEADS = 25
GROUPS = 5
HEAD = 64
INNER = 3200
STATE = 16
CONV = 4
DT_RANK = 100
FF = 5504
REACH = 8
BLOCK = 128
RUNS = 4
SUB = 8
SPAN = 128
SIXTEEN = jnp.bfloat16
WIDE = jnp.float32


norm_eps = 1e-05


def split_flat(flat_vec, layout):
    pieces = []
    offset = 0
    for piece_shape in layout:
        piece_len = math.prod(piece_shape)
        pieces.append(flat_vec[offset : offset + piece_len].reshape(piece_shape))
        offset += piece_len
    return pieces


def mixer_layout():
    return [
        (D, HEADS * HEAD),
        (D, 2 * GROUPS * HEAD),
        (D, 2 * INNER),
        (INNER, DT_RANK + 2 * STATE),
        (DT_RANK, INNER),
        (HEADS * HEAD + INNER, D),
    ]


def ffn_layout():
    return [(D, FF), (D, FF), (FF, D)]


def small_split(flat_vec):
    width = CONV + STATE + 4
    packed_rows = flat_vec[: D * (3 + 2 * width)].reshape(D, 3 + 2 * width)
    channel_part = packed_rows[:, 3:].reshape(INNER, width)
    return packed_rows[:, 0], packed_rows[:, 1], packed_rows[:, 2], channel_part


def rms_norm(values, gain_vec):
    return (
        values * lax.rsqrt(jnp.mean(values * values, axis=-1, keepdims=True) + norm_eps) * gain_vec
    )


def silu_fn(values):
    return values / (1.0 + jnp.exp(-values))


def softplus_fn(values):
    return jnp.maximum(values, 0.0) + jnp.log1p(jnp.exp(-jnp.abs(values)))


def glu_piece(gate_pre, up_pre):
    return silu_fn(gate_pre) * up_pre


def dot_last(left, right):
    return jnp.einsum("...k,kn->...n", left, right, preferred_element_type=WIDE)


def dot_back(grads, right):
    return jnp.einsum("...n,kn->...k", grads, right, preferred_element_type=WIDE)


def dot_weight(left, grads):
    return jnp.einsum("...k,...n->kn", left, grads, preferred_element_type=WIDE)


def heads_of(shards):
    return -(-HEADS // shards)


def runs_of(shards):
    return RUNS if INNER % (RUNS * shards) == 0 else 1


def own_channels(array, axis, shards, place):
    runs = runs_of(shards)
    unit = INNER // (runs * shards)
    shape = array.shape
    cut = array.reshape(shape[:axis] + (runs, shards, unit) + shape[axis + 1 :])
    cut = lax.dynamic_index_in_dim(cut, place, axis + 1, keepdims=False)
    return cut.reshape(shape[:axis] + (runs * unit,) + shape[axis + 1 :])


def pad_heads(array, axis, shards):
    heads = heads_of(shards)
    pads = [(0, 0)] * array.ndim
    pads[axis] = (0, heads * shards - HEADS)
    padded = jnp.pad(array, pads)
    shape = padded.shape
    return padded.reshape(shape[:axis] + (shards, heads * HEAD) + shape[axis + 2 :])


def by_head(w_q, w_kv, shards):
    rows = w_q.shape[0]
    w_kv = w_kv.reshape(rows, 2, GROUPS, 1, HEAD)
    w_kv = jnp.broadcast_to(w_kv, (rows, 2, GROUPS, HEADS // GROUPS, HEAD))
    w_kv = w_kv.reshape(rows, 2, HEADS, HEAD)
    return jnp.concatenate(
        [
            pad_heads(w_q.reshape(rows, HEADS, HEAD), 1, shards),
            pad_heads(w_kv[:, 0], 1, shards),
            pad_heads(w_kv[:, 1], 1, shards),
        ],
        axis=2,
    )


def exchange(value):
    return lax.all_to_all(value, "seq", 0, 0)


def both_halves(value):
    if lax.axis_size("row") != 2:
        return lax.all_gather(value, "row", axis=0, tiled=True)
    other = lax.ppermute(value, "row", [(0, 1), (1, 0)])
    first = lax.axis_index("row") == 0
    return jnp.concatenate(
        [jnp.where(first, value, other), jnp.where(first, other, value)], axis=0
    )


def mixer_fits(length, shards):
    width = INNER // RUNS
    sizes = [math.prod(shape) for shape in mixer_layout()]
    return (
        runs_of(shards) == RUNS
        and length % width == 0
        and all(size % width == 0 for size in sizes)
        and D % shards == 0
        and (HEADS * HEAD * 2) % shards == 0
    )


def mixer_shards_whole(piece):
    shards, place = lax.axis_size("seq"), lax.axis_index("seq")
    whole = lax.all_gather(piece, ("row", "seq"), axis=0, tiled=True)
    w_q, w_kv, w_in, w_x, w_dt, w_out = split_flat(whole, mixer_layout())
    qkv = lax.dynamic_index_in_dim(by_head(w_q, w_kv, shards), place, 1, keepdims=False)
    w_in = own_channels(w_in.reshape(D, 2, INNER), 2, shards, place)
    out_heads = w_out[: HEADS * HEAD].reshape(HEADS, HEAD, D)
    out_heads = lax.dynamic_index_in_dim(pad_heads(out_heads, 0, shards), place, 0, keepdims=False)
    return (
        qkv,
        w_in.reshape(D, -1),
        own_channels(w_x, 0, shards, place),
        own_channels(w_dt, 1, shards, place),
        out_heads,
        own_channels(w_out[HEADS * HEAD :], 0, shards, place),
    )


def mixer_shards(piece):
    shards, place = lax.axis_size("seq"), lax.axis_index("seq")
    if not mixer_fits(piece.shape[0], shards):
        return mixer_shards_whole(piece)
    width = INNER // RUNS
    unit = width // shards
    mine = exchange(piece.reshape(-1, shards, unit).transpose(1, 0, 2))
    mine = both_halves(mine.reshape(-1, unit))
    part_q, part_kv, part_in, part_x, part_dt, part_out = cut_rows(
        mine, [math.prod(shape) // width for shape in mixer_layout()]
    )
    w_in = part_in.reshape(D, -1)
    w_dt = part_dt.reshape(DT_RANK, -1)
    w_x = lax.all_gather(part_x, "seq").transpose(1, 0, 2).reshape(INNER, -1)
    w_x = own_channels(w_x, 0, shards, place)
    rows = D // shards
    by_rows = exchange(
        jnp.concatenate(
            [part_q.reshape(shards, -1, unit), part_kv.reshape(shards, -1, unit)], axis=1
        )
    )
    by_rows = by_rows.transpose(1, 0, 2).reshape(-1, width)
    split = part_q.shape[0] // shards
    cut = by_head(
        by_rows[:split].reshape(rows, HEADS * HEAD),
        by_rows[split:].reshape(rows, 2 * GROUPS * HEAD),
        shards,
    )
    qkv = exchange(cut.transpose(1, 0, 2)).reshape(D, -1)
    per_row = D // width
    head_rows = heads_of(shards) * HEAD
    out_heads = part_out[: HEADS * HEAD * per_row]
    out_heads = jnp.pad(
        out_heads, ((0, (head_rows * shards - HEADS * HEAD) * per_row), (0, 0))
    ).reshape(shards, -1, unit)
    out_inner = part_out[HEADS * HEAD * per_row :].reshape(RUNS, shards, -1, unit)
    out_inner = out_inner.transpose(1, 0, 2, 3).reshape(shards, -1, unit)
    out_both = exchange(jnp.concatenate([out_heads, out_inner], axis=1))
    out_both = out_both.transpose(1, 0, 2).reshape(-1, D)
    return qkv, w_in, w_x, w_dt, out_both[:head_rows], out_both[head_rows:]


def cut_rows(array, counts):
    pieces, offset = [], 0
    for count in counts:
        pieces.append(array[offset : offset + count])
        offset += count
    return pieces


def ffn_shards(piece):
    shards, place = lax.axis_size("seq"), lax.axis_index("seq")
    unit = FF // shards
    if piece.shape[0] % FF or D % shards:
        whole = lax.all_gather(piece, ("row", "seq"), axis=0, tiled=True)
        w_gate, w_up, w_down = split_flat(whole, ffn_layout())
        return (
            lax.dynamic_slice_in_dim(w_gate, place * unit, unit, 1),
            lax.dynamic_slice_in_dim(w_up, place * unit, unit, 1),
            lax.dynamic_slice_in_dim(w_down, place * unit, unit, 0),
        )
    mine = exchange(piece.reshape(-1, shards, unit).transpose(1, 0, 2))
    mine = both_halves(mine.reshape(-1, unit))
    w_gate, w_up, part_down = cut_rows(mine, [D, D, D])
    w_down = exchange(part_down.reshape(shards, -1, unit))
    return w_gate, w_up, w_down.transpose(1, 0, 2).reshape(unit, D)


def small_shards(whole):
    shards, place = lax.axis_size("seq"), lax.axis_index("seq")
    g_one, g_attn, g_two, channel_part = small_split(whole)
    g_attn = pad_heads(g_attn.reshape(HEADS, HEAD), 0, shards)
    return (
        g_one,
        g_two,
        lax.dynamic_index_in_dim(g_attn, place, 0, keepdims=False),
        own_channels(channel_part, 0, shards, place),
    )


def tiles_of(count):
    return -(-count // 128)


def start_blocks(small_params, doc_ids):
    devices = lax.axis_size("row") * lax.axis_size("seq")
    small_rows, id_rows = tiles_of(small_params.shape[0]), tiles_of(doc_ids.shape[0])
    rows = -(-(small_rows + id_rows) // 16) * 16
    small = jnp.pad(small_params, (0, small_rows * 128 - small_params.shape[0]))
    ids = jnp.pad(doc_ids.astype(SIXTEEN), (0, (rows - small_rows) * 128 - doc_ids.shape[0]))
    block = jnp.concatenate([small.reshape(-1, 128), ids.reshape(-1, 128)], axis=0)
    every = push_gather(block, 0)
    small = every[:, :small_rows].reshape(devices, -1)[:, : small_params.shape[0]].reshape(-1)
    ids = every[:, small_rows:].reshape(devices, -1)[:, : doc_ids.shape[0]]
    ids = ids.reshape(lax.axis_size("row"), -1)
    ids = lax.dynamic_index_in_dim(ids, lax.axis_index("row"), 0, keepdims=False)
    return small.astype(WIDE), ids.astype(jnp.int32)


def end_blocks(grad_small, d_meta):
    devices = lax.axis_size("row") * lax.axis_size("seq")
    parts = grad_small.reshape(devices, -1).astype(SIXTEEN)
    small_count = parts.shape[1]
    small_rows = tiles_of(small_count)
    parts = jnp.pad(parts, ((0, 0), (0, small_rows * 128 - small_count)))
    meta = d_meta.astype(SIXTEEN).reshape(devices, -1)
    meta_count = meta.shape[1]
    rows = -(-(small_rows + tiles_of(meta_count)) // 16) * 16
    meta = jnp.pad(meta, ((0, 0), (0, (rows - small_rows) * 128 - meta_count)))
    blocks = jnp.concatenate(
        [parts.reshape(devices, -1, 128), meta.reshape(devices, -1, 128)], axis=1
    )
    own = push_scatter(blocks, 9)
    small = own[:small_rows].reshape(-1)[:small_count]
    meta = own[small_rows:].reshape(-1)[:meta_count].reshape(-1, D)
    return small, meta


def gather_seq(block):
    return lax.all_gather(block, "seq", axis=0, tiled=True)


def scatter_seq(whole):
    return lax.psum_scatter(whole.astype(SIXTEEN), "seq", scatter_dimension=0, tiled=True).astype(
        WIDE
    )


MESH = pl.DeviceIdType.MESH
ANY = pl.BlockSpec(memory_space=pl.ANY)
VMEM = pl.BlockSpec(memory_space=pltpu.VMEM)
MIB = 1024 * 1024


def greet(peers):
    barrier = pltpu.get_barrier_semaphore()
    for peer in peers:
        pl.semaphore_signal(barrier, inc=1, device_id=peer, device_id_type=MESH)
    pl.semaphore_wait(barrier, len(peers))


def ring_place(chip, chips):
    odd = chip % 2
    return odd * (chips - 1 - chip // 2) + (1 - odd) * (chip // 2)


def ring_chip(place, chips):
    place = (place + 2 * chips) % chips
    back = place // (chips // 2)
    return back * (2 * (chips - 1 - place) + 1) + (1 - back) * (2 * place)


def seq_gather_kernel(shards, parts, x_ref, out_ref, ring_send, ring_recv, pair_send, pair_recv, own_sem):
    row, me = lax.axis_index("row"), lax.axis_index("seq")
    chips = shards // 2
    core = me % 2
    place = ring_place(me // 2, chips)

    def device(spot):
        return ring_chip(spot, chips) * 2 + core

    right, left, twin = (row, device(place + 1)), (row, device(place - 1)), (row, me + 1 - 2 * core)
    greet([right, left, twin])
    rows = x_ref.shape[0] // (2 * parts)

    def cut(way, part):
        return pl.ds((way * parts + part) * rows, rows)

    own = pltpu.make_async_copy(x_ref, out_ref.at[me], own_sem)
    own.start()
    started = []

    def send(src, dst, send_sem, recv_sem, to):
        copy = pltpu.make_async_remote_copy(
            src_ref=src, dst_ref=dst, send_sem=send_sem, recv_sem=recv_sem,
            device_id=to, device_id_type=MESH,
        )
        copy.start()
        started.append(copy)
        return copy

    paths = [(way, part) for part in range(parts) for way in range(2)]
    flights = {}
    for way, part in paths:
        flights[way, part] = send(
            x_ref.at[cut(way, part)], out_ref.at[me, cut(way, part)],
            ring_send.at[way, part, 0], ring_recv.at[way, part, 0], (right, left)[way],
        )
    pairs = [send(x_ref, out_ref.at[me], pair_send.at[0, 0, chips - 1], pair_recv.at[0, 0, chips - 1], twin)]
    for step in range(chips - 1):
        for way, part in paths:
            flights[way, part].wait_recv()
            source = device(place - 1 - step if way == 0 else place + 1 + step)
            here = out_ref.at[source, cut(way, part)]
            if step < chips - 2:
                flights[way, part] = send(
                    here, here, ring_send.at[way, part, step + 1],
                    ring_recv.at[way, part, step + 1], (right, left)[way],
                )
            pairs.append(
                send(here, here, pair_send.at[way, part, step], pair_recv.at[way, part, step], twin)
            )
    own.wait()
    for copy in started:
        copy.wait_send()
    for copy in pairs:
        copy.wait_recv()


def ring_seq_gather(block, collective_id, parts=2):
    shards = lax.axis_size("seq")
    chips = shards // 2
    rows, width = block.shape
    ring = pltpu.SemaphoreType.DMA((2, parts, chips - 1))
    pair = pltpu.SemaphoreType.DMA((2, parts, chips))
    gathered = pl.pallas_call(
        functools.partial(seq_gather_kernel, shards, parts),
        out_shape=jax.ShapeDtypeStruct((shards, rows, width), block.dtype),
        in_specs=[ANY],
        out_specs=ANY,
        scratch_shapes=[ring, ring, pair, pair, pltpu.SemaphoreType.DMA],
        compiler_params=pltpu.CompilerParams(collective_id=collective_id, has_side_effects=True),
    )(block)
    return gathered.reshape(shards * rows, width)


def seq_scatter_kernel(
    shards, parts, x_ref, out_ref, mine, pair, arrived, ring_send, ring_recv, pair_send, pair_recv, own_sem
):
    row, me = lax.axis_index("row"), lax.axis_index("seq")
    chips = shards // 2
    core = me % 2
    place = ring_place(me // 2, chips)

    def device(spot, core):
        return ring_chip(spot, chips) * 2 + core

    right = (row, device(place + 1, core))
    left = (row, device(place - 1, core))
    twin = (row, me + 1 - 2 * core)
    greet([right, left, twin])
    rows = x_ref.shape[1] // (2 * parts)

    def cut(way, part):
        return pl.ds((way * parts + part) * rows, rows)

    order = []
    for far in range(1, chips // 2 + 1):
        order += [-far, far] if 2 * far < chips else [far]
    order.append(0)
    waits = {}
    started = []
    for spot in order:
        slot = spot % chips
        load = pltpu.make_async_copy(x_ref.at[device(place + spot, core)], mine.at[slot], own_sem.at[slot])
        load.start()
        copy = pltpu.make_async_remote_copy(
            src_ref=x_ref.at[device(place + spot, 1 - core)],
            dst_ref=pair.at[slot], send_sem=pair_send.at[slot], recv_sem=pair_recv.at[slot],
            device_id=twin, device_id_type=MESH,
        )
        copy.start()
        started.append(copy)
        waits[slot] = (load, copy)

    def ready(slot):
        if slot in waits:
            load, copy = waits.pop(slot)
            load.wait()
            copy.wait_recv()

    flights = {}
    for step in range(chips):
        for part in range(parts):
            for way in range(2):
                slot = (-1 - step if way == 0 else 1 + step) % chips
                ready(slot)
                here = cut(way, part)
                total = mine[slot, here, :].astype(WIDE) + pair[slot, here, :].astype(WIDE)
                if step:
                    flights[way, part].wait_recv()
                    total = total + arrived[way, step - 1, pl.ds(part * rows, rows), :].astype(WIDE)
                if step == chips - 1:
                    out_ref[here, :] = total
                    continue
                mine[slot, here, :] = total.astype(mine.dtype)
                copy = pltpu.make_async_remote_copy(
                    src_ref=mine.at[slot, here], dst_ref=arrived.at[way, step, pl.ds(part * rows, rows)],
                    send_sem=ring_send.at[way, part, step], recv_sem=ring_recv.at[way, part, step],
                    device_id=(right, left)[way], device_id_type=MESH,
                )
                copy.start()
                started.append(copy)
                flights[way, part] = copy
    for copy in started:
        copy.wait_send()


def ring_seq_scatter(whole, collective_id, parts=2):
    shards = lax.axis_size("seq")
    chips = shards // 2
    length, width = whole.shape
    rows = length // shards
    ring = pltpu.SemaphoreType.DMA((2, parts, chips - 1))
    pair = pltpu.SemaphoreType.DMA((chips,))
    return pl.pallas_call(
        functools.partial(seq_scatter_kernel, shards, parts),
        out_shape=jax.ShapeDtypeStruct((rows, width), WIDE),
        in_specs=[ANY],
        out_specs=VMEM,
        scratch_shapes=[
            pltpu.VMEM((chips, rows, width), SIXTEEN),
            pltpu.VMEM((chips, rows, width), SIXTEEN),
            pltpu.VMEM((2, chips - 1, rows // 2, width), SIXTEEN),
            ring, ring, pair, pair, pair,
        ],
        compiler_params=pltpu.CompilerParams(
            collective_id=collective_id, has_side_effects=True, vmem_limit_bytes=56 * MIB
        ),
    )(whole.astype(SIXTEEN).reshape(shards, rows, width))


def bits_of(shards):
    bits = shards.bit_length() - 1
    assert 1 << bits == shards
    return bits


def partner_of(me, bit):
    return me + (1 - 2 * ((me // (1 << bit)) % 2)) * (1 << bit)


def seq_sum_kernel(bits, x_ref, out_ref, total, staged, arrived, send_sem, recv_sem, back_send, back_recv):
    row, me = lax.axis_index("row"), lax.axis_index("seq")
    partners = [(row, partner_of(me, bit)) for bit in range(bits)]
    greet(partners)
    length = x_ref.shape[1]
    total[...] = x_ref[...].astype(WIDE)
    begin = 0
    started = []
    for bit in range(bits):
        half = length >> (bit + 1)
        upper = (me // (1 << bit)) % 2
        kept = pl.multiple_of(begin + upper * half, 128)
        given = pl.multiple_of(begin + (1 - upper) * half, 128)
        staged[:, half : 2 * half] = total[:, pl.ds(given, half)].astype(SIXTEEN)
        copy = pltpu.make_async_remote_copy(
            src_ref=staged.at[:, half : 2 * half], dst_ref=arrived.at[:, half : 2 * half],
            send_sem=send_sem.at[bit], recv_sem=recv_sem.at[bit],
            device_id=partners[bit], device_id_type=MESH,
        )
        copy.start()
        started.append(copy)
        copy.wait_recv()
        total[:, pl.ds(kept, half)] += arrived[:, half : 2 * half].astype(WIDE)
        begin = kept
    half = length >> bits
    out_ref[:, pl.ds(pl.multiple_of(begin, 128), half)] = total[
        :, pl.ds(pl.multiple_of(begin, 128), half)
    ].astype(SIXTEEN)
    for bit in range(bits - 1, -1, -1):
        half = length >> (bit + 1)
        here = out_ref.at[:, pl.ds(pl.multiple_of(begin, 128), half)]
        copy = pltpu.make_async_remote_copy(
            src_ref=here, dst_ref=here, send_sem=back_send.at[bit], recv_sem=back_recv.at[bit],
            device_id=partners[bit], device_id_type=MESH,
        )
        copy.start()
        started.append(copy)
        copy.wait_recv()
        begin = begin - ((me // (1 << bit)) % 2) * half
    for copy in started:
        copy.wait_send()


def seq_sum(values, collective_id):
    bits = bits_of(lax.axis_size("seq"))
    rows, length = values.shape
    sems = pltpu.SemaphoreType.DMA((bits,))
    return pl.pallas_call(
        functools.partial(seq_sum_kernel, bits),
        out_shape=jax.ShapeDtypeStruct((rows, length), SIXTEEN),
        in_specs=[VMEM],
        out_specs=VMEM,
        scratch_shapes=[
            pltpu.VMEM((rows, length), WIDE),
            pltpu.VMEM((rows, length), SIXTEEN),
            pltpu.VMEM((rows, length), SIXTEEN),
            sems, sems, sems, sems,
        ],
        compiler_params=pltpu.CompilerParams(
            collective_id=collective_id, has_side_effects=True, vmem_limit_bytes=48 * MIB
        ),
    )(values)


def seq_sum_small_kernel(bits, x_ref, out_ref, arrived, staged, send_sem, recv_sem):
    row, me = lax.axis_index("row"), lax.axis_index("seq")
    partners = [(row, partner_of(me, bit)) for bit in range(bits)]
    greet(partners)
    total = x_ref[...]
    copies = []
    for bit in range(bits):
        staged[bit] = total
        copy = pltpu.make_async_remote_copy(
            src_ref=staged.at[bit], dst_ref=arrived.at[bit], send_sem=send_sem.at[bit],
            recv_sem=recv_sem.at[bit], device_id=partners[bit], device_id_type=MESH,
        )
        copy.start()
        copies.append(copy)
        copy.wait_recv()
        total = total + arrived[bit]
    out_ref[...] = total
    for copy in copies:
        copy.wait_send()


def seq_sum_small(values, collective_id):
    bits = bits_of(lax.axis_size("seq"))
    shape = values.shape
    tiles = values.reshape(-1, 128)
    sems = pltpu.SemaphoreType.DMA((bits,))
    slots = pltpu.VMEM((bits,) + tiles.shape, WIDE)
    return pl.pallas_call(
        functools.partial(seq_sum_small_kernel, bits),
        out_shape=jax.ShapeDtypeStruct(tiles.shape, WIDE),
        in_specs=[VMEM],
        out_specs=VMEM,
        scratch_shapes=[slots, slots, sems, sems],
        compiler_params=pltpu.CompilerParams(collective_id=collective_id, has_side_effects=True),
    )(tiles).reshape(shape)


def all_peers(rows, shards):
    me = lax.axis_index("row") * shards + lax.axis_index("seq")
    count = rows * shards
    ahead = [(me + far) % count for far in range(1, count)]
    return me, count, [(other, (other // shards, other % shards)) for other in ahead]


def push_gather_kernel(rows, shards, x_ref, out_ref, send_sem, recv_sem):
    me, count, peers = all_peers(rows, shards)
    greet([device for _, device in peers])
    copies = []
    for far, (_, device) in enumerate(peers):
        copy = pltpu.make_async_remote_copy(
            src_ref=x_ref, dst_ref=out_ref.at[me], send_sem=send_sem.at[far],
            recv_sem=recv_sem.at[far], device_id=device, device_id_type=MESH,
        )
        copy.start()
        copies.append(copy)
    out_ref[me] = x_ref[...]
    for copy in copies:
        copy.wait()


def push_gather(block, collective_id):
    rows, shards = lax.axis_size("row"), lax.axis_size("seq")
    sems = pltpu.SemaphoreType.DMA((rows * shards - 1,))
    return pl.pallas_call(
        functools.partial(push_gather_kernel, rows, shards),
        out_shape=jax.ShapeDtypeStruct((rows * shards,) + block.shape, block.dtype),
        in_specs=[VMEM],
        out_specs=VMEM,
        scratch_shapes=[sems, sems],
        compiler_params=pltpu.CompilerParams(collective_id=collective_id, has_side_effects=True),
    )(block)


def push_scatter_kernel(rows, shards, x_ref, out_ref, arrived, send_sem, recv_sem):
    me, count, peers = all_peers(rows, shards)
    greet([device for _, device in peers])
    copies = []
    for far, (other, device) in enumerate(peers):
        copy = pltpu.make_async_remote_copy(
            src_ref=x_ref.at[other], dst_ref=arrived.at[far], send_sem=send_sem.at[far],
            recv_sem=recv_sem.at[far], device_id=device, device_id_type=MESH,
        )
        copy.start()
        copies.append(copy)
    total = x_ref[me].astype(WIDE)
    for far, copy in enumerate(copies):
        copy.wait_recv()
        total = total + arrived[far].astype(WIDE)
    out_ref[...] = total
    for copy in copies:
        copy.wait_send()


def push_scatter(blocks, collective_id):
    rows, shards = lax.axis_size("row"), lax.axis_size("seq")
    count = rows * shards
    sems = pltpu.SemaphoreType.DMA((count - 1,))
    return pl.pallas_call(
        functools.partial(push_scatter_kernel, rows, shards),
        out_shape=jax.ShapeDtypeStruct(blocks.shape[1:], WIDE),
        in_specs=[VMEM],
        out_specs=VMEM,
        scratch_shapes=[pltpu.VMEM((count - 1,) + blocks.shape[1:], blocks.dtype), sems, sems],
        compiler_params=pltpu.CompilerParams(
            collective_id=collective_id, has_side_effects=True, vmem_limit_bytes=32 * MIB
        ),
    )(blocks)


def conv_piece(extended, conv_w, conv_b, lag_masks):
    length = extended.shape[0] - (CONV - 1)
    summed = conv_b
    for j in range(CONV):
        summed = (
            summed + conv_w[j] * extended[CONV - 1 - j : CONV - 1 - j + length] * lag_masks[j]
        )
    return silu_fn(summed)


def nt_dot(left, right):
    return lax.dot_general(left, right, (((1,), (1,)), ((), ())), preferred_element_type=WIDE)


def seen_keys(block, first_row):
    window = (REACH + 1) * BLOCK
    k_pos = (block - REACH) * BLOCK + lax.broadcasted_iota(jnp.int32, (window, BLOCK), 0)
    q_pos = block * BLOCK + lax.broadcasted_iota(jnp.int32, (window, BLOCK), 1)
    return (k_pos >= first_row) & (k_pos <= q_pos) & (k_pos > q_pos - REACH * BLOCK)


def attend_forward_kernel(heads, first_ref, q_ref, kv_ref, turned_ref, meta_ref, meta_turned_ref, out_ref, total_ref):
    block = pl.program_id(0)
    span = pl.ds(pl.multiple_of(block * BLOCK, BLOCK), (REACH + 1) * BLOCK)
    seen = seen_keys(block, first_ref[0])
    outs, totals = [], []
    for h in range(heads):
        cut = slice(h * HEAD, (h + 1) * HEAD)
        v_cut = slice((heads + h) * HEAD, (heads + h + 1) * HEAD)
        query = q_ref[:, cut] * SIXTEEN(HEAD ** (-0.5))
        near = jnp.where(seen, nt_dot(kv_ref[span, cut], query), -1e30)
        meta = nt_dot(meta_ref[:, cut], query)
        top = jnp.maximum(
            jnp.max(near, axis=0, keepdims=True), jnp.max(meta, axis=0, keepdims=True)
        )
        near = jnp.exp(near - top)
        meta = jnp.exp(meta - top)
        total = jnp.sum(near, axis=0, keepdims=True) + jnp.sum(meta, axis=0, keepdims=True)
        out = jnp.dot(turned_ref[v_cut, span], near.astype(SIXTEEN), preferred_element_type=WIDE)
        out += jnp.dot(meta_turned_ref[v_cut, :], meta.astype(SIXTEEN), preferred_element_type=WIDE)
        outs.append(out / total)
        totals.append(top + jnp.log(total))
    out_ref[...] = jnp.concatenate(outs, axis=0).T
    total_ref[0] = jnp.concatenate(totals, axis=0)


def attend_backward_kernel(
    heads, first_ref, q_ref, kv_ref, turned_ref, meta_ref, meta_turned_ref, out_ref, total_ref, do_ref,
    dq_ref, dkv_ref, dmeta_ref,
):
    block = pl.program_id(0)

    @pl.when(block == 0)
    def _():
        dkv_ref[...] = jnp.zeros_like(dkv_ref)
        dmeta_ref[...] = jnp.zeros_like(dmeta_ref)

    span = pl.ds(pl.multiple_of(block * BLOCK, BLOCK), (REACH + 1) * BLOCK)
    seen = seen_keys(block, first_ref[0])
    d_out = do_ref[...]
    row_sums = (d_out * out_ref[...]).T
    d_half = d_out.astype(SIXTEEN)
    d_queries, near_k, near_v, meta_k, meta_v = [], [], [], [], []
    for h in range(heads):
        cut = slice(h * HEAD, (h + 1) * HEAD)
        v_cut = slice((heads + h) * HEAD, (heads + h + 1) * HEAD)
        query = q_ref[:, cut] * SIXTEEN(HEAD ** (-0.5))
        do = d_half[:, cut]
        total = total_ref[0, h : h + 1, :]
        mean = jnp.sum(row_sums[cut], axis=0, keepdims=True)
        near = jnp.where(seen, jnp.exp(nt_dot(kv_ref[span, cut], query) - total), 0.0)
        meta = jnp.exp(nt_dot(meta_ref[:, cut], query) - total)
        d_near = (near * (nt_dot(kv_ref[span, v_cut], do) - mean)).astype(SIXTEEN)
        d_meta = (meta * (nt_dot(meta_ref[:, v_cut], do) - mean)).astype(SIXTEEN)
        near_v.append(jnp.dot(near.astype(SIXTEEN), do, preferred_element_type=WIDE))
        meta_v.append(jnp.dot(meta.astype(SIXTEEN), do, preferred_element_type=WIDE))
        near_k.append(jnp.dot(d_near, query, preferred_element_type=WIDE))
        meta_k.append(jnp.dot(d_meta, query, preferred_element_type=WIDE))
        d_query = jnp.dot(turned_ref[cut, span], d_near, preferred_element_type=WIDE)
        d_query += jnp.dot(meta_turned_ref[cut, :], d_meta, preferred_element_type=WIDE)
        d_queries.append(d_query * HEAD ** (-0.5))
    dq_ref[...] = jnp.concatenate(d_queries, axis=0).T.astype(SIXTEEN)
    dkv_ref[span, :] += jnp.concatenate(near_k + near_v, axis=1)
    dmeta_ref[...] += jnp.concatenate(meta_k + meta_v, axis=1)


def attend_operands(queries, kv_rows, doc_first):
    length = doc_first.shape[0]
    count = length // BLOCK
    near = jnp.pad(kv_rows[:length], ((REACH * BLOCK, 0), (0, 0)))
    meta = kv_rows[length:]
    arrays = (doc_first.reshape(count, 1, BLOCK), queries, near, near.T, meta, meta.T)
    width = queries.shape[1]

    def whole(array):
        return pl.BlockSpec(array.shape, lambda i: (0,) * array.ndim)

    specs = [
        pl.BlockSpec((1, 1, BLOCK), lambda i: (i, 0, 0)),
        pl.BlockSpec((BLOCK, width), lambda i: (i, 0)),
    ] + [whole(a) for a in arrays[2:]]
    return arrays, specs, count, width


def attend_forward(queries, kv_rows, doc_first):
    arrays, specs, count, width = attend_operands(queries, kv_rows, doc_first)
    heads = width // HEAD
    return pl.pallas_call(
        lambda *refs: attend_forward_kernel(heads, *refs),
        grid=(count,),
        in_specs=specs,
        out_specs=[
            pl.BlockSpec((BLOCK, width), lambda i: (i, 0)),
            pl.BlockSpec((1, heads, BLOCK), lambda i: (i, 0, 0)),
        ],
        out_shape=[
            jax.ShapeDtypeStruct(queries.shape, WIDE),
            jax.ShapeDtypeStruct((count, heads, BLOCK), WIDE),
        ],
        compiler_params=pltpu.CompilerParams(vmem_limit_bytes=48 * MIB),
    )(*arrays)


def attend_backward(queries, kv_rows, doc_first, out, log_total, d_out):
    arrays, specs, count, width = attend_operands(queries, kv_rows, doc_first)
    heads = width // HEAD
    near, meta = arrays[2], arrays[4]
    row_spec = pl.BlockSpec((BLOCK, width), lambda i: (i, 0))
    d_queries, d_near, d_meta = pl.pallas_call(
        lambda *refs: attend_backward_kernel(heads, *refs),
        grid=(count,),
        in_specs=specs
        + [row_spec, pl.BlockSpec((1, heads, BLOCK), lambda i: (i, 0, 0)), row_spec],
        out_specs=[
            row_spec,
            pl.BlockSpec(near.shape, lambda i: (0, 0)),
            pl.BlockSpec(meta.shape, lambda i: (0, 0)),
        ],
        out_shape=[
            jax.ShapeDtypeStruct(queries.shape, SIXTEEN),
            jax.ShapeDtypeStruct(near.shape, WIDE),
            jax.ShapeDtypeStruct(meta.shape, WIDE),
        ],
        compiler_params=pltpu.CompilerParams(vmem_limit_bytes=48 * MIB),
    )(*arrays, out, log_total, d_out)
    return d_queries, jnp.concatenate([d_near[REACH * BLOCK :], d_meta], axis=0).astype(SIXTEEN)


def step_sum():
    rows = lax.broadcasted_iota(jnp.int32, (SUB, SUB * STATE), 0)
    cols = lax.broadcasted_iota(jnp.int32, (SUB, SUB * STATE), 1)
    return (cols // STATE == rows).astype(SIXTEEN)


def scan_forward_kernel(keep_ref, conv_ref, delta_ref, b_ref, c_ref, a_ref, y_ref, start_ref, state_ref):
    block = pl.program_id(0)

    @pl.when(block == 0)
    def _():
        state_ref[...] = jnp.zeros_like(state_ref)

    start_ref[0] = state_ref[...]
    decay_rate = a_ref[...]
    fold = step_sum()

    def body(group, state):
        rows = pl.ds(pl.multiple_of(group * SUB, SUB), SUB)
        delta = delta_ref[rows, :]
        drive = delta * conv_ref[rows, :]
        b_tile = b_ref[group]
        c_tile = c_ref[group]
        reads = []
        for i in range(SUB):
            keep = keep_ref[block * SPAN + group * SUB + i]
            decay = jnp.exp(delta[i : i + 1, :] * decay_rate) * keep
            state = decay * state + drive[i : i + 1, :] * b_tile[:, i : i + 1]
            reads.append((state * c_tile[:, i : i + 1]).astype(SIXTEEN))
        y_ref[rows, :] = jnp.dot(
            fold, jnp.concatenate(reads, axis=0), preferred_element_type=WIDE
        )
        return state

    state_ref[...] = lax.fori_loop(0, SPAN // SUB, body, state_ref[...])


def time_tiles(values):
    return values.reshape(values.shape[0] // SUB, SUB, STATE).transpose(0, 2, 1)


def scan_forward(keep, conv_out, delta, b_in, c_read, decay_rate):
    length, lanes = conv_out.shape
    blocks = length // SPAN
    span_spec = pl.BlockSpec((SPAN, lanes), lambda i: (i, 0))
    tile_spec = pl.BlockSpec((SPAN // SUB, STATE, SUB), lambda i: (i, 0, 0))
    return pl.pallas_call(
        scan_forward_kernel,
        grid=(blocks,),
        in_specs=[
            pl.BlockSpec(memory_space=pltpu.SMEM),
            span_spec,
            span_spec,
            tile_spec,
            tile_spec,
            pl.BlockSpec((STATE, lanes), lambda i: (0, 0)),
        ],
        out_specs=[span_spec, pl.BlockSpec((1, STATE, lanes), lambda i: (i, 0, 0))],
        out_shape=[
            jax.ShapeDtypeStruct((length, lanes), WIDE),
            jax.ShapeDtypeStruct((blocks, STATE, lanes), WIDE),
        ],
        scratch_shapes=[pltpu.VMEM((STATE, lanes), WIDE)],
    )(keep, conv_out, delta, time_tiles(b_in), time_tiles(c_read), decay_rate)


def scan_backward_kernel(
    keep_ref, conv_ref, delta_ref, b_ref, c_ref, a_ref, start_ref, dy_ref,
    dconv_ref, ddelta_ref, db_ref, dc_ref, da_ref,
    state_ref, decay_ref, adjoint_ref,
):
    turn = pl.program_id(0)
    block = pl.num_programs(0) - 1 - turn

    @pl.when(turn == 0)
    def _():
        adjoint_ref[...] = jnp.zeros_like(adjoint_ref)
        da_ref[...] = jnp.zeros_like(da_ref)

    decay_rate = a_ref[...]
    fold = step_sum()
    lanes = decay_rate.shape[1]
    ones = jnp.ones((SUB, lanes), SIXTEEN)
    state_ref[0] = start_ref[0]

    def ahead(group, state):
        rows = pl.ds(pl.multiple_of(group * SUB, SUB), SUB)
        delta = delta_ref[rows, :]
        drive = delta * conv_ref[rows, :]
        b_tile = b_ref[group]
        for i in range(SUB):
            keep = keep_ref[block * SPAN + group * SUB + i]
            decay = jnp.exp(delta[i : i + 1, :] * decay_rate) * keep
            state = decay * state + drive[i : i + 1, :] * b_tile[:, i : i + 1]
            decay_ref[group * SUB + i] = decay
            state_ref[group * SUB + i + 1] = state
        return state

    lax.fori_loop(0, SPAN // SUB, ahead, start_ref[0])

    def back(step, carry):
        adjoint, da = carry
        group = SPAN // SUB - 1 - step
        rows = pl.ds(pl.multiple_of(group * SUB, SUB), SUB)
        delta = delta_ref[rows, :]
        conv = conv_ref[rows, :]
        drive = delta * conv
        dy = dy_ref[rows, :]
        b_tile = b_ref[group]
        c_tile = c_ref[group]
        by_c, by_b, by_drive, by_delta = ([None] * SUB for _ in range(4))
        for i in range(SUB - 1, -1, -1):
            index = group * SUB + i
            dy_row = dy[i : i + 1, :]
            total = adjoint + dy_row * c_tile[:, i : i + 1]
            by_c[i] = (dy_row * state_ref[index + 1]).astype(SIXTEEN)
            by_b[i] = (total * drive[i : i + 1, :]).astype(SIXTEEN)
            by_drive[i] = (total * b_tile[:, i : i + 1]).astype(SIXTEEN)
            adjoint = total * decay_ref[index]
            rate = adjoint * state_ref[index]
            by_delta[i] = (rate * decay_rate).astype(SIXTEEN)
            da = da + rate * delta[i : i + 1, :]
        def over_state(parts):
            return jnp.dot(fold, jnp.concatenate(parts, axis=0), preferred_element_type=WIDE)
        def over_lanes(parts):
            return lax.dot_general(
                ones, jnp.concatenate(parts, axis=0), (((1,), (1,)), ((), ())),
                preferred_element_type=WIDE,
            )
        d_drive = over_state(by_drive)
        dconv_ref[rows, :] = d_drive * delta
        ddelta_ref[rows, :] = over_state(by_delta) + d_drive * conv
        db_ref[group] = over_lanes(by_b)
        dc_ref[group] = over_lanes(by_c)
        return adjoint, da

    adjoint, da = lax.fori_loop(0, SPAN // SUB, back, (adjoint_ref[...], da_ref[...]))
    adjoint_ref[...] = adjoint
    da_ref[...] = da


def scan_backward(keep, conv_out, delta, b_in, c_read, decay_rate, starts, dy):
    length, lanes = conv_out.shape
    blocks = length // SPAN
    span_spec = pl.BlockSpec((SPAN, lanes), lambda i: (blocks - 1 - i, 0))
    tile_spec = pl.BlockSpec((SPAN // SUB, STATE, SUB), lambda i: (blocks - 1 - i, 0, 0))
    sums_spec = pl.BlockSpec((SPAN // SUB, SUB, SUB * STATE), lambda i: (blocks - 1 - i, 0, 0))
    whole = pl.BlockSpec((STATE, lanes), lambda i: (0, 0))
    sums = jax.ShapeDtypeStruct((length // SUB, SUB, SUB * STATE), WIDE)
    dconv, ddelta, db, dc, da = pl.pallas_call(
        scan_backward_kernel,
        grid=(blocks,),
        in_specs=[
            pl.BlockSpec(memory_space=pltpu.SMEM),
            span_spec,
            span_spec,
            tile_spec,
            tile_spec,
            whole,
            pl.BlockSpec((1, STATE, lanes), lambda i: (blocks - 1 - i, 0, 0)),
            span_spec,
        ],
        out_specs=[span_spec, span_spec, sums_spec, sums_spec, whole],
        out_shape=[
            jax.ShapeDtypeStruct((length, lanes), WIDE),
            jax.ShapeDtypeStruct((length, lanes), WIDE),
            sums,
            sums,
            jax.ShapeDtypeStruct((STATE, lanes), WIDE),
        ],
        scratch_shapes=[
            pltpu.VMEM((SPAN + 1, STATE, lanes), WIDE),
            pltpu.VMEM((SPAN, STATE, lanes), WIDE),
            pltpu.VMEM((STATE, lanes), WIDE),
        ],
        compiler_params=pltpu.CompilerParams(vmem_limit_bytes=32 * 1024 * 1024),
    )(keep, conv_out, delta, time_tiles(b_in), time_tiles(c_read), decay_rate, starts, dy)
    return dconv, ddelta, db[:, 0].reshape(length, STATE), dc[:, 0].reshape(length, STATE), da


def padded_lanes(array, lanes):
    return jnp.pad(array, ((0, 0), (0, lanes - array.shape[1])))


def rms_pull(values, scale, gain, d_normed, mean):
    d_values = scale * gain * d_normed - values * (scale * scale * scale) * mean
    return d_values, jnp.sum(d_normed * values * scale, axis=0)


def per_device(tokens, doc_ids, meta_tokens, mixer_params, small_params, ffn_params, cotangent):
    tokens, cotangent = tokens[0], cotangent[0]
    small_whole, ids = start_blocks(small_params, doc_ids[0])
    (g_one, g_two, g_attn, channel_part), small_pull = jax.vjp(small_shards, small_whole)
    (w_qkv, w_in, w_x, w_dt, w_out_a, w_out_m), mixer_pull = jax.vjp(mixer_shards, mixer_params)
    (w_gate, w_up, w_down), ffn_pull = jax.vjp(ffn_shards, ffn_params)
    channels = channel_part.shape[0]
    lanes = -(-channels // 128) * 128
    g_ssm = channel_part[:, 0]
    conv_w = channel_part[:, 1 : 1 + CONV].T
    conv_b = channel_part[:, 1 + CONV]
    dt_bias = channel_part[:, 2 + CONV]
    a_log = channel_part[:, 3 + CONV : 3 + CONV + STATE]
    d_skip = channel_part[:, 3 + CONV + STATE]

    length = ids.shape[0]
    positions = jnp.arange(length, dtype=jnp.int32)
    starts = jnp.concatenate([jnp.ones((1,), bool), ids[1:] != ids[:-1]])
    doc_first = lax.cummax(jnp.where(starts, positions, 0), axis=0)
    keep_mask = (positions != doc_first).astype(WIDE)
    lag_masks = jnp.stack(
        [(positions - j >= doc_first).astype(WIDE)[:, None] for j in range(CONV)]
    )

    tokens_f = tokens.astype(WIDE)
    normed_f, norm_pull = jax.vjp(rms_norm, tokens_f, g_one)
    meta_own = meta_tokens.astype(WIDE)
    meta_unit = rms_norm(lax.all_gather(meta_tokens, ("row", "seq"), axis=0, tiled=True).astype(WIDE), 1.0)
    normed = ring_seq_gather(normed_f.astype(SIXTEEN), 1)
    meta_normed = (meta_unit * g_one).astype(SIXTEEN)
    every = jnp.concatenate([normed, meta_normed], axis=0)
    cotangent_all = gather_seq(cotangent)

    xz = dot_last(normed, w_in).astype(SIXTEEN)
    extended = jnp.pad(xz[:, :channels], ((CONV - 1, 0), (0, 0))).astype(WIDE)
    conv_fn = partial(conv_piece, lag_masks=lag_masks)
    conv_out, conv_pull = jax.vjp(conv_fn, extended, conv_w, conv_b)
    conv_half = conv_out.astype(SIXTEEN)
    conv_f = conv_half.astype(WIDE)
    w_x_rows = jnp.pad(w_x.T, ((0, -w_x.shape[1] % 16), (0, 0)))
    projected = seq_sum(jnp.einsum("nc,tc->nt", w_x_rows, conv_half, preferred_element_type=WIDE), 2)
    rank_half = projected[:DT_RANK].T
    b_in = projected[DT_RANK : DT_RANK + STATE].T.astype(WIDE)
    c_read = projected[DT_RANK + STATE : DT_RANK + 2 * STATE].T.astype(WIDE)
    pre_dt = dot_last(rank_half, w_dt)
    delta, delta_pull = jax.vjp(lambda p, b: softplus_fn(p + b), pre_dt, dt_bias)
    a_neg, a_pull = jax.vjp(lambda a: -jnp.exp(a), a_log)
    scan_in = (
        keep_mask,
        padded_lanes(conv_f, lanes),
        padded_lanes(delta, lanes),
        b_in,
        c_read,
        padded_lanes(a_neg.T, lanes),
    )
    y_scan, scan_starts = scan_forward(*scan_in)

    def gate_piece(y, c, skip, z):
        return (y + skip * c) * silu_fn(z)

    z_in = xz[:, channels:].astype(WIDE)
    ssm_out, gate_pull = jax.vjp(gate_piece, y_scan[:, :channels], conv_f, d_skip, z_in)

    own_heads = g_attn.shape[0]
    queries = dot_last(normed, w_qkv[:, :own_heads]).astype(SIXTEEN)
    kv_rows = dot_last(every, w_qkv[:, own_heads:]).astype(SIXTEEN)
    attn_out, log_total = attend_forward(queries, kv_rows, doc_first)

    squares = jnp.stack([jnp.sum(attn_out * attn_out, axis=1), jnp.sum(ssm_out * ssm_out, axis=1)])
    squares = seq_sum_small(squares, 3)
    scale_a = lax.rsqrt(squares[0] / (HEADS * HEAD) + norm_eps)[:, None]
    scale_m = lax.rsqrt(squares[1] / INNER + norm_eps)[:, None]
    mixed = 0.5 * jnp.concatenate(
        [attn_out * scale_a * g_attn, ssm_out * scale_m * g_ssm], axis=1
    )
    mixed = mixed.astype(SIXTEEN)
    w_out = jnp.concatenate([w_out_a, w_out_m], axis=0)
    hidden = tokens_f + ring_seq_scatter(dot_last(mixed, w_out), 4)

    second_f, second_pull = jax.vjp(rms_norm, hidden, g_two)
    second = ring_seq_gather(second_f.astype(SIXTEEN), 5)
    gate_pre = dot_last(second, w_gate)
    up_pre = dot_last(second, w_up)
    act_f, act_pull = jax.vjp(glu_piece, gate_pre, up_pre)
    act = act_f.astype(SIXTEEN)
    d_gate, d_up = act_pull(dot_back(cotangent_all, w_down))
    d_gate, d_up = d_gate.astype(SIXTEEN), d_up.astype(SIXTEEN)
    d_second = ring_seq_scatter(dot_back(d_gate, w_gate) + dot_back(d_up, w_up), 6)
    block_out = (hidden + scatter_seq(dot_last(act, w_down))).astype(SIXTEEN)
    (grad_ffn,) = ffn_pull(
        (
            dot_weight(second, d_gate).astype(SIXTEEN),
            dot_weight(second, d_up).astype(SIXTEEN),
            dot_weight(act, cotangent_all).astype(SIXTEEN),
        )
    )
    d_hidden, grad_g_two = second_pull(d_second)
    d_hidden = d_hidden + cotangent.astype(WIDE)

    d_branch = ring_seq_gather(d_hidden.astype(SIXTEEN), 7)
    grad_out = dot_weight(mixed, d_branch)
    d_mixed = 0.5 * dot_back(d_branch, w_out)
    d_mix_a, d_mix_m = d_mixed[:, :own_heads], d_mixed[:, own_heads:]
    means = jnp.stack(
        [jnp.sum(attn_out * g_attn * d_mix_a, axis=1), jnp.sum(ssm_out * g_ssm * d_mix_m, axis=1)]
    )
    means = seq_sum_small(means, 8)
    d_attn, grad_g_attn = rms_pull(
        attn_out, scale_a, g_attn, d_mix_a, means[0][:, None] / (HEADS * HEAD)
    )
    d_ssm, grad_g_ssm = rms_pull(ssm_out, scale_m, g_ssm, d_mix_m, means[1][:, None] / INNER)

    d_queries, d_kv = attend_backward(
        queries, kv_rows, doc_first, attn_out, log_total, d_attn
    )

    d_y, d_conv, grad_d_skip, d_z = gate_pull(d_ssm)
    d_conv_scan, d_delta, d_b, d_c, d_rate = scan_backward(
        *scan_in, scan_starts, padded_lanes(d_y, lanes)
    )
    d_conv = d_conv + d_conv_scan[:, :channels]
    d_pre, grad_dt_bias = delta_pull(d_delta[:, :channels])
    (grad_a_log,) = a_pull(d_rate[:, :channels].T)
    d_pre = d_pre.astype(SIXTEEN)
    grad_dt = dot_weight(rank_half, d_pre)
    d_rank = jnp.einsum("rc,tc->rt", w_dt, d_pre, preferred_element_type=WIDE)
    d_proj = jnp.concatenate([d_rank, d_b.T, d_c.T], axis=0)
    d_proj = seq_sum(jnp.pad(d_proj, ((0, -d_proj.shape[0] % 16), (0, 0))), 10)
    d_proj = d_proj[: DT_RANK + 2 * STATE].T
    grad_x = dot_weight(conv_half, d_proj)
    d_extended, grad_conv_w, grad_conv_b = conv_pull(d_conv + dot_back(d_proj, w_x))
    d_xz = jnp.concatenate([d_extended[CONV - 1 :], d_z], axis=1).astype(SIXTEEN)
    grad_in = dot_weight(normed, d_xz)
    grad_qkv = jnp.concatenate([dot_weight(normed, d_queries), dot_weight(every, d_kv)], axis=1)
    d_meta = dot_back(d_kv[length:], w_qkv[:, own_heads:])
    d_normed = (
        dot_back(d_xz, w_in)
        + dot_back(d_queries, w_qkv[:, :own_heads])
        + dot_back(d_kv[:length], w_qkv[:, own_heads:])
    )
    grad_from_norm, grad_g_one = norm_pull(ring_seq_scatter(d_normed, 11))
    grad_tokens = d_hidden + grad_from_norm
    grad_g_meta = jnp.sum(d_meta * meta_unit, axis=0)
    grads = (grad_qkv, grad_in, grad_x, grad_dt, grad_out[:own_heads], grad_out[own_heads:])
    (grad_mixer,) = mixer_pull(tuple(g.astype(SIXTEEN) for g in grads))
    grad_channels = jnp.concatenate(
        [
            grad_g_ssm[:, None],
            grad_conv_w.T,
            grad_conv_b[:, None],
            grad_dt_bias[:, None],
            grad_a_log,
            grad_d_skip[:, None],
        ],
        axis=1,
    )
    (grad_small,) = small_pull((grad_g_one + grad_g_meta, grad_g_two, grad_g_attn, grad_channels))
    grad_small, d_meta = end_blocks(grad_small, d_meta)
    _, meta_pull = jax.vjp(lambda v: rms_norm(v, g_one), meta_own)
    (grad_meta,) = meta_pull(d_meta)
    return (
        block_out[None],
        grad_tokens[None],
        grad_meta,
        grad_mixer.astype(WIDE),
        grad_small,
        grad_ffn.astype(WIDE),
    )


def solution(mesh):
    in_specs = (
        P("row", "seq", None),
        P("row", "seq"),
        P(("row", "seq"), None),
        P(("row", "seq")),
        P(("row", "seq")),
        P(("row", "seq")),
        P("row", "seq", None),
    )
    out_specs = (
        P("row", "seq", None),
        P("row", "seq", None),
        P(("row", "seq"), None),
        P(("row", "seq")),
        P(("row", "seq")),
        P(("row", "seq")),
    )
    return jax.shard_map(
        per_device, mesh=mesh, in_specs=in_specs, out_specs=out_specs, check_vma=False
    )
```

```python
import functools
from functools import partial
import math

import jax
import jax.numpy as jnp
from jax import lax
from jax.experimental import pallas as pl
from jax.experimental.pallas import tpu as pltpu
from jax.sharding import PartitionSpec as P

D = 1600
HEADS = 25
GROUPS = 5
HEAD = 64
INNER = 3200
STATE = 16
CONV = 4
DT_RANK = 100
FF = 5504
REACH = 8
BLOCK = 128
RUNS = 4
SUB = 8
SPAN = 128
SIXTEEN = jnp.bfloat16
WIDE = jnp.float32


norm_eps = 1e-05


def split_flat(flat_vec, layout):
    pieces = []
    offset = 0
    for piece_shape in layout:
        piece_len = math.prod(piece_shape)
        pieces.append(flat_vec[offset : offset + piece_len].reshape(piece_shape))
        offset += piece_len
    return pieces


def mixer_layout():
    return [
        (D, HEADS * HEAD),
        (D, 2 * GROUPS * HEAD),
        (D, 2 * INNER),
        (INNER, DT_RANK + 2 * STATE),
        (DT_RANK, INNER),
        (HEADS * HEAD + INNER, D),
    ]


def ffn_layout():
    return [(D, FF), (D, FF), (FF, D)]


def small_split(flat_vec):
    width = CONV + STATE + 4
    packed_rows = flat_vec[: D * (3 + 2 * width)].reshape(D, 3 + 2 * width)
    channel_part = packed_rows[:, 3:].reshape(INNER, width)
    return packed_rows[:, 0], packed_rows[:, 1], packed_rows[:, 2], channel_part


def rms_norm(values, gain_vec):
    return (
        values * lax.rsqrt(jnp.mean(values * values, axis=-1, keepdims=True) + norm_eps) * gain_vec
    )


def silu_fn(values):
    return values / (1.0 + jnp.exp(-values))


def softplus_fn(values):
    return jnp.maximum(values, 0.0) + jnp.log1p(jnp.exp(-jnp.abs(values)))


def glu_piece(gate_pre, up_pre):
    return silu_fn(gate_pre) * up_pre


def dot_last(left, right):
    return jnp.einsum("...k,kn->...n", left, right, preferred_element_type=WIDE)


def dot_back(grads, right):
    return jnp.einsum("...n,kn->...k", grads, right, preferred_element_type=WIDE)


def dot_weight(left, grads):
    return jnp.einsum("...k,...n->kn", left, grads, preferred_element_type=WIDE)


def heads_of(shards):
    return -(-HEADS // shards)


def runs_of(shards):
    return RUNS if INNER % (RUNS * shards) == 0 else 1


def own_channels(array, axis, shards, place):
    runs = runs_of(shards)
    unit = INNER // (runs * shards)
    shape = array.shape
    cut = array.reshape(shape[:axis] + (runs, shards, unit) + shape[axis + 1 :])
    cut = lax.dynamic_index_in_dim(cut, place, axis + 1, keepdims=False)
    return cut.reshape(shape[:axis] + (runs * unit,) + shape[axis + 1 :])


def pad_heads(array, axis, shards):
    heads = heads_of(shards)
    pads = [(0, 0)] * array.ndim
    pads[axis] = (0, heads * shards - HEADS)
    padded = jnp.pad(array, pads)
    shape = padded.shape
    return padded.reshape(shape[:axis] + (shards, heads * HEAD) + shape[axis + 2 :])


def by_head(w_q, w_kv, shards):
    rows = w_q.shape[0]
    w_kv = w_kv.reshape(rows, 2, GROUPS, 1, HEAD)
    w_kv = jnp.broadcast_to(w_kv, (rows, 2, GROUPS, HEADS // GROUPS, HEAD))
    w_kv = w_kv.reshape(rows, 2, HEADS, HEAD)
    return jnp.concatenate(
        [
            pad_heads(w_q.reshape(rows, HEADS, HEAD), 1, shards),
            pad_heads(w_kv[:, 0], 1, shards),
            pad_heads(w_kv[:, 1], 1, shards),
        ],
        axis=2,
    )


def exchange(value):
    return lax.all_to_all(value, "seq", 0, 0)


def both_halves(value):
    if lax.axis_size("row") != 2:
        return lax.all_gather(value, "row", axis=0, tiled=True)
    other = lax.ppermute(value, "row", [(0, 1), (1, 0)])
    first = lax.axis_index("row") == 0
    return jnp.concatenate(
        [jnp.where(first, value, other), jnp.where(first, other, value)], axis=0
    )


def mixer_fits(length, shards):
    width = INNER // RUNS
    sizes = [math.prod(shape) for shape in mixer_layout()]
    return (
        runs_of(shards) == RUNS
        and length % width == 0
        and all(size % width == 0 for size in sizes)
        and D % shards == 0
        and (HEADS * HEAD * 2) % shards == 0
        and shards % x_turns(shards)[0] == 0
    )


def mixer_shards_whole(piece):
    shards, place = lax.axis_size("seq"), lax.axis_index("seq")
    whole = lax.all_gather(piece, ("row", "seq"), axis=0, tiled=True)
    w_q, w_kv, w_in, w_x, w_dt, w_out = split_flat(whole, mixer_layout())
    qkv = lax.dynamic_index_in_dim(by_head(w_q, w_kv, shards), place, 1, keepdims=False)
    w_in = own_channels(w_in.reshape(D, 2, INNER), 2, shards, place)
    out_heads = w_out[: HEADS * HEAD].reshape(HEADS, HEAD, D)
    out_heads = lax.dynamic_index_in_dim(pad_heads(out_heads, 0, shards), place, 0, keepdims=False)
    return (
        qkv,
        w_in.reshape(D, -1),
        own_channels(w_x, 0, shards, place),
        own_channels(w_dt, 1, shards, place),
        jnp.concatenate([out_heads, own_channels(w_out[HEADS * HEAD :], 0, shards, place)], axis=0),
    )


def mixer_columns(piece):
    shards = lax.axis_size("seq")
    if not mixer_fits(piece.shape[0], shards):
        return piece
    unit = INNER // (RUNS * shards)
    return exchange(piece.reshape(-1, shards, unit).transpose(1, 0, 2)).reshape(-1, unit)


def mixer_shards(mine, length):
    shards, place = lax.axis_size("seq"), lax.axis_index("seq")
    if not mixer_fits(length, shards):
        return mixer_shards_whole(mine)
    width = INNER // RUNS
    unit = width // shards
    mine = both_halves(mine)
    part_q, part_kv, part_in, part_x, part_dt, part_out = cut_rows(
        mine, [math.prod(shape) // width for shape in mixer_layout()]
    )
    w_in = part_in.reshape(D, -1)
    w_dt = part_dt.reshape(DT_RANK, -1)
    rows = D // shards
    by_rows = exchange(
        jnp.concatenate(
            [
                part_q.reshape(shards, -1, unit),
                part_kv.reshape(shards, -1, unit),
                x_windows(part_x, shards),
            ],
            axis=1,
        )
    )
    by_rows = by_rows.transpose(1, 0, 2).reshape(-1, width)
    split, end = part_q.shape[0] // shards, (part_q.shape[0] + part_kv.shape[0]) // shards
    w_x = x_from_windows(by_rows[end:], place)
    cut = by_head(
        by_rows[:split].reshape(rows, HEADS * HEAD),
        by_rows[split:end].reshape(rows, 2 * GROUPS * HEAD),
        shards,
    )
    qkv = exchange(cut.transpose(1, 0, 2)).reshape(D, -1)
    per_row = D // width
    head_rows = heads_of(shards) * HEAD
    out_heads = part_out[: HEADS * HEAD * per_row]
    out_heads = jnp.pad(
        out_heads, ((0, (head_rows * shards - HEADS * HEAD) * per_row), (0, 0))
    ).reshape(shards, -1, unit)
    out_inner = part_out[HEADS * HEAD * per_row :].reshape(RUNS, shards, -1, unit)
    out_inner = out_inner.transpose(1, 0, 2, 3).reshape(shards, -1, unit)
    out_both = exchange(jnp.concatenate([out_heads, out_inner], axis=1))
    out_both = out_both.transpose(1, 0, 2).reshape(-1, D)
    return qkv, w_in, w_x, w_dt, out_both


def x_turns(shards):
    width = INNER // RUNS
    run = (width // shards) * (DT_RANK + 2 * STATE)
    common = math.gcd(run, width)
    return width // common, run // common


def x_windows(part_x, shards):
    runs, rows = x_turns(shards)
    need = -(-rows // runs)
    turns = part_x.reshape(-1, rows, part_x.shape[1])
    cuts = [turns[:, (i * rows) // runs : (i * rows) // runs + need] for i in range(runs)]
    cuts = jnp.stack(cuts, axis=1).reshape(RUNS, shards, need, part_x.shape[1])
    return cuts.transpose(1, 0, 2, 3).reshape(shards, RUNS * need, part_x.shape[1])


def x_from_windows(view_rows, place):
    width = view_rows.shape[1]
    shards = lax.axis_size("seq")
    runs, rows = x_turns(shards)
    columns = DT_RANK + 2 * STATE
    count = (width // shards) * columns
    flat = view_rows.reshape(RUNS, -1)
    offset = (place % runs) * rows * (width // runs) % width
    return lax.dynamic_slice_in_dim(flat, offset, count, 1).reshape(-1, columns)


def cut_rows(array, counts):
    pieces, offset = [], 0
    for count in counts:
        pieces.append(array[offset : offset + count])
        offset += count
    return pieces


def ffn_shards(piece):
    shards, place = lax.axis_size("seq"), lax.axis_index("seq")
    unit = FF // shards
    if piece.shape[0] % FF or D % shards:
        whole = lax.all_gather(piece, ("row", "seq"), axis=0, tiled=True)
        w_gate, w_up, w_down = split_flat(whole, ffn_layout())
        return (
            lax.dynamic_slice_in_dim(w_gate, place * unit, unit, 1),
            lax.dynamic_slice_in_dim(w_up, place * unit, unit, 1),
            lax.dynamic_slice_in_dim(w_down, place * unit, unit, 0),
        )
    mine = exchange(piece.reshape(-1, shards, unit).transpose(1, 0, 2))
    mine = both_halves(mine.reshape(-1, unit))
    w_gate, w_up, part_down = cut_rows(mine, [D, D, D])
    w_down = exchange(part_down.reshape(shards, -1, unit))
    return w_gate, w_up, w_down.transpose(1, 0, 2).reshape(unit, D)


def small_shards(whole):
    shards, place = lax.axis_size("seq"), lax.axis_index("seq")
    g_one, g_attn, g_two, channel_part = small_split(whole)
    g_attn = pad_heads(g_attn.reshape(HEADS, HEAD), 0, shards)
    return (
        g_one,
        g_two,
        lax.dynamic_index_in_dim(g_attn, place, 0, keepdims=False),
        own_channels(channel_part, 0, shards, place),
    )


def tiles_of(count):
    return -(-count // 128)


def start_blocks(small_params, doc_ids, meta_tokens):
    devices = lax.axis_size("row") * lax.axis_size("seq")
    parts = [small_params, doc_ids.astype(SIXTEEN), meta_tokens.reshape(-1)]
    rows = [tiles_of(part.shape[0]) for part in parts]
    rows_all = -(-sum(rows) // 16) * 16
    tiles = [
        jnp.pad(part, (0, count * 128 - part.shape[0])).reshape(-1, 128)
        for part, count in zip(parts, rows)
    ]
    block = jnp.concatenate(tiles + [jnp.zeros((rows_all - sum(rows), 128), SIXTEEN)], axis=0)
    every = push_gather(block, 0)
    outs, begin = [], 0
    for part, count in zip(parts, rows):
        cut = every[:, begin : begin + count].reshape(devices, -1)[:, : part.shape[0]]
        outs.append(cut)
        begin += count
    ids = outs[1].reshape(lax.axis_size("row"), -1)
    ids = lax.dynamic_index_in_dim(ids, lax.axis_index("row"), 0, keepdims=False)
    return outs[0].reshape(-1).astype(WIDE), ids.astype(jnp.int32), outs[2].reshape(-1, D)


def end_blocks(grad_small, d_meta):
    devices = lax.axis_size("row") * lax.axis_size("seq")
    parts = grad_small.reshape(devices, -1).astype(SIXTEEN)
    small_count = parts.shape[1]
    small_rows = tiles_of(small_count)
    parts = jnp.pad(parts, ((0, 0), (0, small_rows * 128 - small_count)))
    meta = d_meta.astype(SIXTEEN).reshape(devices, -1)
    meta_count = meta.shape[1]
    rows = -(-(small_rows + tiles_of(meta_count)) // 16) * 16
    meta = jnp.pad(meta, ((0, 0), (0, (rows - small_rows) * 128 - meta_count)))
    blocks = jnp.concatenate(
        [parts.reshape(devices, -1, 128), meta.reshape(devices, -1, 128)], axis=1
    )
    own = push_scatter(blocks, 9)
    small = own[:small_rows].reshape(-1)[:small_count]
    meta = own[small_rows:].reshape(-1)[:meta_count].reshape(-1, D)
    return small, meta


def gather_seq(block):
    return lax.all_gather(block, "seq", axis=0, tiled=True)


def scatter_seq(whole):
    return lax.psum_scatter(whole.astype(SIXTEEN), "seq", scatter_dimension=0, tiled=True).astype(
        WIDE
    )


MESH = pl.DeviceIdType.MESH
ANY = pl.BlockSpec(memory_space=pl.ANY)
VMEM = pl.BlockSpec(memory_space=pltpu.VMEM)
MIB = 1024 * 1024


def greet(peers):
    barrier = pltpu.get_barrier_semaphore()
    for peer in peers:
        pl.semaphore_signal(barrier, inc=1, device_id=peer, device_id_type=MESH)
    pl.semaphore_wait(barrier, len(peers))


def ring_place(chip, chips):
    odd = chip % 2
    return odd * (chips - 1 - chip // 2) + (1 - odd) * (chip // 2)


def ring_chip(place, chips):
    place = (place + 2 * chips) % chips
    back = place // (chips // 2)
    return back * (2 * (chips - 1 - place) + 1) + (1 - back) * (2 * place)


def seq_gather_kernel(shards, parts, x_ref, out_ref, ring_send, ring_recv, pair_send, pair_recv, own_sem):
    row, me = lax.axis_index("row"), lax.axis_index("seq")
    chips = shards // 2
    core = me % 2
    place = ring_place(me // 2, chips)

    def device(spot):
        return ring_chip(spot, chips) * 2 + core

    right, left, twin = (row, device(place + 1)), (row, device(place - 1)), (row, me + 1 - 2 * core)
    greet([right, left, twin])
    rows = x_ref.shape[0] // (2 * parts)

    def cut(way, part):
        return pl.ds((way * parts + part) * rows, rows)

    own = pltpu.make_async_copy(x_ref, out_ref.at[me], own_sem)
    own.start()
    started = []

    def send(src, dst, send_sem, recv_sem, to):
        copy = pltpu.make_async_remote_copy(
            src_ref=src, dst_ref=dst, send_sem=send_sem, recv_sem=recv_sem,
            device_id=to, device_id_type=MESH,
        )
        copy.start()
        started.append(copy)
        return copy

    paths = [(way, part) for part in range(parts) for way in range(2)]
    flights = {}
    for way, part in paths:
        flights[way, part] = send(
            x_ref.at[cut(way, part)], out_ref.at[me, cut(way, part)],
            ring_send.at[way, part, 0], ring_recv.at[way, part, 0], (right, left)[way],
        )
    pairs = [send(x_ref, out_ref.at[me], pair_send.at[0, 0, chips - 1], pair_recv.at[0, 0, chips - 1], twin)]
    for step in range(chips - 1):
        for way, part in paths:
            flights[way, part].wait_recv()
            source = device(place - 1 - step if way == 0 else place + 1 + step)
            here = out_ref.at[source, cut(way, part)]
            if step < chips - 2:
                flights[way, part] = send(
                    here, here, ring_send.at[way, part, step + 1],
                    ring_recv.at[way, part, step + 1], (right, left)[way],
                )
            pairs.append(
                send(here, here, pair_send.at[way, part, step], pair_recv.at[way, part, step], twin)
            )
    own.wait()
    for copy in started:
        copy.wait_send()
    for copy in pairs:
        copy.wait_recv()


def ring_seq_gather(block, collective_id, parts=2):
    shards = lax.axis_size("seq")
    chips = shards // 2
    rows, width = block.shape
    ring = pltpu.SemaphoreType.DMA((2, parts, chips - 1))
    pair = pltpu.SemaphoreType.DMA((2, parts, chips))
    gathered = pl.pallas_call(
        functools.partial(seq_gather_kernel, shards, parts),
        out_shape=jax.ShapeDtypeStruct((shards, rows, width), block.dtype),
        in_specs=[ANY],
        out_specs=ANY,
        scratch_shapes=[ring, ring, pair, pair, pltpu.SemaphoreType.DMA],
        compiler_params=pltpu.CompilerParams(collective_id=collective_id, has_side_effects=True),
        cost_estimate=pl.CostEstimate(flops=0, bytes_accessed=120 * MIB, transcendentals=0),
    )(block)
    return gathered.reshape(shards * rows, width)


def product_scatter_kernel(shards, parts, turned, *refs):
    terms = len(turned)
    lefts, rights = refs[:terms], refs[terms : 2 * terms]
    out_ref, mine, given, pair, arrived = refs[2 * terms : 2 * terms + 5]
    ring_send, ring_recv, pair_send, pair_recv = refs[2 * terms + 5 :]
    row, me = lax.axis_index("row"), lax.axis_index("seq")
    chips = shards // 2
    core = me % 2
    place = ring_place(me // 2, chips)
    block_rows = out_ref.shape[0]

    def device(spot, core):
        return ring_chip(spot, chips) * 2 + core

    right = (row, device(place + 1, core))
    left = (row, device(place - 1, core))
    twin = (row, me + 1 - 2 * core)
    greet([right, left, twin])
    rows = block_rows // (2 * parts)

    def cut(way, part):
        return pl.ds((way * parts + part) * rows, rows)

    def product(index):
        here = pl.ds(pl.multiple_of(index * block_rows, block_rows), block_rows)
        total = None
        for left_ref, right_ref, turn in zip(lefts, rights, turned):
            part = lax.dot_general(
                left_ref[here, :], right_ref[...], (((1,), (1 if turn else 0,)), ((), ())),
                preferred_element_type=WIDE,
            )
            total = part if total is None else total + part
        return total.astype(SIXTEEN)

    def pass_over(slot):
        return pltpu.make_async_remote_copy(
            src_ref=given.at[slot], dst_ref=pair.at[slot], send_sem=pair_send.at[slot],
            recv_sem=pair_recv.at[slot], device_id=twin, device_id_type=MESH,
        )

    def make(far):
        slot = far % chips
        given[slot] = product(device(place + far, 1 - core))
        pass_over(slot).start()
        mine[slot] = product(device(place + far, core))

    def both(step, carry):
        make(-step)
        make(step)
        return carry

    half = chips // 2
    both(1, 0)
    started, flights = [], {}
    fresh = set(range(chips))
    for step in range(chips):
        if step + 2 < half:
            both(step + 2, 0)
        elif step + 2 == half:
            make(half)
            make(0)
        for part in range(parts):
            for way in range(2):
                slot = (-1 - step if way == 0 else 1 + step) % chips
                if slot in fresh:
                    fresh.remove(slot)
                    pass_over(slot).wait_recv()
                here = cut(way, part)
                total = mine[slot, here, :].astype(WIDE) + pair[slot, here, :].astype(WIDE)
                if step:
                    flights[way, part].wait_recv()
                    total = total + arrived[way, step - 1, pl.ds(part * rows, rows), :].astype(WIDE)
                if step == chips - 1:
                    out_ref[here, :] = total
                    continue
                mine[slot, here, :] = total.astype(SIXTEEN)
                copy = pltpu.make_async_remote_copy(
                    src_ref=mine.at[slot, here], dst_ref=arrived.at[way, step, pl.ds(part * rows, rows)],
                    send_sem=ring_send.at[way, part, step], recv_sem=ring_recv.at[way, part, step],
                    device_id=(right, left)[way], device_id_type=MESH,
                )
                copy.start()
                started.append(copy)
                flights[way, part] = copy
    for slot in range(chips):
        pass_over(slot).wait_send()
    for copy in started:
        copy.wait_send()


def padded_bytes(shape, bytes_each):
    return -(-shape[0] // 16) * 16 * -(-shape[1] // 128) * 128 * bytes_each


def product_scatter(terms, collective_id, parts=2):
    shards = lax.axis_size("seq")
    chips = shards // 2
    length = terms[0][0].shape[0]
    width = terms[0][1].shape[0 if terms[0][2] else 1]
    rows = length // shards
    buffers = 4 * chips * padded_bytes((rows, width), 2)
    operands = sum(padded_bytes(t[0].shape, 2) + padded_bytes(t[1].shape, 2) for t in terms)
    if chips < 4 or buffers + operands > 40 * MIB:
        total = 0
        for left, right, turn in terms:
            total = total + lax.dot_general(
                left, right, (((1,), (1 if turn else 0,)), ((), ())), preferred_element_type=WIDE
            )
        return lax.psum_scatter(
            total.astype(SIXTEEN), "seq", scatter_dimension=0, tiled=True
        ).astype(WIDE)
    ring = pltpu.SemaphoreType.DMA((2, parts, chips - 1))
    pair = pltpu.SemaphoreType.DMA((chips,))
    blocks = pltpu.VMEM((chips, rows, width), SIXTEEN)
    return pl.pallas_call(
        functools.partial(product_scatter_kernel, shards, parts, tuple(t[2] for t in terms)),
        out_shape=jax.ShapeDtypeStruct((rows, width), WIDE),
        in_specs=[VMEM] * (2 * len(terms)),
        out_specs=VMEM,
        scratch_shapes=[
            blocks, blocks, blocks,
            pltpu.VMEM((2, chips - 1, rows // 2, width), SIXTEEN),
            ring, ring, pair, pair,
        ],
        compiler_params=pltpu.CompilerParams(
            collective_id=collective_id, has_side_effects=True, vmem_limit_bytes=56 * MIB
        ),
        cost_estimate=pl.CostEstimate(flops=0, bytes_accessed=120 * MIB, transcendentals=0),
    )(*[t[0] for t in terms], *[t[1] for t in terms])


def bits_of(shards):
    bits = shards.bit_length() - 1
    assert 1 << bits == shards
    return bits


def partner_of(me, bit):
    return me + (1 - 2 * ((me // (1 << bit)) % 2)) * (1 << bit)


def seq_sum_kernel(bits, x_ref, out_ref, total, staged, arrived, send_sem, recv_sem, back_send, back_recv):
    row, me = lax.axis_index("row"), lax.axis_index("seq")
    partners = [(row, partner_of(me, bit)) for bit in range(bits)]
    greet(partners)
    length = x_ref.shape[1]
    total[...] = x_ref[...].astype(WIDE)
    begin = 0
    started = []
    for bit in range(bits):
        half = length >> (bit + 1)
        upper = (me // (1 << bit)) % 2
        kept = pl.multiple_of(begin + upper * half, 128)
        given = pl.multiple_of(begin + (1 - upper) * half, 128)
        staged[:, half : 2 * half] = total[:, pl.ds(given, half)].astype(SIXTEEN)
        copy = pltpu.make_async_remote_copy(
            src_ref=staged.at[:, half : 2 * half], dst_ref=arrived.at[:, half : 2 * half],
            send_sem=send_sem.at[bit], recv_sem=recv_sem.at[bit],
            device_id=partners[bit], device_id_type=MESH,
        )
        copy.start()
        started.append(copy)
        copy.wait_recv()
        total[:, pl.ds(kept, half)] += arrived[:, half : 2 * half].astype(WIDE)
        begin = kept
    half = length >> bits
    out_ref[:, pl.ds(pl.multiple_of(begin, 128), half)] = total[
        :, pl.ds(pl.multiple_of(begin, 128), half)
    ].astype(SIXTEEN)
    for bit in range(bits - 1, -1, -1):
        half = length >> (bit + 1)
        here = out_ref.at[:, pl.ds(pl.multiple_of(begin, 128), half)]
        copy = pltpu.make_async_remote_copy(
            src_ref=here, dst_ref=here, send_sem=back_send.at[bit], recv_sem=back_recv.at[bit],
            device_id=partners[bit], device_id_type=MESH,
        )
        copy.start()
        started.append(copy)
        copy.wait_recv()
        begin = begin - ((me // (1 << bit)) % 2) * half
    for copy in started:
        copy.wait_send()


def seq_sum(values, collective_id):
    bits = bits_of(lax.axis_size("seq"))
    rows, length = values.shape
    sems = pltpu.SemaphoreType.DMA((bits,))
    return pl.pallas_call(
        functools.partial(seq_sum_kernel, bits),
        out_shape=jax.ShapeDtypeStruct((rows, length), SIXTEEN),
        in_specs=[VMEM],
        out_specs=VMEM,
        scratch_shapes=[
            pltpu.VMEM((rows, length), WIDE),
            pltpu.VMEM((rows, length), SIXTEEN),
            pltpu.VMEM((rows, length), SIXTEEN),
            sems, sems, sems, sems,
        ],
        compiler_params=pltpu.CompilerParams(
            collective_id=collective_id, has_side_effects=True, vmem_limit_bytes=48 * MIB
        ),
    )(values)


def seq_sum_small_kernel(bits, x_ref, out_ref, arrived, staged, send_sem, recv_sem):
    row, me = lax.axis_index("row"), lax.axis_index("seq")
    partners = [(row, partner_of(me, bit)) for bit in range(bits)]
    greet(partners)
    total = x_ref[...]
    copies = []
    for bit in range(bits):
        staged[bit] = total
        copy = pltpu.make_async_remote_copy(
            src_ref=staged.at[bit], dst_ref=arrived.at[bit], send_sem=send_sem.at[bit],
            recv_sem=recv_sem.at[bit], device_id=partners[bit], device_id_type=MESH,
        )
        copy.start()
        copies.append(copy)
        copy.wait_recv()
        total = total + arrived[bit]
    out_ref[...] = total
    for copy in copies:
        copy.wait_send()


def seq_sum_small(values, collective_id):
    bits = bits_of(lax.axis_size("seq"))
    shape = values.shape
    tiles = values.reshape(-1, 128)
    sems = pltpu.SemaphoreType.DMA((bits,))
    slots = pltpu.VMEM((bits,) + tiles.shape, WIDE)
    return pl.pallas_call(
        functools.partial(seq_sum_small_kernel, bits),
        out_shape=jax.ShapeDtypeStruct(tiles.shape, WIDE),
        in_specs=[VMEM],
        out_specs=VMEM,
        scratch_shapes=[slots, slots, sems, sems],
        compiler_params=pltpu.CompilerParams(collective_id=collective_id, has_side_effects=True),
    )(tiles).reshape(shape)


def all_peers(rows, shards):
    me = lax.axis_index("row") * shards + lax.axis_index("seq")
    count = rows * shards
    ahead = [(me + far) % count for far in range(1, count)]
    return me, count, [(other, (other // shards, other % shards)) for other in ahead]


def push_gather_kernel(rows, shards, x_ref, out_ref, send_sem, recv_sem):
    me, count, peers = all_peers(rows, shards)
    greet([device for _, device in peers])
    copies = []
    for far, (_, device) in enumerate(peers):
        copy = pltpu.make_async_remote_copy(
            src_ref=x_ref, dst_ref=out_ref.at[me], send_sem=send_sem.at[far],
            recv_sem=recv_sem.at[far], device_id=device, device_id_type=MESH,
        )
        copy.start()
        copies.append(copy)
    out_ref[me] = x_ref[...]
    for copy in copies:
        copy.wait()


def push_gather(block, collective_id):
    rows, shards = lax.axis_size("row"), lax.axis_size("seq")
    sems = pltpu.SemaphoreType.DMA((rows * shards - 1,))
    return pl.pallas_call(
        functools.partial(push_gather_kernel, rows, shards),
        out_shape=jax.ShapeDtypeStruct((rows * shards,) + block.shape, block.dtype),
        in_specs=[VMEM],
        out_specs=VMEM,
        scratch_shapes=[sems, sems],
        compiler_params=pltpu.CompilerParams(collective_id=collective_id, has_side_effects=True),
    )(block)


def push_scatter_kernel(rows, shards, x_ref, out_ref, arrived, send_sem, recv_sem):
    me, count, peers = all_peers(rows, shards)
    greet([device for _, device in peers])
    copies = []
    for far, (other, device) in enumerate(peers):
        copy = pltpu.make_async_remote_copy(
            src_ref=x_ref.at[other], dst_ref=arrived.at[far], send_sem=send_sem.at[far],
            recv_sem=recv_sem.at[far], device_id=device, device_id_type=MESH,
        )
        copy.start()
        copies.append(copy)
    total = x_ref[me].astype(WIDE)
    for far, copy in enumerate(copies):
        copy.wait_recv()
        total = total + arrived[far].astype(WIDE)
    out_ref[...] = total
    for copy in copies:
        copy.wait_send()


def push_scatter(blocks, collective_id):
    rows, shards = lax.axis_size("row"), lax.axis_size("seq")
    count = rows * shards
    sems = pltpu.SemaphoreType.DMA((count - 1,))
    return pl.pallas_call(
        functools.partial(push_scatter_kernel, rows, shards),
        out_shape=jax.ShapeDtypeStruct(blocks.shape[1:], WIDE),
        in_specs=[VMEM],
        out_specs=VMEM,
        scratch_shapes=[pltpu.VMEM((count - 1,) + blocks.shape[1:], blocks.dtype), sems, sems],
        compiler_params=pltpu.CompilerParams(
            collective_id=collective_id, has_side_effects=True, vmem_limit_bytes=32 * MIB
        ),
    )(blocks)


def conv_piece(extended, conv_w, conv_b, lag_masks):
    length = extended.shape[0] - (CONV - 1)
    summed = conv_b
    for j in range(CONV):
        summed = (
            summed + conv_w[j] * extended[CONV - 1 - j : CONV - 1 - j + length] * lag_masks[j]
        )
    return silu_fn(summed)


def nt_dot(left, right):
    return lax.dot_general(left, right, (((1,), (1,)), ((), ())), preferred_element_type=WIDE)


def seen_keys(block, first_row):
    window = (REACH + 1) * BLOCK
    k_pos = (block - REACH) * BLOCK + lax.broadcasted_iota(jnp.int32, (window, BLOCK), 0)
    q_pos = block * BLOCK + lax.broadcasted_iota(jnp.int32, (window, BLOCK), 1)
    return (k_pos >= first_row) & (k_pos <= q_pos) & (k_pos > q_pos - REACH * BLOCK)


def attend_forward_kernel(heads, first_ref, q_ref, kv_ref, turned_ref, meta_ref, meta_turned_ref, out_ref, total_ref):
    block = pl.program_id(0)
    span = pl.ds(pl.multiple_of(block * BLOCK, BLOCK), (REACH + 1) * BLOCK)
    seen = seen_keys(block, first_ref[0])
    outs, totals = [], []
    for h in range(heads):
        cut = slice(h * HEAD, (h + 1) * HEAD)
        v_cut = slice((heads + h) * HEAD, (heads + h + 1) * HEAD)
        query = q_ref[:, cut] * SIXTEEN(HEAD ** (-0.5))
        near = jnp.where(seen, nt_dot(kv_ref[span, cut], query), -1e30)
        meta = nt_dot(meta_ref[:, cut], query)
        top = jnp.maximum(
            jnp.max(near, axis=0, keepdims=True), jnp.max(meta, axis=0, keepdims=True)
        )
        near = jnp.exp(near - top)
        meta = jnp.exp(meta - top)
        total = jnp.sum(near, axis=0, keepdims=True) + jnp.sum(meta, axis=0, keepdims=True)
        out = jnp.dot(turned_ref[v_cut, span], near.astype(SIXTEEN), preferred_element_type=WIDE)
        out += jnp.dot(meta_turned_ref[v_cut, :], meta.astype(SIXTEEN), preferred_element_type=WIDE)
        outs.append(out / total)
        totals.append(top + jnp.log(total))
    out_ref[...] = jnp.concatenate(outs, axis=0).T
    total_ref[0] = jnp.concatenate(totals, axis=0)


def attend_backward_kernel(
    heads, first_ref, q_ref, kv_ref, turned_ref, meta_ref, meta_turned_ref, out_ref, total_ref, do_ref,
    dq_ref, dkv_ref, dmeta_ref,
):
    block = pl.program_id(0)

    @pl.when(block == 0)
    def _():
        dkv_ref[...] = jnp.zeros_like(dkv_ref)
        dmeta_ref[...] = jnp.zeros_like(dmeta_ref)

    span = pl.ds(pl.multiple_of(block * BLOCK, BLOCK), (REACH + 1) * BLOCK)
    seen = seen_keys(block, first_ref[0])
    d_out = do_ref[...]
    row_sums = (d_out * out_ref[...]).T
    d_half = d_out.astype(SIXTEEN)
    d_queries, near_k, near_v, meta_k, meta_v = [], [], [], [], []
    for h in range(heads):
        cut = slice(h * HEAD, (h + 1) * HEAD)
        v_cut = slice((heads + h) * HEAD, (heads + h + 1) * HEAD)
        query = q_ref[:, cut] * SIXTEEN(HEAD ** (-0.5))
        do = d_half[:, cut]
        total = total_ref[0, h : h + 1, :]
        mean = jnp.sum(row_sums[cut], axis=0, keepdims=True)
        near = jnp.where(seen, jnp.exp(nt_dot(kv_ref[span, cut], query) - total), 0.0)
        meta = jnp.exp(nt_dot(meta_ref[:, cut], query) - total)
        d_near = (near * (nt_dot(kv_ref[span, v_cut], do) - mean)).astype(SIXTEEN)
        d_meta = (meta * (nt_dot(meta_ref[:, v_cut], do) - mean)).astype(SIXTEEN)
        near_v.append(jnp.dot(near.astype(SIXTEEN), do, preferred_element_type=WIDE))
        meta_v.append(jnp.dot(meta.astype(SIXTEEN), do, preferred_element_type=WIDE))
        near_k.append(jnp.dot(d_near, query, preferred_element_type=WIDE))
        meta_k.append(jnp.dot(d_meta, query, preferred_element_type=WIDE))
        d_query = jnp.dot(turned_ref[cut, span], d_near, preferred_element_type=WIDE)
        d_query += jnp.dot(meta_turned_ref[cut, :], d_meta, preferred_element_type=WIDE)
        d_queries.append(d_query * HEAD ** (-0.5))
    dq_ref[...] = jnp.concatenate(d_queries, axis=0).T.astype(SIXTEEN)
    dkv_ref[span, :] += jnp.concatenate(near_k + near_v, axis=1)
    dmeta_ref[...] += jnp.concatenate(meta_k + meta_v, axis=1)


def attend_operands(queries, kv_rows, doc_first):
    length = doc_first.shape[0]
    count = length // BLOCK
    near = jnp.pad(kv_rows[:length], ((REACH * BLOCK, 0), (0, 0)))
    meta = kv_rows[length:]
    arrays = (doc_first.reshape(count, 1, BLOCK), queries, near, near.T, meta, meta.T)
    width = queries.shape[1]

    def whole(array):
        return pl.BlockSpec(array.shape, lambda i: (0,) * array.ndim)

    specs = [
        pl.BlockSpec((1, 1, BLOCK), lambda i: (i, 0, 0)),
        pl.BlockSpec((BLOCK, width), lambda i: (i, 0)),
    ] + [whole(a) for a in arrays[2:]]
    return arrays, specs, count, width


def attend_forward(queries, kv_rows, doc_first):
    arrays, specs, count, width = attend_operands(queries, kv_rows, doc_first)
    heads = width // HEAD
    return pl.pallas_call(
        lambda *refs: attend_forward_kernel(heads, *refs),
        grid=(count,),
        in_specs=specs,
        out_specs=[
            pl.BlockSpec((BLOCK, width), lambda i: (i, 0)),
            pl.BlockSpec((1, heads, BLOCK), lambda i: (i, 0, 0)),
        ],
        out_shape=[
            jax.ShapeDtypeStruct(queries.shape, WIDE),
            jax.ShapeDtypeStruct((count, heads, BLOCK), WIDE),
        ],
        compiler_params=pltpu.CompilerParams(vmem_limit_bytes=48 * MIB),
    )(*arrays)


def attend_backward(queries, kv_rows, doc_first, out, log_total, d_out):
    arrays, specs, count, width = attend_operands(queries, kv_rows, doc_first)
    heads = width // HEAD
    near, meta = arrays[2], arrays[4]
    row_spec = pl.BlockSpec((BLOCK, width), lambda i: (i, 0))
    d_queries, d_near, d_meta = pl.pallas_call(
        lambda *refs: attend_backward_kernel(heads, *refs),
        grid=(count,),
        in_specs=specs
        + [row_spec, pl.BlockSpec((1, heads, BLOCK), lambda i: (i, 0, 0)), row_spec],
        out_specs=[
            row_spec,
            pl.BlockSpec(near.shape, lambda i: (0, 0)),
            pl.BlockSpec(meta.shape, lambda i: (0, 0)),
        ],
        out_shape=[
            jax.ShapeDtypeStruct(queries.shape, SIXTEEN),
            jax.ShapeDtypeStruct(near.shape, WIDE),
            jax.ShapeDtypeStruct(meta.shape, WIDE),
        ],
        compiler_params=pltpu.CompilerParams(vmem_limit_bytes=48 * MIB),
    )(*arrays, out, log_total, d_out)
    return d_queries, jnp.concatenate([d_near[REACH * BLOCK :], d_meta], axis=0).astype(SIXTEEN)


def step_sum():
    rows = lax.broadcasted_iota(jnp.int32, (SUB, SUB * STATE), 0)
    cols = lax.broadcasted_iota(jnp.int32, (SUB, SUB * STATE), 1)
    return (cols // STATE == rows).astype(SIXTEEN)


def lanes_from(tile, group):
    return pltpu.roll(tile, (SPAN - group * SUB) % SPAN, axis=1)


def scan_forward_kernel(keep_ref, conv_ref, delta_ref, bc_ref, a_ref, y_ref, start_ref, state_ref):
    block = pl.program_id(0)

    @pl.when(block == 0)
    def _():
        state_ref[...] = jnp.zeros_like(state_ref)

    start_ref[0] = state_ref[...]
    decay_rate = a_ref[...]
    fold = step_sum()
    b_span = bc_ref[:STATE, :].astype(WIDE)
    c_span = bc_ref[STATE:, :].astype(WIDE)

    def body(group, state):
        rows = pl.ds(pl.multiple_of(group * SUB, SUB), SUB)
        delta = delta_ref[rows, :]
        drive = delta * conv_ref[rows, :]
        b_tile = lanes_from(b_span, group)
        c_tile = lanes_from(c_span, group)
        reads = []
        for i in range(SUB):
            keep = keep_ref[block * SPAN + group * SUB + i]
            decay = jnp.exp(delta[i : i + 1, :] * decay_rate) * keep
            state = decay * state + drive[i : i + 1, :] * b_tile[:, i : i + 1]
            reads.append((state * c_tile[:, i : i + 1]).astype(SIXTEEN))
        y_ref[rows, :] = jnp.dot(
            fold, jnp.concatenate(reads, axis=0), preferred_element_type=WIDE
        )
        return state

    state_ref[...] = lax.fori_loop(0, SPAN // SUB, body, state_ref[...], unroll=8)


def scan_forward(keep, conv_out, delta, bc_rows, decay_rate):
    length, lanes = conv_out.shape
    blocks = length // SPAN
    span_spec = pl.BlockSpec((SPAN, lanes), lambda i: (i, 0))
    return pl.pallas_call(
        scan_forward_kernel,
        grid=(blocks,),
        in_specs=[
            pl.BlockSpec(memory_space=pltpu.SMEM),
            span_spec,
            span_spec,
            pl.BlockSpec((2 * STATE, SPAN), lambda i: (0, i)),
            pl.BlockSpec((STATE, lanes), lambda i: (0, 0)),
        ],
        out_specs=[span_spec, pl.BlockSpec((1, STATE, lanes), lambda i: (i, 0, 0))],
        out_shape=[
            jax.ShapeDtypeStruct((length, lanes), WIDE),
            jax.ShapeDtypeStruct((blocks, STATE, lanes), WIDE),
        ],
        scratch_shapes=[pltpu.VMEM((STATE, lanes), WIDE)],
    )(keep, conv_out, delta, bc_rows, decay_rate)


def scan_backward_kernel(
    keep_ref, conv_ref, delta_ref, bc_ref, a_ref, start_ref, dy_ref,
    dconv_ref, ddelta_ref, dbc_ref, da_ref,
    state_ref, decay_ref, adjoint_ref,
):
    turn = pl.program_id(0)
    block = pl.num_programs(0) - 1 - turn

    @pl.when(turn == 0)
    def _():
        adjoint_ref[...] = jnp.zeros_like(adjoint_ref)
        da_ref[...] = jnp.zeros_like(da_ref)

    decay_rate = a_ref[...]
    fold = step_sum()
    lanes = decay_rate.shape[1]
    ones = jnp.ones((lanes, SPAN), SIXTEEN)
    spot = lax.broadcasted_iota(jnp.int32, (STATE, SPAN), 1)
    b_span = bc_ref[:STATE, :].astype(WIDE)
    c_span = bc_ref[STATE:, :].astype(WIDE)
    state_ref[0] = start_ref[0]

    def ahead(group, state):
        rows = pl.ds(pl.multiple_of(group * SUB, SUB), SUB)
        delta = delta_ref[rows, :]
        drive = delta * conv_ref[rows, :]
        b_tile = lanes_from(b_span, group)
        for i in range(SUB):
            keep = keep_ref[block * SPAN + group * SUB + i]
            decay = jnp.exp(delta[i : i + 1, :] * decay_rate) * keep
            state = decay * state + drive[i : i + 1, :] * b_tile[:, i : i + 1]
            decay_ref[group * SUB + i] = decay
            state_ref[group * SUB + i + 1] = state
        return state

    lax.fori_loop(0, SPAN // SUB, ahead, start_ref[0], unroll=16)

    def back(step, carry):
        adjoint, da, db, dc = carry
        group = SPAN // SUB - 1 - step
        rows = pl.ds(pl.multiple_of(group * SUB, SUB), SUB)
        delta = delta_ref[rows, :]
        conv = conv_ref[rows, :]
        drive = delta * conv
        dy = dy_ref[rows, :]
        b_tile = lanes_from(b_span, group)
        c_tile = lanes_from(c_span, group)
        by_c, by_b, by_drive, by_delta = ([None] * SUB for _ in range(4))
        for i in range(SUB - 1, -1, -1):
            index = group * SUB + i
            dy_row = dy[i : i + 1, :]
            total = adjoint + dy_row * c_tile[:, i : i + 1]
            by_c[i] = (dy_row * state_ref[index + 1]).astype(SIXTEEN)
            by_b[i] = (total * drive[i : i + 1, :]).astype(SIXTEEN)
            by_drive[i] = (total * b_tile[:, i : i + 1]).astype(SIXTEEN)
            adjoint = total * decay_ref[index]
            rate = adjoint * state_ref[index]
            by_delta[i] = (rate * decay_rate).astype(SIXTEEN)
            da = da + rate * delta[i : i + 1, :]

        def over_state(parts):
            return jnp.dot(fold, jnp.concatenate(parts, axis=0), preferred_element_type=WIDE)

        def over_lanes(parts, tile):
            sums = jnp.dot(jnp.concatenate(parts, axis=0), ones, preferred_element_type=WIDE)
            for i in range(SUB):
                here = spot == group * SUB + i
                tile = jnp.where(here, sums[i * STATE : (i + 1) * STATE, :], tile)
            return tile

        d_drive = over_state(by_drive)
        dconv_ref[rows, :] = d_drive * delta
        ddelta_ref[rows, :] = over_state(by_delta) + d_drive * conv
        return adjoint, da, over_lanes(by_b, db), over_lanes(by_c, dc)

    none = jnp.zeros((STATE, SPAN), WIDE)
    adjoint, da, db, dc = lax.fori_loop(
        0, SPAN // SUB, back, (adjoint_ref[...], da_ref[...], none, none), unroll=16
    )
    adjoint_ref[...] = adjoint
    da_ref[...] = da
    dbc_ref[...] = jnp.concatenate([db, dc], axis=0)


def scan_backward(keep, conv_out, delta, bc_rows, decay_rate, starts, dy):
    length, lanes = conv_out.shape
    blocks = length // SPAN
    span_spec = pl.BlockSpec((SPAN, lanes), lambda i: (blocks - 1 - i, 0))
    rows_spec = pl.BlockSpec((2 * STATE, SPAN), lambda i: (0, blocks - 1 - i))
    whole = pl.BlockSpec((STATE, lanes), lambda i: (0, 0))
    return pl.pallas_call(
        scan_backward_kernel,
        grid=(blocks,),
        in_specs=[
            pl.BlockSpec(memory_space=pltpu.SMEM),
            span_spec,
            span_spec,
            rows_spec,
            whole,
            pl.BlockSpec((1, STATE, lanes), lambda i: (blocks - 1 - i, 0, 0)),
            span_spec,
        ],
        out_specs=[span_spec, span_spec, rows_spec, whole],
        out_shape=[
            jax.ShapeDtypeStruct((length, lanes), WIDE),
            jax.ShapeDtypeStruct((length, lanes), WIDE),
            jax.ShapeDtypeStruct((2 * STATE, length), WIDE),
            jax.ShapeDtypeStruct((STATE, lanes), WIDE),
        ],
        scratch_shapes=[
            pltpu.VMEM((SPAN + 1, STATE, lanes), WIDE),
            pltpu.VMEM((SPAN, STATE, lanes), WIDE),
            pltpu.VMEM((STATE, lanes), WIDE),
        ],
        compiler_params=pltpu.CompilerParams(vmem_limit_bytes=32 * MIB),
    )(keep, conv_out, delta, bc_rows, decay_rate, starts, dy)


def padded_lanes(array, lanes):
    return jnp.pad(array, ((0, 0), (0, lanes - array.shape[1])))


def rms_pull(values, scale, gain, d_normed, mean):
    d_values = scale * gain * d_normed - values * (scale * scale * scale) * mean
    return d_values, jnp.sum(d_normed * values * scale, axis=0)


def per_device(tokens, doc_ids, meta_tokens, mixer_params, small_params, ffn_params, cotangent):
    tokens, cotangent = tokens[0], cotangent[0]
    small_whole, ids, meta_whole = start_blocks(small_params, doc_ids[0], meta_tokens)
    (g_one, g_two, g_attn, channel_part), small_pull = jax.vjp(small_shards, small_whole)
    columns, columns_pull = jax.vjp(mixer_columns, mixer_params)
    channels = channel_part.shape[0]
    lanes = -(-channels // 128) * 128
    g_ssm = channel_part[:, 0]
    conv_w = channel_part[:, 1 : 1 + CONV].T
    conv_b = channel_part[:, 1 + CONV]
    dt_bias = channel_part[:, 2 + CONV]
    a_log = channel_part[:, 3 + CONV : 3 + CONV + STATE]
    d_skip = channel_part[:, 3 + CONV + STATE]

    length = ids.shape[0]
    positions = jnp.arange(length, dtype=jnp.int32)
    starts = jnp.concatenate([jnp.ones((1,), bool), ids[1:] != ids[:-1]])
    doc_first = lax.cummax(jnp.where(starts, positions, 0), axis=0)
    keep_mask = (positions != doc_first).astype(WIDE)
    lag_masks = jnp.stack(
        [(positions - j >= doc_first).astype(WIDE)[:, None] for j in range(CONV)]
    )

    tokens_f = tokens.astype(WIDE)
    normed_f, norm_pull = jax.vjp(rms_norm, tokens_f, g_one)
    meta_own = meta_tokens.astype(WIDE)
    meta_unit = rms_norm(meta_whole.astype(WIDE), 1.0)
    normed_own, columns = lax.optimization_barrier((normed_f.astype(SIXTEEN), columns))
    shards_fn = partial(mixer_shards, length=mixer_params.shape[0])
    (w_qkv, w_in, w_x, w_dt, w_out), mixer_pull = jax.vjp(shards_fn, columns)
    normed = ring_seq_gather(normed_own, 1)
    normed, ffn_later, cotangent_later = lax.optimization_barrier((normed, ffn_params, cotangent))
    (w_gate, w_up, w_down), ffn_pull = jax.vjp(ffn_shards, ffn_later)
    meta_normed = (meta_unit * g_one).astype(SIXTEEN)
    every = jnp.concatenate([normed, meta_normed], axis=0)
    cotangent_all = gather_seq(cotangent_later)

    xz = dot_last(normed, w_in).astype(SIXTEEN)
    extended = jnp.pad(xz[:, :channels], ((CONV - 1, 0), (0, 0))).astype(WIDE)
    conv_fn = partial(conv_piece, lag_masks=lag_masks)
    conv_out, conv_pull = jax.vjp(conv_fn, extended, conv_w, conv_b)
    conv_half = conv_out.astype(SIXTEEN)
    conv_f = conv_half.astype(WIDE)
    w_x_rows = jnp.pad(w_x.T, ((0, -w_x.shape[1] % 16), (0, 0)))
    projected = seq_sum(jnp.einsum("nc,tc->nt", w_x_rows, conv_half, preferred_element_type=WIDE), 2)
    rank_half = projected[:DT_RANK]
    pre_dt = jnp.einsum("rt,rc->tc", rank_half, w_dt, preferred_element_type=WIDE)
    delta, delta_pull = jax.vjp(lambda p, b: softplus_fn(p + b), pre_dt, dt_bias)
    a_neg, a_pull = jax.vjp(lambda a: -jnp.exp(a), a_log)
    scan_in = (
        keep_mask,
        padded_lanes(conv_f, lanes),
        padded_lanes(delta, lanes),
        projected[DT_RANK : DT_RANK + 2 * STATE],
        padded_lanes(a_neg.T, lanes),
    )
    y_scan, scan_starts = scan_forward(*scan_in)

    def gate_piece(y, c, skip, z):
        return (y + skip * c) * silu_fn(z)

    z_in = xz[:, channels:].astype(WIDE)
    ssm_out, gate_pull = jax.vjp(gate_piece, y_scan[:, :channels], conv_f, d_skip, z_in)

    own_heads = g_attn.shape[0]
    queries = dot_last(normed, w_qkv[:, :own_heads]).astype(SIXTEEN)
    kv_rows = dot_last(every, w_qkv[:, own_heads:]).astype(SIXTEEN)
    attn_out, log_total = attend_forward(queries, kv_rows, doc_first)

    squares = jnp.stack([jnp.sum(attn_out * attn_out, axis=1), jnp.sum(ssm_out * ssm_out, axis=1)])
    squares = seq_sum_small(squares, 3)
    scale_a = lax.rsqrt(squares[0] / (HEADS * HEAD) + norm_eps)[:, None]
    scale_m = lax.rsqrt(squares[1] / INNER + norm_eps)[:, None]
    mixed = 0.5 * jnp.concatenate(
        [attn_out * scale_a * g_attn, ssm_out * scale_m * g_ssm], axis=1
    )
    mixed = mixed.astype(SIXTEEN)
    hidden = tokens_f + product_scatter([(mixed, w_out, False)], 4)

    second_f, second_pull = jax.vjp(rms_norm, hidden, g_two)
    second = ring_seq_gather(second_f.astype(SIXTEEN), 5)
    gate_pre = dot_last(second, w_gate)
    up_pre = dot_last(second, w_up)
    act_f, act_pull = jax.vjp(glu_piece, gate_pre, up_pre)
    act = act_f.astype(SIXTEEN)
    d_gate, d_up = act_pull(dot_back(cotangent_all, w_down))
    d_gate, d_up = d_gate.astype(SIXTEEN), d_up.astype(SIXTEEN)
    d_second = product_scatter([(d_gate, w_gate, True), (d_up, w_up, True)], 6)
    block_out = (hidden + scatter_seq(dot_last(act, w_down))).astype(SIXTEEN)
    (grad_ffn,) = ffn_pull(
        (
            dot_weight(second, d_gate).astype(SIXTEEN),
            dot_weight(second, d_up).astype(SIXTEEN),
            dot_weight(act, cotangent_all).astype(SIXTEEN),
        )
    )
    d_hidden, grad_g_two = second_pull(d_second)
    d_hidden = d_hidden + cotangent.astype(WIDE)

    d_branch = ring_seq_gather(d_hidden.astype(SIXTEEN), 7)
    grad_out = dot_weight(mixed, d_branch)
    d_mixed = 0.5 * dot_back(d_branch, w_out)
    d_mix_a, d_mix_m = d_mixed[:, :own_heads], d_mixed[:, own_heads:]
    means = jnp.stack(
        [jnp.sum(attn_out * g_attn * d_mix_a, axis=1), jnp.sum(ssm_out * g_ssm * d_mix_m, axis=1)]
    )
    means = seq_sum_small(means, 8)
    d_attn, grad_g_attn = rms_pull(
        attn_out, scale_a, g_attn, d_mix_a, means[0][:, None] / (HEADS * HEAD)
    )
    d_ssm, grad_g_ssm = rms_pull(ssm_out, scale_m, g_ssm, d_mix_m, means[1][:, None] / INNER)

    d_queries, d_kv = attend_backward(
        queries, kv_rows, doc_first, attn_out, log_total, d_attn
    )

    d_y, d_conv, grad_d_skip, d_z = gate_pull(d_ssm)
    d_conv_scan, d_delta, d_bc, d_rate = scan_backward(
        *scan_in, scan_starts, padded_lanes(d_y, lanes)
    )
    d_conv = d_conv + d_conv_scan[:, :channels]
    d_pre, grad_dt_bias = delta_pull(d_delta[:, :channels])
    (grad_a_log,) = a_pull(d_rate[:, :channels].T)
    d_pre = d_pre.astype(SIXTEEN)
    grad_dt = jnp.einsum("rt,tc->rc", rank_half, d_pre, preferred_element_type=WIDE)
    d_rank = jnp.einsum("rc,tc->rt", w_dt, d_pre, preferred_element_type=WIDE)
    d_proj = jnp.concatenate([d_rank, d_bc], axis=0)
    d_proj = seq_sum(jnp.pad(d_proj, ((0, -d_proj.shape[0] % 16), (0, 0))), 10)
    d_proj = d_proj[: DT_RANK + 2 * STATE].T
    grad_x = dot_weight(conv_half, d_proj)
    d_extended, grad_conv_w, grad_conv_b = conv_pull(d_conv + dot_back(d_proj, w_x))
    d_xz = jnp.concatenate([d_extended[CONV - 1 :], d_z], axis=1).astype(SIXTEEN)
    grad_in = dot_weight(normed, d_xz)
    grad_qkv = jnp.concatenate([dot_weight(normed, d_queries), dot_weight(every, d_kv)], axis=1)
    d_meta = dot_back(d_kv[length:], w_qkv[:, own_heads:])
    d_qkv = jnp.concatenate([d_queries, d_kv[:length]], axis=1)
    d_normed = product_scatter([(d_xz, w_in, True), (d_qkv, w_qkv, True)], 11)
    grad_from_norm, grad_g_one = norm_pull(d_normed)
    grad_tokens = d_hidden + grad_from_norm
    grad_g_meta = jnp.sum(d_meta * meta_unit, axis=0)
    grads = (grad_qkv, grad_in, grad_x, grad_dt, grad_out)
    grads = lax.optimization_barrier(tuple(g.astype(SIXTEEN) for g in grads))
    (grad_mixer,) = columns_pull(mixer_pull(grads)[0])
    grad_channels = jnp.concatenate(
        [
            grad_g_ssm[:, None],
            grad_conv_w.T,
            grad_conv_b[:, None],
            grad_dt_bias[:, None],
            grad_a_log,
            grad_d_skip[:, None],
        ],
        axis=1,
    )
    (grad_small,) = small_pull((grad_g_one + grad_g_meta, grad_g_two, grad_g_attn, grad_channels))
    grad_small, d_meta = end_blocks(grad_small, d_meta)
    _, meta_pull = jax.vjp(lambda v: rms_norm(v, g_one), meta_own)
    (grad_meta,) = meta_pull(d_meta)
    return (
        block_out[None],
        grad_tokens[None],
        grad_meta,
        grad_mixer.astype(WIDE),
        grad_small,
        grad_ffn.astype(WIDE),
    )


def solution(mesh):
    in_specs = (
        P("row", "seq", None),
        P("row", "seq"),
        P(("row", "seq"), None),
        P(("row", "seq")),
        P(("row", "seq")),
        P(("row", "seq")),
        P("row", "seq", None),
    )
    out_specs = (
        P("row", "seq", None),
        P("row", "seq", None),
        P(("row", "seq"), None),
        P(("row", "seq")),
        P(("row", "seq")),
        P(("row", "seq")),
    )
    return jax.shard_map(
        per_device, mesh=mesh, in_specs=in_specs, out_specs=out_specs, check_vma=False
    )
```

```python
import functools
from functools import partial
import math

import jax
import jax.numpy as jnp
from jax import lax
from jax.experimental import pallas as pl
from jax.experimental.pallas import tpu as pltpu
from jax.sharding import PartitionSpec as P

D = 1600
HEADS = 25
GROUPS = 5
HEAD = 64
INNER = 3200
STATE = 16
CONV = 4
DT_RANK = 100
FF = 5504
REACH = 8
BLOCK = 128
RUNS = 4
SUB = 8
SPAN = 128
SIXTEEN = jnp.bfloat16
WIDE = jnp.float32


norm_eps = 1e-05


def split_flat(flat_vec, layout):
    pieces = []
    offset = 0
    for piece_shape in layout:
        piece_len = math.prod(piece_shape)
        pieces.append(flat_vec[offset : offset + piece_len].reshape(piece_shape))
        offset += piece_len
    return pieces


def mixer_layout():
    return [
        (D, HEADS * HEAD),
        (D, 2 * GROUPS * HEAD),
        (D, 2 * INNER),
        (INNER, DT_RANK + 2 * STATE),
        (DT_RANK, INNER),
        (HEADS * HEAD + INNER, D),
    ]


def ffn_layout():
    return [(D, FF), (D, FF), (FF, D)]


def small_split(flat_vec):
    width = CONV + STATE + 4
    packed_rows = flat_vec[: D * (3 + 2 * width)].reshape(D, 3 + 2 * width)
    channel_part = packed_rows[:, 3:].reshape(INNER, width)
    return packed_rows[:, 0], packed_rows[:, 1], packed_rows[:, 2], channel_part


def rms_norm(values, gain_vec):
    return (
        values * lax.rsqrt(jnp.mean(values * values, axis=-1, keepdims=True) + norm_eps) * gain_vec
    )


def silu_fn(values):
    return values / (1.0 + jnp.exp(-values))


def softplus_fn(values):
    return jnp.maximum(values, 0.0) + jnp.log1p(jnp.exp(-jnp.abs(values)))


def glu_piece(gate_pre, up_pre):
    return silu_fn(gate_pre) * up_pre


def dot_last(left, right):
    return jnp.einsum("...k,kn->...n", left, right, preferred_element_type=WIDE)


def dot_back(grads, right):
    return jnp.einsum("...n,kn->...k", grads, right, preferred_element_type=WIDE)


def dot_weight(left, grads):
    return jnp.einsum("...k,...n->kn", left, grads, preferred_element_type=WIDE)


def heads_of(shards):
    return -(-HEADS // shards)


def runs_of(shards):
    return RUNS if INNER % (RUNS * shards) == 0 else 1


def own_channels(array, axis, shards, place):
    runs = runs_of(shards)
    unit = INNER // (runs * shards)
    shape = array.shape
    cut = array.reshape(shape[:axis] + (runs, shards, unit) + shape[axis + 1 :])
    cut = lax.dynamic_index_in_dim(cut, place, axis + 1, keepdims=False)
    return cut.reshape(shape[:axis] + (runs * unit,) + shape[axis + 1 :])


def pad_heads(array, axis, shards):
    heads = heads_of(shards)
    pads = [(0, 0)] * array.ndim
    pads[axis] = (0, heads * shards - HEADS)
    padded = jnp.pad(array, pads)
    shape = padded.shape
    return padded.reshape(shape[:axis] + (shards, heads * HEAD) + shape[axis + 2 :])


def by_head(w_q, w_kv, shards):
    rows = w_q.shape[0]
    w_kv = w_kv.reshape(rows, 2, GROUPS, 1, HEAD)
    w_kv = jnp.broadcast_to(w_kv, (rows, 2, GROUPS, HEADS // GROUPS, HEAD))
    w_kv = w_kv.reshape(rows, 2, HEADS, HEAD)
    return jnp.concatenate(
        [
            pad_heads(w_q.reshape(rows, HEADS, HEAD), 1, shards),
            pad_heads(w_kv[:, 0], 1, shards),
            pad_heads(w_kv[:, 1], 1, shards),
        ],
        axis=2,
    )


def exchange(value):
    return lax.all_to_all(value, "seq", 0, 0)


def tie(*arrays):
    return lax.optimization_barrier(arrays)


def hold(array):
    return lax.optimization_barrier(array)


def both_halves(value):
    other = lax.ppermute(value, "row", [(0, 1), (1, 0)])
    first = lax.axis_index("row") == 0
    return jnp.concatenate(
        [jnp.where(first, value, other), jnp.where(first, other, value)], axis=0
    )


@partial(jax.custom_vjp, nondiff_argnums=(1,))
def cut_rows(array, counts):
    pieces, offset = [], 0
    for count in counts:
        pieces.append(array[offset : offset + count])
        offset += count
    return tuple(pieces)


def cut_rows_forward(array, counts):
    return cut_rows(array, counts), None


def cut_rows_backward(counts, _, grads):
    return (jnp.concatenate(grads, axis=0),)


cut_rows.defvjp(cut_rows_forward, cut_rows_backward)


def view_width():
    return INNER // RUNS


def weights_fit(mixer_length, ffn_length, rows, shards):
    width = view_width()
    sizes = [math.prod(shape) for shape in mixer_layout()]
    return (
        rows == 2
        and runs_of(shards) == RUNS
        and mixer_length % width == 0
        and all(size % width == 0 for size in sizes)
        and D % shards == 0
        and D % width == 0
        and (HEADS * HEAD * 2) % shards == 0
        and shards % x_turns(shards)[0] == 0
        and ffn_length % FF == 0
    )


def to_columns(piece, width):
    shards = lax.axis_size("seq")
    unit = width // shards
    view = hold(piece.reshape(-1, width))
    return exchange(view.reshape(-1, shards, unit).transpose(1, 0, 2)).reshape(-1, unit)


def full_rows(cut):
    received = exchange(cut)
    return hold(received.transpose(1, 0, 2).reshape(received.shape[1], -1))


def mixer_parts(both):
    width, shards = view_width(), lax.axis_size("seq")
    unit = both.shape[1]
    part_q, part_kv, part_in, part_x, part_dt, part_out = cut_rows(
        both, tuple(math.prod(shape) // width for shape in mixer_layout())
    )
    q_rows = jnp.concatenate(
        [part_q.reshape(shards, -1, unit), part_kv.reshape(shards, -1, unit)], axis=1
    )
    per_row = D // width
    head_rows = heads_of(shards) * HEAD
    out_heads, out_inner = cut_rows(part_out, (HEADS * HEAD * per_row, INNER * per_row))
    out_heads = jnp.pad(
        out_heads, ((0, (head_rows * shards - HEADS * HEAD) * per_row), (0, 0))
    ).reshape(shards, -1, unit)
    out_inner = out_inner.reshape(RUNS, shards, -1, unit)
    out_inner = out_inner.transpose(1, 0, 2, 3).reshape(shards, -1, unit)
    return (
        part_in.reshape(D, -1),
        part_dt.reshape(DT_RANK, -1),
        q_rows,
        x_windows(part_x, shards),
        jnp.concatenate([out_heads, out_inner], axis=1),
    )


def heads_cut(q_rows):
    shards = lax.axis_size("seq")
    rows = D // shards
    by_rows = full_rows(q_rows)
    split = rows * HEADS * HEAD // view_width()
    cut = by_head(
        by_rows[:split].reshape(rows, HEADS * HEAD),
        by_rows[split:].reshape(rows, 2 * GROUPS * HEAD),
        shards,
    )
    return cut.transpose(1, 0, 2)


def heads_from(cut):
    return exchange(cut).reshape(D, -1)


def x_from(windows):
    return x_from_windows(full_rows(windows), lax.axis_index("seq"))


def out_from(cut):
    return full_rows(cut).reshape(-1, D)


def ffn_parts(both):
    w_gate, w_up, part_down = cut_rows(both, (D, D, D))
    return w_gate, w_up, part_down.reshape(lax.axis_size("seq"), -1, both.shape[1])


def down_from(cut):
    return full_rows(cut).reshape(-1, D)


def x_turns(shards):
    width = INNER // RUNS
    run = (width // shards) * (DT_RANK + 2 * STATE)
    common = math.gcd(run, width)
    return width // common, run // common


def x_windows(part_x, shards):
    runs, rows = x_turns(shards)
    need = -(-rows // runs)
    turns = part_x.reshape(-1, rows, part_x.shape[1])
    cuts = [turns[:, (i * rows) // runs : (i * rows) // runs + need] for i in range(runs)]
    cuts = jnp.stack(cuts, axis=1).reshape(RUNS, shards, need, part_x.shape[1])
    return cuts.transpose(1, 0, 2, 3).reshape(shards, RUNS * need, part_x.shape[1])


def x_from_windows(view_rows, place):
    width = view_rows.shape[1]
    shards = lax.axis_size("seq")
    runs, rows = x_turns(shards)
    columns = DT_RANK + 2 * STATE
    count = (width // shards) * columns
    flat = view_rows.reshape(RUNS, -1)
    offset = (place % runs) * rows * (width // runs) % width
    return lax.dynamic_slice_in_dim(flat, offset, count, 1).reshape(-1, columns)


def mixer_shards_whole(piece):
    shards, place = lax.axis_size("seq"), lax.axis_index("seq")
    whole = lax.all_gather(piece, ("row", "seq"), axis=0, tiled=True)
    w_q, w_kv, w_in, w_x, w_dt, w_out = split_flat(whole, mixer_layout())
    qkv = lax.dynamic_index_in_dim(by_head(w_q, w_kv, shards), place, 1, keepdims=False)
    w_in = own_channels(w_in.reshape(D, 2, INNER), 2, shards, place)
    out_heads = w_out[: HEADS * HEAD].reshape(HEADS, HEAD, D)
    out_heads = lax.dynamic_index_in_dim(pad_heads(out_heads, 0, shards), place, 0, keepdims=False)
    return (
        qkv,
        w_in.reshape(D, -1),
        own_channels(w_x, 0, shards, place),
        own_channels(w_dt, 1, shards, place),
        jnp.concatenate([out_heads, own_channels(w_out[HEADS * HEAD :], 0, shards, place)], axis=0),
    )


def ffn_shards_whole(piece):
    unit = FF // lax.axis_size("seq")
    start = lax.axis_index("seq") * unit
    whole = lax.all_gather(piece, ("row", "seq"), axis=0, tiled=True)
    w_gate, w_up, w_down = split_flat(whole, ffn_layout())
    return (
        lax.dynamic_slice_in_dim(w_gate, start, unit, 1),
        lax.dynamic_slice_in_dim(w_up, start, unit, 1),
        lax.dynamic_slice_in_dim(w_down, start, unit, 0),
    )


def small_shards(whole):
    shards, place = lax.axis_size("seq"), lax.axis_index("seq")
    g_one, g_attn, g_two, channel_part = small_split(whole)
    g_attn = pad_heads(g_attn.reshape(HEADS, HEAD), 0, shards)
    return (
        g_one,
        g_two,
        lax.dynamic_index_in_dim(g_attn, place, 0, keepdims=False),
        own_channels(channel_part, 0, shards, place),
    )


def tiles_of(count):
    return -(-count // 128)


def start_blocks(small_params, doc_ids, meta_tokens):
    devices = lax.axis_size("row") * lax.axis_size("seq")
    parts = [small_params, doc_ids.astype(SIXTEEN), meta_tokens.reshape(-1)]
    rows = [tiles_of(part.shape[0]) for part in parts]
    rows_all = -(-sum(rows) // 16) * 16
    tiles = [
        jnp.pad(part, (0, count * 128 - part.shape[0])).reshape(-1, 128)
        for part, count in zip(parts, rows)
    ]
    block = jnp.concatenate(tiles + [jnp.zeros((rows_all - sum(rows), 128), SIXTEEN)], axis=0)
    every = push_gather(block, 0)
    outs, begin = [], 0
    for part, count in zip(parts, rows):
        cut = every[:, begin : begin + count].reshape(devices, -1)[:, : part.shape[0]]
        outs.append(cut)
        begin += count
    ids = outs[1].reshape(lax.axis_size("row"), -1)
    ids = lax.dynamic_index_in_dim(ids, lax.axis_index("row"), 0, keepdims=False)
    return outs[0].reshape(-1).astype(WIDE), ids.astype(jnp.int32), outs[2].reshape(-1, D)


def end_blocks(grad_small, d_meta):
    devices = lax.axis_size("row") * lax.axis_size("seq")
    parts = grad_small.reshape(devices, -1).astype(SIXTEEN)
    small_count = parts.shape[1]
    small_rows = tiles_of(small_count)
    parts = jnp.pad(parts, ((0, 0), (0, small_rows * 128 - small_count)))
    meta = d_meta.astype(SIXTEEN).reshape(devices, -1)
    meta_count = meta.shape[1]
    rows = -(-(small_rows + tiles_of(meta_count)) // 16) * 16
    meta = jnp.pad(meta, ((0, 0), (0, (rows - small_rows) * 128 - meta_count)))
    blocks = jnp.concatenate(
        [parts.reshape(devices, -1, 128), meta.reshape(devices, -1, 128)], axis=1
    )
    own = push_scatter(blocks, 9)
    small = own[:small_rows].reshape(-1)[:small_count]
    meta = own[small_rows:].reshape(-1)[:meta_count].reshape(-1, D)
    return small, meta


def gather_seq(block):
    return lax.all_gather(block, "seq", axis=0, tiled=True)


def scatter_seq(whole):
    return lax.psum_scatter(whole.astype(SIXTEEN), "seq", scatter_dimension=0, tiled=True).astype(
        WIDE
    )


MESH = pl.DeviceIdType.MESH
ANY = pl.BlockSpec(memory_space=pl.ANY)
VMEM = pl.BlockSpec(memory_space=pltpu.VMEM)
MIB = 1024 * 1024


def takes(microseconds):
    return pl.CostEstimate(
        flops=0, bytes_accessed=microseconds * 3_500_000, transcendentals=0
    )


def greet(peers):
    barrier = pltpu.get_barrier_semaphore()
    for peer in peers:
        pl.semaphore_signal(barrier, inc=1, device_id=peer, device_id_type=MESH)
    pl.semaphore_wait(barrier, len(peers))


def ring_place(chip, chips):
    odd = chip % 2
    return odd * (chips - 1 - chip // 2) + (1 - odd) * (chip // 2)


def ring_chip(place, chips):
    place = (place + 2 * chips) % chips
    back = place // (chips // 2)
    return back * (2 * (chips - 1 - place) + 1) + (1 - back) * (2 * place)


def seq_gather_kernel(shards, parts, x_ref, out_ref, ring_send, ring_recv, pair_send, pair_recv, own_sem):
    row, me = lax.axis_index("row"), lax.axis_index("seq")
    chips = shards // 2
    core = me % 2
    place = ring_place(me // 2, chips)

    def device(spot):
        return ring_chip(spot, chips) * 2 + core

    right, left, twin = (row, device(place + 1)), (row, device(place - 1)), (row, me + 1 - 2 * core)
    greet([right, left, twin])
    rows = x_ref.shape[0] // (2 * parts)

    def cut(way, part):
        return pl.ds((way * parts + part) * rows, rows)

    own = pltpu.make_async_copy(x_ref, out_ref.at[me], own_sem)
    own.start()
    started = []

    def send(src, dst, send_sem, recv_sem, to):
        copy = pltpu.make_async_remote_copy(
            src_ref=src, dst_ref=dst, send_sem=send_sem, recv_sem=recv_sem,
            device_id=to, device_id_type=MESH,
        )
        copy.start()
        started.append(copy)
        return copy

    paths = [(way, part) for part in range(parts) for way in range(2)]
    flights = {}
    for way, part in paths:
        flights[way, part] = send(
            x_ref.at[cut(way, part)], out_ref.at[me, cut(way, part)],
            ring_send.at[way, part, 0], ring_recv.at[way, part, 0], (right, left)[way],
        )
    pairs = [send(x_ref, out_ref.at[me], pair_send.at[0, 0, chips - 1], pair_recv.at[0, 0, chips - 1], twin)]
    for step in range(chips - 1):
        for way, part in paths:
            flights[way, part].wait_recv()
            source = device(place - 1 - step if way == 0 else place + 1 + step)
            here = out_ref.at[source, cut(way, part)]
            if step < chips - 2:
                flights[way, part] = send(
                    here, here, ring_send.at[way, part, step + 1],
                    ring_recv.at[way, part, step + 1], (right, left)[way],
                )
            pairs.append(
                send(here, here, pair_send.at[way, part, step], pair_recv.at[way, part, step], twin)
            )
    own.wait()
    for copy in started:
        copy.wait_send()
    for copy in pairs:
        copy.wait_recv()


def ring_seq_gather(block, collective_id, parts=2):
    shards = lax.axis_size("seq")
    chips = shards // 2
    rows, width = block.shape
    ring = pltpu.SemaphoreType.DMA((2, parts, chips - 1))
    pair = pltpu.SemaphoreType.DMA((2, parts, chips))
    gathered = pl.pallas_call(
        functools.partial(seq_gather_kernel, shards, parts),
        out_shape=jax.ShapeDtypeStruct((shards, rows, width), block.dtype),
        in_specs=[ANY],
        out_specs=ANY,
        scratch_shapes=[ring, ring, pair, pair, pltpu.SemaphoreType.DMA],
        compiler_params=pltpu.CompilerParams(collective_id=collective_id, has_side_effects=True),
        cost_estimate=takes(40),
    )(block)
    return gathered.reshape(shards * rows, width)


def product_scatter_kernel(shards, parts, turned, *refs):
    terms = len(turned)
    lefts, rights = refs[:terms], refs[terms : 2 * terms]
    out_ref, mine, given, pair, arrived = refs[2 * terms : 2 * terms + 5]
    ring_send, ring_recv, pair_send, pair_recv = refs[2 * terms + 5 :]
    row, me = lax.axis_index("row"), lax.axis_index("seq")
    chips = shards // 2
    core = me % 2
    place = ring_place(me // 2, chips)
    block_rows = out_ref.shape[0]

    def device(spot, core):
        return ring_chip(spot, chips) * 2 + core

    right = (row, device(place + 1, core))
    left = (row, device(place - 1, core))
    twin = (row, me + 1 - 2 * core)
    greet([right, left, twin])
    rows = block_rows // (2 * parts)

    def cut(way, part):
        return pl.ds((way * parts + part) * rows, rows)

    def product(index):
        here = pl.ds(pl.multiple_of(index * block_rows, block_rows), block_rows)
        total = None
        for left_ref, right_ref, turn in zip(lefts, rights, turned):
            part = lax.dot_general(
                left_ref[here, :], right_ref[...], (((1,), (1 if turn else 0,)), ((), ())),
                preferred_element_type=WIDE,
            )
            total = part if total is None else total + part
        return total.astype(SIXTEEN)

    def pass_over(slot):
        return pltpu.make_async_remote_copy(
            src_ref=given.at[slot], dst_ref=pair.at[slot], send_sem=pair_send.at[slot],
            recv_sem=pair_recv.at[slot], device_id=twin, device_id_type=MESH,
        )

    def make(far):
        slot = far % chips
        given[slot] = product(device(place + far, 1 - core))
        pass_over(slot).start()
        mine[slot] = product(device(place + far, core))

    def both(step, carry):
        make(-step)
        make(step)
        return carry

    half = chips // 2
    both(1, 0)
    started, flights = [], {}
    fresh = set(range(chips))
    for step in range(chips):
        if step + 2 < half:
            both(step + 2, 0)
        elif step + 2 == half:
            make(half)
            make(0)
        for part in range(parts):
            for way in range(2):
                slot = (-1 - step if way == 0 else 1 + step) % chips
                if slot in fresh:
                    fresh.remove(slot)
                    pass_over(slot).wait_recv()
                here = cut(way, part)
                total = mine[slot, here, :].astype(WIDE) + pair[slot, here, :].astype(WIDE)
                if step:
                    flights[way, part].wait_recv()
                    total = total + arrived[way, step - 1, pl.ds(part * rows, rows), :].astype(WIDE)
                if step == chips - 1:
                    out_ref[here, :] = total
                    continue
                mine[slot, here, :] = total.astype(SIXTEEN)
                copy = pltpu.make_async_remote_copy(
                    src_ref=mine.at[slot, here], dst_ref=arrived.at[way, step, pl.ds(part * rows, rows)],
                    send_sem=ring_send.at[way, part, step], recv_sem=ring_recv.at[way, part, step],
                    device_id=(right, left)[way], device_id_type=MESH,
                )
                copy.start()
                started.append(copy)
                flights[way, part] = copy
    for slot in range(chips):
        pass_over(slot).wait_send()
    for copy in started:
        copy.wait_send()


def padded_bytes(shape, bytes_each):
    return -(-shape[0] // 16) * 16 * -(-shape[1] // 128) * 128 * bytes_each


def product_scatter(terms, collective_id, parts=2):
    shards = lax.axis_size("seq")
    chips = shards // 2
    length = terms[0][0].shape[0]
    width = terms[0][1].shape[0 if terms[0][2] else 1]
    rows = length // shards
    buffers = 4 * chips * padded_bytes((rows, width), 2)
    operands = sum(padded_bytes(t[0].shape, 2) + padded_bytes(t[1].shape, 2) for t in terms)
    if chips < 4 or buffers + operands > 40 * MIB:
        total = 0
        for left, right, turn in terms:
            total = total + lax.dot_general(
                left, right, (((1,), (1 if turn else 0,)), ((), ())), preferred_element_type=WIDE
            )
        return lax.psum_scatter(
            total.astype(SIXTEEN), "seq", scatter_dimension=0, tiled=True
        ).astype(WIDE)
    ring = pltpu.SemaphoreType.DMA((2, parts, chips - 1))
    pair = pltpu.SemaphoreType.DMA((chips,))
    blocks = pltpu.VMEM((chips, rows, width), SIXTEEN)
    return pl.pallas_call(
        functools.partial(product_scatter_kernel, shards, parts, tuple(t[2] for t in terms)),
        out_shape=jax.ShapeDtypeStruct((rows, width), WIDE),
        in_specs=[VMEM] * (2 * len(terms)),
        out_specs=VMEM,
        scratch_shapes=[
            blocks, blocks, blocks,
            pltpu.VMEM((2, chips - 1, rows // 2, width), SIXTEEN),
            ring, ring, pair, pair,
        ],
        compiler_params=pltpu.CompilerParams(
            collective_id=collective_id, has_side_effects=True, vmem_limit_bytes=56 * MIB
        ),
        cost_estimate=takes(40),
    )(*[t[0] for t in terms], *[t[1] for t in terms])


def bits_of(shards):
    bits = shards.bit_length() - 1
    assert 1 << bits == shards
    return bits


def partner_of(me, bit):
    return me + (1 - 2 * ((me // (1 << bit)) % 2)) * (1 << bit)


def seq_sum_kernel(bits, x_ref, out_ref, total, staged, arrived, send_sem, recv_sem, back_send, back_recv):
    row, me = lax.axis_index("row"), lax.axis_index("seq")
    partners = [(row, partner_of(me, bit)) for bit in range(bits)]
    greet(partners)
    length = x_ref.shape[1]
    total[...] = x_ref[...].astype(WIDE)
    begin = 0
    started = []
    for bit in range(bits):
        half = length >> (bit + 1)
        upper = (me // (1 << bit)) % 2
        kept = pl.multiple_of(begin + upper * half, 128)
        given = pl.multiple_of(begin + (1 - upper) * half, 128)
        staged[:, half : 2 * half] = total[:, pl.ds(given, half)].astype(SIXTEEN)
        copy = pltpu.make_async_remote_copy(
            src_ref=staged.at[:, half : 2 * half], dst_ref=arrived.at[:, half : 2 * half],
            send_sem=send_sem.at[bit], recv_sem=recv_sem.at[bit],
            device_id=partners[bit], device_id_type=MESH,
        )
        copy.start()
        started.append(copy)
        copy.wait_recv()
        total[:, pl.ds(kept, half)] += arrived[:, half : 2 * half].astype(WIDE)
        begin = kept
    half = length >> bits
    out_ref[:, pl.ds(pl.multiple_of(begin, 128), half)] = total[
        :, pl.ds(pl.multiple_of(begin, 128), half)
    ].astype(SIXTEEN)
    for bit in range(bits - 1, -1, -1):
        half = length >> (bit + 1)
        here = out_ref.at[:, pl.ds(pl.multiple_of(begin, 128), half)]
        copy = pltpu.make_async_remote_copy(
            src_ref=here, dst_ref=here, send_sem=back_send.at[bit], recv_sem=back_recv.at[bit],
            device_id=partners[bit], device_id_type=MESH,
        )
        copy.start()
        started.append(copy)
        copy.wait_recv()
        begin = begin - ((me // (1 << bit)) % 2) * half
    for copy in started:
        copy.wait_send()


def seq_sum(values, collective_id):
    bits = bits_of(lax.axis_size("seq"))
    rows, length = values.shape
    sems = pltpu.SemaphoreType.DMA((bits,))
    return pl.pallas_call(
        functools.partial(seq_sum_kernel, bits),
        out_shape=jax.ShapeDtypeStruct((rows, length), SIXTEEN),
        in_specs=[VMEM],
        out_specs=VMEM,
        scratch_shapes=[
            pltpu.VMEM((rows, length), WIDE),
            pltpu.VMEM((rows, length), SIXTEEN),
            pltpu.VMEM((rows, length), SIXTEEN),
            sems, sems, sems, sems,
        ],
        compiler_params=pltpu.CompilerParams(
            collective_id=collective_id, has_side_effects=True, vmem_limit_bytes=48 * MIB
        ),
        cost_estimate=takes(30),
    )(values)


def seq_sum_small_kernel(bits, x_ref, out_ref, arrived, staged, send_sem, recv_sem):
    row, me = lax.axis_index("row"), lax.axis_index("seq")
    partners = [(row, partner_of(me, bit)) for bit in range(bits)]
    greet(partners)
    total = x_ref[...]
    copies = []
    for bit in range(bits):
        staged[bit] = total
        copy = pltpu.make_async_remote_copy(
            src_ref=staged.at[bit], dst_ref=arrived.at[bit], send_sem=send_sem.at[bit],
            recv_sem=recv_sem.at[bit], device_id=partners[bit], device_id_type=MESH,
        )
        copy.start()
        copies.append(copy)
        copy.wait_recv()
        total = total + arrived[bit]
    out_ref[...] = total
    for copy in copies:
        copy.wait_send()


def seq_sum_small(values, collective_id):
    bits = bits_of(lax.axis_size("seq"))
    shape = values.shape
    tiles = values.reshape(-1, 128)
    sems = pltpu.SemaphoreType.DMA((bits,))
    slots = pltpu.VMEM((bits,) + tiles.shape, WIDE)
    return pl.pallas_call(
        functools.partial(seq_sum_small_kernel, bits),
        out_shape=jax.ShapeDtypeStruct(tiles.shape, WIDE),
        in_specs=[VMEM],
        out_specs=VMEM,
        scratch_shapes=[slots, slots, sems, sems],
        compiler_params=pltpu.CompilerParams(collective_id=collective_id, has_side_effects=True),
        cost_estimate=takes(12),
    )(tiles).reshape(shape)


def all_peers(rows, shards):
    me = lax.axis_index("row") * shards + lax.axis_index("seq")
    count = rows * shards
    ahead = [(me + far) % count for far in range(1, count)]
    return me, count, [(other, (other // shards, other % shards)) for other in ahead]


def push_gather_kernel(rows, shards, x_ref, out_ref, send_sem, recv_sem):
    me, count, peers = all_peers(rows, shards)
    greet([device for _, device in peers])
    copies = []
    for far, (_, device) in enumerate(peers):
        copy = pltpu.make_async_remote_copy(
            src_ref=x_ref, dst_ref=out_ref.at[me], send_sem=send_sem.at[far],
            recv_sem=recv_sem.at[far], device_id=device, device_id_type=MESH,
        )
        copy.start()
        copies.append(copy)
    out_ref[me] = x_ref[...]
    for copy in copies:
        copy.wait()


def push_gather(block, collective_id):
    rows, shards = lax.axis_size("row"), lax.axis_size("seq")
    sems = pltpu.SemaphoreType.DMA((rows * shards - 1,))
    return pl.pallas_call(
        functools.partial(push_gather_kernel, rows, shards),
        out_shape=jax.ShapeDtypeStruct((rows * shards,) + block.shape, block.dtype),
        in_specs=[VMEM],
        out_specs=VMEM,
        scratch_shapes=[sems, sems],
        compiler_params=pltpu.CompilerParams(collective_id=collective_id, has_side_effects=True),
        cost_estimate=takes(20),
    )(block)


def push_scatter_kernel(rows, shards, x_ref, out_ref, arrived, send_sem, recv_sem):
    me, count, peers = all_peers(rows, shards)
    greet([device for _, device in peers])
    copies = []
    for far, (other, device) in enumerate(peers):
        copy = pltpu.make_async_remote_copy(
            src_ref=x_ref.at[other], dst_ref=arrived.at[far], send_sem=send_sem.at[far],
            recv_sem=recv_sem.at[far], device_id=device, device_id_type=MESH,
        )
        copy.start()
        copies.append(copy)
    total = x_ref[me].astype(WIDE)
    for far, copy in enumerate(copies):
        copy.wait_recv()
        total = total + arrived[far].astype(WIDE)
    out_ref[...] = total
    for copy in copies:
        copy.wait_send()


def push_scatter(blocks, collective_id):
    rows, shards = lax.axis_size("row"), lax.axis_size("seq")
    count = rows * shards
    sems = pltpu.SemaphoreType.DMA((count - 1,))
    return pl.pallas_call(
        functools.partial(push_scatter_kernel, rows, shards),
        out_shape=jax.ShapeDtypeStruct(blocks.shape[1:], WIDE),
        in_specs=[VMEM],
        out_specs=VMEM,
        scratch_shapes=[pltpu.VMEM((count - 1,) + blocks.shape[1:], blocks.dtype), sems, sems],
        compiler_params=pltpu.CompilerParams(
            collective_id=collective_id, has_side_effects=True, vmem_limit_bytes=32 * MIB
        ),
        cost_estimate=takes(20),
    )(blocks)


def conv_piece(extended, conv_w, conv_b, lag_masks):
    length = extended.shape[0] - (CONV - 1)
    summed = conv_b
    for j in range(CONV):
        summed = (
            summed + conv_w[j] * extended[CONV - 1 - j : CONV - 1 - j + length] * lag_masks[j]
        )
    return silu_fn(summed)


def nt_dot(left, right):
    return lax.dot_general(left, right, (((1,), (1,)), ((), ())), preferred_element_type=WIDE)


def seen_keys(block, first_row):
    window = (REACH + 1) * BLOCK
    k_pos = (block - REACH) * BLOCK + lax.broadcasted_iota(jnp.int32, (window, BLOCK), 0)
    q_pos = block * BLOCK + lax.broadcasted_iota(jnp.int32, (window, BLOCK), 1)
    return (k_pos >= first_row) & (k_pos <= q_pos) & (k_pos > q_pos - REACH * BLOCK)


def attend_forward_kernel(heads, first_ref, q_ref, kv_ref, turned_ref, meta_ref, meta_turned_ref, out_ref, total_ref):
    block = pl.program_id(0)
    span = pl.ds(pl.multiple_of(block * BLOCK, BLOCK), (REACH + 1) * BLOCK)
    seen = seen_keys(block, first_ref[0])
    outs, totals = [], []
    for h in range(heads):
        cut = slice(h * HEAD, (h + 1) * HEAD)
        v_cut = slice((heads + h) * HEAD, (heads + h + 1) * HEAD)
        query = q_ref[:, cut] * SIXTEEN(HEAD ** (-0.5))
        near = jnp.where(seen, nt_dot(kv_ref[span, cut], query), -1e30)
        meta = nt_dot(meta_ref[:, cut], query)
        top = jnp.maximum(
            jnp.max(near, axis=0, keepdims=True), jnp.max(meta, axis=0, keepdims=True)
        )
        near = jnp.exp(near - top)
        meta = jnp.exp(meta - top)
        total = jnp.sum(near, axis=0, keepdims=True) + jnp.sum(meta, axis=0, keepdims=True)
        out = jnp.dot(turned_ref[v_cut, span], near.astype(SIXTEEN), preferred_element_type=WIDE)
        out += jnp.dot(meta_turned_ref[v_cut, :], meta.astype(SIXTEEN), preferred_element_type=WIDE)
        outs.append(out / total)
        totals.append(top + jnp.log(total))
    out_ref[...] = jnp.concatenate(outs, axis=0).T
    total_ref[0] = jnp.concatenate(totals, axis=0)


def attend_backward_kernel(
    heads, first_ref, q_ref, kv_ref, turned_ref, meta_ref, meta_turned_ref, out_ref, total_ref, do_ref,
    dq_ref, dkv_ref, dmeta_ref,
):
    block = pl.program_id(0)

    @pl.when(block == 0)
    def _():
        dkv_ref[...] = jnp.zeros_like(dkv_ref)
        dmeta_ref[...] = jnp.zeros_like(dmeta_ref)

    span = pl.ds(pl.multiple_of(block * BLOCK, BLOCK), (REACH + 1) * BLOCK)
    seen = seen_keys(block, first_ref[0])
    d_out = do_ref[...]
    row_sums = (d_out * out_ref[...]).T
    d_half = d_out.astype(SIXTEEN)
    d_queries, near_k, near_v, meta_k, meta_v = [], [], [], [], []
    for h in range(heads):
        cut = slice(h * HEAD, (h + 1) * HEAD)
        v_cut = slice((heads + h) * HEAD, (heads + h + 1) * HEAD)
        query = q_ref[:, cut] * SIXTEEN(HEAD ** (-0.5))
        do = d_half[:, cut]
        total = total_ref[0, h : h + 1, :]
        mean = jnp.sum(row_sums[cut], axis=0, keepdims=True)
        near = jnp.where(seen, jnp.exp(nt_dot(kv_ref[span, cut], query) - total), 0.0)
        meta = jnp.exp(nt_dot(meta_ref[:, cut], query) - total)
        d_near = (near * (nt_dot(kv_ref[span, v_cut], do) - mean)).astype(SIXTEEN)
        d_meta = (meta * (nt_dot(meta_ref[:, v_cut], do) - mean)).astype(SIXTEEN)
        near_v.append(jnp.dot(near.astype(SIXTEEN), do, preferred_element_type=WIDE))
        meta_v.append(jnp.dot(meta.astype(SIXTEEN), do, preferred_element_type=WIDE))
        near_k.append(jnp.dot(d_near, query, preferred_element_type=WIDE))
        meta_k.append(jnp.dot(d_meta, query, preferred_element_type=WIDE))
        d_query = jnp.dot(turned_ref[cut, span], d_near, preferred_element_type=WIDE)
        d_query += jnp.dot(meta_turned_ref[cut, :], d_meta, preferred_element_type=WIDE)
        d_queries.append(d_query * HEAD ** (-0.5))
    dq_ref[...] = jnp.concatenate(d_queries, axis=0).T.astype(SIXTEEN)
    dkv_ref[span, :] += jnp.concatenate(near_k + near_v, axis=1)
    dmeta_ref[...] += jnp.concatenate(meta_k + meta_v, axis=1)


def attend_operands(queries, kv_rows, doc_first):
    length = doc_first.shape[0]
    count = length // BLOCK
    near = jnp.pad(kv_rows[:length], ((REACH * BLOCK, 0), (0, 0)))
    meta = kv_rows[length:]
    arrays = (doc_first.reshape(count, 1, BLOCK), queries, near, near.T, meta, meta.T)
    width = queries.shape[1]

    def whole(array):
        return pl.BlockSpec(array.shape, lambda i: (0,) * array.ndim)

    specs = [
        pl.BlockSpec((1, 1, BLOCK), lambda i: (i, 0, 0)),
        pl.BlockSpec((BLOCK, width), lambda i: (i, 0)),
    ] + [whole(a) for a in arrays[2:]]
    return arrays, specs, count, width


def attend_forward(queries, kv_rows, doc_first):
    arrays, specs, count, width = attend_operands(queries, kv_rows, doc_first)
    heads = width // HEAD
    return pl.pallas_call(
        lambda *refs: attend_forward_kernel(heads, *refs),
        grid=(count,),
        in_specs=specs,
        out_specs=[
            pl.BlockSpec((BLOCK, width), lambda i: (i, 0)),
            pl.BlockSpec((1, heads, BLOCK), lambda i: (i, 0, 0)),
        ],
        out_shape=[
            jax.ShapeDtypeStruct(queries.shape, WIDE),
            jax.ShapeDtypeStruct((count, heads, BLOCK), WIDE),
        ],
        compiler_params=pltpu.CompilerParams(vmem_limit_bytes=48 * MIB),
        cost_estimate=takes(24),
    )(*arrays)


def attend_backward(queries, kv_rows, doc_first, out, log_total, d_out):
    arrays, specs, count, width = attend_operands(queries, kv_rows, doc_first)
    heads = width // HEAD
    near, meta = arrays[2], arrays[4]
    row_spec = pl.BlockSpec((BLOCK, width), lambda i: (i, 0))
    d_queries, d_near, d_meta = pl.pallas_call(
        lambda *refs: attend_backward_kernel(heads, *refs),
        grid=(count,),
        in_specs=specs
        + [row_spec, pl.BlockSpec((1, heads, BLOCK), lambda i: (i, 0, 0)), row_spec],
        out_specs=[
            row_spec,
            pl.BlockSpec(near.shape, lambda i: (0, 0)),
            pl.BlockSpec(meta.shape, lambda i: (0, 0)),
        ],
        out_shape=[
            jax.ShapeDtypeStruct(queries.shape, SIXTEEN),
            jax.ShapeDtypeStruct(near.shape, WIDE),
            jax.ShapeDtypeStruct(meta.shape, WIDE),
        ],
        compiler_params=pltpu.CompilerParams(vmem_limit_bytes=48 * MIB),
        cost_estimate=takes(24),
    )(*arrays, out, log_total, d_out)
    return d_queries, jnp.concatenate([d_near[REACH * BLOCK :], d_meta], axis=0).astype(SIXTEEN)


def step_sum():
    rows = lax.broadcasted_iota(jnp.int32, (SUB, SUB * STATE), 0)
    cols = lax.broadcasted_iota(jnp.int32, (SUB, SUB * STATE), 1)
    return (cols // STATE == rows).astype(SIXTEEN)


def lanes_from(tile, group):
    return pltpu.roll(tile, (SPAN - group * SUB) % SPAN, axis=1)


def scan_forward_kernel(keep_ref, conv_ref, delta_ref, bc_ref, a_ref, y_ref, start_ref, state_ref):
    block = pl.program_id(0)

    @pl.when(block == 0)
    def _():
        state_ref[...] = jnp.zeros_like(state_ref)

    start_ref[0] = state_ref[...]
    decay_rate = a_ref[...]
    fold = step_sum()
    b_span = bc_ref[:STATE, :].astype(WIDE)
    c_span = bc_ref[STATE:, :].astype(WIDE)

    def body(group, state):
        rows = pl.ds(pl.multiple_of(group * SUB, SUB), SUB)
        delta = delta_ref[rows, :]
        drive = delta * conv_ref[rows, :]
        b_tile = lanes_from(b_span, group)
        c_tile = lanes_from(c_span, group)
        reads = []
        for i in range(SUB):
            keep = keep_ref[block * SPAN + group * SUB + i]
            decay = jnp.exp(delta[i : i + 1, :] * decay_rate) * keep
            state = decay * state + drive[i : i + 1, :] * b_tile[:, i : i + 1]
            reads.append((state * c_tile[:, i : i + 1]).astype(SIXTEEN))
        y_ref[rows, :] = jnp.dot(
            fold, jnp.concatenate(reads, axis=0), preferred_element_type=WIDE
        )
        return state

    state_ref[...] = lax.fori_loop(0, SPAN // SUB, body, state_ref[...], unroll=8)


def scan_forward(keep, conv_out, delta, bc_rows, decay_rate):
    length, lanes = conv_out.shape
    blocks = length // SPAN
    span_spec = pl.BlockSpec((SPAN, lanes), lambda i: (i, 0))
    return pl.pallas_call(
        scan_forward_kernel,
        grid=(blocks,),
        in_specs=[
            pl.BlockSpec(memory_space=pltpu.SMEM),
            span_spec,
            span_spec,
            pl.BlockSpec((2 * STATE, SPAN), lambda i: (0, i)),
            pl.BlockSpec((STATE, lanes), lambda i: (0, 0)),
        ],
        out_specs=[span_spec, pl.BlockSpec((1, STATE, lanes), lambda i: (i, 0, 0))],
        out_shape=[
            jax.ShapeDtypeStruct((length, lanes), WIDE),
            jax.ShapeDtypeStruct((blocks, STATE, lanes), WIDE),
        ],
        scratch_shapes=[pltpu.VMEM((STATE, lanes), WIDE)],
        cost_estimate=takes(24),
    )(keep, conv_out, delta, bc_rows, decay_rate)


def scan_backward_kernel(
    keep_ref, conv_ref, delta_ref, bc_ref, a_ref, start_ref, dy_ref,
    dconv_ref, ddelta_ref, dbc_ref, da_ref,
    state_ref, decay_ref, adjoint_ref,
):
    turn = pl.program_id(0)
    block = pl.num_programs(0) - 1 - turn

    @pl.when(turn == 0)
    def _():
        adjoint_ref[...] = jnp.zeros_like(adjoint_ref)
        da_ref[...] = jnp.zeros_like(da_ref)

    decay_rate = a_ref[...]
    fold = step_sum()
    lanes = decay_rate.shape[1]
    ones = jnp.ones((lanes, SPAN), SIXTEEN)
    spot = lax.broadcasted_iota(jnp.int32, (STATE, SPAN), 1)
    b_span = bc_ref[:STATE, :].astype(WIDE)
    c_span = bc_ref[STATE:, :].astype(WIDE)
    state_ref[0] = start_ref[0]

    def ahead(group, state):
        rows = pl.ds(pl.multiple_of(group * SUB, SUB), SUB)
        delta = delta_ref[rows, :]
        drive = delta * conv_ref[rows, :]
        b_tile = lanes_from(b_span, group)
        for i in range(SUB):
            keep = keep_ref[block * SPAN + group * SUB + i]
            decay = jnp.exp(delta[i : i + 1, :] * decay_rate) * keep
            state = decay * state + drive[i : i + 1, :] * b_tile[:, i : i + 1]
            decay_ref[group * SUB + i] = decay
            state_ref[group * SUB + i + 1] = state
        return state

    lax.fori_loop(0, SPAN // SUB, ahead, start_ref[0], unroll=16)

    def back(step, carry):
        adjoint, da, db, dc = carry
        group = SPAN // SUB - 1 - step
        rows = pl.ds(pl.multiple_of(group * SUB, SUB), SUB)
        delta = delta_ref[rows, :]
        conv = conv_ref[rows, :]
        drive = delta * conv
        dy = dy_ref[rows, :]
        b_tile = lanes_from(b_span, group)
        c_tile = lanes_from(c_span, group)
        by_c, by_b, by_drive, by_delta = ([None] * SUB for _ in range(4))
        for i in range(SUB - 1, -1, -1):
            index = group * SUB + i
            dy_row = dy[i : i + 1, :]
            total = adjoint + dy_row * c_tile[:, i : i + 1]
            by_c[i] = (dy_row * state_ref[index + 1]).astype(SIXTEEN)
            by_b[i] = (total * drive[i : i + 1, :]).astype(SIXTEEN)
            by_drive[i] = (total * b_tile[:, i : i + 1]).astype(SIXTEEN)
            adjoint = total * decay_ref[index]
            rate = adjoint * state_ref[index]
            by_delta[i] = (rate * decay_rate).astype(SIXTEEN)
            da = da + rate * delta[i : i + 1, :]

        def over_state(parts):
            return jnp.dot(fold, jnp.concatenate(parts, axis=0), preferred_element_type=WIDE)

        def over_lanes(parts, tile):
            sums = jnp.dot(jnp.concatenate(parts, axis=0), ones, preferred_element_type=WIDE)
            for i in range(SUB):
                here = spot == group * SUB + i
                tile = jnp.where(here, sums[i * STATE : (i + 1) * STATE, :], tile)
            return tile

        d_drive = over_state(by_drive)
        dconv_ref[rows, :] = d_drive * delta
        ddelta_ref[rows, :] = over_state(by_delta) + d_drive * conv
        return adjoint, da, over_lanes(by_b, db), over_lanes(by_c, dc)

    none = jnp.zeros((STATE, SPAN), WIDE)
    adjoint, da, db, dc = lax.fori_loop(
        0, SPAN // SUB, back, (adjoint_ref[...], da_ref[...], none, none), unroll=16
    )
    adjoint_ref[...] = adjoint
    da_ref[...] = da
    dbc_ref[...] = jnp.concatenate([db, dc], axis=0)


def scan_backward(keep, conv_out, delta, bc_rows, decay_rate, starts, dy):
    length, lanes = conv_out.shape
    blocks = length // SPAN
    span_spec = pl.BlockSpec((SPAN, lanes), lambda i: (blocks - 1 - i, 0))
    rows_spec = pl.BlockSpec((2 * STATE, SPAN), lambda i: (0, blocks - 1 - i))
    whole = pl.BlockSpec((STATE, lanes), lambda i: (0, 0))
    return pl.pallas_call(
        scan_backward_kernel,
        grid=(blocks,),
        in_specs=[
            pl.BlockSpec(memory_space=pltpu.SMEM),
            span_spec,
            span_spec,
            rows_spec,
            whole,
            pl.BlockSpec((1, STATE, lanes), lambda i: (blocks - 1 - i, 0, 0)),
            span_spec,
        ],
        out_specs=[span_spec, span_spec, rows_spec, whole],
        out_shape=[
            jax.ShapeDtypeStruct((length, lanes), WIDE),
            jax.ShapeDtypeStruct((length, lanes), WIDE),
            jax.ShapeDtypeStruct((2 * STATE, length), WIDE),
            jax.ShapeDtypeStruct((STATE, lanes), WIDE),
        ],
        scratch_shapes=[
            pltpu.VMEM((SPAN + 1, STATE, lanes), WIDE),
            pltpu.VMEM((SPAN, STATE, lanes), WIDE),
            pltpu.VMEM((STATE, lanes), WIDE),
        ],
        compiler_params=pltpu.CompilerParams(vmem_limit_bytes=32 * MIB),
        cost_estimate=takes(40),
    )(keep, conv_out, delta, bc_rows, decay_rate, starts, dy)


def padded_lanes(array, lanes):
    return jnp.pad(array, ((0, 0), (0, lanes - array.shape[1])))


def rms_pull(values, scale, gain, d_normed, mean):
    d_values = scale * gain * d_normed - values * (scale * scale * scale) * mean
    return d_values, jnp.sum(d_normed * values * scale, axis=0)


def per_device(tokens, doc_ids, meta_tokens, mixer_params, small_params, ffn_params, cotangent):
    tokens, cotangent = tokens[0], cotangent[0]
    small_whole, ids, meta_whole = start_blocks(small_params, doc_ids[0], meta_tokens)
    (g_one, g_two, g_attn, channel_part), small_pull = jax.vjp(small_shards, small_whole)
    rows, shards = lax.axis_size("row"), lax.axis_size("seq")
    staged = weights_fit(mixer_params.shape[0], ffn_params.shape[0], rows, shards)
    if staged:
        columns, pull_columns = jax.vjp(partial(to_columns, width=view_width()), mixer_params)
    channels = channel_part.shape[0]
    lanes = -(-channels // 128) * 128
    g_ssm = channel_part[:, 0]
    conv_w = channel_part[:, 1 : 1 + CONV].T
    conv_b = channel_part[:, 1 + CONV]
    dt_bias = channel_part[:, 2 + CONV]
    a_log = channel_part[:, 3 + CONV : 3 + CONV + STATE]
    d_skip = channel_part[:, 3 + CONV + STATE]

    length = ids.shape[0]
    positions = jnp.arange(length, dtype=jnp.int32)
    starts = jnp.concatenate([jnp.ones((1,), bool), ids[1:] != ids[:-1]])
    doc_first = lax.cummax(jnp.where(starts, positions, 0), axis=0)
    keep_mask = (positions != doc_first).astype(WIDE)
    lag_masks = jnp.stack(
        [(positions - j >= doc_first).astype(WIDE)[:, None] for j in range(CONV)]
    )

    tokens_f = tokens.astype(WIDE)
    normed_f, norm_pull = jax.vjp(rms_norm, tokens_f, g_one)
    meta_own = meta_tokens.astype(WIDE)
    meta_unit = rms_norm(meta_whole.astype(WIDE), 1.0)
    normed_own = normed_f.astype(SIXTEEN)
    if staged:
        normed_own, columns = tie(normed_own, columns)
        both, pull_both = jax.vjp(both_halves, columns)
    normed = ring_seq_gather(normed_own, 1)
    cotangent_later = cotangent
    if staged:
        normed, both, cotangent_later = tie(normed, both, cotangent)
        (w_in, w_dt, q_rows, x_rows, out_rows), pull_parts = jax.vjp(mixer_parts, both)
        w_x, pull_x = jax.vjp(x_from, x_rows)
        by_heads, pull_rows = jax.vjp(heads_cut, q_rows)
    else:
        (w_qkv, w_in, w_x, w_dt, w_out), pull_mixer = jax.vjp(mixer_shards_whole, mixer_params)
        (w_gate, w_up, w_down), pull_ffn = jax.vjp(ffn_shards_whole, ffn_params)
    meta_normed = (meta_unit * g_one).astype(SIXTEEN)
    every = jnp.concatenate([normed, meta_normed], axis=0)
    cotangent_all = gather_seq(cotangent_later)

    xz = dot_last(normed, w_in).astype(SIXTEEN)
    extended = jnp.pad(xz[:, :channels], ((CONV - 1, 0), (0, 0))).astype(WIDE)
    conv_fn = partial(conv_piece, lag_masks=lag_masks)
    conv_out, conv_pull = jax.vjp(conv_fn, extended, conv_w, conv_b)
    conv_half = conv_out.astype(SIXTEEN)
    if staged:
        conv_half, w_x = tie(conv_half, w_x)
    conv_f = conv_half.astype(WIDE)
    w_x_rows = jnp.pad(w_x.T, ((0, -w_x.shape[1] % 16), (0, 0)))
    projected = seq_sum(jnp.einsum("nc,tc->nt", w_x_rows, conv_half, preferred_element_type=WIDE), 2)
    rank_half = projected[:DT_RANK]
    pre_dt = jnp.einsum("rt,rc->tc", rank_half, w_dt, preferred_element_type=WIDE)
    delta, delta_pull = jax.vjp(lambda p, b: softplus_fn(p + b), pre_dt, dt_bias)
    a_neg, a_pull = jax.vjp(lambda a: -jnp.exp(a), a_log)
    if staged:
        delta, by_heads, out_rows = tie(delta, by_heads, out_rows)
        w_qkv, pull_heads = jax.vjp(heads_from, by_heads)
    scan_in = (
        keep_mask,
        padded_lanes(conv_f, lanes),
        padded_lanes(delta, lanes),
        projected[DT_RANK : DT_RANK + 2 * STATE],
        padded_lanes(a_neg.T, lanes),
    )
    y_scan, scan_starts = scan_forward(*scan_in)

    def gate_piece(y, c, skip, z):
        return (y + skip * c) * silu_fn(z)

    z_in = xz[:, channels:].astype(WIDE)
    ssm_out, gate_pull = jax.vjp(gate_piece, y_scan[:, :channels], conv_f, d_skip, z_in)

    if staged:
        ssm_out, w_qkv, out_rows = tie(ssm_out, w_qkv, out_rows)
        w_out, pull_out = jax.vjp(out_from, out_rows)
    own_heads = g_attn.shape[0]
    queries = dot_last(normed, w_qkv[:, :own_heads]).astype(SIXTEEN)
    kv_rows = dot_last(every, w_qkv[:, own_heads:]).astype(SIXTEEN)
    if staged:
        queries, w_out, ffn_later = tie(queries, w_out, ffn_params)
        ffn_columns, pull_ffn_columns = jax.vjp(partial(to_columns, width=FF), ffn_later)
    attn_out, log_total = attend_forward(queries, kv_rows, doc_first)

    squares = jnp.stack([jnp.sum(attn_out * attn_out, axis=1), jnp.sum(ssm_out * ssm_out, axis=1)])
    squares = seq_sum_small(squares, 3)
    if staged:
        squares, ffn_columns = tie(squares, ffn_columns)
        ffn_both, pull_ffn_both = jax.vjp(both_halves, ffn_columns)
    scale_a = lax.rsqrt(squares[0] / (HEADS * HEAD) + norm_eps)[:, None]
    scale_m = lax.rsqrt(squares[1] / INNER + norm_eps)[:, None]
    mixed = 0.5 * jnp.concatenate(
        [attn_out * scale_a * g_attn, ssm_out * scale_m * g_ssm], axis=1
    )
    mixed = mixed.astype(SIXTEEN)
    hidden = tokens_f + product_scatter([(mixed, w_out, False)], 4)

    if staged:
        hidden, ffn_both = tie(hidden, ffn_both)
        (w_gate, w_up, down_rows), pull_ffn_parts = jax.vjp(ffn_parts, ffn_both)
        w_down, pull_down = jax.vjp(down_from, down_rows)
    second_f, second_pull = jax.vjp(rms_norm, hidden, g_two)
    second = ring_seq_gather(second_f.astype(SIXTEEN), 5)
    gate_pre = dot_last(second, w_gate)
    up_pre = dot_last(second, w_up)
    act_f, act_pull = jax.vjp(glu_piece, gate_pre, up_pre)
    act = act_f.astype(SIXTEEN)
    d_gate, d_up = act_pull(dot_back(cotangent_all, w_down))
    d_gate, d_up = d_gate.astype(SIXTEEN), d_up.astype(SIXTEEN)
    d_second = product_scatter([(d_gate, w_gate, True), (d_up, w_up, True)], 6)
    block_out = (hidden + scatter_seq(dot_last(act, w_down))).astype(SIXTEEN)
    d_hidden, grad_g_two = second_pull(d_second)
    d_hidden = d_hidden + cotangent.astype(WIDE)

    d_branch = ring_seq_gather(d_hidden.astype(SIXTEEN), 7)
    grads_ffn = hold(
        (
            dot_weight(second, d_gate).astype(SIXTEEN),
            dot_weight(second, d_up).astype(SIXTEEN),
            dot_weight(act, cotangent_all).astype(SIXTEEN),
        )
    )
    grad_out = hold(dot_weight(mixed, d_branch).astype(SIXTEEN))
    if staged:
        (d_down_rows,) = pull_down(grads_ffn[2])
    d_mixed = 0.5 * dot_back(d_branch, w_out)
    d_mix_a, d_mix_m = d_mixed[:, :own_heads], d_mixed[:, own_heads:]
    means = jnp.stack(
        [jnp.sum(attn_out * g_attn * d_mix_a, axis=1), jnp.sum(ssm_out * g_ssm * d_mix_m, axis=1)]
    )
    means = seq_sum_small(means, 8)
    if staged:
        means, d_down_rows, grad_gate, grad_up = tie(
            means, d_down_rows, grads_ffn[0], grads_ffn[1]
        )
        (d_ffn_both,) = pull_ffn_parts((grad_gate, grad_up, d_down_rows))
        (d_ffn_columns,) = pull_ffn_both(d_ffn_both)
        (d_out_rows,) = pull_out(grad_out)
    d_attn, grad_g_attn = rms_pull(
        attn_out, scale_a, g_attn, d_mix_a, means[0][:, None] / (HEADS * HEAD)
    )
    d_ssm, grad_g_ssm = rms_pull(ssm_out, scale_m, g_ssm, d_mix_m, means[1][:, None] / INNER)

    d_queries, d_kv = attend_backward(
        queries, kv_rows, doc_first, attn_out, log_total, d_attn
    )

    if staged:
        d_queries, d_kv, d_ffn_columns, d_out_rows = tie(
            d_queries, d_kv, d_ffn_columns, d_out_rows
        )
        (grad_ffn,) = pull_ffn_columns(d_ffn_columns)
    grad_qkv = jnp.concatenate([dot_weight(normed, d_queries), dot_weight(every, d_kv)], axis=1)
    grad_qkv = hold(grad_qkv.astype(SIXTEEN))

    d_y, d_conv, grad_d_skip, d_z = gate_pull(d_ssm)
    if staged:
        d_y, grad_qkv = tie(d_y, grad_qkv)
    d_conv_scan, d_delta, d_bc, d_rate = scan_backward(
        *scan_in, scan_starts, padded_lanes(d_y, lanes)
    )
    if staged:
        d_conv_scan, d_delta, grad_ffn, grad_qkv = tie(d_conv_scan, d_delta, grad_ffn, grad_qkv)
        (d_by_heads,) = pull_heads(grad_qkv)
    d_conv = d_conv + d_conv_scan[:, :channels]
    d_pre, grad_dt_bias = delta_pull(d_delta[:, :channels])
    (grad_a_log,) = a_pull(d_rate[:, :channels].T)
    d_pre = d_pre.astype(SIXTEEN)
    grad_dt = jnp.einsum("rt,tc->rc", rank_half, d_pre, preferred_element_type=WIDE)
    d_rank = jnp.einsum("rc,tc->rt", w_dt, d_pre, preferred_element_type=WIDE)
    d_proj = jnp.concatenate([d_rank, d_bc], axis=0)
    d_proj = seq_sum(jnp.pad(d_proj, ((0, -d_proj.shape[0] % 16), (0, 0))), 10)
    if staged:
        d_proj, d_by_heads = tie(d_proj, d_by_heads)
        (d_q_rows,) = pull_rows(d_by_heads)
    d_proj = d_proj[: DT_RANK + 2 * STATE].T
    grad_x = hold(dot_weight(conv_half, d_proj).astype(SIXTEEN))
    if staged:
        (d_x_rows,) = pull_x(grad_x)
    d_extended, grad_conv_w, grad_conv_b = conv_pull(d_conv + dot_back(d_proj, w_x))
    d_xz = jnp.concatenate([d_extended[CONV - 1 :], d_z], axis=1).astype(SIXTEEN)
    grad_in = hold(dot_weight(normed, d_xz).astype(SIXTEEN))
    grad_dt = grad_dt.astype(SIXTEEN)
    if staged:
        (d_both,) = pull_parts((grad_in, grad_dt, d_q_rows, d_x_rows, d_out_rows))
        d_xz, d_both = tie(d_xz, d_both)
        (d_columns,) = pull_both(d_both)
    d_meta = dot_back(d_kv[length:], w_qkv[:, own_heads:])
    d_qkv = jnp.concatenate([d_queries, d_kv[:length]], axis=1)
    d_normed = product_scatter([(d_xz, w_in, True), (d_qkv, w_qkv, True)], 11)
    if staged:
        d_normed, d_columns = tie(d_normed, d_columns)
        (grad_mixer,) = pull_columns(d_columns)
    else:
        (grad_mixer,) = pull_mixer((grad_qkv, grad_in, grad_x, grad_dt, grad_out))
        (grad_ffn,) = pull_ffn(grads_ffn)
    grad_from_norm, grad_g_one = norm_pull(d_normed)
    grad_tokens = d_hidden + grad_from_norm
    grad_g_meta = jnp.sum(d_meta * meta_unit, axis=0)
    grad_channels = jnp.concatenate(
        [
            grad_g_ssm[:, None],
            grad_conv_w.T,
            grad_conv_b[:, None],
            grad_dt_bias[:, None],
            grad_a_log,
            grad_d_skip[:, None],
        ],
        axis=1,
    )
    (grad_small,) = small_pull((grad_g_one + grad_g_meta, grad_g_two, grad_g_attn, grad_channels))
    grad_small, d_meta = end_blocks(grad_small, d_meta)
    _, meta_pull = jax.vjp(lambda v: rms_norm(v, g_one), meta_own)
    (grad_meta,) = meta_pull(d_meta)
    return (
        block_out[None],
        grad_tokens[None],
        grad_meta,
        hold(grad_mixer).astype(WIDE),
        grad_small,
        hold(grad_ffn).astype(WIDE),
    )


def solution(mesh):
    in_specs = (
        P("row", "seq", None),
        P("row", "seq"),
        P(("row", "seq"), None),
        P(("row", "seq")),
        P(("row", "seq")),
        P(("row", "seq")),
        P("row", "seq", None),
    )
    out_specs = (
        P("row", "seq", None),
        P("row", "seq", None),
        P(("row", "seq"), None),
        P(("row", "seq")),
        P(("row", "seq")),
        P(("row", "seq")),
    )
    return jax.shard_map(
        per_device, mesh=mesh, in_specs=in_specs, out_specs=out_specs, check_vma=False
    )
```

```python
import functools
from functools import partial
import math

import jax
import jax.numpy as jnp
from jax import lax
from jax.experimental import pallas as pl
from jax.experimental.layout import Layout, with_layout_constraint
from jax.experimental.pallas import tpu as pltpu
from jax.sharding import PartitionSpec as P

D = 1600
HEADS = 25
GROUPS = 5
HEAD = 64
INNER = 3200
STATE = 16
CONV = 4
DT_RANK = 100
FF = 5504
REACH = 8
BLOCK = 128
RUNS = 4
SUB = 8
SPAN = 128
SIXTEEN = jnp.bfloat16
WIDE = jnp.float32


norm_eps = 1e-05


def split_flat(flat_vec, layout):
    pieces = []
    offset = 0
    for piece_shape in layout:
        piece_len = math.prod(piece_shape)
        pieces.append(flat_vec[offset : offset + piece_len].reshape(piece_shape))
        offset += piece_len
    return pieces


def mixer_layout():
    return [
        (D, HEADS * HEAD),
        (D, 2 * GROUPS * HEAD),
        (D, 2 * INNER),
        (INNER, DT_RANK + 2 * STATE),
        (DT_RANK, INNER),
        (HEADS * HEAD + INNER, D),
    ]


def ffn_layout():
    return [(D, FF), (D, FF), (FF, D)]


def small_split(flat_vec):
    width = CONV + STATE + 4
    packed_rows = flat_vec[: D * (3 + 2 * width)].reshape(D, 3 + 2 * width)
    channel_part = packed_rows[:, 3:].reshape(INNER, width)
    return packed_rows[:, 0], packed_rows[:, 1], packed_rows[:, 2], channel_part


def rms_norm(values, gain_vec):
    return (
        values * lax.rsqrt(jnp.mean(values * values, axis=-1, keepdims=True) + norm_eps) * gain_vec
    )


def silu_fn(values):
    return values / (1.0 + jnp.exp(-values))


def softplus_fn(values):
    return jnp.maximum(values, 0.0) + jnp.log1p(jnp.exp(-jnp.abs(values)))


def glu_piece(gate_pre, up_pre):
    return silu_fn(gate_pre) * up_pre


def dot_last(left, right):
    return jnp.einsum("...k,kn->...n", left, right, preferred_element_type=WIDE)


def dot_back(grads, right):
    return jnp.einsum("...n,kn->...k", grads, right, preferred_element_type=WIDE)


def dot_weight(left, grads):
    return jnp.einsum("...k,...n->kn", left, grads, preferred_element_type=WIDE)


def heads_of(shards):
    return -(-HEADS // shards)


def runs_of(shards):
    return RUNS if INNER % (RUNS * shards) == 0 else 1


def own_channels(array, axis, shards, place):
    runs = runs_of(shards)
    unit = INNER // (runs * shards)
    shape = array.shape
    cut = array.reshape(shape[:axis] + (runs, shards, unit) + shape[axis + 1 :])
    cut = lax.dynamic_index_in_dim(cut, place, axis + 1, keepdims=False)
    return cut.reshape(shape[:axis] + (runs * unit,) + shape[axis + 1 :])


def pad_heads(array, axis, shards):
    heads = heads_of(shards)
    pads = [(0, 0)] * array.ndim
    pads[axis] = (0, heads * shards - HEADS)
    padded = jnp.pad(array, pads)
    shape = padded.shape
    return padded.reshape(shape[:axis] + (shards, heads * HEAD) + shape[axis + 2 :])


def by_head(w_q, w_kv, shards):
    rows = w_q.shape[0]
    w_kv = w_kv.reshape(rows, 2, GROUPS, 1, HEAD)
    w_kv = jnp.broadcast_to(w_kv, (rows, 2, GROUPS, HEADS // GROUPS, HEAD))
    w_kv = w_kv.reshape(rows, 2, HEADS, HEAD)
    return jnp.concatenate(
        [
            pad_heads(w_q.reshape(rows, HEADS, HEAD), 1, shards),
            pad_heads(w_kv[:, 0], 1, shards),
            pad_heads(w_kv[:, 1], 1, shards),
        ],
        axis=2,
    )


def exchange(value):
    return lax.all_to_all(value, "seq", 0, 0)


def tie(*arrays):
    return lax.optimization_barrier(arrays)


def hold(array):
    return lax.optimization_barrier(array)


@jax.custom_vjp
def rows_major(value):
    return with_layout_constraint(value, Layout(major_to_minor=(0, 1)))


rows_major.defvjp(lambda value: (rows_major(value), None), lambda _, grad: (rows_major(grad),))


def both_halves(value):
    if value.shape[1] > 128:
        value = rows_major(value)
    other = lax.ppermute(value, "row", [(0, 1), (1, 0)])
    if value.shape[1] > 128:
        other = rows_major(other)
    first = lax.axis_index("row") == 0
    return jnp.concatenate(
        [jnp.where(first, value, other), jnp.where(first, other, value)], axis=0
    )


@partial(jax.custom_vjp, nondiff_argnums=(1,))
def cut_rows(array, counts):
    pieces, offset = [], 0
    for count in counts:
        pieces.append(array[offset : offset + count])
        offset += count
    return tuple(pieces)


def cut_rows_forward(array, counts):
    return cut_rows(array, counts), None


def cut_rows_backward(counts, _, grads):
    return (jnp.concatenate(grads, axis=0),)


cut_rows.defvjp(cut_rows_forward, cut_rows_backward)


def view_width():
    return INNER // RUNS


def weights_fit(mixer_length, ffn_length, rows, shards):
    width = view_width()
    sizes = [math.prod(shape) for shape in mixer_layout()]
    return (
        rows == 2
        and runs_of(shards) == RUNS
        and mixer_length % width == 0
        and all(size % width == 0 for size in sizes)
        and D % shards == 0
        and D % width == 0
        and (HEADS * HEAD * 2) % shards == 0
        and shards % x_turns(shards)[0] == 0
        and ffn_length % FF == 0
    )


def to_columns(piece, width):
    shards = lax.axis_size("seq")
    unit = width // shards
    view = hold(piece.reshape(-1, width))
    return exchange(view.reshape(-1, shards, unit).transpose(1, 0, 2)).reshape(-1, unit)


def full_rows(cut):
    received = exchange(cut)
    return hold(received.transpose(1, 0, 2).reshape(received.shape[1], -1))


def mixer_parts(both):
    width, shards = view_width(), lax.axis_size("seq")
    unit = both.shape[1]
    part_q, part_kv, part_in, part_x, part_dt, part_out = cut_rows(
        both, tuple(math.prod(shape) // width for shape in mixer_layout())
    )
    q_rows = jnp.concatenate(
        [part_q.reshape(shards, -1, unit), part_kv.reshape(shards, -1, unit)], axis=1
    )
    per_row = D // width
    head_rows = heads_of(shards) * HEAD
    out_heads, out_inner = cut_rows(part_out, (HEADS * HEAD * per_row, INNER * per_row))
    out_heads = jnp.pad(
        out_heads, ((0, (head_rows * shards - HEADS * HEAD) * per_row), (0, 0))
    ).reshape(shards, -1, unit)
    out_inner = out_inner.reshape(RUNS, shards, -1, unit)
    out_inner = out_inner.transpose(1, 0, 2, 3).reshape(shards, -1, unit)
    return (
        part_in.reshape(D, -1),
        part_dt.reshape(DT_RANK, -1),
        q_rows,
        x_windows(part_x, shards),
        jnp.concatenate([out_heads, out_inner], axis=1),
    )


def heads_cut(q_rows):
    shards = lax.axis_size("seq")
    rows = D // shards
    by_rows = full_rows(q_rows)
    split = rows * HEADS * HEAD // view_width()
    cut = by_head(
        by_rows[:split].reshape(rows, HEADS * HEAD),
        by_rows[split:].reshape(rows, 2 * GROUPS * HEAD),
        shards,
    )
    return cut.transpose(1, 0, 2)


def heads_from(cut):
    return exchange(cut).reshape(D, -1)


def x_from(windows):
    return x_from_windows(full_rows(windows), lax.axis_index("seq"))


def out_from(cut):
    return full_rows(cut).reshape(-1, D)


def ffn_parts(both):
    w_gate, w_up, part_down = cut_rows(both, (D, D, D))
    return w_gate, w_up, part_down.reshape(lax.axis_size("seq"), -1, both.shape[1])


def down_from(cut):
    return full_rows(cut).reshape(-1, D)


def x_turns(shards):
    width = INNER // RUNS
    run = (width // shards) * (DT_RANK + 2 * STATE)
    common = math.gcd(run, width)
    return width // common, run // common


def x_windows(part_x, shards):
    runs, rows = x_turns(shards)
    need = -(-rows // runs)
    turns = part_x.reshape(-1, rows, part_x.shape[1])
    cuts = [turns[:, (i * rows) // runs : (i * rows) // runs + need] for i in range(runs)]
    cuts = jnp.stack(cuts, axis=1).reshape(RUNS, shards, need, part_x.shape[1])
    return cuts.transpose(1, 0, 2, 3).reshape(shards, RUNS * need, part_x.shape[1])


def x_from_windows(view_rows, place):
    width = view_rows.shape[1]
    shards = lax.axis_size("seq")
    runs, rows = x_turns(shards)
    columns = DT_RANK + 2 * STATE
    count = (width // shards) * columns
    flat = view_rows.reshape(RUNS, -1)
    offset = (place % runs) * rows * (width // runs) % width
    return lax.dynamic_slice_in_dim(flat, offset, count, 1).reshape(-1, columns)


def mixer_shards_whole(piece):
    shards, place = lax.axis_size("seq"), lax.axis_index("seq")
    whole = lax.all_gather(piece, ("row", "seq"), axis=0, tiled=True)
    w_q, w_kv, w_in, w_x, w_dt, w_out = split_flat(whole, mixer_layout())
    qkv = lax.dynamic_index_in_dim(by_head(w_q, w_kv, shards), place, 1, keepdims=False)
    w_in = own_channels(w_in.reshape(D, 2, INNER), 2, shards, place)
    out_heads = w_out[: HEADS * HEAD].reshape(HEADS, HEAD, D)
    out_heads = lax.dynamic_index_in_dim(pad_heads(out_heads, 0, shards), place, 0, keepdims=False)
    return (
        qkv,
        w_in.reshape(D, -1),
        own_channels(w_x, 0, shards, place),
        own_channels(w_dt, 1, shards, place),
        jnp.concatenate([out_heads, own_channels(w_out[HEADS * HEAD :], 0, shards, place)], axis=0),
    )


def ffn_shards_whole(piece):
    unit = FF // lax.axis_size("seq")
    start = lax.axis_index("seq") * unit
    whole = lax.all_gather(piece, ("row", "seq"), axis=0, tiled=True)
    w_gate, w_up, w_down = split_flat(whole, ffn_layout())
    return (
        lax.dynamic_slice_in_dim(w_gate, start, unit, 1),
        lax.dynamic_slice_in_dim(w_up, start, unit, 1),
        lax.dynamic_slice_in_dim(w_down, start, unit, 0),
    )


def small_shards(whole):
    shards, place = lax.axis_size("seq"), lax.axis_index("seq")
    g_one, g_attn, g_two, channel_part = small_split(whole)
    g_attn = pad_heads(g_attn.reshape(HEADS, HEAD), 0, shards)
    return (
        g_one,
        g_two,
        lax.dynamic_index_in_dim(g_attn, place, 0, keepdims=False),
        own_channels(channel_part, 0, shards, place),
    )


def tiles_of(count):
    return -(-count // 128)


def start_blocks(small_params, doc_ids, meta_tokens):
    devices = lax.axis_size("row") * lax.axis_size("seq")
    parts = [small_params, doc_ids.astype(SIXTEEN), meta_tokens.reshape(-1)]
    rows = [tiles_of(part.shape[0]) for part in parts]
    rows_all = -(-sum(rows) // 16) * 16
    tiles = [
        jnp.pad(part, (0, count * 128 - part.shape[0])).reshape(-1, 128)
        for part, count in zip(parts, rows)
    ]
    block = jnp.concatenate(tiles + [jnp.zeros((rows_all - sum(rows), 128), SIXTEEN)], axis=0)
    every = push_gather(block, 0)
    outs, begin = [], 0
    for part, count in zip(parts, rows):
        cut = every[:, begin : begin + count].reshape(devices, -1)[:, : part.shape[0]]
        outs.append(cut)
        begin += count
    ids = outs[1].reshape(lax.axis_size("row"), -1)
    ids = lax.dynamic_index_in_dim(ids, lax.axis_index("row"), 0, keepdims=False)
    return outs[0].reshape(-1).astype(WIDE), ids.astype(jnp.int32), outs[2].reshape(-1, D)


def end_blocks(grad_small, d_meta):
    devices = lax.axis_size("row") * lax.axis_size("seq")
    parts = grad_small.reshape(devices, -1).astype(SIXTEEN)
    small_count = parts.shape[1]
    small_rows = tiles_of(small_count)
    parts = jnp.pad(parts, ((0, 0), (0, small_rows * 128 - small_count)))
    meta = d_meta.astype(SIXTEEN).reshape(devices, -1)
    meta_count = meta.shape[1]
    rows = -(-(small_rows + tiles_of(meta_count)) // 16) * 16
    meta = jnp.pad(meta, ((0, 0), (0, (rows - small_rows) * 128 - meta_count)))
    blocks = jnp.concatenate(
        [parts.reshape(devices, -1, 128), meta.reshape(devices, -1, 128)], axis=1
    )
    own = push_scatter(blocks, 9)
    small = own[:small_rows].reshape(-1)[:small_count]
    meta = own[small_rows:].reshape(-1)[:meta_count].reshape(-1, D)
    return small, meta


def gather_seq(block):
    return lax.all_gather(block, "seq", axis=0, tiled=True)


def scatter_seq(whole):
    return lax.psum_scatter(whole.astype(SIXTEEN), "seq", scatter_dimension=0, tiled=True).astype(
        WIDE
    )


MESH = pl.DeviceIdType.MESH
ANY = pl.BlockSpec(memory_space=pl.ANY)
VMEM = pl.BlockSpec(memory_space=pltpu.VMEM)
MIB = 1024 * 1024


def takes(microseconds):
    return pl.CostEstimate(
        flops=0, bytes_accessed=microseconds * 3_500_000, transcendentals=0
    )


def greet(peers):
    barrier = pltpu.get_barrier_semaphore()
    for peer in peers:
        pl.semaphore_signal(barrier, inc=1, device_id=peer, device_id_type=MESH)
    pl.semaphore_wait(barrier, len(peers))


def ring_place(chip, chips):
    odd = chip % 2
    return odd * (chips - 1 - chip // 2) + (1 - odd) * (chip // 2)


def ring_chip(place, chips):
    place = (place + 2 * chips) % chips
    back = place // (chips // 2)
    return back * (2 * (chips - 1 - place) + 1) + (1 - back) * (2 * place)


def ring_gather_loop(shards, parts, x_ref, out_ref, ring_send, ring_recv, pair_send, pair_recv, work):
    row, me = lax.axis_index("row"), lax.axis_index("seq")
    chips = shards // 2
    core = me % 2
    place = ring_place(me // 2, chips)

    def device(spot):
        return ring_chip(spot, chips) * 2 + core

    right, left, twin = (row, device(place + 1)), (row, device(place - 1)), (row, me + 1 - 2 * core)
    greet([right, left, twin])
    rows = x_ref.shape[0] // (2 * parts)
    paths = [(way, part) for part in range(parts) for way in range(2)]

    def piece(way, part, step):
        source = device(place - 1 - step if way == 0 else place + 1 + step)
        return out_ref.at[source, pl.ds((way * parts + part) * rows, rows)]

    def ring(way, part, step):
        here = piece(way, part, step - 1)
        return pltpu.make_async_remote_copy(
            src_ref=here, dst_ref=here, send_sem=ring_send.at[way, part, step],
            recv_sem=ring_recv.at[way, part, step], device_id=(right, left)[way], device_id_type=MESH,
        )

    def pair(way, part, step):
        here = piece(way, part, step - 1)
        return pltpu.make_async_remote_copy(
            src_ref=here, dst_ref=here, send_sem=pair_send.at[way, part, step],
            recv_sem=pair_recv.at[way, part, step], device_id=twin, device_id_type=MESH,
        )

    out_ref[me] = x_ref[...]
    for way, part in paths:
        ring(way, part, 0).start()
    for way, part in paths:
        pair(way, part, 0).start()

    def body(step, carry):
        @pl.when(step < chips - 1)
        def _():
            for way, part in paths:
                ring(way, part, step).wait_recv()

                @pl.when(step < chips - 2)
                def _():
                    ring(way, part, step + 1).start()

                pair(way, part, step + 1).start()

        for way, part in paths:
            pair(way, part, step).wait_recv()
        work(step, place)
        return carry

    lax.fori_loop(0, chips, body, 0)

    def finish(step, carry):
        for way, part in paths:
            pair(way, part, step).wait_send()

            @pl.when(step < chips - 1)
            def _():
                ring(way, part, step).wait_send()

        return carry

    lax.fori_loop(0, chips, finish, 0)


def ring_semaphores(chips, parts):
    ring = pltpu.SemaphoreType.DMA((2, parts, chips - 1))
    pair = pltpu.SemaphoreType.DMA((2, parts, chips))
    return [ring, ring, pair, pair]


def seq_gather_kernel(shards, parts, x_ref, out_ref, *sems):
    ring_gather_loop(shards, parts, x_ref, out_ref, *sems, lambda step, place: None)


def fits_vmem(*shapes):
    return sum(padded_bytes(shape, 2) for shape in shapes) < 48 * MIB


def ring_seq_gather(block, collective_id, parts=2):
    shards = lax.axis_size("seq")
    rows, width = block.shape
    if not fits_vmem((shards * rows, width)):
        return lax.all_gather(block, "seq", axis=0, tiled=True)
    gathered = pl.pallas_call(
        functools.partial(seq_gather_kernel, shards, parts),
        out_shape=jax.ShapeDtypeStruct((shards, rows, width), block.dtype),
        in_specs=[VMEM],
        out_specs=VMEM,
        scratch_shapes=ring_semaphores(shards // 2, parts),
        compiler_params=pltpu.CompilerParams(
            collective_id=collective_id, has_side_effects=True, vmem_limit_bytes=56 * MIB
        ),
        cost_estimate=takes(40),
    )(block)
    return gathered.reshape(shards * rows, width)


def gather_ffn_kernel(
    shards, parts, x_ref, cot_ref, gate_ref, up_ref, down_ref,
    out_ref, act_ref, d_gate_ref, d_up_ref, *sems,
):
    chips = shards // 2
    rows = x_ref.shape[0]
    half = rows // 2

    def work(step, place):
        back, ahead = ring_chip(place - step, chips) * 2, ring_chip(place + step, chips) * 2
        spots = [(back, 0), (back + 1, 0), (ahead, half), (ahead + 1, half)]
        starts = [pl.multiple_of(index * rows + first, half) for index, first in spots]
        tokens = jnp.concatenate([out_ref[index, pl.ds(first, half), :] for index, first in spots], axis=0)
        cot = jnp.concatenate([cot_ref[pl.ds(start, half), :] for start in starts], axis=0)
        gate = jnp.dot(tokens, gate_ref[...], preferred_element_type=WIDE)
        up = jnp.dot(tokens, up_ref[...], preferred_element_type=WIDE)
        d_act = lax.dot_general(
            cot, down_ref[...], (((1,), (1,)), ((), ())), preferred_element_type=WIDE
        )
        share = 1.0 / (1.0 + jnp.exp(-gate))
        passed = gate * share
        results = (
            (act_ref, passed * up),
            (d_gate_ref, d_act * up * (share * (1.0 + gate * (1.0 - share)))),
            (d_up_ref, d_act * passed),
        )
        for ref, value in results:
            value = value.astype(SIXTEEN)
            for i, start in enumerate(starts):
                ref[pl.ds(start, half), :] = value[i * half : (i + 1) * half]

    ring_gather_loop(shards, parts, x_ref, out_ref, *sems, work)


def gather_ffn(block, cotangent, w_gate, w_up, w_down, collective_id, parts=2):
    shards = lax.axis_size("seq")
    rows, width = block.shape
    units = w_gate.shape[1]
    if not fits_vmem((shards * rows, width), (shards * rows, width), (3 * shards * rows, units)):
        second = ring_seq_gather(block, collective_id)
        gate, up = dot_last(second, w_gate), dot_last(second, w_up)
        act, pull = jax.vjp(glu_piece, gate, up)
        d_gate, d_up = pull(dot_back(cotangent, w_down))
        return second, act.astype(SIXTEEN), d_gate.astype(SIXTEEN), d_up.astype(SIXTEEN)
    hidden = jax.ShapeDtypeStruct((shards * rows, units), SIXTEEN)
    outs = pl.pallas_call(
        functools.partial(gather_ffn_kernel, shards, parts),
        out_shape=[jax.ShapeDtypeStruct((shards, rows, width), SIXTEEN), hidden, hidden, hidden],
        in_specs=[VMEM] * 5,
        out_specs=[VMEM] * 4,
        scratch_shapes=ring_semaphores(shards // 2, parts),
        compiler_params=pltpu.CompilerParams(
            collective_id=collective_id, has_side_effects=True, vmem_limit_bytes=56 * MIB
        ),
        cost_estimate=takes(45),
    )(block, cotangent, w_gate, w_up, w_down)
    return (outs[0].reshape(shards * rows, width),) + tuple(outs[1:])


def gather_beside_kernel(
    shards, parts, x_ref, second_ref, cot_ref, act_ref, d_gate_ref, d_up_ref, down_ref,
    out_ref, g_gate_ref, g_up_ref, g_down_ref, product_ref, *sems,
):
    chips = shards // 2
    width = second_ref.shape[1]
    block = 256
    turns = width // block
    share = act_ref.shape[0] // chips

    def tn_dot(left, right):
        return lax.dot_general(
            left, right, (((0,), (0,)), ((), ())), preferred_element_type=WIDE
        ).astype(SIXTEEN)

    def columns(cut):
        tokens = second_ref[:, cut]
        g_gate_ref[cut, :] = tn_dot(tokens, d_gate_ref[...])
        g_up_ref[cut, :] = tn_dot(tokens, d_up_ref[...])
        g_down_ref[:, cut] = tn_dot(act_ref[...], cot_ref[:, cut])

    def work(step, place):
        @pl.when(step < turns)
        def _():
            columns(pl.ds(pl.multiple_of(step * block, block), block))

        @pl.when(step == turns)
        def _():
            columns(slice(turns * block, width))

        here = pl.ds(pl.multiple_of(step * share, share), share)
        product_ref[here, :] = jnp.dot(
            act_ref[here, :], down_ref[...], preferred_element_type=WIDE
        ).astype(SIXTEEN)

    ring_gather_loop(shards, parts, x_ref, out_ref, *sems, work)


def gather_beside_ffn(block, second, cotangent, act, d_gate, d_up, w_down, collective_id, parts=2):
    shards = lax.axis_size("seq")
    rows, width = block.shape
    length, units = act.shape
    chips = shards // 2
    if width // 256 >= chips or not fits_vmem(
        (4 * length, width), (3 * length, units), (3 * width, units)
    ):
        return (
            ring_seq_gather(block, collective_id),
            dot_weight(second, d_gate).astype(SIXTEEN),
            dot_weight(second, d_up).astype(SIXTEEN),
            dot_weight(act, cotangent).astype(SIXTEEN),
            dot_last(act, w_down).astype(SIXTEEN),
        )
    outs = pl.pallas_call(
        functools.partial(gather_beside_kernel, shards, parts),
        out_shape=[
            jax.ShapeDtypeStruct((shards, rows, width), SIXTEEN),
            jax.ShapeDtypeStruct((width, units), SIXTEEN),
            jax.ShapeDtypeStruct((width, units), SIXTEEN),
            jax.ShapeDtypeStruct((units, width), SIXTEEN),
            jax.ShapeDtypeStruct((length, width), SIXTEEN),
        ],
        in_specs=[VMEM] * 7,
        out_specs=[VMEM] * 5,
        scratch_shapes=ring_semaphores(shards // 2, parts),
        compiler_params=pltpu.CompilerParams(
            collective_id=collective_id, has_side_effects=True, vmem_limit_bytes=60 * MIB
        ),
        cost_estimate=takes(45),
    )(block, second, cotangent, act, d_gate, d_up, w_down)
    return (outs[0].reshape(shards * rows, width),) + tuple(outs[1:])


def product_scatter_kernel(shards, parts, turned, *refs):
    terms = len(turned)
    lefts, rights = refs[:terms], refs[terms : 2 * terms]
    out_ref, mine, given, pair, arrived = refs[2 * terms : 2 * terms + 5]
    ring_send, ring_recv, pair_send, pair_recv = refs[2 * terms + 5 :]
    row, me = lax.axis_index("row"), lax.axis_index("seq")
    chips = shards // 2
    core = me % 2
    place = ring_place(me // 2, chips)
    block_rows = out_ref.shape[0]

    def device(spot, core):
        return ring_chip(spot, chips) * 2 + core

    right = (row, device(place + 1, core))
    left = (row, device(place - 1, core))
    twin = (row, me + 1 - 2 * core)
    greet([right, left, twin])
    rows = block_rows // (2 * parts)

    def cut(way, part):
        return pl.ds((way * parts + part) * rows, rows)

    def product(index):
        here = pl.ds(pl.multiple_of(index * block_rows, block_rows), block_rows)
        total = None
        for left_ref, right_ref, turn in zip(lefts, rights, turned):
            part = lax.dot_general(
                left_ref[here, :], right_ref[...], (((1,), (1 if turn else 0,)), ((), ())),
                preferred_element_type=WIDE,
            )
            total = part if total is None else total + part
        return total.astype(SIXTEEN)

    def pass_over(slot):
        return pltpu.make_async_remote_copy(
            src_ref=given.at[slot], dst_ref=pair.at[slot], send_sem=pair_send.at[slot],
            recv_sem=pair_recv.at[slot], device_id=twin, device_id_type=MESH,
        )

    def make(far):
        slot = far % chips
        given[slot] = product(device(place + far, 1 - core))
        pass_over(slot).start()
        mine[slot] = product(device(place + far, core))

    def both(step, carry):
        make(-step)
        make(step)
        return carry

    half = chips // 2
    both(1, 0)
    started, flights = [], {}
    fresh = set(range(chips))
    for step in range(chips):
        if step + 2 < half:
            both(step + 2, 0)
        elif step + 2 == half:
            make(half)
            make(0)
        for part in range(parts):
            for way in range(2):
                slot = (-1 - step if way == 0 else 1 + step) % chips
                if slot in fresh:
                    fresh.remove(slot)
                    pass_over(slot).wait_recv()
                here = cut(way, part)
                total = mine[slot, here, :].astype(WIDE) + pair[slot, here, :].astype(WIDE)
                if step:
                    flights[way, part].wait_recv()
                    total = total + arrived[way, step - 1, pl.ds(part * rows, rows), :].astype(WIDE)
                if step == chips - 1:
                    out_ref[here, :] = total
                    continue
                mine[slot, here, :] = total.astype(SIXTEEN)
                copy = pltpu.make_async_remote_copy(
                    src_ref=mine.at[slot, here], dst_ref=arrived.at[way, step, pl.ds(part * rows, rows)],
                    send_sem=ring_send.at[way, part, step], recv_sem=ring_recv.at[way, part, step],
                    device_id=(right, left)[way], device_id_type=MESH,
                )
                copy.start()
                started.append(copy)
                flights[way, part] = copy
    for slot in range(chips):
        pass_over(slot).wait_send()
    for copy in started:
        copy.wait_send()


def padded_bytes(shape, bytes_each):
    return -(-shape[0] // 16) * 16 * -(-shape[1] // 128) * 128 * bytes_each


def product_scatter(terms, collective_id, parts=2):
    shards = lax.axis_size("seq")
    chips = shards // 2
    length = terms[0][0].shape[0]
    width = terms[0][1].shape[0 if terms[0][2] else 1]
    rows = length // shards
    buffers = 4 * chips * padded_bytes((rows, width), 2)
    operands = sum(padded_bytes(t[0].shape, 2) + padded_bytes(t[1].shape, 2) for t in terms)
    if chips < 4 or buffers + operands > 40 * MIB:
        total = 0
        for left, right, turn in terms:
            total = total + lax.dot_general(
                left, right, (((1,), (1 if turn else 0,)), ((), ())), preferred_element_type=WIDE
            )
        return lax.psum_scatter(
            total.astype(SIXTEEN), "seq", scatter_dimension=0, tiled=True
        ).astype(WIDE)
    ring = pltpu.SemaphoreType.DMA((2, parts, chips - 1))
    pair = pltpu.SemaphoreType.DMA((chips,))
    blocks = pltpu.VMEM((chips, rows, width), SIXTEEN)
    return pl.pallas_call(
        functools.partial(product_scatter_kernel, shards, parts, tuple(t[2] for t in terms)),
        out_shape=jax.ShapeDtypeStruct((rows, width), WIDE),
        in_specs=[VMEM] * (2 * len(terms)),
        out_specs=VMEM,
        scratch_shapes=[
            blocks, blocks, blocks,
            pltpu.VMEM((2, chips - 1, rows // 2, width), SIXTEEN),
            ring, ring, pair, pair,
        ],
        compiler_params=pltpu.CompilerParams(
            collective_id=collective_id, has_side_effects=True, vmem_limit_bytes=56 * MIB
        ),
        cost_estimate=takes(40),
    )(*[t[0] for t in terms], *[t[1] for t in terms])


def bits_of(shards):
    bits = shards.bit_length() - 1
    assert 1 << bits == shards
    return bits


def partner_of(me, bit):
    return me + (1 - 2 * ((me // (1 << bit)) % 2)) * (1 << bit)


def seq_sum_kernel(bits, x_ref, out_ref, total, staged, arrived, send_sem, recv_sem, back_send, back_recv):
    row, me = lax.axis_index("row"), lax.axis_index("seq")
    partners = [(row, partner_of(me, bit)) for bit in range(bits)]
    greet(partners)
    length = x_ref.shape[1]
    total[...] = x_ref[...].astype(WIDE)
    begin = 0
    started = []
    for bit in range(bits):
        half = length >> (bit + 1)
        upper = (me // (1 << bit)) % 2
        kept = pl.multiple_of(begin + upper * half, 128)
        given = pl.multiple_of(begin + (1 - upper) * half, 128)
        staged[:, half : 2 * half] = total[:, pl.ds(given, half)].astype(SIXTEEN)
        copy = pltpu.make_async_remote_copy(
            src_ref=staged.at[:, half : 2 * half], dst_ref=arrived.at[:, half : 2 * half],
            send_sem=send_sem.at[bit], recv_sem=recv_sem.at[bit],
            device_id=partners[bit], device_id_type=MESH,
        )
        copy.start()
        started.append(copy)
        copy.wait_recv()
        total[:, pl.ds(kept, half)] += arrived[:, half : 2 * half].astype(WIDE)
        begin = kept
    half = length >> bits
    out_ref[:, pl.ds(pl.multiple_of(begin, 128), half)] = total[
        :, pl.ds(pl.multiple_of(begin, 128), half)
    ].astype(SIXTEEN)
    for bit in range(bits - 1, -1, -1):
        half = length >> (bit + 1)
        here = out_ref.at[:, pl.ds(pl.multiple_of(begin, 128), half)]
        copy = pltpu.make_async_remote_copy(
            src_ref=here, dst_ref=here, send_sem=back_send.at[bit], recv_sem=back_recv.at[bit],
            device_id=partners[bit], device_id_type=MESH,
        )
        copy.start()
        started.append(copy)
        copy.wait_recv()
        begin = begin - ((me // (1 << bit)) % 2) * half
    for copy in started:
        copy.wait_send()


def seq_sum(values, collective_id):
    bits = bits_of(lax.axis_size("seq"))
    rows, length = values.shape
    sems = pltpu.SemaphoreType.DMA((bits,))
    return pl.pallas_call(
        functools.partial(seq_sum_kernel, bits),
        out_shape=jax.ShapeDtypeStruct((rows, length), SIXTEEN),
        in_specs=[VMEM],
        out_specs=VMEM,
        scratch_shapes=[
            pltpu.VMEM((rows, length), WIDE),
            pltpu.VMEM((rows, length), SIXTEEN),
            pltpu.VMEM((rows, length), SIXTEEN),
            sems, sems, sems, sems,
        ],
        compiler_params=pltpu.CompilerParams(
            collective_id=collective_id, has_side_effects=True, vmem_limit_bytes=48 * MIB
        ),
        cost_estimate=takes(30),
    )(values)


def seq_sum_small_kernel(bits, x_ref, out_ref, arrived, staged, send_sem, recv_sem):
    row, me = lax.axis_index("row"), lax.axis_index("seq")
    partners = [(row, partner_of(me, bit)) for bit in range(bits)]
    greet(partners)
    total = x_ref[...]
    copies = []
    for bit in range(bits):
        staged[bit] = total
        copy = pltpu.make_async_remote_copy(
            src_ref=staged.at[bit], dst_ref=arrived.at[bit], send_sem=send_sem.at[bit],
            recv_sem=recv_sem.at[bit], device_id=partners[bit], device_id_type=MESH,
        )
        copy.start()
        copies.append(copy)
        copy.wait_recv()
        total = total + arrived[bit]
    out_ref[...] = total
    for copy in copies:
        copy.wait_send()


def seq_sum_small(values, collective_id):
    bits = bits_of(lax.axis_size("seq"))
    shape = values.shape
    tiles = values.reshape(-1, 128)
    sems = pltpu.SemaphoreType.DMA((bits,))
    slots = pltpu.VMEM((bits,) + tiles.shape, WIDE)
    return pl.pallas_call(
        functools.partial(seq_sum_small_kernel, bits),
        out_shape=jax.ShapeDtypeStruct(tiles.shape, WIDE),
        in_specs=[VMEM],
        out_specs=VMEM,
        scratch_shapes=[slots, slots, sems, sems],
        compiler_params=pltpu.CompilerParams(collective_id=collective_id, has_side_effects=True),
        cost_estimate=takes(12),
    )(tiles).reshape(shape)


def all_peers(rows, shards):
    me = lax.axis_index("row") * shards + lax.axis_index("seq")
    count = rows * shards
    ahead = [(me + far) % count for far in range(1, count)]
    return me, count, [(other, (other // shards, other % shards)) for other in ahead]


def push_gather_kernel(rows, shards, x_ref, out_ref, send_sem, recv_sem):
    me, count, peers = all_peers(rows, shards)
    greet([device for _, device in peers])
    copies = []
    for far, (_, device) in enumerate(peers):
        copy = pltpu.make_async_remote_copy(
            src_ref=x_ref, dst_ref=out_ref.at[me], send_sem=send_sem.at[far],
            recv_sem=recv_sem.at[far], device_id=device, device_id_type=MESH,
        )
        copy.start()
        copies.append(copy)
    out_ref[me] = x_ref[...]
    for copy in copies:
        copy.wait()


def push_gather(block, collective_id):
    rows, shards = lax.axis_size("row"), lax.axis_size("seq")
    sems = pltpu.SemaphoreType.DMA((rows * shards - 1,))
    return pl.pallas_call(
        functools.partial(push_gather_kernel, rows, shards),
        out_shape=jax.ShapeDtypeStruct((rows * shards,) + block.shape, block.dtype),
        in_specs=[VMEM],
        out_specs=VMEM,
        scratch_shapes=[sems, sems],
        compiler_params=pltpu.CompilerParams(collective_id=collective_id, has_side_effects=True),
        cost_estimate=takes(20),
    )(block)


def push_scatter_kernel(rows, shards, x_ref, out_ref, arrived, send_sem, recv_sem):
    me, count, peers = all_peers(rows, shards)
    greet([device for _, device in peers])
    copies = []
    for far, (other, device) in enumerate(peers):
        copy = pltpu.make_async_remote_copy(
            src_ref=x_ref.at[other], dst_ref=arrived.at[far], send_sem=send_sem.at[far],
            recv_sem=recv_sem.at[far], device_id=device, device_id_type=MESH,
        )
        copy.start()
        copies.append(copy)
    total = x_ref[me].astype(WIDE)
    for far, copy in enumerate(copies):
        copy.wait_recv()
        total = total + arrived[far].astype(WIDE)
    out_ref[...] = total
    for copy in copies:
        copy.wait_send()


def push_scatter(blocks, collective_id):
    rows, shards = lax.axis_size("row"), lax.axis_size("seq")
    count = rows * shards
    sems = pltpu.SemaphoreType.DMA((count - 1,))
    return pl.pallas_call(
        functools.partial(push_scatter_kernel, rows, shards),
        out_shape=jax.ShapeDtypeStruct(blocks.shape[1:], WIDE),
        in_specs=[VMEM],
        out_specs=VMEM,
        scratch_shapes=[pltpu.VMEM((count - 1,) + blocks.shape[1:], blocks.dtype), sems, sems],
        compiler_params=pltpu.CompilerParams(
            collective_id=collective_id, has_side_effects=True, vmem_limit_bytes=32 * MIB
        ),
        cost_estimate=takes(20),
    )(blocks)


def conv_piece(extended, conv_w, conv_b, lag_masks):
    length = extended.shape[0] - (CONV - 1)
    summed = conv_b
    for j in range(CONV):
        summed = (
            summed + conv_w[j] * extended[CONV - 1 - j : CONV - 1 - j + length] * lag_masks[j]
        )
    return silu_fn(summed)


def nt_dot(left, right):
    return lax.dot_general(left, right, (((1,), (1,)), ((), ())), preferred_element_type=WIDE)


def seen_keys(block, first_row):
    window = (REACH + 1) * BLOCK
    k_pos = (block - REACH) * BLOCK + lax.broadcasted_iota(jnp.int32, (window, BLOCK), 0)
    q_pos = block * BLOCK + lax.broadcasted_iota(jnp.int32, (window, BLOCK), 1)
    return (k_pos >= first_row) & (k_pos <= q_pos) & (k_pos > q_pos - REACH * BLOCK)


def attend_forward_kernel(heads, first_ref, q_ref, kv_ref, turned_ref, meta_ref, meta_turned_ref, out_ref, total_ref):
    block = pl.program_id(0)
    span = pl.ds(pl.multiple_of(block * BLOCK, BLOCK), (REACH + 1) * BLOCK)
    seen = seen_keys(block, first_ref[0])
    outs, totals = [], []
    for h in range(heads):
        cut = slice(h * HEAD, (h + 1) * HEAD)
        v_cut = slice((heads + h) * HEAD, (heads + h + 1) * HEAD)
        query = q_ref[:, cut] * SIXTEEN(HEAD ** (-0.5))
        near = jnp.where(seen, nt_dot(kv_ref[span, cut], query), -1e30)
        meta = nt_dot(meta_ref[:, cut], query)
        top = jnp.maximum(
            jnp.max(near, axis=0, keepdims=True), jnp.max(meta, axis=0, keepdims=True)
        )
        near = jnp.exp(near - top)
        meta = jnp.exp(meta - top)
        total = jnp.sum(near, axis=0, keepdims=True) + jnp.sum(meta, axis=0, keepdims=True)
        out = jnp.dot(turned_ref[v_cut, span], near.astype(SIXTEEN), preferred_element_type=WIDE)
        out += jnp.dot(meta_turned_ref[v_cut, :], meta.astype(SIXTEEN), preferred_element_type=WIDE)
        outs.append(out / total)
        totals.append(top + jnp.log(total))
    out_ref[...] = jnp.concatenate(outs, axis=0).T
    total_ref[0] = jnp.concatenate(totals, axis=0)


def attend_backward_kernel(
    heads, first_ref, q_ref, kv_ref, turned_ref, meta_ref, meta_turned_ref, out_ref, total_ref, do_ref,
    dq_ref, dkv_ref, dmeta_ref,
):
    block = pl.program_id(0)

    @pl.when(block == 0)
    def _():
        dkv_ref[...] = jnp.zeros_like(dkv_ref)
        dmeta_ref[...] = jnp.zeros_like(dmeta_ref)

    span = pl.ds(pl.multiple_of(block * BLOCK, BLOCK), (REACH + 1) * BLOCK)
    seen = seen_keys(block, first_ref[0])
    d_out = do_ref[...]
    row_sums = (d_out * out_ref[...]).T
    d_half = d_out.astype(SIXTEEN)
    d_queries, near_k, near_v, meta_k, meta_v = [], [], [], [], []
    for h in range(heads):
        cut = slice(h * HEAD, (h + 1) * HEAD)
        v_cut = slice((heads + h) * HEAD, (heads + h + 1) * HEAD)
        query = q_ref[:, cut] * SIXTEEN(HEAD ** (-0.5))
        do = d_half[:, cut]
        total = total_ref[0, h : h + 1, :]
        mean = jnp.sum(row_sums[cut], axis=0, keepdims=True)
        near = jnp.where(seen, jnp.exp(nt_dot(kv_ref[span, cut], query) - total), 0.0)
        meta = jnp.exp(nt_dot(meta_ref[:, cut], query) - total)
        d_near = (near * (nt_dot(kv_ref[span, v_cut], do) - mean)).astype(SIXTEEN)
        d_meta = (meta * (nt_dot(meta_ref[:, v_cut], do) - mean)).astype(SIXTEEN)
        near_v.append(jnp.dot(near.astype(SIXTEEN), do, preferred_element_type=WIDE))
        meta_v.append(jnp.dot(meta.astype(SIXTEEN), do, preferred_element_type=WIDE))
        near_k.append(jnp.dot(d_near, query, preferred_element_type=WIDE))
        meta_k.append(jnp.dot(d_meta, query, preferred_element_type=WIDE))
        d_query = jnp.dot(turned_ref[cut, span], d_near, preferred_element_type=WIDE)
        d_query += jnp.dot(meta_turned_ref[cut, :], d_meta, preferred_element_type=WIDE)
        d_queries.append(d_query * HEAD ** (-0.5))
    dq_ref[...] = jnp.concatenate(d_queries, axis=0).T.astype(SIXTEEN)
    dkv_ref[span, :] += jnp.concatenate(near_k + near_v, axis=1)
    dmeta_ref[...] += jnp.concatenate(meta_k + meta_v, axis=1)


def attend_operands(queries, kv_rows, doc_first):
    length = doc_first.shape[0]
    count = length // BLOCK
    near = jnp.pad(kv_rows[:length], ((REACH * BLOCK, 0), (0, 0)))
    meta = kv_rows[length:]
    arrays = (doc_first.reshape(count, 1, BLOCK), queries, near, near.T, meta, meta.T)
    width = queries.shape[1]

    def whole(array):
        return pl.BlockSpec(array.shape, lambda i: (0,) * array.ndim)

    specs = [
        pl.BlockSpec((1, 1, BLOCK), lambda i: (i, 0, 0)),
        pl.BlockSpec((BLOCK, width), lambda i: (i, 0)),
    ] + [whole(a) for a in arrays[2:]]
    return arrays, specs, count, width


def attend_forward(queries, kv_rows, doc_first):
    arrays, specs, count, width = attend_operands(queries, kv_rows, doc_first)
    heads = width // HEAD
    return pl.pallas_call(
        lambda *refs: attend_forward_kernel(heads, *refs),
        grid=(count,),
        in_specs=specs,
        out_specs=[
            pl.BlockSpec((BLOCK, width), lambda i: (i, 0)),
            pl.BlockSpec((1, heads, BLOCK), lambda i: (i, 0, 0)),
        ],
        out_shape=[
            jax.ShapeDtypeStruct(queries.shape, WIDE),
            jax.ShapeDtypeStruct((count, heads, BLOCK), WIDE),
        ],
        compiler_params=pltpu.CompilerParams(vmem_limit_bytes=48 * MIB),
        cost_estimate=takes(24),
    )(*arrays)


def attend_backward(queries, kv_rows, doc_first, out, log_total, d_out):
    arrays, specs, count, width = attend_operands(queries, kv_rows, doc_first)
    heads = width // HEAD
    near, meta = arrays[2], arrays[4]
    row_spec = pl.BlockSpec((BLOCK, width), lambda i: (i, 0))
    d_queries, d_near, d_meta = pl.pallas_call(
        lambda *refs: attend_backward_kernel(heads, *refs),
        grid=(count,),
        in_specs=specs
        + [row_spec, pl.BlockSpec((1, heads, BLOCK), lambda i: (i, 0, 0)), row_spec],
        out_specs=[
            row_spec,
            pl.BlockSpec(near.shape, lambda i: (0, 0)),
            pl.BlockSpec(meta.shape, lambda i: (0, 0)),
        ],
        out_shape=[
            jax.ShapeDtypeStruct(queries.shape, SIXTEEN),
            jax.ShapeDtypeStruct(near.shape, WIDE),
            jax.ShapeDtypeStruct(meta.shape, WIDE),
        ],
        compiler_params=pltpu.CompilerParams(vmem_limit_bytes=48 * MIB),
        cost_estimate=takes(24),
    )(*arrays, out, log_total, d_out)
    return d_queries, jnp.concatenate([d_near[REACH * BLOCK :], d_meta], axis=0).astype(SIXTEEN)


def step_sum():
    rows = lax.broadcasted_iota(jnp.int32, (SUB, SUB * STATE), 0)
    cols = lax.broadcasted_iota(jnp.int32, (SUB, SUB * STATE), 1)
    return (cols // STATE == rows).astype(SIXTEEN)


def lanes_from(tile, group):
    return pltpu.roll(tile, (SPAN - group * SUB) % SPAN, axis=1)


def scan_forward_kernel(keep_ref, conv_ref, delta_ref, bc_ref, a_ref, y_ref, start_ref, state_ref):
    block = pl.program_id(0)

    @pl.when(block == 0)
    def _():
        state_ref[...] = jnp.zeros_like(state_ref)

    start_ref[0] = state_ref[...]
    decay_rate = a_ref[...]
    fold = step_sum()
    b_span = bc_ref[:STATE, :].astype(WIDE)
    c_span = bc_ref[STATE:, :].astype(WIDE)

    def body(group, state):
        rows = pl.ds(pl.multiple_of(group * SUB, SUB), SUB)
        delta = delta_ref[rows, :]
        drive = delta * conv_ref[rows, :]
        b_tile = lanes_from(b_span, group)
        c_tile = lanes_from(c_span, group)
        reads = []
        for i in range(SUB):
            keep = keep_ref[block * SPAN + group * SUB + i]
            decay = jnp.exp(delta[i : i + 1, :] * decay_rate) * keep
            state = decay * state + drive[i : i + 1, :] * b_tile[:, i : i + 1]
            reads.append((state * c_tile[:, i : i + 1]).astype(SIXTEEN))
        y_ref[rows, :] = jnp.dot(
            fold, jnp.concatenate(reads, axis=0), preferred_element_type=WIDE
        )
        return state

    state_ref[...] = lax.fori_loop(0, SPAN // SUB, body, state_ref[...], unroll=8)


def scan_forward(keep, conv_out, delta, bc_rows, decay_rate):
    length, lanes = conv_out.shape
    blocks = length // SPAN
    span_spec = pl.BlockSpec((SPAN, lanes), lambda i: (i, 0))
    return pl.pallas_call(
        scan_forward_kernel,
        grid=(blocks,),
        in_specs=[
            pl.BlockSpec(memory_space=pltpu.SMEM),
            span_spec,
            span_spec,
            pl.BlockSpec((2 * STATE, SPAN), lambda i: (0, i)),
            pl.BlockSpec((STATE, lanes), lambda i: (0, 0)),
        ],
        out_specs=[span_spec, pl.BlockSpec((1, STATE, lanes), lambda i: (i, 0, 0))],
        out_shape=[
            jax.ShapeDtypeStruct((length, lanes), WIDE),
            jax.ShapeDtypeStruct((blocks, STATE, lanes), WIDE),
        ],
        scratch_shapes=[pltpu.VMEM((STATE, lanes), WIDE)],
        cost_estimate=takes(24),
    )(keep, conv_out, delta, bc_rows, decay_rate)


def scan_backward_kernel(
    keep_ref, conv_ref, delta_ref, bc_ref, a_ref, start_ref, dy_ref,
    dconv_ref, ddelta_ref, dbc_ref, da_ref,
    state_ref, decay_ref, adjoint_ref,
):
    turn = pl.program_id(0)
    block = pl.num_programs(0) - 1 - turn

    @pl.when(turn == 0)
    def _():
        adjoint_ref[...] = jnp.zeros_like(adjoint_ref)
        da_ref[...] = jnp.zeros_like(da_ref)

    decay_rate = a_ref[...]
    fold = step_sum()
    lanes = decay_rate.shape[1]
    ones = jnp.ones((lanes, SPAN), SIXTEEN)
    spot = lax.broadcasted_iota(jnp.int32, (STATE, SPAN), 1)
    b_span = bc_ref[:STATE, :].astype(WIDE)
    c_span = bc_ref[STATE:, :].astype(WIDE)
    state_ref[0] = start_ref[0]

    def ahead(group, state):
        rows = pl.ds(pl.multiple_of(group * SUB, SUB), SUB)
        delta = delta_ref[rows, :]
        drive = delta * conv_ref[rows, :]
        b_tile = lanes_from(b_span, group)
        for i in range(SUB):
            keep = keep_ref[block * SPAN + group * SUB + i]
            decay = jnp.exp(delta[i : i + 1, :] * decay_rate) * keep
            state = decay * state + drive[i : i + 1, :] * b_tile[:, i : i + 1]
            decay_ref[group * SUB + i] = decay
            state_ref[group * SUB + i + 1] = state
        return state

    lax.fori_loop(0, SPAN // SUB, ahead, start_ref[0], unroll=16)

    def back(step, carry):
        adjoint, da, db, dc = carry
        group = SPAN // SUB - 1 - step
        rows = pl.ds(pl.multiple_of(group * SUB, SUB), SUB)
        delta = delta_ref[rows, :]
        conv = conv_ref[rows, :]
        drive = delta * conv
        dy = dy_ref[rows, :]
        b_tile = lanes_from(b_span, group)
        c_tile = lanes_from(c_span, group)
        by_c, by_b, by_drive, by_delta = ([None] * SUB for _ in range(4))
        for i in range(SUB - 1, -1, -1):
            index = group * SUB + i
            dy_row = dy[i : i + 1, :]
            total = adjoint + dy_row * c_tile[:, i : i + 1]
            by_c[i] = (dy_row * state_ref[index + 1]).astype(SIXTEEN)
            by_b[i] = (total * drive[i : i + 1, :]).astype(SIXTEEN)
            by_drive[i] = (total * b_tile[:, i : i + 1]).astype(SIXTEEN)
            adjoint = total * decay_ref[index]
            rate = adjoint * state_ref[index]
            by_delta[i] = (rate * decay_rate).astype(SIXTEEN)
            da = da + rate * delta[i : i + 1, :]

        def over_state(parts):
            return jnp.dot(fold, jnp.concatenate(parts, axis=0), preferred_element_type=WIDE)

        def over_lanes(parts, tile):
            sums = jnp.dot(jnp.concatenate(parts, axis=0), ones, preferred_element_type=WIDE)
            for i in range(SUB):
                here = spot == group * SUB + i
                tile = jnp.where(here, sums[i * STATE : (i + 1) * STATE, :], tile)
            return tile

        d_drive = over_state(by_drive)
        dconv_ref[rows, :] = d_drive * delta
        ddelta_ref[rows, :] = over_state(by_delta) + d_drive * conv
        return adjoint, da, over_lanes(by_b, db), over_lanes(by_c, dc)

    none = jnp.zeros((STATE, SPAN), WIDE)
    adjoint, da, db, dc = lax.fori_loop(
        0, SPAN // SUB, back, (adjoint_ref[...], da_ref[...], none, none), unroll=16
    )
    adjoint_ref[...] = adjoint
    da_ref[...] = da
    dbc_ref[...] = jnp.concatenate([db, dc], axis=0)


def scan_backward(keep, conv_out, delta, bc_rows, decay_rate, starts, dy):
    length, lanes = conv_out.shape
    blocks = length // SPAN
    span_spec = pl.BlockSpec((SPAN, lanes), lambda i: (blocks - 1 - i, 0))
    rows_spec = pl.BlockSpec((2 * STATE, SPAN), lambda i: (0, blocks - 1 - i))
    whole = pl.BlockSpec((STATE, lanes), lambda i: (0, 0))
    return pl.pallas_call(
        scan_backward_kernel,
        grid=(blocks,),
        in_specs=[
            pl.BlockSpec(memory_space=pltpu.SMEM),
            span_spec,
            span_spec,
            rows_spec,
            whole,
            pl.BlockSpec((1, STATE, lanes), lambda i: (blocks - 1 - i, 0, 0)),
            span_spec,
        ],
        out_specs=[span_spec, span_spec, rows_spec, whole],
        out_shape=[
            jax.ShapeDtypeStruct((length, lanes), WIDE),
            jax.ShapeDtypeStruct((length, lanes), WIDE),
            jax.ShapeDtypeStruct((2 * STATE, length), WIDE),
            jax.ShapeDtypeStruct((STATE, lanes), WIDE),
        ],
        scratch_shapes=[
            pltpu.VMEM((SPAN + 1, STATE, lanes), WIDE),
            pltpu.VMEM((SPAN, STATE, lanes), WIDE),
            pltpu.VMEM((STATE, lanes), WIDE),
        ],
        compiler_params=pltpu.CompilerParams(vmem_limit_bytes=32 * MIB),
        cost_estimate=takes(40),
    )(keep, conv_out, delta, bc_rows, decay_rate, starts, dy)


def padded_lanes(array, lanes):
    return jnp.pad(array, ((0, 0), (0, lanes - array.shape[1])))


def rms_pull(values, scale, gain, d_normed, mean):
    d_values = scale * gain * d_normed - values * (scale * scale * scale) * mean
    return d_values, jnp.sum(d_normed * values * scale, axis=0)


def per_device(tokens, doc_ids, meta_tokens, mixer_params, small_params, ffn_params, cotangent):
    tokens, cotangent = tokens[0], cotangent[0]
    small_whole, ids, meta_whole = start_blocks(small_params, doc_ids[0], meta_tokens)
    (g_one, g_two, g_attn, channel_part), small_pull = jax.vjp(small_shards, small_whole)
    rows, shards = lax.axis_size("row"), lax.axis_size("seq")
    staged = weights_fit(mixer_params.shape[0], ffn_params.shape[0], rows, shards)
    if staged:
        columns, pull_columns = jax.vjp(partial(to_columns, width=view_width()), mixer_params)
    channels = channel_part.shape[0]
    lanes = -(-channels // 128) * 128
    g_ssm = channel_part[:, 0]
    conv_w = channel_part[:, 1 : 1 + CONV].T
    conv_b = channel_part[:, 1 + CONV]
    dt_bias = channel_part[:, 2 + CONV]
    a_log = channel_part[:, 3 + CONV : 3 + CONV + STATE]
    d_skip = channel_part[:, 3 + CONV + STATE]

    length = ids.shape[0]
    positions = jnp.arange(length, dtype=jnp.int32)
    starts = jnp.concatenate([jnp.ones((1,), bool), ids[1:] != ids[:-1]])
    doc_first = lax.cummax(jnp.where(starts, positions, 0), axis=0)
    keep_mask = (positions != doc_first).astype(WIDE)
    lag_masks = jnp.stack(
        [(positions - j >= doc_first).astype(WIDE)[:, None] for j in range(CONV)]
    )

    tokens_f = tokens.astype(WIDE)
    normed_f, norm_pull = jax.vjp(rms_norm, tokens_f, g_one)
    meta_own = meta_tokens.astype(WIDE)
    meta_unit = rms_norm(meta_whole.astype(WIDE), 1.0)
    normed_own = normed_f.astype(SIXTEEN)
    if staged:
        normed_own, columns = tie(normed_own, columns)
        both, pull_both = jax.vjp(both_halves, columns)
    normed = ring_seq_gather(normed_own, 1)
    cotangent_later = cotangent
    if staged:
        normed, both, cotangent_later, ffn_later = tie(normed, both, cotangent, ffn_params)
        (w_in, w_dt, q_rows, x_rows, out_rows), pull_parts = jax.vjp(mixer_parts, both)
        w_x, pull_x = jax.vjp(x_from, x_rows)
        by_heads, pull_rows = jax.vjp(heads_cut, q_rows)
        ffn_columns, pull_ffn_columns = jax.vjp(partial(to_columns, width=FF), ffn_later)
    else:
        (w_qkv, w_in, w_x, w_dt, w_out), pull_mixer = jax.vjp(mixer_shards_whole, mixer_params)
        (w_gate, w_up, w_down), pull_ffn = jax.vjp(ffn_shards_whole, ffn_params)
    meta_normed = (meta_unit * g_one).astype(SIXTEEN)
    every = jnp.concatenate([normed, meta_normed], axis=0)
    cotangent_all = gather_seq(cotangent_later)

    xz = dot_last(normed, w_in).astype(SIXTEEN)
    extended = jnp.pad(xz[:, :channels], ((CONV - 1, 0), (0, 0))).astype(WIDE)
    conv_fn = partial(conv_piece, lag_masks=lag_masks)
    conv_out, conv_pull = jax.vjp(conv_fn, extended, conv_w, conv_b)
    conv_half = conv_out.astype(SIXTEEN)
    if staged:
        conv_half, w_x = tie(conv_half, w_x)
    conv_f = conv_half.astype(WIDE)
    w_x_rows = jnp.pad(w_x.T, ((0, -w_x.shape[1] % 16), (0, 0)))
    projected = seq_sum(jnp.einsum("nc,tc->nt", w_x_rows, conv_half, preferred_element_type=WIDE), 2)
    rank_half = projected[:DT_RANK]
    pre_dt = jnp.einsum("rt,rc->tc", rank_half, w_dt, preferred_element_type=WIDE)
    delta, delta_pull = jax.vjp(lambda p, b: softplus_fn(p + b), pre_dt, dt_bias)
    a_neg, a_pull = jax.vjp(lambda a: -jnp.exp(a), a_log)
    if staged:
        delta, by_heads, out_rows, ffn_columns = tie(delta, by_heads, out_rows, ffn_columns)
        w_qkv, pull_heads = jax.vjp(heads_from, by_heads)
        ffn_both, pull_ffn_both = jax.vjp(both_halves, ffn_columns)
    scan_in = (
        keep_mask,
        padded_lanes(conv_f, lanes),
        padded_lanes(delta, lanes),
        projected[DT_RANK : DT_RANK + 2 * STATE],
        padded_lanes(a_neg.T, lanes),
    )
    y_scan, scan_starts = scan_forward(*scan_in)

    def gate_piece(y, c, skip, z):
        return (y + skip * c) * silu_fn(z)

    z_in = xz[:, channels:].astype(WIDE)
    ssm_out, gate_pull = jax.vjp(gate_piece, y_scan[:, :channels], conv_f, d_skip, z_in)

    if staged:
        ssm_out, w_qkv, out_rows, ffn_both = tie(ssm_out, w_qkv, out_rows, ffn_both)
        w_out, pull_out = jax.vjp(out_from, out_rows)
        (w_gate, w_up, down_rows), pull_ffn_parts = jax.vjp(ffn_parts, ffn_both)
        w_down, pull_down = jax.vjp(down_from, down_rows)
    own_heads = g_attn.shape[0]
    queries = dot_last(normed, w_qkv[:, :own_heads]).astype(SIXTEEN)
    kv_rows = dot_last(every, w_qkv[:, own_heads:]).astype(SIXTEEN)
    attn_out, log_total = attend_forward(queries, kv_rows, doc_first)

    squares = jnp.stack([jnp.sum(attn_out * attn_out, axis=1), jnp.sum(ssm_out * ssm_out, axis=1)])
    squares = seq_sum_small(squares, 3)
    scale_a = lax.rsqrt(squares[0] / (HEADS * HEAD) + norm_eps)[:, None]
    scale_m = lax.rsqrt(squares[1] / INNER + norm_eps)[:, None]
    mixed = 0.5 * jnp.concatenate(
        [attn_out * scale_a * g_attn, ssm_out * scale_m * g_ssm], axis=1
    )
    mixed = mixed.astype(SIXTEEN)
    hidden = tokens_f + product_scatter([(mixed, w_out, False)], 4)

    second_f, second_pull = jax.vjp(rms_norm, hidden, g_two)
    second, act, d_gate, d_up = gather_ffn(
        second_f.astype(SIXTEEN), cotangent_all, w_gate, w_up, w_down, 5
    )
    d_second = product_scatter([(d_gate, w_gate, True), (d_up, w_up, True)], 6)
    d_hidden, grad_g_two = second_pull(d_second)
    d_hidden = d_hidden + cotangent.astype(WIDE)

    d_branch, grad_gate, grad_up, grad_down, down_product = gather_beside_ffn(
        d_hidden.astype(SIXTEEN), second, cotangent_all, act, d_gate, d_up, w_down, 7
    )
    grads_ffn = (grad_gate, grad_up, grad_down)
    block_out = (hidden + scatter_seq(down_product)).astype(SIXTEEN)
    grad_out = hold(dot_weight(mixed, d_branch).astype(SIXTEEN))
    if staged:
        (d_down_rows,) = pull_down(grads_ffn[2])
    d_mixed = 0.5 * dot_back(d_branch, w_out)
    d_mix_a, d_mix_m = d_mixed[:, :own_heads], d_mixed[:, own_heads:]
    means = jnp.stack(
        [jnp.sum(attn_out * g_attn * d_mix_a, axis=1), jnp.sum(ssm_out * g_ssm * d_mix_m, axis=1)]
    )
    means = seq_sum_small(means, 8)
    if staged:
        means, d_down_rows, grad_gate, grad_up = tie(
            means, d_down_rows, grads_ffn[0], grads_ffn[1]
        )
        (d_ffn_both,) = pull_ffn_parts((grad_gate, grad_up, d_down_rows))
        (d_ffn_columns,) = pull_ffn_both(d_ffn_both)
        (d_out_rows,) = pull_out(grad_out)
    d_attn, grad_g_attn = rms_pull(
        attn_out, scale_a, g_attn, d_mix_a, means[0][:, None] / (HEADS * HEAD)
    )
    d_ssm, grad_g_ssm = rms_pull(ssm_out, scale_m, g_ssm, d_mix_m, means[1][:, None] / INNER)

    d_queries, d_kv = attend_backward(
        queries, kv_rows, doc_first, attn_out, log_total, d_attn
    )

    if staged:
        d_queries, d_kv, d_ffn_columns, d_out_rows = tie(
            d_queries, d_kv, d_ffn_columns, d_out_rows
        )
        (grad_ffn,) = pull_ffn_columns(d_ffn_columns)
    grad_qkv = jnp.concatenate([dot_weight(normed, d_queries), dot_weight(every, d_kv)], axis=1)
    grad_qkv = hold(grad_qkv.astype(SIXTEEN))

    d_y, d_conv, grad_d_skip, d_z = gate_pull(d_ssm)
    if staged:
        d_y, grad_qkv = tie(d_y, grad_qkv)
    d_conv_scan, d_delta, d_bc, d_rate = scan_backward(
        *scan_in, scan_starts, padded_lanes(d_y, lanes)
    )
    if staged:
        d_conv_scan, d_delta, grad_ffn, grad_qkv = tie(d_conv_scan, d_delta, grad_ffn, grad_qkv)
        (d_by_heads,) = pull_heads(grad_qkv)
    d_conv = d_conv + d_conv_scan[:, :channels]
    d_pre, grad_dt_bias = delta_pull(d_delta[:, :channels])
    (grad_a_log,) = a_pull(d_rate[:, :channels].T)
    d_pre = d_pre.astype(SIXTEEN)
    grad_dt = jnp.einsum("rt,tc->rc", rank_half, d_pre, preferred_element_type=WIDE)
    d_rank = jnp.einsum("rc,tc->rt", w_dt, d_pre, preferred_element_type=WIDE)
    d_proj = jnp.concatenate([d_rank, d_bc], axis=0)
    d_proj = seq_sum(jnp.pad(d_proj, ((0, -d_proj.shape[0] % 16), (0, 0))), 10)
    if staged:
        d_proj, d_by_heads = tie(d_proj, d_by_heads)
        (d_q_rows,) = pull_rows(d_by_heads)
    d_proj = d_proj[: DT_RANK + 2 * STATE].T
    grad_x = hold(dot_weight(conv_half, d_proj).astype(SIXTEEN))
    if staged:
        (d_x_rows,) = pull_x(grad_x)
    d_extended, grad_conv_w, grad_conv_b = conv_pull(d_conv + dot_back(d_proj, w_x))
    d_xz = jnp.concatenate([d_extended[CONV - 1 :], d_z], axis=1).astype(SIXTEEN)
    grad_in = hold(dot_weight(normed, d_xz).astype(SIXTEEN))
    grad_dt = grad_dt.astype(SIXTEEN)
    if staged:
        (d_both,) = pull_parts((grad_in, grad_dt, d_q_rows, d_x_rows, d_out_rows))
        d_xz, d_both = tie(d_xz, d_both)
        (d_columns,) = pull_both(d_both)
    d_meta = dot_back(d_kv[length:], w_qkv[:, own_heads:])
    d_qkv = jnp.concatenate([d_queries, d_kv[:length]], axis=1)
    d_normed = product_scatter([(d_xz, w_in, True), (d_qkv, w_qkv, True)], 11)
    if staged:
        d_normed, d_columns = tie(d_normed, d_columns)
        (grad_mixer,) = pull_columns(d_columns)
    else:
        (grad_mixer,) = pull_mixer((grad_qkv, grad_in, grad_x, grad_dt, grad_out))
        (grad_ffn,) = pull_ffn(grads_ffn)
    grad_from_norm, grad_g_one = norm_pull(d_normed)
    grad_tokens = d_hidden + grad_from_norm
    grad_g_meta = jnp.sum(d_meta * meta_unit, axis=0)
    grad_channels = jnp.concatenate(
        [
            grad_g_ssm[:, None],
            grad_conv_w.T,
            grad_conv_b[:, None],
            grad_dt_bias[:, None],
            grad_a_log,
            grad_d_skip[:, None],
        ],
        axis=1,
    )
    (grad_small,) = small_pull((grad_g_one + grad_g_meta, grad_g_two, grad_g_attn, grad_channels))
    grad_small, d_meta = end_blocks(grad_small, d_meta)
    _, meta_pull = jax.vjp(lambda v: rms_norm(v, g_one), meta_own)
    (grad_meta,) = meta_pull(d_meta)
    return (
        block_out[None],
        grad_tokens[None],
        grad_meta,
        hold(grad_mixer).astype(WIDE),
        grad_small,
        hold(grad_ffn).astype(WIDE),
    )


def solution(mesh):
    in_specs = (
        P("row", "seq", None),
        P("row", "seq"),
        P(("row", "seq"), None),
        P(("row", "seq")),
        P(("row", "seq")),
        P(("row", "seq")),
        P("row", "seq", None),
    )
    out_specs = (
        P("row", "seq", None),
        P("row", "seq", None),
        P(("row", "seq"), None),
        P(("row", "seq")),
        P(("row", "seq")),
        P(("row", "seq")),
    )
    return jax.shard_map(
        per_device, mesh=mesh, in_specs=in_specs, out_specs=out_specs, check_vma=False
    )
```

```python
import functools
from functools import partial
import math

import jax
import jax.numpy as jnp
from jax import lax
from jax.experimental import pallas as pl
from jax.experimental.pallas import tpu as pltpu
from jax.sharding import PartitionSpec as P

D = 1600
HEADS = 25
GROUPS = 5
HEAD = 64
INNER = 3200
STATE = 16
CONV = 4
DT_RANK = 100
FF = 5504
REACH = 8
BLOCK = 128
RUNS = 4
SUB = 8
SPAN = 128
SIXTEEN = jnp.bfloat16
WIDE = jnp.float32


norm_eps = 1e-05


def split_flat(flat_vec, layout):
    pieces = []
    offset = 0
    for piece_shape in layout:
        piece_len = math.prod(piece_shape)
        pieces.append(flat_vec[offset : offset + piece_len].reshape(piece_shape))
        offset += piece_len
    return pieces


def mixer_layout():
    return [
        (D, HEADS * HEAD),
        (D, 2 * GROUPS * HEAD),
        (D, 2 * INNER),
        (INNER, DT_RANK + 2 * STATE),
        (DT_RANK, INNER),
        (HEADS * HEAD + INNER, D),
    ]


def ffn_layout():
    return [(D, FF), (D, FF), (FF, D)]


def small_split(flat_vec):
    width = CONV + STATE + 4
    packed_rows = flat_vec[: D * (3 + 2 * width)].reshape(D, 3 + 2 * width)
    channel_part = packed_rows[:, 3:].reshape(INNER, width)
    return packed_rows[:, 0], packed_rows[:, 1], packed_rows[:, 2], channel_part


def rms_norm(values, gain_vec):
    return (
        values * lax.rsqrt(jnp.mean(values * values, axis=-1, keepdims=True) + norm_eps) * gain_vec
    )


def silu_fn(values):
    return values / (1.0 + jnp.exp(-values))


def softplus_fn(values):
    return jnp.maximum(values, 0.0) + jnp.log1p(jnp.exp(-jnp.abs(values)))


def glu_piece(gate_pre, up_pre):
    return silu_fn(gate_pre) * up_pre


def dot_last(left, right):
    return jnp.einsum("...k,kn->...n", left, right, preferred_element_type=WIDE)


def dot_back(grads, right):
    return jnp.einsum("...n,kn->...k", grads, right, preferred_element_type=WIDE)


def dot_weight(left, grads):
    return jnp.einsum("...k,...n->kn", left, grads, preferred_element_type=WIDE)


def heads_of(shards):
    return -(-HEADS // shards)


def runs_of(shards):
    return RUNS if INNER % (RUNS * shards) == 0 else 1


def own_channels(array, axis, shards, place):
    runs = runs_of(shards)
    unit = INNER // (runs * shards)
    shape = array.shape
    cut = array.reshape(shape[:axis] + (runs, shards, unit) + shape[axis + 1 :])
    cut = lax.dynamic_index_in_dim(cut, place, axis + 1, keepdims=False)
    return cut.reshape(shape[:axis] + (runs * unit,) + shape[axis + 1 :])


def pad_heads(array, axis, shards):
    heads = heads_of(shards)
    pads = [(0, 0)] * array.ndim
    pads[axis] = (0, heads * shards - HEADS)
    padded = jnp.pad(array, pads)
    shape = padded.shape
    return padded.reshape(shape[:axis] + (shards, heads * HEAD) + shape[axis + 2 :])


def by_head(w_q, w_kv, shards):
    rows = w_q.shape[0]
    w_kv = w_kv.reshape(rows, 2, GROUPS, 1, HEAD)
    w_kv = jnp.broadcast_to(w_kv, (rows, 2, GROUPS, HEADS // GROUPS, HEAD))
    w_kv = w_kv.reshape(rows, 2, HEADS, HEAD)
    return jnp.concatenate(
        [
            pad_heads(w_q.reshape(rows, HEADS, HEAD), 1, shards),
            pad_heads(w_kv[:, 0], 1, shards),
            pad_heads(w_kv[:, 1], 1, shards),
        ],
        axis=2,
    )


def exchange(value):
    return lax.all_to_all(value, "seq", 0, 0)


def tie(*arrays):
    return lax.optimization_barrier(arrays)


def hold(array):
    return lax.optimization_barrier(array)


def hand_on(array, after):
    return pl.pallas_call(
        lambda *refs: None,
        out_shape=jax.ShapeDtypeStruct(array.shape, array.dtype),
        in_specs=[ANY, ANY],
        out_specs=ANY,
        input_output_aliases={0: 0},
    )(array, after)


def other_row(value):
    return lax.ppermute(value, "row", [(0, 1), (1, 0)])


def in_turn(first_row, one, two):
    return jnp.where(first_row, one, two), jnp.where(first_row, two, one)


@jax.custom_vjp
def both_halves(value):
    first_row = lax.axis_index("row") == 0
    return jnp.concatenate(in_turn(first_row, value, other_row(value)), axis=0)


def both_halves_backward(_, grad):
    half = grad.shape[0] // 2
    own, other = in_turn(lax.axis_index("row") == 0, grad[:half], grad[half:])
    return (own + other_row(other),)


both_halves.defvjp(lambda value: (both_halves(value), None), both_halves_backward)


@partial(jax.custom_vjp, nondiff_argnums=(1,))
def cut_rows(array, counts):
    pieces, offset = [], 0
    for count in counts:
        pieces.append(array[offset : offset + count])
        offset += count
    return tuple(pieces)


def cut_rows_forward(array, counts):
    return cut_rows(array, counts), None


def cut_rows_backward(counts, _, grads):
    return (jnp.concatenate(grads, axis=0),)


cut_rows.defvjp(cut_rows_forward, cut_rows_backward)


def view_width():
    return INNER // RUNS


def weights_fit(mixer_length, ffn_length, rows, shards):
    width = view_width()
    sizes = [math.prod(shape) for shape in mixer_layout()]
    return (
        rows == 2
        and runs_of(shards) == RUNS
        and mixer_length % width == 0
        and all(size % width == 0 for size in sizes)
        and D % shards == 0
        and D % width == 0
        and (HEADS * HEAD * 2) % shards == 0
        and shards % x_turns(shards)[0] == 0
        and ffn_length % FF == 0
    )


def to_columns(piece, width):
    shards = lax.axis_size("seq")
    unit = width // shards
    view = hold(piece.reshape(-1, width))
    return exchange(view.reshape(-1, shards, unit).transpose(1, 0, 2)).reshape(-1, unit)


def full_rows(cut):
    received = exchange(cut)
    return hold(received.transpose(1, 0, 2).reshape(received.shape[1], -1))


def mixer_parts(both):
    width, shards = view_width(), lax.axis_size("seq")
    unit = both.shape[1]
    part_q, part_kv, part_in, part_x, part_dt, part_out = cut_rows(
        both, tuple(math.prod(shape) // width for shape in mixer_layout())
    )
    q_rows = jnp.concatenate(
        [
            part_q.reshape(shards, -1, unit),
            part_kv.reshape(shards, -1, unit),
            x_windows(part_x, shards),
        ],
        axis=1,
    )
    per_row = D // width
    head_rows = heads_of(shards) * HEAD
    out_heads, out_inner = cut_rows(part_out, (HEADS * HEAD * per_row, INNER * per_row))
    out_heads = jnp.pad(
        out_heads, ((0, (head_rows * shards - HEADS * HEAD) * per_row), (0, 0))
    ).reshape(shards, -1, unit)
    out_inner = out_inner.reshape(RUNS, shards, -1, unit)
    out_inner = out_inner.transpose(1, 0, 2, 3).reshape(shards, -1, unit)
    return (
        part_in.reshape(D, -1),
        part_dt.reshape(DT_RANK, -1),
        q_rows,
        jnp.concatenate([out_heads, out_inner], axis=1),
    )


def heads_cut(q_rows):
    shards = lax.axis_size("seq")
    rows = D // shards
    by_rows = full_rows(q_rows)
    split = rows * HEADS * HEAD // view_width()
    end = split + rows * 2 * GROUPS * HEAD // view_width()
    cut = by_head(
        by_rows[:split].reshape(rows, HEADS * HEAD),
        by_rows[split:end].reshape(rows, 2 * GROUPS * HEAD),
        shards,
    )
    return cut.transpose(1, 0, 2), x_from_windows(by_rows[end:], lax.axis_index("seq"))


def heads_from(cut):
    return exchange(cut).reshape(D, -1)


def out_from(received):
    rows = received.shape[1]
    return hold(received.transpose(1, 0, 2).reshape(rows, -1)).reshape(-1, D)


def ffn_blocks(piece):
    shards = lax.axis_size("seq")
    return piece.reshape(-1, shards, FF // shards).transpose(1, 0, 2)


def ffn_parts(both):
    unit = both.shape[2]
    w_gate, w_up, part_down = cut_rows(both.reshape(-1, unit), (D, D, D))
    return w_gate, w_up, part_down.reshape(lax.axis_size("seq"), -1, unit)


def down_from(cut):
    return exchange(cut).transpose(1, 0, 2).reshape(-1, D)


def x_turns(shards):
    width = INNER // RUNS
    run = (width // shards) * (DT_RANK + 2 * STATE)
    common = math.gcd(run, width)
    return width // common, run // common


def x_windows(part_x, shards):
    runs, rows = x_turns(shards)
    need = -(-rows // runs)
    turns = part_x.reshape(-1, rows, part_x.shape[1])
    cuts = [turns[:, (i * rows) // runs : (i * rows) // runs + need] for i in range(runs)]
    cuts = jnp.stack(cuts, axis=1).reshape(RUNS, shards, need, part_x.shape[1])
    return cuts.transpose(1, 0, 2, 3).reshape(shards, RUNS * need, part_x.shape[1])


def x_from_windows(view_rows, place):
    width = view_rows.shape[1]
    shards = lax.axis_size("seq")
    runs, rows = x_turns(shards)
    columns = DT_RANK + 2 * STATE
    count = (width // shards) * columns
    flat = view_rows.reshape(RUNS, -1)
    offset = (place % runs) * rows * (width // runs) % width
    return lax.dynamic_slice_in_dim(flat, offset, count, 1).reshape(-1, columns)


def mixer_shards_whole(piece):
    shards, place = lax.axis_size("seq"), lax.axis_index("seq")
    whole = lax.all_gather(piece, ("row", "seq"), axis=0, tiled=True)
    w_q, w_kv, w_in, w_x, w_dt, w_out = split_flat(whole, mixer_layout())
    qkv = lax.dynamic_index_in_dim(by_head(w_q, w_kv, shards), place, 1, keepdims=False)
    w_in = own_channels(w_in.reshape(D, 2, INNER), 2, shards, place)
    out_heads = w_out[: HEADS * HEAD].reshape(HEADS, HEAD, D)
    out_heads = lax.dynamic_index_in_dim(pad_heads(out_heads, 0, shards), place, 0, keepdims=False)
    return (
        qkv,
        w_in.reshape(D, -1),
        own_channels(w_x, 0, shards, place),
        own_channels(w_dt, 1, shards, place),
        jnp.concatenate([out_heads, own_channels(w_out[HEADS * HEAD :], 0, shards, place)], axis=0),
    )


def ffn_shards_whole(piece):
    unit = FF // lax.axis_size("seq")
    start = lax.axis_index("seq") * unit
    whole = lax.all_gather(piece, ("row", "seq"), axis=0, tiled=True)
    w_gate, w_up, w_down = split_flat(whole, ffn_layout())
    return (
        lax.dynamic_slice_in_dim(w_gate, start, unit, 1),
        lax.dynamic_slice_in_dim(w_up, start, unit, 1),
        lax.dynamic_slice_in_dim(w_down, start, unit, 0),
    )


def small_shards(whole):
    shards, place = lax.axis_size("seq"), lax.axis_index("seq")
    g_one, g_attn, g_two, channel_part = small_split(whole)
    g_attn = pad_heads(g_attn.reshape(HEADS, HEAD), 0, shards)
    return (
        g_one,
        g_two,
        lax.dynamic_index_in_dim(g_attn, place, 0, keepdims=False),
        own_channels(channel_part, 0, shards, place),
    )


def tiles_of(count):
    return -(-count // 128)


def start_blocks(small_params, doc_ids, meta_tokens):
    devices = lax.axis_size("row") * lax.axis_size("seq")
    parts = [small_params, doc_ids.astype(SIXTEEN), meta_tokens.reshape(-1)]
    rows = [tiles_of(part.shape[0]) for part in parts]
    rows_all = -(-sum(rows) // 16) * 16
    tiles = [
        jnp.pad(part, (0, count * 128 - part.shape[0])).reshape(-1, 128)
        for part, count in zip(parts, rows)
    ]
    block = jnp.concatenate(tiles + [jnp.zeros((rows_all - sum(rows), 128), SIXTEEN)], axis=0)
    every = push_gather(block, 0)
    outs, begin = [], 0
    for part, count in zip(parts, rows):
        cut = every[:, begin : begin + count].reshape(devices, -1)[:, : part.shape[0]]
        outs.append(cut)
        begin += count
    ids = outs[1].reshape(lax.axis_size("row"), -1)
    ids = lax.dynamic_index_in_dim(ids, lax.axis_index("row"), 0, keepdims=False)
    return outs[0].reshape(-1).astype(WIDE), ids.astype(jnp.int32), outs[2].reshape(-1, D)


def end_blocks(grad_small, d_meta):
    devices = lax.axis_size("row") * lax.axis_size("seq")
    parts = grad_small.reshape(devices, -1).astype(SIXTEEN)
    small_count = parts.shape[1]
    small_rows = tiles_of(small_count)
    parts = jnp.pad(parts, ((0, 0), (0, small_rows * 128 - small_count)))
    meta = d_meta.astype(SIXTEEN).reshape(devices, -1)
    meta_count = meta.shape[1]
    rows = -(-(small_rows + tiles_of(meta_count)) // 16) * 16
    meta = jnp.pad(meta, ((0, 0), (0, (rows - small_rows) * 128 - meta_count)))
    blocks = jnp.concatenate(
        [parts.reshape(devices, -1, 128), meta.reshape(devices, -1, 128)], axis=1
    )
    own = push_scatter(blocks, 9)
    small = own[:small_rows].reshape(-1)[:small_count]
    meta = own[small_rows:].reshape(-1)[:meta_count].reshape(-1, D)
    return small, meta


def gather_seq(block):
    return lax.all_gather(block, "seq", axis=0, tiled=True)


def scatter_seq(whole):
    return lax.psum_scatter(whole.astype(SIXTEEN), "seq", scatter_dimension=0, tiled=True).astype(
        WIDE
    )


MESH = pl.DeviceIdType.MESH
ANY = pl.BlockSpec(memory_space=pl.ANY)
VMEM = pl.BlockSpec(memory_space=pltpu.VMEM)
MIB = 1024 * 1024


def takes(microseconds):
    return pl.CostEstimate(
        flops=0, bytes_accessed=microseconds * 3_500_000, transcendentals=0
    )


def greet(peers):
    barrier = pltpu.get_barrier_semaphore()
    for peer in peers:
        pl.semaphore_signal(barrier, inc=1, device_id=peer, device_id_type=MESH)
    pl.semaphore_wait(barrier, len(peers))


def ring_place(chip, chips):
    odd = chip % 2
    return odd * (chips - 1 - chip // 2) + (1 - odd) * (chip // 2)


def ring_chip(place, chips):
    place = (place + 2 * chips) % chips
    back = place // (chips // 2)
    return back * (2 * (chips - 1 - place) + 1) + (1 - back) * (2 * place)


def ring_gather_loop(shards, parts, x_ref, out_ref, ring_send, ring_recv, pair_send, pair_recv, work):
    row, me = lax.axis_index("row"), lax.axis_index("seq")
    chips = shards // 2
    core = me % 2
    place = ring_place(me // 2, chips)

    def device(spot):
        return ring_chip(spot, chips) * 2 + core

    right, left, twin = (row, device(place + 1)), (row, device(place - 1)), (row, me + 1 - 2 * core)
    greet([right, left, twin])
    rows = x_ref.shape[0] // (2 * parts)
    paths = [(way, part) for part in range(parts) for way in range(2)]

    def piece(way, part, step):
        source = device(place - 1 - step if way == 0 else place + 1 + step)
        return out_ref.at[source, pl.ds((way * parts + part) * rows, rows)]

    def ring(way, part, step):
        here = piece(way, part, step - 1)
        return pltpu.make_async_remote_copy(
            src_ref=here, dst_ref=here, send_sem=ring_send.at[way, part, step],
            recv_sem=ring_recv.at[way, part, step], device_id=(right, left)[way], device_id_type=MESH,
        )

    def pair(way, part, step):
        here = piece(way, part, step - 1)
        return pltpu.make_async_remote_copy(
            src_ref=here, dst_ref=here, send_sem=pair_send.at[way, part, step],
            recv_sem=pair_recv.at[way, part, step], device_id=twin, device_id_type=MESH,
        )

    out_ref[me] = x_ref[...]
    for way, part in paths:
        ring(way, part, 0).start()
    for way, part in paths:
        pair(way, part, 0).start()

    def body(step, carry):
        @pl.when(step < chips - 1)
        def _():
            for way, part in paths:
                ring(way, part, step).wait_recv()

                @pl.when(step < chips - 2)
                def _():
                    ring(way, part, step + 1).start()

                pair(way, part, step + 1).start()

        for way, part in paths:
            pair(way, part, step).wait_recv()
        work(step, place)
        return carry

    lax.fori_loop(0, chips, body, 0)

    def finish(step, carry):
        for way, part in paths:
            pair(way, part, step).wait_send()

            @pl.when(step < chips - 1)
            def _():
                ring(way, part, step).wait_send()

        return carry

    lax.fori_loop(0, chips, finish, 0)


def ring_semaphores(chips, parts):
    ring = pltpu.SemaphoreType.DMA((2, parts, chips - 1))
    pair = pltpu.SemaphoreType.DMA((2, parts, chips))
    return [ring, ring, pair, pair]


def seq_gather_kernel(shards, parts, x_ref, out_ref, *sems):
    ring_gather_loop(shards, parts, x_ref, out_ref, *sems, lambda step, place: None)


def fits_vmem(*shapes):
    return sum(padded_bytes(shape, 2) for shape in shapes) < 48 * MIB


def ring_seq_gather(block, collective_id, parts=2):
    shards = lax.axis_size("seq")
    rows, width = block.shape
    if not fits_vmem((shards * rows, width)):
        return lax.all_gather(block, "seq", axis=0, tiled=True)
    gathered = pl.pallas_call(
        functools.partial(seq_gather_kernel, shards, parts),
        out_shape=jax.ShapeDtypeStruct((shards, rows, width), block.dtype),
        in_specs=[VMEM],
        out_specs=VMEM,
        scratch_shapes=ring_semaphores(shards // 2, parts),
        compiler_params=pltpu.CompilerParams(
            collective_id=collective_id, has_side_effects=True, vmem_limit_bytes=56 * MIB
        ),
        cost_estimate=takes(40),
    )(block)
    return gathered.reshape(shards * rows, width)


def gather_ffn_kernel(
    shards, parts, x_ref, cot_ref, gate_ref, up_ref, down_ref,
    out_ref, act_ref, d_gate_ref, d_up_ref, *sems,
):
    chips = shards // 2
    rows = x_ref.shape[0]
    half = rows // 2

    def work(step, place):
        back, ahead = ring_chip(place - step, chips) * 2, ring_chip(place + step, chips) * 2
        spots = [(back, 0), (back + 1, 0), (ahead, half), (ahead + 1, half)]
        starts = [pl.multiple_of(index * rows + first, half) for index, first in spots]
        tokens = jnp.concatenate([out_ref[index, pl.ds(first, half), :] for index, first in spots], axis=0)
        cot = jnp.concatenate([cot_ref[pl.ds(start, half), :] for start in starts], axis=0)
        gate = jnp.dot(tokens, gate_ref[...], preferred_element_type=WIDE)
        up = jnp.dot(tokens, up_ref[...], preferred_element_type=WIDE)
        d_act = lax.dot_general(
            cot, down_ref[...], (((1,), (1,)), ((), ())), preferred_element_type=WIDE
        )
        share = 1.0 / (1.0 + jnp.exp(-gate))
        passed = gate * share
        results = (
            (act_ref, passed * up),
            (d_gate_ref, d_act * up * (share * (1.0 + gate * (1.0 - share)))),
            (d_up_ref, d_act * passed),
        )
        for ref, value in results:
            value = value.astype(SIXTEEN)
            for i, start in enumerate(starts):
                ref[pl.ds(start, half), :] = value[i * half : (i + 1) * half]

    ring_gather_loop(shards, parts, x_ref, out_ref, *sems, work)


def gather_ffn(block, cotangent, w_gate, w_up, w_down, collective_id, parts=2):
    shards = lax.axis_size("seq")
    rows, width = block.shape
    units = w_gate.shape[1]
    if not fits_vmem((shards * rows, width), (shards * rows, width), (3 * shards * rows, units)):
        second = ring_seq_gather(block, collective_id)
        gate, up = dot_last(second, w_gate), dot_last(second, w_up)
        act, pull = jax.vjp(glu_piece, gate, up)
        d_gate, d_up = pull(dot_back(cotangent, w_down))
        return second, act.astype(SIXTEEN), d_gate.astype(SIXTEEN), d_up.astype(SIXTEEN)
    hidden = jax.ShapeDtypeStruct((shards * rows, units), SIXTEEN)
    outs = pl.pallas_call(
        functools.partial(gather_ffn_kernel, shards, parts),
        out_shape=[jax.ShapeDtypeStruct((shards, rows, width), SIXTEEN), hidden, hidden, hidden],
        in_specs=[VMEM] * 5,
        out_specs=[VMEM] * 4,
        scratch_shapes=ring_semaphores(shards // 2, parts),
        compiler_params=pltpu.CompilerParams(
            collective_id=collective_id, has_side_effects=True, vmem_limit_bytes=56 * MIB
        ),
        cost_estimate=takes(45),
    )(block, cotangent, w_gate, w_up, w_down)
    return (outs[0].reshape(shards * rows, width),) + tuple(outs[1:])


def gather_beside_kernel(
    shards, parts, x_ref, second_ref, cot_ref, act_ref, d_gate_ref, d_up_ref, down_ref,
    out_ref, g_gate_ref, g_up_ref, g_down_ref, product_ref, *sems,
):
    chips = shards // 2
    width = second_ref.shape[1]
    block = 256
    turns = width // block
    share = act_ref.shape[0] // chips

    def tn_dot(left, right):
        return lax.dot_general(
            left, right, (((0,), (0,)), ((), ())), preferred_element_type=WIDE
        ).astype(SIXTEEN)

    def columns(cut):
        tokens = second_ref[:, cut]
        g_gate_ref[cut, :] = tn_dot(tokens, d_gate_ref[...])
        g_up_ref[cut, :] = tn_dot(tokens, d_up_ref[...])
        g_down_ref[:, cut] = tn_dot(act_ref[...], cot_ref[:, cut])

    def work(step, place):
        @pl.when(step < turns)
        def _():
            columns(pl.ds(pl.multiple_of(step * block, block), block))

        @pl.when(step == turns)
        def _():
            columns(slice(turns * block, width))

        here = pl.ds(pl.multiple_of(step * share, share), share)
        product_ref[here, :] = jnp.dot(
            act_ref[here, :], down_ref[...], preferred_element_type=WIDE
        ).astype(SIXTEEN)

    ring_gather_loop(shards, parts, x_ref, out_ref, *sems, work)


def gather_beside_ffn(block, second, cotangent, act, d_gate, d_up, w_down, collective_id, parts=2):
    shards = lax.axis_size("seq")
    rows, width = block.shape
    length, units = act.shape
    chips = shards // 2
    if width // 256 >= chips or not fits_vmem(
        (4 * length, width), (3 * length, units), (3 * width, units)
    ):
        return (
            ring_seq_gather(block, collective_id),
            dot_weight(second, d_gate).astype(SIXTEEN),
            dot_weight(second, d_up).astype(SIXTEEN),
            dot_weight(act, cotangent).astype(SIXTEEN),
            dot_last(act, w_down).astype(SIXTEEN),
        )
    outs = pl.pallas_call(
        functools.partial(gather_beside_kernel, shards, parts),
        out_shape=[
            jax.ShapeDtypeStruct((shards, rows, width), SIXTEEN),
            jax.ShapeDtypeStruct((width, units), SIXTEEN),
            jax.ShapeDtypeStruct((width, units), SIXTEEN),
            jax.ShapeDtypeStruct((units, width), SIXTEEN),
            jax.ShapeDtypeStruct((length, width), SIXTEEN),
        ],
        in_specs=[VMEM] * 7,
        out_specs=[VMEM] * 5,
        scratch_shapes=ring_semaphores(shards // 2, parts),
        compiler_params=pltpu.CompilerParams(
            collective_id=collective_id, has_side_effects=True, vmem_limit_bytes=60 * MIB
        ),
        cost_estimate=takes(45),
    )(block, second, cotangent, act, d_gate, d_up, w_down)
    return (outs[0].reshape(shards * rows, width),) + tuple(outs[1:])


def product_scatter_kernel(shards, parts, turned, *refs):
    terms = len(turned)
    lefts, rights = refs[:terms], refs[terms : 2 * terms]
    out_ref, mine, given, pair, arrived = refs[2 * terms : 2 * terms + 5]
    ring_send, ring_recv, pair_send, pair_recv = refs[2 * terms + 5 :]
    row, me = lax.axis_index("row"), lax.axis_index("seq")
    chips = shards // 2
    core = me % 2
    place = ring_place(me // 2, chips)
    block_rows = out_ref.shape[0]

    def device(spot, core):
        return ring_chip(spot, chips) * 2 + core

    right = (row, device(place + 1, core))
    left = (row, device(place - 1, core))
    twin = (row, me + 1 - 2 * core)
    greet([right, left, twin])
    rows = block_rows // (2 * parts)

    def cut(way, part):
        return pl.ds((way * parts + part) * rows, rows)

    def product(index):
        here = pl.ds(pl.multiple_of(index * block_rows, block_rows), block_rows)
        total = None
        for left_ref, right_ref, turn in zip(lefts, rights, turned):
            part = lax.dot_general(
                left_ref[here, :], right_ref[...], (((1,), (1 if turn else 0,)), ((), ())),
                preferred_element_type=WIDE,
            )
            total = part if total is None else total + part
        return total.astype(SIXTEEN)

    def pass_over(slot):
        return pltpu.make_async_remote_copy(
            src_ref=given.at[slot], dst_ref=pair.at[slot], send_sem=pair_send.at[slot],
            recv_sem=pair_recv.at[slot], device_id=twin, device_id_type=MESH,
        )

    def make(far):
        slot = far % chips
        given[slot] = product(device(place + far, 1 - core))
        pass_over(slot).start()
        mine[slot] = product(device(place + far, core))

    def both(step, carry):
        make(-step)
        make(step)
        return carry

    half = chips // 2
    both(1, 0)
    started, flights = [], {}
    fresh = set(range(chips))
    for step in range(chips):
        if step + 2 < half:
            both(step + 2, 0)
        elif step + 2 == half:
            make(half)
            make(0)
        for part in range(parts):
            for way in range(2):
                slot = (-1 - step if way == 0 else 1 + step) % chips
                if slot in fresh:
                    fresh.remove(slot)
                    pass_over(slot).wait_recv()
                here = cut(way, part)
                total = mine[slot, here, :].astype(WIDE) + pair[slot, here, :].astype(WIDE)
                if step:
                    flights[way, part].wait_recv()
                    total = total + arrived[way, step - 1, pl.ds(part * rows, rows), :].astype(WIDE)
                if step == chips - 1:
                    out_ref[here, :] = total
                    continue
                mine[slot, here, :] = total.astype(SIXTEEN)
                copy = pltpu.make_async_remote_copy(
                    src_ref=mine.at[slot, here], dst_ref=arrived.at[way, step, pl.ds(part * rows, rows)],
                    send_sem=ring_send.at[way, part, step], recv_sem=ring_recv.at[way, part, step],
                    device_id=(right, left)[way], device_id_type=MESH,
                )
                copy.start()
                started.append(copy)
                flights[way, part] = copy
    for slot in range(chips):
        pass_over(slot).wait_send()
    for copy in started:
        copy.wait_send()


def padded_bytes(shape, bytes_each):
    return -(-shape[0] // 16) * 16 * -(-shape[1] // 128) * 128 * bytes_each


def product_scatter(terms, collective_id, parts=2):
    shards = lax.axis_size("seq")
    chips = shards // 2
    length = terms[0][0].shape[0]
    width = terms[0][1].shape[0 if terms[0][2] else 1]
    rows = length // shards
    buffers = 4 * chips * padded_bytes((rows, width), 2)
    operands = sum(padded_bytes(t[0].shape, 2) + padded_bytes(t[1].shape, 2) for t in terms)
    if chips < 4 or buffers + operands > 40 * MIB:
        total = 0
        for left, right, turn in terms:
            total = total + lax.dot_general(
                left, right, (((1,), (1 if turn else 0,)), ((), ())), preferred_element_type=WIDE
            )
        return lax.psum_scatter(
            total.astype(SIXTEEN), "seq", scatter_dimension=0, tiled=True
        ).astype(WIDE)
    ring = pltpu.SemaphoreType.DMA((2, parts, chips - 1))
    pair = pltpu.SemaphoreType.DMA((chips,))
    blocks = pltpu.VMEM((chips, rows, width), SIXTEEN)
    return pl.pallas_call(
        functools.partial(product_scatter_kernel, shards, parts, tuple(t[2] for t in terms)),
        out_shape=jax.ShapeDtypeStruct((rows, width), WIDE),
        in_specs=[VMEM] * (2 * len(terms)),
        out_specs=VMEM,
        scratch_shapes=[
            blocks, blocks, blocks,
            pltpu.VMEM((2, chips - 1, rows // 2, width), SIXTEEN),
            ring, ring, pair, pair,
        ],
        compiler_params=pltpu.CompilerParams(
            collective_id=collective_id, has_side_effects=True, vmem_limit_bytes=56 * MIB
        ),
        cost_estimate=takes(40),
    )(*[t[0] for t in terms], *[t[1] for t in terms])


def bits_of(shards):
    bits = shards.bit_length() - 1
    assert 1 << bits == shards
    return bits


def partner_of(me, bit):
    return me + (1 - 2 * ((me // (1 << bit)) % 2)) * (1 << bit)


def seq_sum_kernel(bits, waits, x_ref, *refs):
    out_ref, total, staged, arrived, send_sem, recv_sem, back_send, back_recv = refs[waits:]
    row, me = lax.axis_index("row"), lax.axis_index("seq")
    partners = [(row, partner_of(me, bit)) for bit in range(bits)]
    greet(partners)
    length = x_ref.shape[1]
    total[...] = x_ref[...].astype(WIDE)
    begin = 0
    started = []
    for bit in range(bits):
        half = length >> (bit + 1)
        upper = (me // (1 << bit)) % 2
        kept = pl.multiple_of(begin + upper * half, 128)
        given = pl.multiple_of(begin + (1 - upper) * half, 128)
        staged[:, half : 2 * half] = total[:, pl.ds(given, half)].astype(SIXTEEN)
        copy = pltpu.make_async_remote_copy(
            src_ref=staged.at[:, half : 2 * half], dst_ref=arrived.at[:, half : 2 * half],
            send_sem=send_sem.at[bit], recv_sem=recv_sem.at[bit],
            device_id=partners[bit], device_id_type=MESH,
        )
        copy.start()
        started.append(copy)
        copy.wait_recv()
        total[:, pl.ds(kept, half)] += arrived[:, half : 2 * half].astype(WIDE)
        begin = kept
    half = length >> bits
    out_ref[:, pl.ds(pl.multiple_of(begin, 128), half)] = total[
        :, pl.ds(pl.multiple_of(begin, 128), half)
    ].astype(SIXTEEN)
    for bit in range(bits - 1, -1, -1):
        half = length >> (bit + 1)
        here = out_ref.at[:, pl.ds(pl.multiple_of(begin, 128), half)]
        copy = pltpu.make_async_remote_copy(
            src_ref=here, dst_ref=here, send_sem=back_send.at[bit], recv_sem=back_recv.at[bit],
            device_id=partners[bit], device_id_type=MESH,
        )
        copy.start()
        started.append(copy)
        copy.wait_recv()
        begin = begin - ((me // (1 << bit)) % 2) * half
    for copy in started:
        copy.wait_send()


def seq_sum(values, collective_id, after=()):
    bits = bits_of(lax.axis_size("seq"))
    rows, length = values.shape
    sems = pltpu.SemaphoreType.DMA((bits,))
    return pl.pallas_call(
        functools.partial(seq_sum_kernel, bits, len(after)),
        out_shape=jax.ShapeDtypeStruct((rows, length), SIXTEEN),
        in_specs=[VMEM] + [ANY] * len(after),
        out_specs=VMEM,
        scratch_shapes=[
            pltpu.VMEM((rows, length), WIDE),
            pltpu.VMEM((rows, length), SIXTEEN),
            pltpu.VMEM((rows, length), SIXTEEN),
            sems, sems, sems, sems,
        ],
        compiler_params=pltpu.CompilerParams(
            collective_id=collective_id, has_side_effects=True, vmem_limit_bytes=48 * MIB
        ),
        cost_estimate=takes(30),
    )(values, *after)


def seq_sum_small_kernel(groups, x_ref, out_ref, arrived, staged, send_sem, recv_sem):
    row, me = lax.axis_index("row"), lax.axis_index("seq")
    phases = []
    for size, stride in groups:
        spot = (me // stride) % size
        phases.append(
            [(row, me + ((spot + far) % size - spot) * stride) for far in range(1, size)]
        )
    greet([peer for peers in phases for peer in peers])
    total = x_ref[...]
    copies, slot = [], 0
    for phase, peers in enumerate(phases):
        staged[phase] = total
        flights = []
        for peer in peers:
            copy = pltpu.make_async_remote_copy(
                src_ref=staged.at[phase], dst_ref=arrived.at[slot], send_sem=send_sem.at[slot],
                recv_sem=recv_sem.at[slot], device_id=peer, device_id_type=MESH,
            )
            copy.start()
            flights.append((copy, slot))
            slot += 1
        for copy, here in flights:
            copy.wait_recv()
            total = total + arrived[here]
        copies += flights
    out_ref[...] = total
    for copy, _ in copies:
        copy.wait_send()


def seq_sum_small(values, collective_id):
    bits = bits_of(lax.axis_size("seq"))
    low = 1 << (bits // 2)
    groups = ((low, 1), ((1 << bits) // low, low))
    count = sum(size - 1 for size, _ in groups)
    shape = values.shape
    tiles = values.reshape(-1, 128)
    sems = pltpu.SemaphoreType.DMA((count,))
    return pl.pallas_call(
        functools.partial(seq_sum_small_kernel, groups),
        out_shape=jax.ShapeDtypeStruct(tiles.shape, WIDE),
        in_specs=[VMEM],
        out_specs=VMEM,
        scratch_shapes=[
            pltpu.VMEM((count,) + tiles.shape, WIDE),
            pltpu.VMEM((len(groups),) + tiles.shape, WIDE),
            sems, sems,
        ],
        compiler_params=pltpu.CompilerParams(collective_id=collective_id, has_side_effects=True),
        cost_estimate=takes(12),
    )(tiles).reshape(shape)


def all_peers(rows, shards):
    me = lax.axis_index("row") * shards + lax.axis_index("seq")
    count = rows * shards
    ahead = [(me + far) % count for far in range(1, count)]
    return me, count, [(other, (other // shards, other % shards)) for other in ahead]


def push_gather_kernel(rows, shards, x_ref, out_ref, send_sem, recv_sem):
    me, count, peers = all_peers(rows, shards)
    greet([device for _, device in peers])
    copies = []
    for far, (_, device) in enumerate(peers):
        copy = pltpu.make_async_remote_copy(
            src_ref=x_ref, dst_ref=out_ref.at[me], send_sem=send_sem.at[far],
            recv_sem=recv_sem.at[far], device_id=device, device_id_type=MESH,
        )
        copy.start()
        copies.append(copy)
    out_ref[me] = x_ref[...]
    for copy in copies:
        copy.wait()


def push_gather(block, collective_id):
    rows, shards = lax.axis_size("row"), lax.axis_size("seq")
    sems = pltpu.SemaphoreType.DMA((rows * shards - 1,))
    return pl.pallas_call(
        functools.partial(push_gather_kernel, rows, shards),
        out_shape=jax.ShapeDtypeStruct((rows * shards,) + block.shape, block.dtype),
        in_specs=[VMEM],
        out_specs=VMEM,
        scratch_shapes=[sems, sems],
        compiler_params=pltpu.CompilerParams(collective_id=collective_id, has_side_effects=True),
        cost_estimate=takes(20),
    )(block)


def push_scatter_kernel(rows, shards, x_ref, out_ref, arrived, send_sem, recv_sem):
    me, count, peers = all_peers(rows, shards)
    greet([device for _, device in peers])
    copies = []
    for far, (other, device) in enumerate(peers):
        copy = pltpu.make_async_remote_copy(
            src_ref=x_ref.at[other], dst_ref=arrived.at[far], send_sem=send_sem.at[far],
            recv_sem=recv_sem.at[far], device_id=device, device_id_type=MESH,
        )
        copy.start()
        copies.append(copy)
    total = x_ref[me].astype(WIDE)
    for far, copy in enumerate(copies):
        copy.wait_recv()
        total = total + arrived[far].astype(WIDE)
    out_ref[...] = total
    for copy in copies:
        copy.wait_send()


def push_scatter(blocks, collective_id):
    rows, shards = lax.axis_size("row"), lax.axis_size("seq")
    count = rows * shards
    sems = pltpu.SemaphoreType.DMA((count - 1,))
    return pl.pallas_call(
        functools.partial(push_scatter_kernel, rows, shards),
        out_shape=jax.ShapeDtypeStruct(blocks.shape[1:], WIDE),
        in_specs=[VMEM],
        out_specs=VMEM,
        scratch_shapes=[pltpu.VMEM((count - 1,) + blocks.shape[1:], blocks.dtype), sems, sems],
        compiler_params=pltpu.CompilerParams(
            collective_id=collective_id, has_side_effects=True, vmem_limit_bytes=32 * MIB
        ),
        cost_estimate=takes(20),
    )(blocks)


def conv_piece(extended, conv_w, conv_b, lag_masks):
    length = extended.shape[0] - (CONV - 1)
    summed = conv_b
    for j in range(CONV):
        summed = (
            summed + conv_w[j] * extended[CONV - 1 - j : CONV - 1 - j + length] * lag_masks[j]
        )
    return silu_fn(summed)


def nt_dot(left, right):
    return lax.dot_general(left, right, (((1,), (1,)), ((), ())), preferred_element_type=WIDE)


def seen_keys(block, first_row):
    window = (REACH + 1) * BLOCK
    k_pos = (block - REACH) * BLOCK + lax.broadcasted_iota(jnp.int32, (window, BLOCK), 0)
    q_pos = block * BLOCK + lax.broadcasted_iota(jnp.int32, (window, BLOCK), 1)
    return (k_pos >= first_row) & (k_pos <= q_pos) & (k_pos > q_pos - REACH * BLOCK)


PER = 4


def attend_forward_kernel(heads, waits, *refs):
    first_ref, q_ref, kv_ref, turned_ref, meta_ref, meta_turned_ref = refs[:6]
    out_ref, total_ref = refs[6 + waits : 8 + waits]
    for sub in range(PER):
        block = pl.program_id(0) * PER + sub
        here = slice(sub * BLOCK, (sub + 1) * BLOCK)
        span = pl.ds(pl.multiple_of(block * BLOCK, BLOCK), (REACH + 1) * BLOCK)
        seen = seen_keys(block, first_ref[sub])
        outs, totals = [], []
        for h in range(heads):
            cut = slice(h * HEAD, (h + 1) * HEAD)
            v_cut = slice((heads + h) * HEAD, (heads + h + 1) * HEAD)
            query = q_ref[here, cut] * SIXTEEN(HEAD ** (-0.5))
            near = jnp.where(seen, nt_dot(kv_ref[span, cut], query), -1e30)
            meta = nt_dot(meta_ref[:, cut], query)
            top = jnp.maximum(
                jnp.max(near, axis=0, keepdims=True), jnp.max(meta, axis=0, keepdims=True)
            )
            near = jnp.exp(near - top)
            meta = jnp.exp(meta - top)
            total = jnp.sum(near, axis=0, keepdims=True) + jnp.sum(meta, axis=0, keepdims=True)
            out = jnp.dot(turned_ref[v_cut, span], near.astype(SIXTEEN), preferred_element_type=WIDE)
            out += jnp.dot(meta_turned_ref[v_cut, :], meta.astype(SIXTEEN), preferred_element_type=WIDE)
            outs.append(out / total)
            totals.append(top + jnp.log(total))
        out_ref[here, :] = jnp.concatenate(outs, axis=0).T
        total_ref[sub] = jnp.concatenate(totals, axis=0)


def attend_backward_kernel(
    heads, first_ref, q_ref, kv_ref, turned_ref, meta_ref, meta_turned_ref, out_ref, total_ref, do_ref,
    dq_ref, dkv_ref, dmeta_ref,
):
    block = pl.program_id(0)

    @pl.when(block == 0)
    def _():
        dkv_ref[...] = jnp.zeros_like(dkv_ref)
        dmeta_ref[...] = jnp.zeros_like(dmeta_ref)

    span = pl.ds(pl.multiple_of(block * BLOCK, BLOCK), (REACH + 1) * BLOCK)
    seen = seen_keys(block, first_ref[0])
    d_out = do_ref[...]
    row_sums = (d_out * out_ref[...]).T
    d_half = d_out.astype(SIXTEEN)
    d_queries, near_k, near_v, meta_k, meta_v = [], [], [], [], []
    for h in range(heads):
        cut = slice(h * HEAD, (h + 1) * HEAD)
        v_cut = slice((heads + h) * HEAD, (heads + h + 1) * HEAD)
        query = q_ref[:, cut] * SIXTEEN(HEAD ** (-0.5))
        do = d_half[:, cut]
        total = total_ref[0, h : h + 1, :]
        mean = jnp.sum(row_sums[cut], axis=0, keepdims=True)
        near = jnp.where(seen, jnp.exp(nt_dot(kv_ref[span, cut], query) - total), 0.0)
        meta = jnp.exp(nt_dot(meta_ref[:, cut], query) - total)
        d_near = (near * (nt_dot(kv_ref[span, v_cut], do) - mean)).astype(SIXTEEN)
        d_meta = (meta * (nt_dot(meta_ref[:, v_cut], do) - mean)).astype(SIXTEEN)
        near_v.append(jnp.dot(near.astype(SIXTEEN), do, preferred_element_type=WIDE))
        meta_v.append(jnp.dot(meta.astype(SIXTEEN), do, preferred_element_type=WIDE))
        near_k.append(jnp.dot(d_near, query, preferred_element_type=WIDE))
        meta_k.append(jnp.dot(d_meta, query, preferred_element_type=WIDE))
        d_query = jnp.dot(turned_ref[cut, span], d_near, preferred_element_type=WIDE)
        d_query += jnp.dot(meta_turned_ref[cut, :], d_meta, preferred_element_type=WIDE)
        d_queries.append(d_query * HEAD ** (-0.5))
    dq_ref[...] = jnp.concatenate(d_queries, axis=0).T.astype(SIXTEEN)
    dkv_ref[span, :] += jnp.concatenate(near_k + near_v, axis=1)
    dmeta_ref[...] += jnp.concatenate(meta_k + meta_v, axis=1)


def attend_operands(queries, kv_rows, doc_first):
    length = doc_first.shape[0]
    count = length // BLOCK
    near = jnp.pad(kv_rows[:length], ((REACH * BLOCK, 0), (0, 0)))
    meta = kv_rows[length:]
    arrays = (doc_first.reshape(count, 1, BLOCK), queries, near, near.T, meta, meta.T)
    width = queries.shape[1]

    def whole(array):
        return pl.BlockSpec(array.shape, lambda i: (0,) * array.ndim)

    specs = [
        pl.BlockSpec((1, 1, BLOCK), lambda i: (i, 0, 0)),
        pl.BlockSpec((BLOCK, width), lambda i: (i, 0)),
    ] + [whole(a) for a in arrays[2:]]
    return arrays, specs, count, width


def attend_forward(queries, kv_rows, doc_first, through=()):
    arrays, specs, count, width = attend_operands(queries, kv_rows, doc_first)
    heads = width // HEAD
    specs = [
        pl.BlockSpec((PER, 1, BLOCK), lambda i: (i, 0, 0)),
        pl.BlockSpec((PER * BLOCK, width), lambda i: (i, 0)),
    ] + specs[2:]
    return pl.pallas_call(
        lambda *refs: attend_forward_kernel(heads, len(through), *refs),
        grid=(count // PER,),
        in_specs=specs + [ANY] * len(through),
        out_specs=[
            pl.BlockSpec((PER * BLOCK, width), lambda i: (i, 0)),
            pl.BlockSpec((PER, heads, BLOCK), lambda i: (i, 0, 0)),
        ]
        + [ANY] * len(through),
        out_shape=[
            jax.ShapeDtypeStruct(queries.shape, WIDE),
            jax.ShapeDtypeStruct((count, heads, BLOCK), WIDE),
        ]
        + [jax.ShapeDtypeStruct(x.shape, x.dtype) for x in through],
        input_output_aliases={6 + i: 2 + i for i in range(len(through))},
        compiler_params=pltpu.CompilerParams(vmem_limit_bytes=48 * MIB),
        cost_estimate=takes(24),
    )(*arrays, *through)


def attend_backward(queries, kv_rows, doc_first, out, log_total, d_out):
    arrays, specs, count, width = attend_operands(queries, kv_rows, doc_first)
    heads = width // HEAD
    near, meta = arrays[2], arrays[4]
    row_spec = pl.BlockSpec((BLOCK, width), lambda i: (i, 0))
    d_queries, d_near, d_meta = pl.pallas_call(
        lambda *refs: attend_backward_kernel(heads, *refs),
        grid=(count,),
        in_specs=specs
        + [row_spec, pl.BlockSpec((1, heads, BLOCK), lambda i: (i, 0, 0)), row_spec],
        out_specs=[
            row_spec,
            pl.BlockSpec(near.shape, lambda i: (0, 0)),
            pl.BlockSpec(meta.shape, lambda i: (0, 0)),
        ],
        out_shape=[
            jax.ShapeDtypeStruct(queries.shape, SIXTEEN),
            jax.ShapeDtypeStruct(near.shape, WIDE),
            jax.ShapeDtypeStruct(meta.shape, WIDE),
        ],
        compiler_params=pltpu.CompilerParams(vmem_limit_bytes=48 * MIB),
        cost_estimate=takes(24),
    )(*arrays, out, log_total, d_out)
    return d_queries, d_near[REACH * BLOCK :].astype(SIXTEEN), d_meta.astype(SIXTEEN)


def step_sum():
    rows = lax.broadcasted_iota(jnp.int32, (SUB, SUB * STATE), 0)
    cols = lax.broadcasted_iota(jnp.int32, (SUB, SUB * STATE), 1)
    return (cols // STATE == rows).astype(SIXTEEN)


def lanes_from(tile, group):
    return pltpu.roll(tile, (SPAN - group * SUB) % SPAN, axis=1)


def scan_forward_kernel(waits, *refs):
    keep_ref, conv_ref, delta_ref, bc_ref, a_ref = refs[:5]
    y_ref, start_ref, kept_ref = refs[5 + waits : 8 + waits]
    state_ref = refs[-1]
    block = pl.program_id(0)

    @pl.when(block == 0)
    def _():
        state_ref[...] = jnp.zeros_like(state_ref)

    start_ref[0] = state_ref[...]
    decay_rate = a_ref[...]
    fold = step_sum()
    b_span = bc_ref[:STATE, :].astype(WIDE)
    c_span = bc_ref[STATE:, :].astype(WIDE)

    def body(group, state):
        rows = pl.ds(pl.multiple_of(group * SUB, SUB), SUB)
        delta = delta_ref[rows, :]
        drive = delta * conv_ref[rows, :]
        b_tile = lanes_from(b_span, group)
        c_tile = lanes_from(c_span, group)
        reads = []
        for i in range(SUB):
            keep = keep_ref[block * SPAN + group * SUB + i]
            decay = jnp.exp(delta[i : i + 1, :] * decay_rate) * keep
            state = decay * state + drive[i : i + 1, :] * b_tile[:, i : i + 1]
            kept_ref[group * SUB + i] = state.astype(SIXTEEN)
            reads.append((state * c_tile[:, i : i + 1]).astype(SIXTEEN))
        y_ref[rows, :] = jnp.dot(
            fold, jnp.concatenate(reads, axis=0), preferred_element_type=WIDE
        )
        return state

    state_ref[...] = lax.fori_loop(0, SPAN // SUB, body, state_ref[...], unroll=8)


def scan_forward(keep, conv_out, delta, bc_rows, decay_rate, after=(), through=()):
    length, lanes = conv_out.shape
    waits = len(after) + len(through)
    blocks = length // SPAN
    span_spec = pl.BlockSpec((SPAN, lanes), lambda i: (i, 0))
    return pl.pallas_call(
        functools.partial(scan_forward_kernel, waits),
        grid=(blocks,),
        in_specs=[
            pl.BlockSpec(memory_space=pltpu.SMEM),
            span_spec,
            span_spec,
            pl.BlockSpec((2 * STATE, SPAN), lambda i: (0, i)),
            pl.BlockSpec((STATE, lanes), lambda i: (0, 0)),
        ]
        + [ANY] * waits,
        out_specs=[
            span_spec,
            pl.BlockSpec((1, STATE, lanes), lambda i: (i, 0, 0)),
            pl.BlockSpec((SPAN, STATE, lanes), lambda i: (i, 0, 0)),
        ]
        + [ANY] * len(through),
        out_shape=[
            jax.ShapeDtypeStruct((length, lanes), WIDE),
            jax.ShapeDtypeStruct((blocks, STATE, lanes), WIDE),
            jax.ShapeDtypeStruct((length, STATE, lanes), SIXTEEN),
        ]
        + [jax.ShapeDtypeStruct(x.shape, x.dtype) for x in through],
        input_output_aliases={5 + len(after) + i: 3 + i for i in range(len(through))},
        scratch_shapes=[pltpu.VMEM((STATE, lanes), WIDE)],
        cost_estimate=takes(24),
    )(keep, conv_out, delta, bc_rows, decay_rate, *after, *through)


def scan_backward_kernel(
    keep_ref, conv_ref, delta_ref, bc_ref, a_ref, start_ref, kept_ref, dy_ref,
    dconv_ref, ddelta_ref, dbc_ref, da_ref,
    adjoint_ref,
):
    turn = pl.program_id(0)
    block = pl.num_programs(0) - 1 - turn

    @pl.when(turn == 0)
    def _():
        adjoint_ref[...] = jnp.zeros_like(adjoint_ref)
        da_ref[...] = jnp.zeros_like(da_ref)

    decay_rate = a_ref[...]
    fold = step_sum()
    lanes = decay_rate.shape[1]
    ones = jnp.ones((lanes, SPAN), SIXTEEN)
    spot = lax.broadcasted_iota(jnp.int32, (STATE, SPAN), 1)
    b_span = bc_ref[:STATE, :].astype(WIDE)
    c_span = bc_ref[STATE:, :].astype(WIDE)
    def back(step, carry):
        adjoint, da, db, dc = carry
        group = SPAN // SUB - 1 - step
        rows = pl.ds(pl.multiple_of(group * SUB, SUB), SUB)
        delta = delta_ref[rows, :]
        conv = conv_ref[rows, :]
        drive = delta * conv
        dy = dy_ref[rows, :]
        b_tile = lanes_from(b_span, group)
        c_tile = lanes_from(c_span, group)
        before = kept_ref[jnp.maximum(group * SUB - 1, 0)].astype(WIDE)
        before = jnp.where(group == 0, start_ref[0], before)
        states = [before] + [kept_ref[group * SUB + i].astype(WIDE) for i in range(SUB)]
        by_c, by_b, by_drive, by_delta = ([None] * SUB for _ in range(4))
        for i in range(SUB - 1, -1, -1):
            keep = keep_ref[block * SPAN + group * SUB + i]
            decay = jnp.exp(delta[i : i + 1, :] * decay_rate) * keep
            dy_row = dy[i : i + 1, :]
            total = adjoint + dy_row * c_tile[:, i : i + 1]
            by_c[i] = (dy_row * states[i + 1]).astype(SIXTEEN)
            by_b[i] = (total * drive[i : i + 1, :]).astype(SIXTEEN)
            by_drive[i] = (total * b_tile[:, i : i + 1]).astype(SIXTEEN)
            adjoint = total * decay
            rate = adjoint * states[i]
            by_delta[i] = (rate * decay_rate).astype(SIXTEEN)
            da = da + rate * delta[i : i + 1, :]

        def over_state(parts):
            return jnp.dot(fold, jnp.concatenate(parts, axis=0), preferred_element_type=WIDE)

        def over_lanes(parts, tile):
            sums = jnp.dot(jnp.concatenate(parts, axis=0), ones, preferred_element_type=WIDE)
            for i in range(SUB):
                here = spot == group * SUB + i
                tile = jnp.where(here, sums[i * STATE : (i + 1) * STATE, :], tile)
            return tile

        d_drive = over_state(by_drive)
        dconv_ref[rows, :] = d_drive * delta
        ddelta_ref[rows, :] = over_state(by_delta) + d_drive * conv
        return adjoint, da, over_lanes(by_b, db), over_lanes(by_c, dc)

    none = jnp.zeros((STATE, SPAN), WIDE)
    adjoint, da, db, dc = lax.fori_loop(
        0, SPAN // SUB, back, (adjoint_ref[...], da_ref[...], none, none), unroll=16
    )
    adjoint_ref[...] = adjoint
    da_ref[...] = da
    dbc_ref[...] = jnp.concatenate([db, dc], axis=0)


def scan_backward(keep, conv_out, delta, bc_rows, decay_rate, starts, kept, dy):
    length, lanes = conv_out.shape
    blocks = length // SPAN
    span_spec = pl.BlockSpec((SPAN, lanes), lambda i: (blocks - 1 - i, 0))
    rows_spec = pl.BlockSpec((2 * STATE, SPAN), lambda i: (0, blocks - 1 - i))
    whole = pl.BlockSpec((STATE, lanes), lambda i: (0, 0))
    return pl.pallas_call(
        scan_backward_kernel,
        grid=(blocks,),
        in_specs=[
            pl.BlockSpec(memory_space=pltpu.SMEM),
            span_spec,
            span_spec,
            rows_spec,
            whole,
            pl.BlockSpec((1, STATE, lanes), lambda i: (blocks - 1 - i, 0, 0)),
            pl.BlockSpec((SPAN, STATE, lanes), lambda i: (blocks - 1 - i, 0, 0)),
            span_spec,
        ],
        out_specs=[span_spec, span_spec, rows_spec, whole],
        out_shape=[
            jax.ShapeDtypeStruct((length, lanes), WIDE),
            jax.ShapeDtypeStruct((length, lanes), WIDE),
            jax.ShapeDtypeStruct((2 * STATE, length), WIDE),
            jax.ShapeDtypeStruct((STATE, lanes), WIDE),
        ],
        scratch_shapes=[
            pltpu.VMEM((STATE, lanes), WIDE),
        ],
        compiler_params=pltpu.CompilerParams(vmem_limit_bytes=32 * MIB),
        cost_estimate=takes(40),
    )(keep, conv_out, delta, bc_rows, decay_rate, starts, kept, dy)


def padded_lanes(array, lanes):
    return jnp.pad(array, ((0, 0), (0, lanes - array.shape[1])))


def rms_pull(values, scale, gain, d_normed, mean):
    d_values = scale * gain * d_normed - values * (scale * scale * scale) * mean
    return d_values, jnp.sum(d_normed * values * scale, axis=0)


def per_device(tokens, doc_ids, meta_tokens, mixer_params, small_params, ffn_params, cotangent):
    tokens, cotangent = tokens[0], cotangent[0]
    small_whole, ids, meta_whole = start_blocks(small_params, doc_ids[0], meta_tokens)
    g_one = small_shards(small_whole)[0]
    rows, shards = lax.axis_size("row"), lax.axis_size("seq")
    staged = weights_fit(mixer_params.shape[0], ffn_params.shape[0], rows, shards)
    if staged:
        columns, pull_columns = jax.vjp(partial(to_columns, width=view_width()), mixer_params)
    length = ids.shape[0]
    positions = jnp.arange(length, dtype=jnp.int32)
    starts = jnp.concatenate([jnp.ones((1,), bool), ids[1:] != ids[:-1]])
    doc_first = lax.cummax(jnp.where(starts, positions, 0), axis=0)
    keep_mask = (positions != doc_first).astype(WIDE)
    lag_masks = jnp.stack(
        [(positions - j >= doc_first).astype(WIDE)[:, None] for j in range(CONV)]
    )

    tokens_f = tokens.astype(WIDE)
    normed_f, norm_pull = jax.vjp(rms_norm, tokens_f, g_one)
    meta_own = meta_tokens.astype(WIDE)
    meta_unit = rms_norm(meta_whole.astype(WIDE), 1.0)
    normed_own = normed_f.astype(SIXTEEN)
    if staged:
        normed_own, columns = tie(normed_own, columns)
        both, pull_both = jax.vjp(both_halves, columns)
    normed = ring_seq_gather(normed_own, 1)
    cotangent_later = cotangent
    if staged:
        normed, both, cotangent_later = tie(normed, both, cotangent)
        (w_in, w_dt, q_rows, out_rows), pull_parts = jax.vjp(mixer_parts, both)
        (by_heads, w_x), pull_rows = jax.vjp(heads_cut, q_rows)
    else:
        (w_qkv, w_in, w_x, w_dt, w_out), pull_mixer = jax.vjp(mixer_shards_whole, mixer_params)
        (w_gate, w_up, w_down), pull_ffn = jax.vjp(ffn_shards_whole, ffn_params)
    normed, small_later = tie(normed, small_whole)
    (_, g_two, g_attn, channel_part), small_pull = jax.vjp(small_shards, small_later)
    channels = channel_part.shape[0]
    lanes = -(-channels // 128) * 128
    g_ssm = channel_part[:, 0]
    conv_w = channel_part[:, 1 : 1 + CONV].T
    conv_b = channel_part[:, 1 + CONV]
    dt_bias = channel_part[:, 2 + CONV]
    a_log = channel_part[:, 3 + CONV : 3 + CONV + STATE]
    d_skip = channel_part[:, 3 + CONV + STATE]
    meta_normed = (meta_unit * g_one).astype(SIXTEEN)
    every = jnp.concatenate([normed, meta_normed], axis=0)
    cotangent_all = gather_seq(cotangent_later)

    xz = dot_last(normed, w_in).astype(SIXTEEN)
    extended = jnp.pad(xz[:, :channels], ((CONV - 1, 0), (0, 0))).astype(WIDE)
    conv_fn = partial(conv_piece, lag_masks=lag_masks)
    conv_out, conv_pull = jax.vjp(conv_fn, extended, conv_w, conv_b)
    conv_half = conv_out.astype(SIXTEEN)
    if staged:
        conv_half, by_heads, w_x, ffn_later = tie(conv_half, by_heads, w_x, ffn_params)
        w_qkv, pull_heads = jax.vjp(heads_from, by_heads)
        ffn_cut, pull_ffn_cut = jax.vjp(ffn_blocks, ffn_later)
    conv_f = conv_half.astype(WIDE)
    w_x_rows = jnp.pad(w_x.T, ((0, -w_x.shape[1] % 16), (0, 0)))
    projected = seq_sum(jnp.einsum("nc,tc->nt", w_x_rows, conv_half, preferred_element_type=WIDE), 2)
    rank_half = projected[:DT_RANK]
    pre_dt = jnp.einsum("rt,rc->tc", rank_half, w_dt, preferred_element_type=WIDE)
    delta, delta_pull = jax.vjp(lambda p, b: softplus_fn(p + b), pre_dt, dt_bias)
    a_neg, a_pull = jax.vjp(lambda a: -jnp.exp(a), a_log)
    if staged:
        after, through = (w_qkv, cotangent_all), (ffn_cut,)
    else:
        after, through = (), ()
    scan_in = (
        keep_mask,
        padded_lanes(conv_f, lanes),
        padded_lanes(delta, lanes),
        projected[DT_RANK : DT_RANK + 2 * STATE],
        padded_lanes(a_neg.T, lanes),
    )
    y_scan, scan_starts, scan_states, *through = scan_forward(*scan_in, after, through)
    if staged:
        (ffn_cut,) = through
        ffn_columns, pull_ffn_columns = jax.vjp(exchange, ffn_cut)
        ffn_both, pull_ffn_both = jax.vjp(both_halves, ffn_columns)
        (w_gate, w_up, down_rows), pull_ffn_parts = jax.vjp(ffn_parts, ffn_both)
        w_down, pull_down = jax.vjp(down_from, down_rows)

    def gate_piece(y, c, skip, z):
        return (y + skip * c) * silu_fn(z)

    z_in = xz[:, channels:].astype(WIDE)
    ssm_out, gate_pull = jax.vjp(gate_piece, y_scan[:, :channels], conv_f, d_skip, z_in)

    own_heads = g_attn.shape[0]
    queries = dot_last(normed, w_qkv[:, :own_heads]).astype(SIXTEEN)
    kv_rows = dot_last(every, w_qkv[:, own_heads:]).astype(SIXTEEN)
    through = (out_rows.transpose(0, 2, 1),) if staged else ()
    attn_out, log_total, *through = attend_forward(queries, kv_rows, doc_first, through)
    if staged:
        out_received, pull_out_exchange = jax.vjp(exchange, through[0].transpose(0, 2, 1))

    squares = jnp.stack([jnp.sum(attn_out * attn_out, axis=1), jnp.sum(ssm_out * ssm_out, axis=1)])
    squares = seq_sum_small(squares, 3)
    if staged:
        out_received = hand_on(out_received.transpose(0, 2, 1), squares).transpose(0, 2, 1)
        w_out, pull_out = jax.vjp(out_from, out_received)
    scale_a = lax.rsqrt(squares[0] / (HEADS * HEAD) + norm_eps)[:, None]
    scale_m = lax.rsqrt(squares[1] / INNER + norm_eps)[:, None]
    mixed = 0.5 * jnp.concatenate(
        [attn_out * scale_a * g_attn, ssm_out * scale_m * g_ssm], axis=1
    )
    mixed = mixed.astype(SIXTEEN)
    hidden = tokens_f + product_scatter([(mixed, w_out, False)], 4)

    second_f, second_pull = jax.vjp(rms_norm, hidden, g_two)
    second, act, d_gate, d_up = gather_ffn(
        second_f.astype(SIXTEEN), cotangent_all, w_gate, w_up, w_down, 5
    )
    d_second = product_scatter([(d_gate, w_gate, True), (d_up, w_up, True)], 6)
    d_hidden, grad_g_two = second_pull(d_second)
    d_hidden = d_hidden + cotangent.astype(WIDE)

    d_branch, grad_gate, grad_up, grad_down, down_product = gather_beside_ffn(
        d_hidden.astype(SIXTEEN), second, cotangent_all, act, d_gate, d_up, w_down, 7
    )
    grads_ffn = (grad_gate, grad_up, grad_down)
    block_out = (hidden + scatter_seq(down_product)).astype(SIXTEEN)
    grad_out = hold(dot_weight(mixed, d_branch).astype(SIXTEEN))
    if staged:
        (d_down_rows,) = pull_down(grads_ffn[2])
    d_mixed = 0.5 * dot_back(d_branch, w_out)
    d_mix_a, d_mix_m = d_mixed[:, :own_heads], d_mixed[:, own_heads:]
    means = jnp.stack(
        [jnp.sum(attn_out * g_attn * d_mix_a, axis=1), jnp.sum(ssm_out * g_ssm * d_mix_m, axis=1)]
    )
    means = seq_sum_small(means, 8)
    if staged:
        means, d_down_rows, grad_gate, grad_up = tie(
            means, d_down_rows, grads_ffn[0], grads_ffn[1]
        )
        (d_ffn_both,) = pull_ffn_parts((grad_gate, grad_up, d_down_rows))
        (d_ffn_columns,) = pull_ffn_both(d_ffn_both)
        (d_out_rows,) = pull_out_exchange(pull_out(grad_out)[0])
    d_attn, grad_g_attn = rms_pull(
        attn_out, scale_a, g_attn, d_mix_a, means[0][:, None] / (HEADS * HEAD)
    )
    d_ssm, grad_g_ssm = rms_pull(ssm_out, scale_m, g_ssm, d_mix_m, means[1][:, None] / INNER)

    d_queries, d_kv, d_meta_kv = attend_backward(
        queries, kv_rows, doc_first, attn_out, log_total, d_attn
    )

    if staged:
        d_queries, d_kv, d_ffn_columns, d_out_rows = tie(
            d_queries, d_kv, d_ffn_columns, d_out_rows
        )
        (grad_ffn,) = pull_ffn_cut(pull_ffn_columns(d_ffn_columns)[0])
    grad_kv = dot_weight(normed, d_kv) + dot_weight(meta_normed, d_meta_kv)
    grad_qkv = jnp.concatenate([dot_weight(normed, d_queries), grad_kv], axis=1)
    grad_qkv = hold(grad_qkv.astype(SIXTEEN))

    d_y, d_conv, grad_d_skip, d_z = gate_pull(d_ssm)
    if staged:
        d_y, grad_qkv = tie(d_y, grad_qkv)
    d_conv_scan, d_delta, d_bc, d_rate = scan_backward(
        *scan_in, scan_starts, scan_states, padded_lanes(d_y, lanes)
    )
    if staged:
        d_conv_scan, d_delta, grad_ffn, grad_qkv = tie(d_conv_scan, d_delta, grad_ffn, grad_qkv)
        (d_by_heads,) = pull_heads(grad_qkv)
    d_conv = d_conv + d_conv_scan[:, :channels]
    d_pre, grad_dt_bias = delta_pull(d_delta[:, :channels])
    (grad_a_log,) = a_pull(d_rate[:, :channels].T)
    d_pre = d_pre.astype(SIXTEEN)
    grad_dt = jnp.einsum("rt,tc->rc", rank_half, d_pre, preferred_element_type=WIDE)
    d_rank = jnp.einsum("rc,tc->rt", w_dt, d_pre, preferred_element_type=WIDE)
    d_proj = jnp.concatenate([d_rank, d_bc], axis=0)
    d_proj = seq_sum(jnp.pad(d_proj, ((0, -d_proj.shape[0] % 16), (0, 0))), 10, (block_out,))
    if staged:
        d_proj, d_by_heads = tie(d_proj, d_by_heads)
    d_proj = d_proj[: DT_RANK + 2 * STATE].T
    grad_x = hold(dot_weight(conv_half, d_proj).astype(SIXTEEN))
    if staged:
        (d_q_rows,) = pull_rows((d_by_heads, grad_x))
    d_extended, grad_conv_w, grad_conv_b = conv_pull(d_conv + dot_back(d_proj, w_x))
    d_xz = jnp.concatenate([d_extended[CONV - 1 :], d_z], axis=1).astype(SIXTEEN)
    grad_in = hold(dot_weight(normed, d_xz).astype(SIXTEEN))
    grad_dt = grad_dt.astype(SIXTEEN)
    if staged:
        (d_both,) = pull_parts((grad_in, grad_dt, d_q_rows, d_out_rows))
        d_xz, d_both = tie(d_xz, d_both)
        (d_columns,) = pull_both(d_both)
    w_q, w_kv = w_qkv[:, :own_heads], w_qkv[:, own_heads:]
    d_meta = dot_back(d_meta_kv, w_kv)
    d_normed = product_scatter(
        [(d_xz, w_in, True), (d_queries, w_q, True), (d_kv, w_kv, True)], 11
    )
    if staged:
        d_normed, d_columns = tie(d_normed, d_columns)
        (grad_mixer,) = pull_columns(d_columns)
    else:
        (grad_mixer,) = pull_mixer((grad_qkv, grad_in, grad_x, grad_dt, grad_out))
        (grad_ffn,) = pull_ffn(grads_ffn)
    grad_from_norm, grad_g_one = norm_pull(d_normed)
    grad_tokens = d_hidden + grad_from_norm
    grad_g_meta = jnp.sum(d_meta * meta_unit, axis=0)
    grad_channels = jnp.concatenate(
        [
            grad_g_ssm[:, None],
            grad_conv_w.T,
            grad_conv_b[:, None],
            grad_dt_bias[:, None],
            grad_a_log,
            grad_d_skip[:, None],
        ],
        axis=1,
    )
    (grad_small,) = small_pull((grad_g_one + grad_g_meta, grad_g_two, grad_g_attn, grad_channels))
    grad_small, d_meta = end_blocks(grad_small, d_meta)
    _, meta_pull = jax.vjp(lambda v: rms_norm(v, g_one), meta_own)
    (grad_meta,) = meta_pull(d_meta)
    return (
        block_out[None],
        grad_tokens[None],
        grad_meta,
        hold(grad_mixer).astype(WIDE),
        grad_small,
        hold(grad_ffn).astype(WIDE),
    )


def solution(mesh):
    in_specs = (
        P("row", "seq", None),
        P("row", "seq"),
        P(("row", "seq"), None),
        P(("row", "seq")),
        P(("row", "seq")),
        P(("row", "seq")),
        P("row", "seq", None),
    )
    out_specs = (
        P("row", "seq", None),
        P("row", "seq", None),
        P(("row", "seq"), None),
        P(("row", "seq")),
        P(("row", "seq")),
        P(("row", "seq")),
    )
    return jax.shard_map(
        per_device, mesh=mesh, in_specs=in_specs, out_specs=out_specs, check_vma=False
    )
```

```python
import functools
from functools import partial
import math

import jax
import jax.numpy as jnp
from jax import lax
from jax.experimental import pallas as pl
from jax.experimental.pallas import tpu as pltpu
from jax.sharding import PartitionSpec as P

D = 1600
HEADS = 25
GROUPS = 5
HEAD = 64
INNER = 3200
STATE = 16
CONV = 4
DT_RANK = 100
FF = 5504
REACH = 8
BLOCK = 128
RUNS = 4
SUB = 8
SPAN = 128
SIXTEEN = jnp.bfloat16
WIDE = jnp.float32


norm_eps = 1e-05


def split_flat(flat_vec, layout):
    pieces = []
    offset = 0
    for piece_shape in layout:
        piece_len = math.prod(piece_shape)
        pieces.append(flat_vec[offset : offset + piece_len].reshape(piece_shape))
        offset += piece_len
    return pieces


def mixer_layout():
    return [
        (D, HEADS * HEAD),
        (D, 2 * GROUPS * HEAD),
        (D, 2 * INNER),
        (INNER, DT_RANK + 2 * STATE),
        (DT_RANK, INNER),
        (HEADS * HEAD + INNER, D),
    ]


def ffn_layout():
    return [(D, FF), (D, FF), (FF, D)]


def small_split(flat_vec):
    width = CONV + STATE + 4
    packed_rows = flat_vec[: D * (3 + 2 * width)].reshape(D, 3 + 2 * width)
    channel_part = packed_rows[:, 3:].reshape(INNER, width)
    return packed_rows[:, 0], packed_rows[:, 1], packed_rows[:, 2], channel_part


def rms_norm(values, gain_vec):
    return (
        values * lax.rsqrt(jnp.mean(values * values, axis=-1, keepdims=True) + norm_eps) * gain_vec
    )


def silu_fn(values):
    return values / (1.0 + jnp.exp(-values))


def softplus_fn(values):
    return jnp.maximum(values, 0.0) + jnp.log1p(jnp.exp(-jnp.abs(values)))


def glu_piece(gate_pre, up_pre):
    return silu_fn(gate_pre) * up_pre


def dot_last(left, right):
    return jnp.einsum("...k,kn->...n", left, right, preferred_element_type=WIDE)


def dot_back(grads, right):
    return jnp.einsum("...n,kn->...k", grads, right, preferred_element_type=WIDE)


def dot_weight(left, grads):
    return jnp.einsum("...k,...n->kn", left, grads, preferred_element_type=WIDE)


def heads_of(shards):
    return -(-HEADS // shards)


def runs_of(shards):
    return RUNS if INNER % (RUNS * shards) == 0 else 1


def own_channels(array, axis, shards, place):
    runs = runs_of(shards)
    unit = INNER // (runs * shards)
    shape = array.shape
    cut = array.reshape(shape[:axis] + (runs, shards, unit) + shape[axis + 1 :])
    cut = lax.dynamic_index_in_dim(cut, place, axis + 1, keepdims=False)
    return cut.reshape(shape[:axis] + (runs * unit,) + shape[axis + 1 :])


def pad_heads(array, axis, shards):
    heads = heads_of(shards)
    pads = [(0, 0)] * array.ndim
    pads[axis] = (0, heads * shards - HEADS)
    padded = jnp.pad(array, pads)
    shape = padded.shape
    return padded.reshape(shape[:axis] + (shards, heads * HEAD) + shape[axis + 2 :])


def by_head(w_q, w_kv, shards):
    rows = w_q.shape[0]
    w_kv = w_kv.reshape(rows, 2, GROUPS, 1, HEAD)
    w_kv = jnp.broadcast_to(w_kv, (rows, 2, GROUPS, HEADS // GROUPS, HEAD))
    w_kv = w_kv.reshape(rows, 2, HEADS, HEAD)
    return jnp.concatenate(
        [
            pad_heads(w_q.reshape(rows, HEADS, HEAD), 1, shards),
            pad_heads(w_kv[:, 0], 1, shards),
            pad_heads(w_kv[:, 1], 1, shards),
        ],
        axis=2,
    )


def exchange(value):
    return lax.all_to_all(value, "seq", 0, 0)


def tie(*arrays):
    return lax.optimization_barrier(arrays)


def hold(array):
    return lax.optimization_barrier(array)


def hand_on(array, *after):
    return pl.pallas_call(
        lambda *refs: None,
        out_shape=jax.ShapeDtypeStruct(array.shape, array.dtype),
        in_specs=[ANY] * (1 + len(after)),
        out_specs=ANY,
        input_output_aliases={0: 0},
    )(array, *after)


def other_row(value):
    return lax.ppermute(value, "row", [(0, 1), (1, 0)])


def in_turn(first_row, one, two):
    return jnp.where(first_row, one, two), jnp.where(first_row, two, one)


@jax.custom_vjp
def both_halves(value):
    first_row = lax.axis_index("row") == 0
    return jnp.concatenate(in_turn(first_row, value, other_row(value)), axis=0)


def row_parts(grad):
    half = grad.shape[0] // 2
    return in_turn(lax.axis_index("row") == 0, grad[:half], grad[half:])


def both_halves_backward(_, grad):
    own, other = row_parts(grad)
    return (own + other_row(other),)


both_halves.defvjp(lambda value: (both_halves(value), None), both_halves_backward)


@partial(jax.custom_vjp, nondiff_argnums=(1,))
def cut_rows(array, counts):
    pieces, offset = [], 0
    for count in counts:
        pieces.append(array[offset : offset + count])
        offset += count
    return tuple(pieces)


def cut_rows_forward(array, counts):
    return cut_rows(array, counts), None


def cut_rows_backward(counts, _, grads):
    return (jnp.concatenate(grads, axis=0),)


cut_rows.defvjp(cut_rows_forward, cut_rows_backward)


def view_width():
    return INNER // RUNS


def weights_fit(mixer_length, ffn_length, rows, shards):
    width = view_width()
    sizes = [math.prod(shape) for shape in mixer_layout()]
    return (
        rows == 2
        and runs_of(shards) == RUNS
        and mixer_length % width == 0
        and all(size % width == 0 for size in sizes)
        and D % shards == 0
        and D % width == 0
        and (HEADS * HEAD * 2) % shards == 0
        and shards % x_turns(shards)[0] == 0
        and ffn_length % FF == 0
    )


def to_columns(piece, width):
    shards = lax.axis_size("seq")
    unit = width // shards
    view = hold(piece.reshape(-1, width))
    return exchange(view.reshape(-1, shards, unit).transpose(1, 0, 2)).reshape(-1, unit)


def full_rows(cut):
    received = exchange(cut)
    return hold(received.transpose(1, 0, 2).reshape(received.shape[1], -1))


def mixer_parts(both):
    width, shards = view_width(), lax.axis_size("seq")
    unit = both.shape[1]
    part_q, part_kv, part_in, part_x, part_dt, part_out = cut_rows(
        both, tuple(math.prod(shape) // width for shape in mixer_layout())
    )
    q_rows = jnp.concatenate(
        [
            part_q.reshape(shards, -1, unit),
            part_kv.reshape(shards, -1, unit),
            x_windows(part_x, shards),
        ],
        axis=1,
    )
    per_row = D // width
    head_rows = heads_of(shards) * HEAD
    out_heads, out_inner = cut_rows(part_out, (HEADS * HEAD * per_row, INNER * per_row))
    out_heads = jnp.pad(
        out_heads, ((0, (head_rows * shards - HEADS * HEAD) * per_row), (0, 0))
    ).reshape(shards, -1, unit)
    out_inner = out_inner.reshape(RUNS, shards, -1, unit)
    out_inner = out_inner.transpose(1, 0, 2, 3).reshape(shards, -1, unit)
    return (
        part_in.reshape(D, -1),
        part_dt.reshape(DT_RANK, -1),
        q_rows,
        jnp.concatenate([out_heads, out_inner], axis=1),
    )


def heads_cut(q_rows):
    shards = lax.axis_size("seq")
    rows = D // shards
    by_rows = full_rows(q_rows)
    split = rows * HEADS * HEAD // view_width()
    end = split + rows * 2 * GROUPS * HEAD // view_width()
    cut = by_head(
        by_rows[:split].reshape(rows, HEADS * HEAD),
        by_rows[split:end].reshape(rows, 2 * GROUPS * HEAD),
        shards,
    )
    return cut.transpose(1, 0, 2), x_from_windows(by_rows[end:], lax.axis_index("seq"))


def heads_from(cut):
    return exchange(cut).reshape(D, -1)


def out_from(received):
    rows = received.shape[1]
    return hold(received.transpose(1, 0, 2).reshape(rows, -1)).reshape(-1, D)


def ffn_blocks(piece):
    shards = lax.axis_size("seq")
    return piece.reshape(-1, shards, FF // shards).transpose(1, 0, 2)


def ffn_parts(both):
    unit = both.shape[2]
    w_gate, w_up, part_down = cut_rows(both.reshape(-1, unit), (D, D, D))
    return w_gate, w_up, part_down.reshape(lax.axis_size("seq"), -1, unit)


def down_from(received):
    return received.transpose(1, 0, 2).reshape(-1, D)


def x_turns(shards):
    width = INNER // RUNS
    run = (width // shards) * (DT_RANK + 2 * STATE)
    common = math.gcd(run, width)
    return width // common, run // common


def x_windows(part_x, shards):
    runs, rows = x_turns(shards)
    need = -(-rows // runs)
    turns = part_x.reshape(-1, rows, part_x.shape[1])
    cuts = [turns[:, (i * rows) // runs : (i * rows) // runs + need] for i in range(runs)]
    cuts = jnp.stack(cuts, axis=1).reshape(RUNS, shards, need, part_x.shape[1])
    return cuts.transpose(1, 0, 2, 3).reshape(shards, RUNS * need, part_x.shape[1])


def x_from_windows(view_rows, place):
    width = view_rows.shape[1]
    shards = lax.axis_size("seq")
    runs, rows = x_turns(shards)
    columns = DT_RANK + 2 * STATE
    count = (width // shards) * columns
    flat = view_rows.reshape(RUNS, -1)
    offset = (place % runs) * rows * (width // runs) % width
    return lax.dynamic_slice_in_dim(flat, offset, count, 1).reshape(-1, columns)


def mixer_shards_whole(piece):
    shards, place = lax.axis_size("seq"), lax.axis_index("seq")
    whole = lax.all_gather(piece, ("row", "seq"), axis=0, tiled=True)
    w_q, w_kv, w_in, w_x, w_dt, w_out = split_flat(whole, mixer_layout())
    qkv = lax.dynamic_index_in_dim(by_head(w_q, w_kv, shards), place, 1, keepdims=False)
    w_in = own_channels(w_in.reshape(D, 2, INNER), 2, shards, place)
    out_heads = w_out[: HEADS * HEAD].reshape(HEADS, HEAD, D)
    out_heads = lax.dynamic_index_in_dim(pad_heads(out_heads, 0, shards), place, 0, keepdims=False)
    return (
        qkv,
        w_in.reshape(D, -1),
        own_channels(w_x, 0, shards, place),
        own_channels(w_dt, 1, shards, place),
        jnp.concatenate([out_heads, own_channels(w_out[HEADS * HEAD :], 0, shards, place)], axis=0),
    )


def ffn_shards_whole(piece):
    unit = FF // lax.axis_size("seq")
    start = lax.axis_index("seq") * unit
    whole = lax.all_gather(piece, ("row", "seq"), axis=0, tiled=True)
    w_gate, w_up, w_down = split_flat(whole, ffn_layout())
    return (
        lax.dynamic_slice_in_dim(w_gate, start, unit, 1),
        lax.dynamic_slice_in_dim(w_up, start, unit, 1),
        lax.dynamic_slice_in_dim(w_down, start, unit, 0),
    )


def small_shards(whole):
    shards, place = lax.axis_size("seq"), lax.axis_index("seq")
    g_one, g_attn, g_two, channel_part = small_split(whole)
    g_attn = pad_heads(g_attn.reshape(HEADS, HEAD), 0, shards)
    return (
        g_one,
        g_two,
        lax.dynamic_index_in_dim(g_attn, place, 0, keepdims=False),
        own_channels(channel_part, 0, shards, place),
    )


def tiles_of(count):
    return -(-count // 128)


def start_blocks(small_params, doc_ids, meta_tokens):
    devices = lax.axis_size("row") * lax.axis_size("seq")
    parts = [small_params, doc_ids.astype(SIXTEEN), meta_tokens.reshape(-1)]
    rows = [tiles_of(part.shape[0]) for part in parts]
    rows_all = -(-sum(rows) // 16) * 16
    tiles = [
        jnp.pad(part, (0, count * 128 - part.shape[0])).reshape(-1, 128)
        for part, count in zip(parts, rows)
    ]
    block = jnp.concatenate(tiles + [jnp.zeros((rows_all - sum(rows), 128), SIXTEEN)], axis=0)
    every = push_gather(block, 0)
    outs, begin = [], 0
    for part, count in zip(parts, rows):
        cut = every[:, begin : begin + count].reshape(devices, -1)[:, : part.shape[0]]
        outs.append(cut)
        begin += count
    ids = outs[1].reshape(lax.axis_size("row"), -1)
    ids = lax.dynamic_index_in_dim(ids, lax.axis_index("row"), 0, keepdims=False)
    return outs[0].reshape(-1).astype(WIDE), ids.astype(jnp.int32), outs[2].reshape(-1, D)


def end_blocks(grad_small, d_meta):
    devices = lax.axis_size("row") * lax.axis_size("seq")
    parts = grad_small.reshape(devices, -1).astype(SIXTEEN)
    small_count = parts.shape[1]
    small_rows = tiles_of(small_count)
    parts = jnp.pad(parts, ((0, 0), (0, small_rows * 128 - small_count)))
    meta = d_meta.astype(SIXTEEN).reshape(devices, -1)
    meta_count = meta.shape[1]
    rows = -(-(small_rows + tiles_of(meta_count)) // 16) * 16
    meta = jnp.pad(meta, ((0, 0), (0, (rows - small_rows) * 128 - meta_count)))
    blocks = jnp.concatenate(
        [parts.reshape(devices, -1, 128), meta.reshape(devices, -1, 128)], axis=1
    )
    own = push_scatter(blocks, 9)
    small = own[:small_rows].reshape(-1)[:small_count]
    meta = own[small_rows:].reshape(-1)[:meta_count].reshape(-1, D)
    return small, meta


def gather_seq(block):
    return lax.all_gather(block, "seq", axis=0, tiled=True)


def scatter_seq(whole):
    return lax.psum_scatter(whole.astype(SIXTEEN), "seq", scatter_dimension=0, tiled=True).astype(
        WIDE
    )


MESH = pl.DeviceIdType.MESH
ANY = pl.BlockSpec(memory_space=pl.ANY)
VMEM = pl.BlockSpec(memory_space=pltpu.VMEM)
MIB = 1024 * 1024


def takes(microseconds):
    return pl.CostEstimate(
        flops=0, bytes_accessed=microseconds * 3_500_000, transcendentals=0
    )


def greet(peers):
    barrier = pltpu.get_barrier_semaphore()
    for peer in peers:
        pl.semaphore_signal(barrier, inc=1, device_id=peer, device_id_type=MESH)
    pl.semaphore_wait(barrier, len(peers))


def ring_place(chip, chips):
    odd = chip % 2
    return odd * (chips - 1 - chip // 2) + (1 - odd) * (chip // 2)


def ring_chip(place, chips):
    place = (place + 2 * chips) % chips
    back = place // (chips // 2)
    return back * (2 * (chips - 1 - place) + 1) + (1 - back) * (2 * place)


def ring_gather_loop(
    shards, parts, x_ref, out_ref, ring_send, ring_recv, pair_send, pair_recv, work, begin=None
):
    row, me = lax.axis_index("row"), lax.axis_index("seq")
    chips = shards // 2
    core = me % 2
    place = ring_place(me // 2, chips)

    def device(spot):
        return ring_chip(spot, chips) * 2 + core

    right, left, twin = (row, device(place + 1)), (row, device(place - 1)), (row, me + 1 - 2 * core)
    greet([right, left, twin])
    rows = x_ref.shape[0] // (2 * parts)
    paths = [(way, part) for part in range(parts) for way in range(2)]

    def piece(way, part, step):
        source = device(place - 1 - step if way == 0 else place + 1 + step)
        return out_ref.at[source, pl.ds((way * parts + part) * rows, rows)]

    def ring(way, part, step):
        here = piece(way, part, step - 1)
        return pltpu.make_async_remote_copy(
            src_ref=here, dst_ref=here, send_sem=ring_send.at[way, part, step],
            recv_sem=ring_recv.at[way, part, step], device_id=(right, left)[way], device_id_type=MESH,
        )

    def pair(way, part, step):
        here = piece(way, part, step - 1)
        return pltpu.make_async_remote_copy(
            src_ref=here, dst_ref=here, send_sem=pair_send.at[way, part, step],
            recv_sem=pair_recv.at[way, part, step], device_id=twin, device_id_type=MESH,
        )

    out_ref[me] = x_ref[...]
    for way, part in paths:
        ring(way, part, 0).start()
    for way, part in paths:
        pair(way, part, 0).start()
    if begin is not None:
        begin()

    def body(step, carry):
        @pl.when(step < chips - 1)
        def _():
            for way, part in paths:
                ring(way, part, step).wait_recv()

                @pl.when(step < chips - 2)
                def _():
                    ring(way, part, step + 1).start()

                pair(way, part, step + 1).start()

        for way, part in paths:
            pair(way, part, step).wait_recv()
        work(step, place)
        return carry

    lax.fori_loop(0, chips, body, 0)

    def finish(step, carry):
        for way, part in paths:
            pair(way, part, step).wait_send()

            @pl.when(step < chips - 1)
            def _():
                ring(way, part, step).wait_send()

        return carry

    lax.fori_loop(0, chips, finish, 0)


def ring_semaphores(chips, parts):
    ring = pltpu.SemaphoreType.DMA((2, parts, chips - 1))
    pair = pltpu.SemaphoreType.DMA((2, parts, chips))
    return [ring, ring, pair, pair]


def seq_gather_kernel(shards, parts, x_ref, out_ref, *sems):
    ring_gather_loop(shards, parts, x_ref, out_ref, *sems, lambda step, place: None)


def fits_vmem(*shapes):
    return sum(padded_bytes(shape, 2) for shape in shapes) < 48 * MIB


def ring_seq_gather(block, collective_id, parts=2):
    shards = lax.axis_size("seq")
    rows, width = block.shape
    if not fits_vmem((shards * rows, width)):
        return lax.all_gather(block, "seq", axis=0, tiled=True)
    gathered = pl.pallas_call(
        functools.partial(seq_gather_kernel, shards, parts),
        out_shape=jax.ShapeDtypeStruct((shards, rows, width), block.dtype),
        in_specs=[VMEM],
        out_specs=VMEM,
        scratch_shapes=ring_semaphores(shards // 2, parts),
        compiler_params=pltpu.CompilerParams(
            collective_id=collective_id, has_side_effects=True, vmem_limit_bytes=56 * MIB
        ),
        cost_estimate=takes(40),
    )(block)
    return gathered.reshape(shards * rows, width)


def gather_ffn_kernel(
    shards, parts, x_ref, cot_ref, gate_ref, up_ref, down_ref,
    out_ref, act_ref, d_gate_ref, d_up_ref, *sems,
):
    chips = shards // 2
    rows = x_ref.shape[0]
    half = rows // 2

    def work(step, place):
        back, ahead = ring_chip(place - step, chips) * 2, ring_chip(place + step, chips) * 2
        spots = [(back, 0), (back + 1, 0), (ahead, half), (ahead + 1, half)]
        starts = [pl.multiple_of(index * rows + first, half) for index, first in spots]
        tokens = jnp.concatenate([out_ref[index, pl.ds(first, half), :] for index, first in spots], axis=0)
        cot = jnp.concatenate([cot_ref[pl.ds(start, half), :] for start in starts], axis=0)
        gate = jnp.dot(tokens, gate_ref[...], preferred_element_type=WIDE)
        up = jnp.dot(tokens, up_ref[...], preferred_element_type=WIDE)
        d_act = lax.dot_general(
            cot, down_ref[...], (((1,), (1,)), ((), ())), preferred_element_type=WIDE
        )
        share = 1.0 / (1.0 + jnp.exp(-gate))
        passed = gate * share
        results = (
            (act_ref, passed * up),
            (d_gate_ref, d_act * up * (share * (1.0 + gate * (1.0 - share)))),
            (d_up_ref, d_act * passed),
        )
        for ref, value in results:
            value = value.astype(SIXTEEN)
            for i, start in enumerate(starts):
                ref[pl.ds(start, half), :] = value[i * half : (i + 1) * half]

    ring_gather_loop(shards, parts, x_ref, out_ref, *sems, work)


def gather_ffn(block, cotangent, w_gate, w_up, w_down, collective_id, parts=2):
    shards = lax.axis_size("seq")
    rows, width = block.shape
    units = w_gate.shape[1]
    if not fits_vmem((shards * rows, width), (shards * rows, width), (3 * shards * rows, units)):
        second = ring_seq_gather(block, collective_id)
        gate, up = dot_last(second, w_gate), dot_last(second, w_up)
        act, pull = jax.vjp(glu_piece, gate, up)
        d_gate, d_up = pull(dot_back(cotangent, w_down))
        return second, act.astype(SIXTEEN), d_gate.astype(SIXTEEN), d_up.astype(SIXTEEN)
    hidden = jax.ShapeDtypeStruct((shards * rows, units), SIXTEEN)
    outs = pl.pallas_call(
        functools.partial(gather_ffn_kernel, shards, parts),
        out_shape=[jax.ShapeDtypeStruct((shards, rows, width), SIXTEEN), hidden, hidden, hidden],
        in_specs=[VMEM] * 5,
        out_specs=[VMEM] * 4,
        scratch_shapes=ring_semaphores(shards // 2, parts),
        compiler_params=pltpu.CompilerParams(
            collective_id=collective_id, has_side_effects=True, vmem_limit_bytes=56 * MIB
        ),
        cost_estimate=takes(45),
    )(block, cotangent, w_gate, w_up, w_down)
    return (outs[0].reshape(shards * rows, width),) + tuple(outs[1:])


def gather_beside_kernel(
    shards, parts, x_ref, second_any, cot_any, act_ref, d_gate_ref, d_up_ref, down_ref, mixed_ref, w_out_ref,
    out_ref, g_gate_ref, g_up_ref, g_down_ref, product_ref, d_mixed_ref, g_out_ref,
    second_ref, cot_ref, total_ref, load_sem, *sems,
):
    chips = shards // 2
    width = second_ref.shape[1]
    rows = x_ref.shape[0]
    half = rows // 2
    loads = [
        pltpu.make_async_copy(second_any, second_ref, load_sem.at[0]),
        pltpu.make_async_copy(cot_any, cot_ref, load_sem.at[1]),
    ]
    block = 256
    turns = width // block
    share = act_ref.shape[0] // chips

    def tn_dot(left, right):
        return lax.dot_general(
            left, right, (((0,), (0,)), ((), ())), preferred_element_type=WIDE
        ).astype(SIXTEEN)

    def columns(cut):
        tokens = second_ref[:, cut]
        g_gate_ref[cut, :] = tn_dot(tokens, d_gate_ref[...])
        g_up_ref[cut, :] = tn_dot(tokens, d_up_ref[...])
        g_down_ref[:, cut] = tn_dot(act_ref[...], cot_ref[:, cut])

    def begin():
        for load in loads:
            load.start()

    def work(step, place):
        @pl.when(step == 0)
        def _():
            for load in loads:
                load.wait()

        back, ahead = ring_chip(place - step, chips) * 2, ring_chip(place + step, chips) * 2
        spots = [(back, 0), (back + 1, 0), (ahead, half), (ahead + 1, half)]
        starts = [pl.multiple_of(index * rows + first, half) for index, first in spots]
        grads = jnp.concatenate([out_ref[index, pl.ds(first, half), :] for index, first in spots], axis=0)
        mixed = jnp.concatenate([mixed_ref[pl.ds(start, half), :] for start in starts], axis=0)
        d_mixed = lax.dot_general(
            grads, w_out_ref[...], (((1,), (1,)), ((), ())), preferred_element_type=WIDE
        )
        for i, start in enumerate(starts):
            d_mixed_ref[pl.ds(start, half), :] = d_mixed[i * half : (i + 1) * half]
        part = lax.dot_general(mixed, grads, (((0,), (0,)), ((), ())), preferred_element_type=WIDE)

        @pl.when(step == 0)
        def _():
            total_ref[...] = part

        @pl.when(step > 0)
        def _():
            total_ref[...] += part

        @pl.when(step < turns)
        def _():
            columns(pl.ds(pl.multiple_of(step * block, block), block))

        @pl.when(step == turns)
        def _():
            columns(slice(turns * block, width))

        here = pl.ds(pl.multiple_of(step * share, share), share)
        product_ref[here, :] = jnp.dot(
            act_ref[here, :], down_ref[...], preferred_element_type=WIDE
        ).astype(SIXTEEN)

    ring_gather_loop(shards, parts, x_ref, out_ref, *sems, work, begin)
    g_out_ref[...] = total_ref[...].astype(SIXTEEN)


def gather_beside_ffn(
    block, second, cotangent, act, d_gate, d_up, w_down, mixed, w_out, collective_id, parts=2
):
    shards = lax.axis_size("seq")
    rows, width = block.shape
    length, units = act.shape
    chips = shards // 2
    if width // 256 >= chips or not fits_vmem(
        (4 * length, width), (3 * length, units), (3 * width, units), (4 * mixed.shape[1], width),
        (3 * length, mixed.shape[1])
    ):
        gathered = ring_seq_gather(block, collective_id)
        return (
            gathered,
            dot_weight(second, d_gate).astype(SIXTEEN),
            dot_weight(second, d_up).astype(SIXTEEN),
            dot_weight(act, cotangent).astype(SIXTEEN),
            dot_last(act, w_down).astype(SIXTEEN),
            dot_back(gathered, w_out),
            dot_weight(mixed, gathered).astype(SIXTEEN),
        )
    outs = pl.pallas_call(
        functools.partial(gather_beside_kernel, shards, parts),
        out_shape=[
            jax.ShapeDtypeStruct((shards, rows, width), SIXTEEN),
            jax.ShapeDtypeStruct((width, units), SIXTEEN),
            jax.ShapeDtypeStruct((width, units), SIXTEEN),
            jax.ShapeDtypeStruct((units, width), SIXTEEN),
            jax.ShapeDtypeStruct((length, width), SIXTEEN),
            jax.ShapeDtypeStruct(mixed.shape, WIDE),
            jax.ShapeDtypeStruct(w_out.shape, SIXTEEN),
        ],
        in_specs=[VMEM, ANY, ANY] + [VMEM] * 6,
        out_specs=[VMEM] * 7,
        scratch_shapes=[
            pltpu.VMEM(second.shape, SIXTEEN),
            pltpu.VMEM(cotangent.shape, SIXTEEN),
            pltpu.VMEM(w_out.shape, WIDE),
            pltpu.SemaphoreType.DMA((2,)),
        ]
        + ring_semaphores(chips, parts),
        compiler_params=pltpu.CompilerParams(
            collective_id=collective_id, has_side_effects=True, vmem_limit_bytes=60 * MIB
        ),
        cost_estimate=takes(45),
    )(block, second, cotangent, act, d_gate, d_up, w_down, mixed, w_out)
    return (outs[0].reshape(shards * rows, width),) + tuple(outs[1:])


def product_scatter_kernel(shards, parts, turned, *refs):
    terms = len(turned)
    lefts, rights = refs[:terms], refs[terms : 2 * terms]
    out_ref, mine, given, pair, arrived = refs[2 * terms : 2 * terms + 5]
    ring_send, ring_recv, pair_send, pair_recv = refs[2 * terms + 5 :]
    row, me = lax.axis_index("row"), lax.axis_index("seq")
    chips = shards // 2
    core = me % 2
    place = ring_place(me // 2, chips)
    block_rows = out_ref.shape[0]

    def device(spot, core):
        return ring_chip(spot, chips) * 2 + core

    right = (row, device(place + 1, core))
    left = (row, device(place - 1, core))
    twin = (row, me + 1 - 2 * core)
    greet([right, left, twin])
    rows = block_rows // (2 * parts)

    def cut(way, part):
        return pl.ds((way * parts + part) * rows, rows)

    def product(index):
        here = pl.ds(pl.multiple_of(index * block_rows, block_rows), block_rows)
        total = None
        for left_ref, right_ref, turn in zip(lefts, rights, turned):
            part = lax.dot_general(
                left_ref[here, :], right_ref[...], (((1,), (1 if turn else 0,)), ((), ())),
                preferred_element_type=WIDE,
            )
            total = part if total is None else total + part
        return total.astype(SIXTEEN)

    def pass_over(slot):
        return pltpu.make_async_remote_copy(
            src_ref=given.at[slot], dst_ref=pair.at[slot], send_sem=pair_send.at[slot],
            recv_sem=pair_recv.at[slot], device_id=twin, device_id_type=MESH,
        )

    def make(far):
        slot = far % chips
        given[slot] = product(device(place + far, 1 - core))
        pass_over(slot).start()
        mine[slot] = product(device(place + far, core))

    def both(step, carry):
        make(-step)
        make(step)
        return carry

    half = chips // 2
    both(1, 0)
    started, flights = [], {}
    fresh = set(range(chips))
    for step in range(chips):
        if step + 2 < half:
            both(step + 2, 0)
        elif step + 2 == half:
            make(half)
            make(0)
        for part in range(parts):
            for way in range(2):
                slot = (-1 - step if way == 0 else 1 + step) % chips
                if slot in fresh:
                    fresh.remove(slot)
                    pass_over(slot).wait_recv()
                here = cut(way, part)
                total = mine[slot, here, :].astype(WIDE) + pair[slot, here, :].astype(WIDE)
                if step:
                    flights[way, part].wait_recv()
                    total = total + arrived[way, step - 1, pl.ds(part * rows, rows), :].astype(WIDE)
                if step == chips - 1:
                    out_ref[here, :] = total
                    continue
                mine[slot, here, :] = total.astype(SIXTEEN)
                copy = pltpu.make_async_remote_copy(
                    src_ref=mine.at[slot, here], dst_ref=arrived.at[way, step, pl.ds(part * rows, rows)],
                    send_sem=ring_send.at[way, part, step], recv_sem=ring_recv.at[way, part, step],
                    device_id=(right, left)[way], device_id_type=MESH,
                )
                copy.start()
                started.append(copy)
                flights[way, part] = copy
    for slot in range(chips):
        pass_over(slot).wait_send()
    for copy in started:
        copy.wait_send()


def padded_bytes(shape, bytes_each):
    return -(-shape[0] // 16) * 16 * -(-shape[1] // 128) * 128 * bytes_each


def product_scatter(terms, collective_id, parts=2):
    shards = lax.axis_size("seq")
    chips = shards // 2
    length = terms[0][0].shape[0]
    width = terms[0][1].shape[0 if terms[0][2] else 1]
    rows = length // shards
    buffers = 4 * chips * padded_bytes((rows, width), 2)
    operands = sum(padded_bytes(t[0].shape, 2) + padded_bytes(t[1].shape, 2) for t in terms)
    if chips < 4 or buffers + operands > 40 * MIB:
        total = 0
        for left, right, turn in terms:
            total = total + lax.dot_general(
                left, right, (((1,), (1 if turn else 0,)), ((), ())), preferred_element_type=WIDE
            )
        return lax.psum_scatter(
            total.astype(SIXTEEN), "seq", scatter_dimension=0, tiled=True
        ).astype(WIDE)
    ring = pltpu.SemaphoreType.DMA((2, parts, chips - 1))
    pair = pltpu.SemaphoreType.DMA((chips,))
    blocks = pltpu.VMEM((chips, rows, width), SIXTEEN)
    return pl.pallas_call(
        functools.partial(product_scatter_kernel, shards, parts, tuple(t[2] for t in terms)),
        out_shape=jax.ShapeDtypeStruct((rows, width), WIDE),
        in_specs=[VMEM] * (2 * len(terms)),
        out_specs=VMEM,
        scratch_shapes=[
            blocks, blocks, blocks,
            pltpu.VMEM((2, chips - 1, rows // 2, width), SIXTEEN),
            ring, ring, pair, pair,
        ],
        compiler_params=pltpu.CompilerParams(
            collective_id=collective_id, has_side_effects=True, vmem_limit_bytes=56 * MIB
        ),
        cost_estimate=takes(40),
    )(*[t[0] for t in terms], *[t[1] for t in terms])


def bits_of(shards):
    bits = shards.bit_length() - 1
    assert 1 << bits == shards
    return bits


def partner_of(me, bit):
    return me + (1 - 2 * ((me // (1 << bit)) % 2)) * (1 << bit)


def seq_sum_kernel(bits, waits, x_ref, *refs):
    out_ref, total, staged, arrived, send_sem, recv_sem, back_send, back_recv = refs[waits:]
    row, me = lax.axis_index("row"), lax.axis_index("seq")
    partners = [(row, partner_of(me, bit)) for bit in range(bits)]
    greet(partners)
    length = x_ref.shape[1]
    total[...] = x_ref[...].astype(WIDE)
    begin = 0
    started = []
    for bit in range(bits):
        half = length >> (bit + 1)
        upper = (me // (1 << bit)) % 2
        kept = pl.multiple_of(begin + upper * half, 128)
        given = pl.multiple_of(begin + (1 - upper) * half, 128)
        staged[:, half : 2 * half] = total[:, pl.ds(given, half)].astype(SIXTEEN)
        copy = pltpu.make_async_remote_copy(
            src_ref=staged.at[:, half : 2 * half], dst_ref=arrived.at[:, half : 2 * half],
            send_sem=send_sem.at[bit], recv_sem=recv_sem.at[bit],
            device_id=partners[bit], device_id_type=MESH,
        )
        copy.start()
        started.append(copy)
        copy.wait_recv()
        total[:, pl.ds(kept, half)] += arrived[:, half : 2 * half].astype(WIDE)
        begin = kept
    half = length >> bits
    out_ref[:, pl.ds(pl.multiple_of(begin, 128), half)] = total[
        :, pl.ds(pl.multiple_of(begin, 128), half)
    ].astype(SIXTEEN)
    for bit in range(bits - 1, -1, -1):
        half = length >> (bit + 1)
        here = out_ref.at[:, pl.ds(pl.multiple_of(begin, 128), half)]
        copy = pltpu.make_async_remote_copy(
            src_ref=here, dst_ref=here, send_sem=back_send.at[bit], recv_sem=back_recv.at[bit],
            device_id=partners[bit], device_id_type=MESH,
        )
        copy.start()
        started.append(copy)
        copy.wait_recv()
        begin = begin - ((me // (1 << bit)) % 2) * half
    for copy in started:
        copy.wait_send()


def seq_sum(values, collective_id, after=()):
    bits = bits_of(lax.axis_size("seq"))
    rows, length = values.shape
    sems = pltpu.SemaphoreType.DMA((bits,))
    return pl.pallas_call(
        functools.partial(seq_sum_kernel, bits, len(after)),
        out_shape=jax.ShapeDtypeStruct((rows, length), SIXTEEN),
        in_specs=[VMEM] + [ANY] * len(after),
        out_specs=VMEM,
        scratch_shapes=[
            pltpu.VMEM((rows, length), WIDE),
            pltpu.VMEM((rows, length), SIXTEEN),
            pltpu.VMEM((rows, length), SIXTEEN),
            sems, sems, sems, sems,
        ],
        compiler_params=pltpu.CompilerParams(
            collective_id=collective_id, has_side_effects=True, vmem_limit_bytes=48 * MIB
        ),
        cost_estimate=takes(30),
    )(values, *after)


def seq_sum_small_kernel(groups, x_ref, out_ref, arrived, staged, send_sem, recv_sem):
    row, me = lax.axis_index("row"), lax.axis_index("seq")
    phases = []
    for size, stride in groups:
        spot = (me // stride) % size
        phases.append(
            [(row, me + ((spot + far) % size - spot) * stride) for far in range(1, size)]
        )
    greet([peer for peers in phases for peer in peers])
    total = x_ref[...]
    copies, slot = [], 0
    for phase, peers in enumerate(phases):
        staged[phase] = total
        flights = []
        for peer in peers:
            copy = pltpu.make_async_remote_copy(
                src_ref=staged.at[phase], dst_ref=arrived.at[slot], send_sem=send_sem.at[slot],
                recv_sem=recv_sem.at[slot], device_id=peer, device_id_type=MESH,
            )
            copy.start()
            flights.append((copy, slot))
            slot += 1
        for copy, here in flights:
            copy.wait_recv()
            total = total + arrived[here]
        copies += flights
    out_ref[...] = total
    for copy, _ in copies:
        copy.wait_send()


def seq_sum_small(values, collective_id):
    bits = bits_of(lax.axis_size("seq"))
    low = 1 << (bits // 2)
    groups = ((low, 1), ((1 << bits) // low, low))
    count = sum(size - 1 for size, _ in groups)
    shape = values.shape
    tiles = values.reshape(-1, 128)
    sems = pltpu.SemaphoreType.DMA((count,))
    return pl.pallas_call(
        functools.partial(seq_sum_small_kernel, groups),
        out_shape=jax.ShapeDtypeStruct(tiles.shape, WIDE),
        in_specs=[VMEM],
        out_specs=VMEM,
        scratch_shapes=[
            pltpu.VMEM((count,) + tiles.shape, WIDE),
            pltpu.VMEM((len(groups),) + tiles.shape, WIDE),
            sems, sems,
        ],
        compiler_params=pltpu.CompilerParams(collective_id=collective_id, has_side_effects=True),
        cost_estimate=takes(12),
    )(tiles).reshape(shape)


def all_peers(rows, shards):
    me = lax.axis_index("row") * shards + lax.axis_index("seq")
    count = rows * shards
    ahead = [(me + far) % count for far in range(1, count)]
    return me, count, [(other, (other // shards, other % shards)) for other in ahead]


def push_gather_kernel(rows, shards, x_ref, out_ref, send_sem, recv_sem):
    me, count, peers = all_peers(rows, shards)
    greet([device for _, device in peers])
    copies = []
    for far, (_, device) in enumerate(peers):
        copy = pltpu.make_async_remote_copy(
            src_ref=x_ref, dst_ref=out_ref.at[me], send_sem=send_sem.at[far],
            recv_sem=recv_sem.at[far], device_id=device, device_id_type=MESH,
        )
        copy.start()
        copies.append(copy)
    out_ref[me] = x_ref[...]
    for copy in copies:
        copy.wait()


def push_gather(block, collective_id):
    rows, shards = lax.axis_size("row"), lax.axis_size("seq")
    sems = pltpu.SemaphoreType.DMA((rows * shards - 1,))
    return pl.pallas_call(
        functools.partial(push_gather_kernel, rows, shards),
        out_shape=jax.ShapeDtypeStruct((rows * shards,) + block.shape, block.dtype),
        in_specs=[VMEM],
        out_specs=VMEM,
        scratch_shapes=[sems, sems],
        compiler_params=pltpu.CompilerParams(collective_id=collective_id, has_side_effects=True),
        cost_estimate=takes(20),
    )(block)


def push_scatter_kernel(rows, shards, x_ref, out_ref, arrived, send_sem, recv_sem):
    me, count, peers = all_peers(rows, shards)
    greet([device for _, device in peers])
    copies = []
    for far, (other, device) in enumerate(peers):
        copy = pltpu.make_async_remote_copy(
            src_ref=x_ref.at[other], dst_ref=arrived.at[far], send_sem=send_sem.at[far],
            recv_sem=recv_sem.at[far], device_id=device, device_id_type=MESH,
        )
        copy.start()
        copies.append(copy)
    total = x_ref[me].astype(WIDE)
    for far, copy in enumerate(copies):
        copy.wait_recv()
        total = total + arrived[far].astype(WIDE)
    out_ref[...] = total
    for copy in copies:
        copy.wait_send()


def push_scatter(blocks, collective_id):
    rows, shards = lax.axis_size("row"), lax.axis_size("seq")
    count = rows * shards
    sems = pltpu.SemaphoreType.DMA((count - 1,))
    return pl.pallas_call(
        functools.partial(push_scatter_kernel, rows, shards),
        out_shape=jax.ShapeDtypeStruct(blocks.shape[1:], WIDE),
        in_specs=[VMEM],
        out_specs=VMEM,
        scratch_shapes=[pltpu.VMEM((count - 1,) + blocks.shape[1:], blocks.dtype), sems, sems],
        compiler_params=pltpu.CompilerParams(
            collective_id=collective_id, has_side_effects=True, vmem_limit_bytes=32 * MIB
        ),
        cost_estimate=takes(20),
    )(blocks)


def conv_piece(extended, conv_w, conv_b, lag_masks):
    length = extended.shape[0] - (CONV - 1)
    summed = conv_b
    for j in range(CONV):
        summed = (
            summed + conv_w[j] * extended[CONV - 1 - j : CONV - 1 - j + length] * lag_masks[j]
        )
    return silu_fn(summed)


def nt_dot(left, right):
    return lax.dot_general(left, right, (((1,), (1,)), ((), ())), preferred_element_type=WIDE)


def seen_keys(block, first_row):
    window = (REACH + 1) * BLOCK
    k_pos = (block - REACH) * BLOCK + lax.broadcasted_iota(jnp.int32, (window, BLOCK), 0)
    q_pos = block * BLOCK + lax.broadcasted_iota(jnp.int32, (window, BLOCK), 1)
    return (k_pos >= first_row) & (k_pos <= q_pos) & (k_pos > q_pos - REACH * BLOCK)


PER = 4


def attend_forward_kernel(heads, waits, *refs):
    first_ref, q_ref, kv_ref, turned_ref, meta_ref, meta_turned_ref = refs[:6]
    out_ref, total_ref = refs[6 + waits : 8 + waits]
    for sub in range(PER):
        block = pl.program_id(0) * PER + sub
        here = slice(sub * BLOCK, (sub + 1) * BLOCK)
        span = pl.ds(pl.multiple_of(block * BLOCK, BLOCK), (REACH + 1) * BLOCK)
        seen = seen_keys(block, first_ref[sub])
        outs, totals = [], []
        for h in range(heads):
            cut = slice(h * HEAD, (h + 1) * HEAD)
            v_cut = slice((heads + h) * HEAD, (heads + h + 1) * HEAD)
            query = q_ref[here, cut] * SIXTEEN(HEAD ** (-0.5))
            near = jnp.where(seen, nt_dot(kv_ref[span, cut], query), -1e30)
            meta = nt_dot(meta_ref[:, cut], query)
            top = jnp.maximum(
                jnp.max(near, axis=0, keepdims=True), jnp.max(meta, axis=0, keepdims=True)
            )
            near = jnp.exp(near - top)
            meta = jnp.exp(meta - top)
            total = jnp.sum(near, axis=0, keepdims=True) + jnp.sum(meta, axis=0, keepdims=True)
            out = jnp.dot(turned_ref[v_cut, span], near.astype(SIXTEEN), preferred_element_type=WIDE)
            out += jnp.dot(meta_turned_ref[v_cut, :], meta.astype(SIXTEEN), preferred_element_type=WIDE)
            outs.append(out / total)
            totals.append(top + jnp.log(total))
        out_ref[here, :] = jnp.concatenate(outs, axis=0).T
        total_ref[sub] = jnp.concatenate(totals, axis=0)


def attend_backward_kernel(heads, waits, *refs):
    first_ref, q_ref, kv_ref, turned_ref, meta_ref, meta_turned_ref = refs[:6]
    out_ref, total_ref, do_ref = refs[6:9]
    dq_ref, dkv_ref, dmeta_ref = refs[9 + waits : 12 + waits]
    block = pl.program_id(0)

    @pl.when(block == 0)
    def _():
        dkv_ref[...] = jnp.zeros_like(dkv_ref)
        dmeta_ref[...] = jnp.zeros_like(dmeta_ref)

    span = pl.ds(pl.multiple_of(block * BLOCK, BLOCK), (REACH + 1) * BLOCK)
    seen = seen_keys(block, first_ref[0])
    d_out = do_ref[...]
    row_sums = (d_out * out_ref[...]).T
    d_half = d_out.astype(SIXTEEN)
    d_queries, near_k, near_v, meta_k, meta_v = [], [], [], [], []
    for h in range(heads):
        cut = slice(h * HEAD, (h + 1) * HEAD)
        v_cut = slice((heads + h) * HEAD, (heads + h + 1) * HEAD)
        query = q_ref[:, cut] * SIXTEEN(HEAD ** (-0.5))
        do = d_half[:, cut]
        total = total_ref[0, h : h + 1, :]
        mean = jnp.sum(row_sums[cut], axis=0, keepdims=True)
        near = jnp.where(seen, jnp.exp(nt_dot(kv_ref[span, cut], query) - total), 0.0)
        meta = jnp.exp(nt_dot(meta_ref[:, cut], query) - total)
        d_near = (near * (nt_dot(kv_ref[span, v_cut], do) - mean)).astype(SIXTEEN)
        d_meta = (meta * (nt_dot(meta_ref[:, v_cut], do) - mean)).astype(SIXTEEN)
        near_v.append(jnp.dot(near.astype(SIXTEEN), do, preferred_element_type=WIDE))
        meta_v.append(jnp.dot(meta.astype(SIXTEEN), do, preferred_element_type=WIDE))
        near_k.append(jnp.dot(d_near, query, preferred_element_type=WIDE))
        meta_k.append(jnp.dot(d_meta, query, preferred_element_type=WIDE))
        d_query = jnp.dot(turned_ref[cut, span], d_near, preferred_element_type=WIDE)
        d_query += jnp.dot(meta_turned_ref[cut, :], d_meta, preferred_element_type=WIDE)
        d_queries.append(d_query * HEAD ** (-0.5))
    dq_ref[...] = jnp.concatenate(d_queries, axis=0).T.astype(SIXTEEN)
    dkv_ref[span, :] += jnp.concatenate(near_k + near_v, axis=1)
    dmeta_ref[...] += jnp.concatenate(meta_k + meta_v, axis=1)


def attend_operands(queries, kv_rows, doc_first):
    length = doc_first.shape[0]
    count = length // BLOCK
    near = jnp.pad(kv_rows[:length], ((REACH * BLOCK, 0), (0, 0)))
    meta = kv_rows[length:]
    arrays = (doc_first.reshape(count, 1, BLOCK), queries, near, near.T, meta, meta.T)
    width = queries.shape[1]

    def whole(array):
        return pl.BlockSpec(array.shape, lambda i: (0,) * array.ndim)

    specs = [
        pl.BlockSpec((1, 1, BLOCK), lambda i: (i, 0, 0)),
        pl.BlockSpec((BLOCK, width), lambda i: (i, 0)),
    ] + [whole(a) for a in arrays[2:]]
    return arrays, specs, count, width


def attend_forward(queries, kv_rows, doc_first, through=()):
    arrays, specs, count, width = attend_operands(queries, kv_rows, doc_first)
    heads = width // HEAD
    specs = [
        pl.BlockSpec((PER, 1, BLOCK), lambda i: (i, 0, 0)),
        pl.BlockSpec((PER * BLOCK, width), lambda i: (i, 0)),
    ] + specs[2:]
    return pl.pallas_call(
        lambda *refs: attend_forward_kernel(heads, len(through), *refs),
        grid=(count // PER,),
        in_specs=specs + [ANY] * len(through),
        out_specs=[
            pl.BlockSpec((PER * BLOCK, width), lambda i: (i, 0)),
            pl.BlockSpec((PER, heads, BLOCK), lambda i: (i, 0, 0)),
        ]
        + [ANY] * len(through),
        out_shape=[
            jax.ShapeDtypeStruct(queries.shape, WIDE),
            jax.ShapeDtypeStruct((count, heads, BLOCK), WIDE),
        ]
        + [jax.ShapeDtypeStruct(x.shape, x.dtype) for x in through],
        input_output_aliases={6 + i: 2 + i for i in range(len(through))},
        compiler_params=pltpu.CompilerParams(vmem_limit_bytes=48 * MIB),
        cost_estimate=takes(24),
    )(*arrays, *through)


def attend_backward(queries, kv_rows, doc_first, out, log_total, d_out, through=()):
    arrays, specs, count, width = attend_operands(queries, kv_rows, doc_first)
    heads = width // HEAD
    near, meta = arrays[2], arrays[4]
    row_spec = pl.BlockSpec((BLOCK, width), lambda i: (i, 0))
    d_queries, d_near, d_meta, *through = pl.pallas_call(
        lambda *refs: attend_backward_kernel(heads, len(through), *refs),
        grid=(count,),
        in_specs=specs
        + [row_spec, pl.BlockSpec((1, heads, BLOCK), lambda i: (i, 0, 0)), row_spec]
        + [ANY] * len(through),
        out_specs=[
            row_spec,
            pl.BlockSpec(near.shape, lambda i: (0, 0)),
            pl.BlockSpec(meta.shape, lambda i: (0, 0)),
        ]
        + [ANY] * len(through),
        out_shape=[
            jax.ShapeDtypeStruct(queries.shape, SIXTEEN),
            jax.ShapeDtypeStruct(near.shape, WIDE),
            jax.ShapeDtypeStruct(meta.shape, WIDE),
        ]
        + [jax.ShapeDtypeStruct(x.shape, x.dtype) for x in through],
        input_output_aliases={9 + i: 3 + i for i in range(len(through))},
        compiler_params=pltpu.CompilerParams(vmem_limit_bytes=48 * MIB),
        cost_estimate=takes(24),
    )(*arrays, out, log_total, d_out, *through)
    return d_queries, d_near[REACH * BLOCK :].astype(SIXTEEN), d_meta.astype(SIXTEEN), *through


def step_sum():
    rows = lax.broadcasted_iota(jnp.int32, (SUB, SUB * STATE), 0)
    cols = lax.broadcasted_iota(jnp.int32, (SUB, SUB * STATE), 1)
    return (cols // STATE == rows).astype(SIXTEEN)


def lanes_from(tile, group):
    return pltpu.roll(tile, (SPAN - group * SUB) % SPAN, axis=1)


def scan_forward_kernel(waits, *refs):
    keep_ref, conv_ref, delta_ref, bc_ref, a_ref = refs[:5]
    y_ref, start_ref, kept_ref = refs[5 + waits : 8 + waits]
    state_ref = refs[-1]
    block = pl.program_id(0)

    @pl.when(block == 0)
    def _():
        state_ref[...] = jnp.zeros_like(state_ref)

    start_ref[0] = state_ref[...]
    decay_rate = a_ref[...]
    fold = step_sum()
    b_span = bc_ref[:STATE, :].astype(WIDE)
    c_span = bc_ref[STATE:, :].astype(WIDE)

    def body(group, state):
        rows = pl.ds(pl.multiple_of(group * SUB, SUB), SUB)
        delta = delta_ref[rows, :]
        drive = delta * conv_ref[rows, :]
        b_tile = lanes_from(b_span, group)
        c_tile = lanes_from(c_span, group)
        reads = []
        for i in range(SUB):
            keep = keep_ref[block * SPAN + group * SUB + i]
            decay = jnp.exp(delta[i : i + 1, :] * decay_rate) * keep
            state = decay * state + drive[i : i + 1, :] * b_tile[:, i : i + 1]
            kept_ref[group * SUB + i] = state.astype(SIXTEEN)
            reads.append((state * c_tile[:, i : i + 1]).astype(SIXTEEN))
        y_ref[rows, :] = jnp.dot(
            fold, jnp.concatenate(reads, axis=0), preferred_element_type=WIDE
        )
        return state

    state_ref[...] = lax.fori_loop(0, SPAN // SUB, body, state_ref[...], unroll=8)


def scan_forward(keep, conv_out, delta, bc_rows, decay_rate, after=(), through=()):
    length, lanes = conv_out.shape
    waits = len(after) + len(through)
    blocks = length // SPAN
    span_spec = pl.BlockSpec((SPAN, lanes), lambda i: (i, 0))
    return pl.pallas_call(
        functools.partial(scan_forward_kernel, waits),
        grid=(blocks,),
        in_specs=[
            pl.BlockSpec(memory_space=pltpu.SMEM),
            span_spec,
            span_spec,
            pl.BlockSpec((2 * STATE, SPAN), lambda i: (0, i)),
            pl.BlockSpec((STATE, lanes), lambda i: (0, 0)),
        ]
        + [ANY] * waits,
        out_specs=[
            span_spec,
            pl.BlockSpec((1, STATE, lanes), lambda i: (i, 0, 0)),
            pl.BlockSpec((SPAN, STATE, lanes), lambda i: (i, 0, 0)),
        ]
        + [ANY] * len(through),
        out_shape=[
            jax.ShapeDtypeStruct((length, lanes), WIDE),
            jax.ShapeDtypeStruct((blocks, STATE, lanes), WIDE),
            jax.ShapeDtypeStruct((length, STATE, lanes), SIXTEEN),
        ]
        + [jax.ShapeDtypeStruct(x.shape, x.dtype) for x in through],
        input_output_aliases={5 + len(after) + i: 3 + i for i in range(len(through))},
        scratch_shapes=[pltpu.VMEM((STATE, lanes), WIDE)],
        cost_estimate=takes(24),
    )(keep, conv_out, delta, bc_rows, decay_rate, *after, *through)


def scan_backward_kernel(waits, *refs):
    keep_ref, conv_ref, delta_ref, bc_ref, a_ref, start_ref, kept_ref, dy_ref = refs[:8]
    dconv_ref, ddelta_ref, dbc_ref, da_ref, adjoint_ref = refs[8 + waits :]
    turn = pl.program_id(0)
    block = pl.num_programs(0) - 1 - turn

    @pl.when(turn == 0)
    def _():
        adjoint_ref[...] = jnp.zeros_like(adjoint_ref)
        da_ref[...] = jnp.zeros_like(da_ref)

    decay_rate = a_ref[...]
    fold = step_sum()
    lanes = decay_rate.shape[1]
    ones = jnp.ones((lanes, SPAN), SIXTEEN)
    spot = lax.broadcasted_iota(jnp.int32, (STATE, SPAN), 1)
    b_span = bc_ref[:STATE, :].astype(WIDE)
    c_span = bc_ref[STATE:, :].astype(WIDE)
    def back(step, carry):
        adjoint, da, db, dc = carry
        group = SPAN // SUB - 1 - step
        rows = pl.ds(pl.multiple_of(group * SUB, SUB), SUB)
        delta = delta_ref[rows, :]
        conv = conv_ref[rows, :]
        drive = delta * conv
        dy = dy_ref[rows, :]
        b_tile = lanes_from(b_span, group)
        c_tile = lanes_from(c_span, group)
        before = kept_ref[jnp.maximum(group * SUB - 1, 0)].astype(WIDE)
        before = jnp.where(group == 0, start_ref[0], before)
        states = [before] + [kept_ref[group * SUB + i].astype(WIDE) for i in range(SUB)]
        by_c, by_b, by_drive, by_delta = ([None] * SUB for _ in range(4))
        for i in range(SUB - 1, -1, -1):
            keep = keep_ref[block * SPAN + group * SUB + i]
            decay = jnp.exp(delta[i : i + 1, :] * decay_rate) * keep
            dy_row = dy[i : i + 1, :]
            total = adjoint + dy_row * c_tile[:, i : i + 1]
            by_c[i] = (dy_row * states[i + 1]).astype(SIXTEEN)
            by_b[i] = (total * drive[i : i + 1, :]).astype(SIXTEEN)
            by_drive[i] = (total * b_tile[:, i : i + 1]).astype(SIXTEEN)
            adjoint = total * decay
            rate = adjoint * states[i]
            by_delta[i] = (rate * decay_rate).astype(SIXTEEN)
            da = da + rate * delta[i : i + 1, :]

        def over_state(parts):
            return jnp.dot(fold, jnp.concatenate(parts, axis=0), preferred_element_type=WIDE)

        def over_lanes(parts, tile):
            sums = jnp.dot(jnp.concatenate(parts, axis=0), ones, preferred_element_type=WIDE)
            for i in range(SUB):
                here = spot == group * SUB + i
                tile = jnp.where(here, sums[i * STATE : (i + 1) * STATE, :], tile)
            return tile

        d_drive = over_state(by_drive)
        dconv_ref[rows, :] = d_drive * delta
        ddelta_ref[rows, :] = over_state(by_delta) + d_drive * conv
        return adjoint, da, over_lanes(by_b, db), over_lanes(by_c, dc)

    none = jnp.zeros((STATE, SPAN), WIDE)
    adjoint, da, db, dc = lax.fori_loop(
        0, SPAN // SUB, back, (adjoint_ref[...], da_ref[...], none, none), unroll=16
    )
    adjoint_ref[...] = adjoint
    da_ref[...] = da
    dbc_ref[...] = jnp.concatenate([db, dc], axis=0)


def scan_backward(keep, conv_out, delta, bc_rows, decay_rate, starts, kept, dy, after=()):
    length, lanes = conv_out.shape
    blocks = length // SPAN
    span_spec = pl.BlockSpec((SPAN, lanes), lambda i: (blocks - 1 - i, 0))
    rows_spec = pl.BlockSpec((2 * STATE, SPAN), lambda i: (0, blocks - 1 - i))
    whole = pl.BlockSpec((STATE, lanes), lambda i: (0, 0))
    return pl.pallas_call(
        functools.partial(scan_backward_kernel, len(after)),
        grid=(blocks,),
        in_specs=[
            pl.BlockSpec(memory_space=pltpu.SMEM),
            span_spec,
            span_spec,
            rows_spec,
            whole,
            pl.BlockSpec((1, STATE, lanes), lambda i: (blocks - 1 - i, 0, 0)),
            pl.BlockSpec((SPAN, STATE, lanes), lambda i: (blocks - 1 - i, 0, 0)),
            span_spec,
        ]
        + [ANY] * len(after),
        out_specs=[span_spec, span_spec, rows_spec, whole],
        out_shape=[
            jax.ShapeDtypeStruct((length, lanes), WIDE),
            jax.ShapeDtypeStruct((length, lanes), WIDE),
            jax.ShapeDtypeStruct((2 * STATE, length), WIDE),
            jax.ShapeDtypeStruct((STATE, lanes), WIDE),
        ],
        scratch_shapes=[
            pltpu.VMEM((STATE, lanes), WIDE),
        ],
        compiler_params=pltpu.CompilerParams(vmem_limit_bytes=32 * MIB),
        cost_estimate=takes(40),
    )(keep, conv_out, delta, bc_rows, decay_rate, starts, kept, dy, *after)


def padded_lanes(array, lanes):
    return jnp.pad(array, ((0, 0), (0, lanes - array.shape[1])))


def rms_pull(values, scale, gain, d_normed, mean):
    d_values = scale * gain * d_normed - values * (scale * scale * scale) * mean
    return d_values, jnp.sum(d_normed * values * scale, axis=0)


def per_device(tokens, doc_ids, meta_tokens, mixer_params, small_params, ffn_params, cotangent):
    tokens, cotangent = tokens[0], cotangent[0]
    small_whole, ids, meta_whole = start_blocks(small_params, doc_ids[0], meta_tokens)
    g_one = small_shards(small_whole)[0]
    rows, shards = lax.axis_size("row"), lax.axis_size("seq")
    staged = weights_fit(mixer_params.shape[0], ffn_params.shape[0], rows, shards)
    if staged:
        columns, pull_columns = jax.vjp(partial(to_columns, width=view_width()), mixer_params)
    length = ids.shape[0]
    positions = jnp.arange(length, dtype=jnp.int32)
    starts = jnp.concatenate([jnp.ones((1,), bool), ids[1:] != ids[:-1]])
    doc_first = lax.cummax(jnp.where(starts, positions, 0), axis=0)
    keep_mask = (positions != doc_first).astype(WIDE)
    lag_masks = jnp.stack(
        [(positions - j >= doc_first).astype(WIDE)[:, None] for j in range(CONV)]
    )

    tokens_f = tokens.astype(WIDE)
    normed_f, norm_pull = jax.vjp(rms_norm, tokens_f, g_one)
    meta_own = meta_tokens.astype(WIDE)
    meta_unit = rms_norm(meta_whole.astype(WIDE), 1.0)
    normed_own = normed_f.astype(SIXTEEN)
    if staged:
        normed_own, columns = tie(normed_own, columns)
        both, pull_both = jax.vjp(both_halves, columns)
    normed = ring_seq_gather(normed_own, 1)
    cotangent_later = cotangent
    if staged:
        normed, both, cotangent_later = tie(normed, both, cotangent)
        (w_in, w_dt, q_rows, out_rows), pull_parts = jax.vjp(mixer_parts, both)
        (by_heads, w_x), pull_rows = jax.vjp(heads_cut, q_rows)
    else:
        (w_qkv, w_in, w_x, w_dt, w_out), pull_mixer = jax.vjp(mixer_shards_whole, mixer_params)
        (w_gate, w_up, w_down), pull_ffn = jax.vjp(ffn_shards_whole, ffn_params)
    normed, small_later = tie(normed, small_whole)
    (_, g_two, g_attn, channel_part), small_pull = jax.vjp(small_shards, small_later)
    channels = channel_part.shape[0]
    lanes = -(-channels // 128) * 128
    g_ssm = channel_part[:, 0]
    conv_w = channel_part[:, 1 : 1 + CONV].T
    conv_b = channel_part[:, 1 + CONV]
    dt_bias = channel_part[:, 2 + CONV]
    a_log = channel_part[:, 3 + CONV : 3 + CONV + STATE]
    d_skip = channel_part[:, 3 + CONV + STATE]
    meta_normed = (meta_unit * g_one).astype(SIXTEEN)
    every = jnp.concatenate([normed, meta_normed], axis=0)
    cotangent_all = gather_seq(cotangent_later)

    xz = dot_last(normed, w_in).astype(SIXTEEN)
    extended = jnp.pad(xz[:, :channels], ((CONV - 1, 0), (0, 0))).astype(WIDE)
    conv_fn = partial(conv_piece, lag_masks=lag_masks)
    conv_out, conv_pull = jax.vjp(conv_fn, extended, conv_w, conv_b)
    conv_half = conv_out.astype(SIXTEEN)
    if staged:
        conv_half, by_heads, w_x, ffn_later = tie(conv_half, by_heads, w_x, ffn_params)
        w_qkv, pull_heads = jax.vjp(heads_from, by_heads)
        ffn_cut, pull_ffn_cut = jax.vjp(ffn_blocks, ffn_later)
    conv_f = conv_half.astype(WIDE)
    w_x_rows = jnp.pad(w_x.T, ((0, -w_x.shape[1] % 16), (0, 0)))
    projected = seq_sum(jnp.einsum("nc,tc->nt", w_x_rows, conv_half, preferred_element_type=WIDE), 2)
    rank_half = projected[:DT_RANK]
    pre_dt = jnp.einsum("rt,rc->tc", rank_half, w_dt, preferred_element_type=WIDE)
    delta, delta_pull = jax.vjp(lambda p, b: softplus_fn(p + b), pre_dt, dt_bias)
    a_neg, a_pull = jax.vjp(lambda a: -jnp.exp(a), a_log)
    if staged:
        after, through = (w_qkv, cotangent_all), (ffn_cut,)
    else:
        after, through = (), ()
    scan_in = (
        keep_mask,
        padded_lanes(conv_f, lanes),
        padded_lanes(delta, lanes),
        projected[DT_RANK : DT_RANK + 2 * STATE],
        padded_lanes(a_neg.T, lanes),
    )
    y_scan, scan_starts, scan_states, *through = scan_forward(*scan_in, after, through)
    if staged:
        (ffn_cut,) = through
        ffn_columns, pull_ffn_columns = jax.vjp(exchange, ffn_cut)
        ffn_both, pull_ffn_both = jax.vjp(both_halves, ffn_columns)
        (w_gate, w_up, down_rows), pull_ffn_parts = jax.vjp(ffn_parts, ffn_both)
        down_received, pull_down_exchange = jax.vjp(exchange, down_rows)
        w_down, pull_down = jax.vjp(down_from, down_received)

    def gate_piece(y, c, skip, z):
        return (y + skip * c) * silu_fn(z)

    z_in = xz[:, channels:].astype(WIDE)
    ssm_out, gate_pull = jax.vjp(gate_piece, y_scan[:, :channels], conv_f, d_skip, z_in)

    own_heads = g_attn.shape[0]
    queries = dot_last(normed, w_qkv[:, :own_heads]).astype(SIXTEEN)
    kv_rows = dot_last(every, w_qkv[:, own_heads:]).astype(SIXTEEN)
    through = (out_rows.transpose(0, 2, 1),) if staged else ()
    attn_out, log_total, *through = attend_forward(queries, kv_rows, doc_first, through)
    if staged:
        out_received, pull_out_exchange = jax.vjp(exchange, through[0].transpose(0, 2, 1))

    squares = jnp.stack([jnp.sum(attn_out * attn_out, axis=1), jnp.sum(ssm_out * ssm_out, axis=1)])
    squares = seq_sum_small(squares, 3)
    if staged:
        out_received = hand_on(out_received.transpose(0, 2, 1), squares).transpose(0, 2, 1)
        w_out, pull_out = jax.vjp(out_from, out_received)
    scale_a = lax.rsqrt(squares[0] / (HEADS * HEAD) + norm_eps)[:, None]
    scale_m = lax.rsqrt(squares[1] / INNER + norm_eps)[:, None]
    mixed = 0.5 * jnp.concatenate(
        [attn_out * scale_a * g_attn, ssm_out * scale_m * g_ssm], axis=1
    )
    mixed = mixed.astype(SIXTEEN)
    hidden = tokens_f + product_scatter([(mixed, w_out, False)], 4)

    second_f, second_pull = jax.vjp(rms_norm, hidden, g_two)
    second, act, d_gate, d_up = gather_ffn(
        second_f.astype(SIXTEEN), cotangent_all, w_gate, w_up, w_down, 5
    )
    d_second = product_scatter([(d_gate, w_gate, True), (d_up, w_up, True)], 6)
    d_hidden, grad_g_two = second_pull(d_second)
    d_hidden = d_hidden + cotangent.astype(WIDE)

    _, grad_gate, grad_up, grad_down, down_product, d_mixed, grad_out = gather_beside_ffn(
        d_hidden.astype(SIXTEEN), second, cotangent_all, act, d_gate, d_up, w_down, mixed, w_out, 7
    )
    grads_ffn = (grad_gate, grad_up, grad_down)
    block_out = (hidden + scatter_seq(down_product)).astype(SIXTEEN)
    d_mixed = 0.5 * d_mixed
    d_mix_a, d_mix_m = d_mixed[:, :own_heads], d_mixed[:, own_heads:]
    means = jnp.stack(
        [jnp.sum(attn_out * g_attn * d_mix_a, axis=1), jnp.sum(ssm_out * g_ssm * d_mix_m, axis=1)]
    )
    means = seq_sum_small(means, 8)
    d_attn, grad_g_attn = rms_pull(
        attn_out, scale_a, g_attn, d_mix_a, means[0][:, None] / (HEADS * HEAD)
    )
    d_ssm, grad_g_ssm = rms_pull(ssm_out, scale_m, g_ssm, d_mix_m, means[1][:, None] / INNER)

    through = ()
    if staged:
        d_down_cut = hand_on(pull_down(grad_down)[0], means)
        (d_down_rows,) = pull_down_exchange(d_down_cut)
        through = (pull_out(grad_out)[0].transpose(0, 2, 1),)
    d_queries, d_kv, d_meta_kv, *through = attend_backward(
        queries, kv_rows, doc_first, attn_out, log_total, d_attn, through
    )

    if staged:
        (d_ffn_both,) = pull_ffn_parts((grad_gate, grad_up, d_down_rows))
        d_ffn_own, d_ffn_other = row_parts(d_ffn_both)
        (d_out_rows,) = pull_out_exchange(through[0].transpose(0, 2, 1))
    grad_kv = dot_weight(normed, d_kv) + dot_weight(meta_normed, d_meta_kv)
    grad_qkv = jnp.concatenate([dot_weight(normed, d_queries), grad_kv], axis=1)
    grad_qkv = hold(grad_qkv.astype(SIXTEEN))

    d_y, d_conv, grad_d_skip, d_z = gate_pull(d_ssm)
    if staged:
        d_y, grad_qkv = tie(d_y, grad_qkv)
    after = (d_ffn_other,) if staged else ()
    d_conv_scan, d_delta, d_bc, d_rate = scan_backward(
        *scan_in, scan_starts, scan_states, padded_lanes(d_y, lanes), after
    )
    if staged:
        d_ffn_columns = d_ffn_own + other_row(d_ffn_other)
        d_out_rows = hand_on(d_out_rows.transpose(0, 2, 1), d_delta).transpose(0, 2, 1)
    d_conv = d_conv + d_conv_scan[:, :channels]
    d_pre, grad_dt_bias = delta_pull(d_delta[:, :channels])
    (grad_a_log,) = a_pull(d_rate[:, :channels].T)
    d_pre = d_pre.astype(SIXTEEN)
    grad_dt = jnp.einsum("rt,tc->rc", rank_half, d_pre, preferred_element_type=WIDE)
    d_rank = jnp.einsum("rc,tc->rt", w_dt, d_pre, preferred_element_type=WIDE)
    d_proj = jnp.concatenate([d_rank, d_bc], axis=0)
    d_proj = seq_sum(jnp.pad(d_proj, ((0, -d_proj.shape[0] % 16), (0, 0))), 10, (block_out,))
    if staged:
        d_proj = hand_on(d_proj, d_ffn_columns)
        (d_by_heads,) = pull_heads(hand_on(grad_qkv, d_proj))
        (grad_ffn,) = pull_ffn_cut(pull_ffn_columns(d_ffn_columns)[0])
    d_proj = d_proj[: DT_RANK + 2 * STATE].T
    grad_x = hold(dot_weight(conv_half, d_proj).astype(SIXTEEN))
    if staged:
        (d_q_rows,) = pull_rows((d_by_heads, grad_x))
    d_extended, grad_conv_w, grad_conv_b = conv_pull(d_conv + dot_back(d_proj, w_x))
    d_xz = jnp.concatenate([d_extended[CONV - 1 :], d_z], axis=1).astype(SIXTEEN)
    grad_in = hold(dot_weight(normed, d_xz).astype(SIXTEEN))
    grad_dt = grad_dt.astype(SIXTEEN)
    if staged:
        (d_both,) = pull_parts((grad_in, grad_dt, d_q_rows, d_out_rows))
        d_xz, d_both = tie(d_xz, d_both)
        (d_columns,) = pull_both(d_both)
    w_q, w_kv = w_qkv[:, :own_heads], w_qkv[:, own_heads:]
    d_meta = dot_back(d_meta_kv, w_kv)
    d_normed = product_scatter(
        [(d_xz, w_in, True), (d_queries, w_q, True), (d_kv, w_kv, True)], 11
    )
    if staged:
        d_normed, d_columns = tie(d_normed, d_columns)
        (grad_mixer,) = pull_columns(d_columns)
    else:
        (grad_mixer,) = pull_mixer((grad_qkv, grad_in, grad_x, grad_dt, grad_out))
        (grad_ffn,) = pull_ffn(grads_ffn)
    grad_from_norm, grad_g_one = norm_pull(d_normed)
    grad_tokens = d_hidden + grad_from_norm
    grad_g_meta = jnp.sum(d_meta * meta_unit, axis=0)
    grad_channels = jnp.concatenate(
        [
            grad_g_ssm[:, None],
            grad_conv_w.T,
            grad_conv_b[:, None],
            grad_dt_bias[:, None],
            grad_a_log,
            grad_d_skip[:, None],
        ],
        axis=1,
    )
    (grad_small,) = small_pull((grad_g_one + grad_g_meta, grad_g_two, grad_g_attn, grad_channels))
    grad_small, d_meta = end_blocks(grad_small, d_meta)
    _, meta_pull = jax.vjp(lambda v: rms_norm(v, g_one), meta_own)
    (grad_meta,) = meta_pull(d_meta)
    return (
        block_out[None],
        grad_tokens[None],
        grad_meta,
        hold(grad_mixer).astype(WIDE),
        grad_small,
        hold(grad_ffn).astype(WIDE),
    )


def solution(mesh):
    in_specs = (
        P("row", "seq", None),
        P("row", "seq"),
        P(("row", "seq"), None),
        P(("row", "seq")),
        P(("row", "seq")),
        P(("row", "seq")),
        P("row", "seq", None),
    )
    out_specs = (
        P("row", "seq", None),
        P("row", "seq", None),
        P(("row", "seq"), None),
        P(("row", "seq")),
        P(("row", "seq")),
        P(("row", "seq")),
    )
    return jax.shard_map(
        per_device, mesh=mesh, in_specs=in_specs, out_specs=out_specs, check_vma=False
    )
```

```python
import functools
from functools import partial
import math

import jax
import jax.numpy as jnp
from jax import lax
from jax.experimental import pallas as pl
from jax.experimental.pallas import tpu as pltpu
from jax.sharding import PartitionSpec as P

D = 1600
HEADS = 25
GROUPS = 5
HEAD = 64
INNER = 3200
STATE = 16
CONV = 4
DT_RANK = 100
FF = 5504
REACH = 8
BLOCK = 128
RUNS = 4
SUB = 8
SPAN = 128
SIXTEEN = jnp.bfloat16
WIDE = jnp.float32


norm_eps = 1e-05


def split_flat(flat_vec, layout):
    pieces = []
    offset = 0
    for piece_shape in layout:
        piece_len = math.prod(piece_shape)
        pieces.append(flat_vec[offset : offset + piece_len].reshape(piece_shape))
        offset += piece_len
    return pieces


def mixer_layout():
    return [
        (D, HEADS * HEAD),
        (D, 2 * GROUPS * HEAD),
        (D, 2 * INNER),
        (INNER, DT_RANK + 2 * STATE),
        (DT_RANK, INNER),
        (HEADS * HEAD + INNER, D),
    ]


def ffn_layout():
    return [(D, FF), (D, FF), (FF, D)]


def small_split(flat_vec):
    width = CONV + STATE + 4
    packed_rows = flat_vec[: D * (3 + 2 * width)].reshape(D, 3 + 2 * width)
    channel_part = packed_rows[:, 3:].reshape(INNER, width)
    return packed_rows[:, 0], packed_rows[:, 1], packed_rows[:, 2], channel_part


def rms_norm(values, gain_vec):
    return (
        values * lax.rsqrt(jnp.mean(values * values, axis=-1, keepdims=True) + norm_eps) * gain_vec
    )


def silu_fn(values):
    return values / (1.0 + jnp.exp(-values))


def softplus_fn(values):
    return jnp.maximum(values, 0.0) + jnp.log1p(jnp.exp(-jnp.abs(values)))


def glu_piece(gate_pre, up_pre):
    return silu_fn(gate_pre) * up_pre


def dot_last(left, right):
    return jnp.einsum("...k,kn->...n", left, right, preferred_element_type=WIDE)


def dot_back(grads, right):
    return jnp.einsum("...n,kn->...k", grads, right, preferred_element_type=WIDE)


def dot_weight(left, grads):
    return jnp.einsum("...k,...n->kn", left, grads, preferred_element_type=WIDE)


def heads_of(shards):
    return -(-HEADS // shards)


def runs_of(shards):
    return RUNS if INNER % (RUNS * shards) == 0 else 1


def own_channels(array, axis, shards, place):
    runs = runs_of(shards)
    unit = INNER // (runs * shards)
    shape = array.shape
    cut = array.reshape(shape[:axis] + (runs, shards, unit) + shape[axis + 1 :])
    cut = lax.dynamic_index_in_dim(cut, place, axis + 1, keepdims=False)
    return cut.reshape(shape[:axis] + (runs * unit,) + shape[axis + 1 :])


def pad_heads(array, axis, shards):
    heads = heads_of(shards)
    pads = [(0, 0)] * array.ndim
    pads[axis] = (0, heads * shards - HEADS)
    padded = jnp.pad(array, pads)
    shape = padded.shape
    return padded.reshape(shape[:axis] + (shards, heads * HEAD) + shape[axis + 2 :])


def by_head(w_q, w_kv, shards):
    rows = w_q.shape[0]
    w_kv = w_kv.reshape(rows, 2, GROUPS, 1, HEAD)
    w_kv = jnp.broadcast_to(w_kv, (rows, 2, GROUPS, HEADS // GROUPS, HEAD))
    w_kv = w_kv.reshape(rows, 2, HEADS, HEAD)
    return jnp.concatenate(
        [
            pad_heads(w_q.reshape(rows, HEADS, HEAD), 1, shards),
            pad_heads(w_kv[:, 0], 1, shards),
            pad_heads(w_kv[:, 1], 1, shards),
        ],
        axis=2,
    )


def exchange(value):
    return lax.all_to_all(value, "seq", 0, 0)


def tie(*arrays):
    return lax.optimization_barrier(arrays)


def hold(array):
    return lax.optimization_barrier(array)


def hand_on(array, *after):
    return pl.pallas_call(
        lambda *refs: None,
        out_shape=jax.ShapeDtypeStruct(array.shape, array.dtype),
        in_specs=[ANY] * (1 + len(after)),
        out_specs=ANY,
        input_output_aliases={0: 0},
    )(array, *after)


def other_row(value):
    return lax.ppermute(value, "row", [(0, 1), (1, 0)])


def in_turn(first_row, one, two):
    return jnp.where(first_row, one, two), jnp.where(first_row, two, one)


@jax.custom_vjp
def both_halves(value):
    first_row = lax.axis_index("row") == 0
    return jnp.concatenate(in_turn(first_row, value, other_row(value)), axis=0)


def row_parts(grad):
    half = grad.shape[0] // 2
    return in_turn(lax.axis_index("row") == 0, grad[:half], grad[half:])


def both_halves_backward(_, grad):
    own, other = row_parts(grad)
    return (own + other_row(other),)


both_halves.defvjp(lambda value: (both_halves(value), None), both_halves_backward)


@partial(jax.custom_vjp, nondiff_argnums=(1,))
def cut_rows(array, counts):
    pieces, offset = [], 0
    for count in counts:
        pieces.append(array[offset : offset + count])
        offset += count
    return tuple(pieces)


def cut_rows_forward(array, counts):
    return cut_rows(array, counts), None


def cut_rows_backward(counts, _, grads):
    return (jnp.concatenate(grads, axis=0),)


cut_rows.defvjp(cut_rows_forward, cut_rows_backward)


def view_width():
    return INNER // RUNS


def weights_fit(mixer_length, ffn_length, rows, shards):
    width = view_width()
    sizes = [math.prod(shape) for shape in mixer_layout()]
    return (
        rows == 2
        and runs_of(shards) == RUNS
        and mixer_length % width == 0
        and all(size % width == 0 for size in sizes)
        and D % shards == 0
        and D % width == 0
        and (HEADS * HEAD * 2) % shards == 0
        and shards % x_turns(shards)[0] == 0
        and ffn_length % FF == 0
    )


def to_columns(piece, width):
    shards = lax.axis_size("seq")
    unit = width // shards
    view = hold(piece.reshape(-1, width))
    return exchange(view.reshape(-1, shards, unit).transpose(1, 0, 2)).reshape(-1, unit)


def full_rows(cut):
    received = exchange(cut)
    return hold(received.transpose(1, 0, 2).reshape(received.shape[1], -1))


def mixer_parts(both):
    width, shards = view_width(), lax.axis_size("seq")
    unit = both.shape[1]
    part_q, part_kv, part_in, part_x, part_dt, part_out = cut_rows(
        both, tuple(math.prod(shape) // width for shape in mixer_layout())
    )
    q_rows = jnp.concatenate(
        [
            part_q.reshape(shards, -1, unit),
            part_kv.reshape(shards, -1, unit),
            x_windows(part_x, shards),
        ],
        axis=1,
    )
    per_row = D // width
    head_rows = heads_of(shards) * HEAD
    out_heads, out_inner = cut_rows(part_out, (HEADS * HEAD * per_row, INNER * per_row))
    out_heads = jnp.pad(
        out_heads, ((0, (head_rows * shards - HEADS * HEAD) * per_row), (0, 0))
    ).reshape(shards, -1, unit)
    out_inner = out_inner.reshape(RUNS, shards, -1, unit)
    out_inner = out_inner.transpose(1, 0, 2, 3).reshape(shards, -1, unit)
    return (
        part_in.reshape(D, -1),
        part_dt.reshape(DT_RANK, -1),
        q_rows,
        jnp.concatenate([out_heads, out_inner], axis=1),
    )


def heads_cut(q_rows):
    shards = lax.axis_size("seq")
    rows = D // shards
    by_rows = full_rows(q_rows)
    split = rows * HEADS * HEAD // view_width()
    end = split + rows * 2 * GROUPS * HEAD // view_width()
    cut = by_head(
        by_rows[:split].reshape(rows, HEADS * HEAD),
        by_rows[split:end].reshape(rows, 2 * GROUPS * HEAD),
        shards,
    )
    return cut.transpose(1, 0, 2), x_from_windows(by_rows[end:], lax.axis_index("seq"))


def heads_from(cut):
    return exchange(cut).reshape(D, -1)


def out_from(received):
    rows = received.shape[1]
    return hold(received.transpose(1, 0, 2).reshape(rows, -1)).reshape(-1, D)


def ffn_blocks(piece):
    shards = lax.axis_size("seq")
    return piece.reshape(-1, shards, FF // shards).transpose(1, 0, 2)


def ffn_parts(both):
    unit = both.shape[2]
    w_gate, w_up, part_down = cut_rows(both.reshape(-1, unit), (D, D, D))
    return w_gate, w_up, part_down.reshape(lax.axis_size("seq"), -1, unit)


def down_from(received):
    return received.transpose(1, 0, 2).reshape(-1, D)


def x_turns(shards):
    width = INNER // RUNS
    run = (width // shards) * (DT_RANK + 2 * STATE)
    common = math.gcd(run, width)
    return width // common, run // common


def x_windows(part_x, shards):
    runs, rows = x_turns(shards)
    need = -(-rows // runs)
    turns = part_x.reshape(-1, rows, part_x.shape[1])
    cuts = [turns[:, (i * rows) // runs : (i * rows) // runs + need] for i in range(runs)]
    cuts = jnp.stack(cuts, axis=1).reshape(RUNS, shards, need, part_x.shape[1])
    return cuts.transpose(1, 0, 2, 3).reshape(shards, RUNS * need, part_x.shape[1])


def x_from_windows(view_rows, place):
    width = view_rows.shape[1]
    shards = lax.axis_size("seq")
    runs, rows = x_turns(shards)
    columns = DT_RANK + 2 * STATE
    count = (width // shards) * columns
    flat = view_rows.reshape(RUNS, -1)
    offset = (place % runs) * rows * (width // runs) % width
    return lax.dynamic_slice_in_dim(flat, offset, count, 1).reshape(-1, columns)


def mixer_shards_whole(piece):
    shards, place = lax.axis_size("seq"), lax.axis_index("seq")
    whole = lax.all_gather(piece, ("row", "seq"), axis=0, tiled=True)
    w_q, w_kv, w_in, w_x, w_dt, w_out = split_flat(whole, mixer_layout())
    qkv = lax.dynamic_index_in_dim(by_head(w_q, w_kv, shards), place, 1, keepdims=False)
    w_in = own_channels(w_in.reshape(D, 2, INNER), 2, shards, place)
    out_heads = w_out[: HEADS * HEAD].reshape(HEADS, HEAD, D)
    out_heads = lax.dynamic_index_in_dim(pad_heads(out_heads, 0, shards), place, 0, keepdims=False)
    return (
        qkv,
        w_in.reshape(D, -1),
        own_channels(w_x, 0, shards, place),
        own_channels(w_dt, 1, shards, place),
        jnp.concatenate([out_heads, own_channels(w_out[HEADS * HEAD :], 0, shards, place)], axis=0),
    )


def ffn_shards_whole(piece):
    unit = FF // lax.axis_size("seq")
    start = lax.axis_index("seq") * unit
    whole = lax.all_gather(piece, ("row", "seq"), axis=0, tiled=True)
    w_gate, w_up, w_down = split_flat(whole, ffn_layout())
    return (
        lax.dynamic_slice_in_dim(w_gate, start, unit, 1),
        lax.dynamic_slice_in_dim(w_up, start, unit, 1),
        lax.dynamic_slice_in_dim(w_down, start, unit, 0),
    )


def small_shards(whole):
    shards, place = lax.axis_size("seq"), lax.axis_index("seq")
    g_one, g_attn, g_two, channel_part = small_split(whole)
    g_attn = pad_heads(g_attn.reshape(HEADS, HEAD), 0, shards)
    return (
        g_one,
        g_two,
        lax.dynamic_index_in_dim(g_attn, place, 0, keepdims=False),
        own_channels(channel_part, 0, shards, place),
    )


def tiles_of(count):
    return -(-count // 128)


def start_blocks(small_params, doc_ids, meta_tokens):
    devices = lax.axis_size("row") * lax.axis_size("seq")
    parts = [small_params, doc_ids.astype(SIXTEEN), meta_tokens.reshape(-1)]
    rows = [tiles_of(part.shape[0]) for part in parts]
    rows_all = -(-sum(rows) // 16) * 16
    tiles = [
        jnp.pad(part, (0, count * 128 - part.shape[0])).reshape(-1, 128)
        for part, count in zip(parts, rows)
    ]
    block = jnp.concatenate(tiles + [jnp.zeros((rows_all - sum(rows), 128), SIXTEEN)], axis=0)
    every = push_gather(block, 0)
    outs, begin = [], 0
    for part, count in zip(parts, rows):
        cut = every[:, begin : begin + count].reshape(devices, -1)[:, : part.shape[0]]
        outs.append(cut)
        begin += count
    ids = outs[1].reshape(lax.axis_size("row"), -1)
    ids = lax.dynamic_index_in_dim(ids, lax.axis_index("row"), 0, keepdims=False)
    return outs[0].reshape(-1).astype(WIDE), ids.astype(jnp.int32), outs[2].reshape(-1, D)


def end_blocks(grad_small, d_meta):
    devices = lax.axis_size("row") * lax.axis_size("seq")
    parts = grad_small.reshape(devices, -1).astype(SIXTEEN)
    small_count = parts.shape[1]
    small_rows = tiles_of(small_count)
    parts = jnp.pad(parts, ((0, 0), (0, small_rows * 128 - small_count)))
    meta = d_meta.astype(SIXTEEN).reshape(devices, -1)
    meta_count = meta.shape[1]
    rows = -(-(small_rows + tiles_of(meta_count)) // 16) * 16
    meta = jnp.pad(meta, ((0, 0), (0, (rows - small_rows) * 128 - meta_count)))
    blocks = jnp.concatenate(
        [parts.reshape(devices, -1, 128), meta.reshape(devices, -1, 128)], axis=1
    )
    own = push_scatter(blocks, 9)
    small = own[:small_rows].reshape(-1)[:small_count]
    meta = own[small_rows:].reshape(-1)[:meta_count].reshape(-1, D)
    return small, meta


def gather_seq(block):
    return lax.all_gather(block, "seq", axis=0, tiled=True)


def scatter_seq(whole):
    return lax.psum_scatter(whole.astype(SIXTEEN), "seq", scatter_dimension=0, tiled=True).astype(
        WIDE
    )


MESH = pl.DeviceIdType.MESH
ANY = pl.BlockSpec(memory_space=pl.ANY)
VMEM = pl.BlockSpec(memory_space=pltpu.VMEM)
MIB = 1024 * 1024


def takes(microseconds):
    return pl.CostEstimate(
        flops=0, bytes_accessed=microseconds * 3_500_000, transcendentals=0
    )


def greet(peers):
    barrier = pltpu.get_barrier_semaphore()
    for peer in peers:
        pl.semaphore_signal(barrier, inc=1, device_id=peer, device_id_type=MESH)
    pl.semaphore_wait(barrier, len(peers))


def ring_place(chip, chips):
    odd = chip % 2
    return odd * (chips - 1 - chip // 2) + (1 - odd) * (chip // 2)


def ring_chip(place, chips):
    place = (place + 2 * chips) % chips
    back = place // (chips // 2)
    return back * (2 * (chips - 1 - place) + 1) + (1 - back) * (2 * place)


def ring_gather_loop(
    shards, parts, x_ref, out_ref, ring_send, ring_recv, pair_send, pair_recv, work, begin=None
):
    row, me = lax.axis_index("row"), lax.axis_index("seq")
    chips = shards // 2
    core = me % 2
    place = ring_place(me // 2, chips)

    def device(spot):
        return ring_chip(spot, chips) * 2 + core

    right, left, twin = (row, device(place + 1)), (row, device(place - 1)), (row, me + 1 - 2 * core)
    greet([right, left, twin])
    rows = x_ref.shape[0] // (2 * parts)
    paths = [(way, part) for part in range(parts) for way in range(2)]

    def piece(way, part, step):
        source = device(place - 1 - step if way == 0 else place + 1 + step)
        return out_ref.at[source, pl.ds((way * parts + part) * rows, rows)]

    def ring(way, part, step):
        here = piece(way, part, step - 1)
        return pltpu.make_async_remote_copy(
            src_ref=here, dst_ref=here, send_sem=ring_send.at[way, part, step],
            recv_sem=ring_recv.at[way, part, step], device_id=(right, left)[way], device_id_type=MESH,
        )

    def pair(way, part, step):
        here = piece(way, part, step - 1)
        return pltpu.make_async_remote_copy(
            src_ref=here, dst_ref=here, send_sem=pair_send.at[way, part, step],
            recv_sem=pair_recv.at[way, part, step], device_id=twin, device_id_type=MESH,
        )

    out_ref[me] = x_ref[...]
    for way, part in paths:
        ring(way, part, 0).start()
    for way, part in paths:
        pair(way, part, 0).start()
    if begin is not None:
        begin()

    def body(step, carry):
        @pl.when(step < chips - 1)
        def _():
            for way, part in paths:
                ring(way, part, step).wait_recv()

                @pl.when(step < chips - 2)
                def _():
                    ring(way, part, step + 1).start()

                pair(way, part, step + 1).start()

        for way, part in paths:
            pair(way, part, step).wait_recv()
        work(step, place)
        return carry

    lax.fori_loop(0, chips, body, 0)

    def finish(step, carry):
        for way, part in paths:
            pair(way, part, step).wait_send()

            @pl.when(step < chips - 1)
            def _():
                ring(way, part, step).wait_send()

        return carry

    lax.fori_loop(0, chips, finish, 0)


def ring_semaphores(chips, parts):
    ring = pltpu.SemaphoreType.DMA((2, parts, chips - 1))
    pair = pltpu.SemaphoreType.DMA((2, parts, chips))
    return [ring, ring, pair, pair]


def seq_gather_kernel(shards, parts, x_ref, out_ref, *sems):
    ring_gather_loop(shards, parts, x_ref, out_ref, *sems, lambda step, place: None)


def fits_vmem(*shapes):
    return sum(padded_bytes(shape, 2) for shape in shapes) < 48 * MIB


def ring_seq_gather(block, collective_id, parts=4):
    shards = lax.axis_size("seq")
    rows, width = block.shape
    if not fits_vmem((shards * rows, width)):
        return lax.all_gather(block, "seq", axis=0, tiled=True)
    gathered = pl.pallas_call(
        functools.partial(seq_gather_kernel, shards, parts),
        out_shape=jax.ShapeDtypeStruct((shards, rows, width), block.dtype),
        in_specs=[VMEM],
        out_specs=VMEM,
        scratch_shapes=ring_semaphores(shards // 2, parts),
        compiler_params=pltpu.CompilerParams(
            collective_id=collective_id, has_side_effects=True, vmem_limit_bytes=56 * MIB
        ),
        cost_estimate=takes(40),
    )(block)
    return gathered.reshape(shards * rows, width)


def gather_ffn_kernel(
    shards, parts, x_ref, cot_ref, gate_ref, up_ref, down_ref,
    out_ref, act_ref, d_gate_ref, d_up_ref, *sems,
):
    chips = shards // 2
    rows = x_ref.shape[0]
    half = rows // 2

    def work(step, place):
        back, ahead = ring_chip(place - step, chips) * 2, ring_chip(place + step, chips) * 2
        spots = [(back, 0), (back + 1, 0), (ahead, half), (ahead + 1, half)]
        starts = [pl.multiple_of(index * rows + first, half) for index, first in spots]
        tokens = jnp.concatenate([out_ref[index, pl.ds(first, half), :] for index, first in spots], axis=0)
        cot = jnp.concatenate([cot_ref[pl.ds(start, half), :] for start in starts], axis=0)
        gate = jnp.dot(tokens, gate_ref[...], preferred_element_type=WIDE)
        up = jnp.dot(tokens, up_ref[...], preferred_element_type=WIDE)
        d_act = lax.dot_general(
            cot, down_ref[...], (((1,), (1,)), ((), ())), preferred_element_type=WIDE
        )
        share = 1.0 / (1.0 + jnp.exp(-gate))
        passed = gate * share
        results = (
            (act_ref, passed * up),
            (d_gate_ref, d_act * up * (share * (1.0 + gate * (1.0 - share)))),
            (d_up_ref, d_act * passed),
        )
        for ref, value in results:
            value = value.astype(SIXTEEN)
            for i, start in enumerate(starts):
                ref[pl.ds(start, half), :] = value[i * half : (i + 1) * half]

    ring_gather_loop(shards, parts, x_ref, out_ref, *sems, work)


def gather_ffn(block, cotangent, w_gate, w_up, w_down, collective_id, parts=4):
    shards = lax.axis_size("seq")
    rows, width = block.shape
    units = w_gate.shape[1]
    if not fits_vmem((shards * rows, width), (shards * rows, width), (3 * shards * rows, units)):
        second = ring_seq_gather(block, collective_id)
        gate, up = dot_last(second, w_gate), dot_last(second, w_up)
        act, pull = jax.vjp(glu_piece, gate, up)
        d_gate, d_up = pull(dot_back(cotangent, w_down))
        return second, act.astype(SIXTEEN), d_gate.astype(SIXTEEN), d_up.astype(SIXTEEN)
    hidden = jax.ShapeDtypeStruct((shards * rows, units), SIXTEEN)
    outs = pl.pallas_call(
        functools.partial(gather_ffn_kernel, shards, parts),
        out_shape=[jax.ShapeDtypeStruct((shards, rows, width), SIXTEEN), hidden, hidden, hidden],
        in_specs=[VMEM] * 5,
        out_specs=[VMEM] * 4,
        scratch_shapes=ring_semaphores(shards // 2, parts),
        compiler_params=pltpu.CompilerParams(
            collective_id=collective_id, has_side_effects=True, vmem_limit_bytes=56 * MIB
        ),
        cost_estimate=takes(45),
    )(block, cotangent, w_gate, w_up, w_down)
    return (outs[0].reshape(shards * rows, width),) + tuple(outs[1:])


def gather_beside_kernel(
    shards, parts, x_ref, second_any, cot_any, act_ref, d_gate_ref, d_up_ref, down_ref, mixed_ref, w_out_ref,
    out_ref, g_gate_ref, g_up_ref, g_down_ref, product_ref, d_mixed_ref, g_out_ref,
    second_ref, cot_ref, total_ref, load_sem, *sems,
):
    chips = shards // 2
    width = second_ref.shape[1]
    rows = x_ref.shape[0]
    half = rows // 2
    loads = [
        pltpu.make_async_copy(second_any, second_ref, load_sem.at[0]),
        pltpu.make_async_copy(cot_any, cot_ref, load_sem.at[1]),
    ]
    block = 256
    turns = width // block
    share = act_ref.shape[0] // chips

    def tn_dot(left, right):
        return lax.dot_general(
            left, right, (((0,), (0,)), ((), ())), preferred_element_type=WIDE
        ).astype(SIXTEEN)

    def columns(cut):
        tokens = second_ref[:, cut]
        g_gate_ref[cut, :] = tn_dot(tokens, d_gate_ref[...])
        g_up_ref[cut, :] = tn_dot(tokens, d_up_ref[...])
        g_down_ref[:, cut] = tn_dot(act_ref[...], cot_ref[:, cut])

    def begin():
        for load in loads:
            load.start()

    def work(step, place):
        @pl.when(step == 0)
        def _():
            for load in loads:
                load.wait()

        back, ahead = ring_chip(place - step, chips) * 2, ring_chip(place + step, chips) * 2
        spots = [(back, 0), (back + 1, 0), (ahead, half), (ahead + 1, half)]
        starts = [pl.multiple_of(index * rows + first, half) for index, first in spots]
        grads = jnp.concatenate([out_ref[index, pl.ds(first, half), :] for index, first in spots], axis=0)
        mixed = jnp.concatenate([mixed_ref[pl.ds(start, half), :] for start in starts], axis=0)
        d_mixed = lax.dot_general(
            grads, w_out_ref[...], (((1,), (1,)), ((), ())), preferred_element_type=WIDE
        )
        for i, start in enumerate(starts):
            d_mixed_ref[pl.ds(start, half), :] = d_mixed[i * half : (i + 1) * half]
        part = lax.dot_general(mixed, grads, (((0,), (0,)), ((), ())), preferred_element_type=WIDE)

        @pl.when(step == 0)
        def _():
            total_ref[...] = part

        @pl.when(step > 0)
        def _():
            total_ref[...] += part

        @pl.when(step < turns)
        def _():
            columns(pl.ds(pl.multiple_of(step * block, block), block))

        @pl.when(step == turns)
        def _():
            columns(slice(turns * block, width))

        here = pl.ds(pl.multiple_of(step * share, share), share)
        product_ref[here, :] = jnp.dot(
            act_ref[here, :], down_ref[...], preferred_element_type=WIDE
        ).astype(SIXTEEN)

    ring_gather_loop(shards, parts, x_ref, out_ref, *sems, work, begin)
    g_out_ref[...] = total_ref[...].astype(SIXTEEN)


def gather_beside_ffn(
    block, second, cotangent, act, d_gate, d_up, w_down, mixed, w_out, collective_id, parts=4
):
    shards = lax.axis_size("seq")
    rows, width = block.shape
    length, units = act.shape
    chips = shards // 2
    if width // 256 >= chips or not fits_vmem(
        (4 * length, width), (3 * length, units), (3 * width, units), (4 * mixed.shape[1], width),
        (3 * length, mixed.shape[1])
    ):
        gathered = ring_seq_gather(block, collective_id)
        return (
            gathered,
            dot_weight(second, d_gate).astype(SIXTEEN),
            dot_weight(second, d_up).astype(SIXTEEN),
            dot_weight(act, cotangent).astype(SIXTEEN),
            dot_last(act, w_down).astype(SIXTEEN),
            dot_back(gathered, w_out),
            dot_weight(mixed, gathered).astype(SIXTEEN),
        )
    outs = pl.pallas_call(
        functools.partial(gather_beside_kernel, shards, parts),
        out_shape=[
            jax.ShapeDtypeStruct((shards, rows, width), SIXTEEN),
            jax.ShapeDtypeStruct((width, units), SIXTEEN),
            jax.ShapeDtypeStruct((width, units), SIXTEEN),
            jax.ShapeDtypeStruct((units, width), SIXTEEN),
            jax.ShapeDtypeStruct((length, width), SIXTEEN),
            jax.ShapeDtypeStruct(mixed.shape, WIDE),
            jax.ShapeDtypeStruct(w_out.shape, SIXTEEN),
        ],
        in_specs=[VMEM, ANY, ANY] + [VMEM] * 6,
        out_specs=[VMEM] * 7,
        scratch_shapes=[
            pltpu.VMEM(second.shape, SIXTEEN),
            pltpu.VMEM(cotangent.shape, SIXTEEN),
            pltpu.VMEM(w_out.shape, WIDE),
            pltpu.SemaphoreType.DMA((2,)),
        ]
        + ring_semaphores(chips, parts),
        compiler_params=pltpu.CompilerParams(
            collective_id=collective_id, has_side_effects=True, vmem_limit_bytes=60 * MIB
        ),
        cost_estimate=takes(45),
    )(block, second, cotangent, act, d_gate, d_up, w_down, mixed, w_out)
    return (outs[0].reshape(shards * rows, width),) + tuple(outs[1:])


def product_scatter_kernel(shards, parts, turned, *refs):
    terms = len(turned)
    lefts, rights = refs[:terms], refs[terms : 2 * terms]
    out_ref, mine, given, pair, arrived = refs[2 * terms : 2 * terms + 5]
    ring_send, ring_recv, pair_send, pair_recv = refs[2 * terms + 5 :]
    row, me = lax.axis_index("row"), lax.axis_index("seq")
    chips = shards // 2
    core = me % 2
    place = ring_place(me // 2, chips)
    block_rows = out_ref.shape[0]

    def device(spot, core):
        return ring_chip(spot, chips) * 2 + core

    right = (row, device(place + 1, core))
    left = (row, device(place - 1, core))
    twin = (row, me + 1 - 2 * core)
    greet([right, left, twin])
    rows = block_rows // (2 * parts)

    def cut(way, part):
        return pl.ds((way * parts + part) * rows, rows)

    def product(index):
        here = pl.ds(pl.multiple_of(index * block_rows, block_rows), block_rows)
        total = None
        for left_ref, right_ref, turn in zip(lefts, rights, turned):
            part = lax.dot_general(
                left_ref[here, :], right_ref[...], (((1,), (1 if turn else 0,)), ((), ())),
                preferred_element_type=WIDE,
            )
            total = part if total is None else total + part
        return total.astype(SIXTEEN)

    def pass_over(slot):
        return pltpu.make_async_remote_copy(
            src_ref=given.at[slot], dst_ref=pair.at[slot], send_sem=pair_send.at[slot],
            recv_sem=pair_recv.at[slot], device_id=twin, device_id_type=MESH,
        )

    def make(far):
        slot = far % chips
        given[slot] = product(device(place + far, 1 - core))
        pass_over(slot).start()
        mine[slot] = product(device(place + far, core))

    def both(step, carry):
        make(-step)
        make(step)
        return carry

    half = chips // 2
    both(1, 0)
    started, flights = [], {}
    fresh = set(range(chips))
    for step in range(chips):
        if step + 2 < half:
            both(step + 2, 0)
        elif step + 2 == half:
            make(half)
            make(0)
        for part in range(parts):
            for way in range(2):
                slot = (-1 - step if way == 0 else 1 + step) % chips
                if slot in fresh:
                    fresh.remove(slot)
                    pass_over(slot).wait_recv()
                here = cut(way, part)
                total = mine[slot, here, :].astype(WIDE) + pair[slot, here, :].astype(WIDE)
                if step:
                    flights[way, part].wait_recv()
                    total = total + arrived[way, step - 1, pl.ds(part * rows, rows), :].astype(WIDE)
                if step == chips - 1:
                    out_ref[here, :] = total
                    continue
                mine[slot, here, :] = total.astype(SIXTEEN)
                copy = pltpu.make_async_remote_copy(
                    src_ref=mine.at[slot, here], dst_ref=arrived.at[way, step, pl.ds(part * rows, rows)],
                    send_sem=ring_send.at[way, part, step], recv_sem=ring_recv.at[way, part, step],
                    device_id=(right, left)[way], device_id_type=MESH,
                )
                copy.start()
                started.append(copy)
                flights[way, part] = copy
    for slot in range(chips):
        pass_over(slot).wait_send()
    for copy in started:
        copy.wait_send()


def padded_bytes(shape, bytes_each):
    return -(-shape[0] // 16) * 16 * -(-shape[1] // 128) * 128 * bytes_each


def product_scatter(terms, collective_id, parts=4):
    shards = lax.axis_size("seq")
    chips = shards // 2
    length = terms[0][0].shape[0]
    width = terms[0][1].shape[0 if terms[0][2] else 1]
    rows = length // shards
    buffers = 4 * chips * padded_bytes((rows, width), 2)
    operands = sum(padded_bytes(t[0].shape, 2) + padded_bytes(t[1].shape, 2) for t in terms)
    if chips < 4 or buffers + operands > 40 * MIB:
        total = 0
        for left, right, turn in terms:
            total = total + lax.dot_general(
                left, right, (((1,), (1 if turn else 0,)), ((), ())), preferred_element_type=WIDE
            )
        return lax.psum_scatter(
            total.astype(SIXTEEN), "seq", scatter_dimension=0, tiled=True
        ).astype(WIDE)
    ring = pltpu.SemaphoreType.DMA((2, parts, chips - 1))
    pair = pltpu.SemaphoreType.DMA((chips,))
    blocks = pltpu.VMEM((chips, rows, width), SIXTEEN)
    return pl.pallas_call(
        functools.partial(product_scatter_kernel, shards, parts, tuple(t[2] for t in terms)),
        out_shape=jax.ShapeDtypeStruct((rows, width), WIDE),
        in_specs=[VMEM] * (2 * len(terms)),
        out_specs=VMEM,
        scratch_shapes=[
            blocks, blocks, blocks,
            pltpu.VMEM((2, chips - 1, rows // 2, width), SIXTEEN),
            ring, ring, pair, pair,
        ],
        compiler_params=pltpu.CompilerParams(
            collective_id=collective_id, has_side_effects=True, vmem_limit_bytes=56 * MIB
        ),
        cost_estimate=takes(40),
    )(*[t[0] for t in terms], *[t[1] for t in terms])


def bits_of(shards):
    bits = shards.bit_length() - 1
    assert 1 << bits == shards
    return bits


def partner_of(me, bit):
    return me + (1 - 2 * ((me // (1 << bit)) % 2)) * (1 << bit)


def seq_sum_kernel(bits, waits, x_ref, *refs):
    out_ref, total, staged, arrived, send_sem, recv_sem, back_send, back_recv = refs[waits:]
    row, me = lax.axis_index("row"), lax.axis_index("seq")
    partners = [(row, partner_of(me, bit)) for bit in range(bits)]
    greet(partners)
    length = x_ref.shape[1]
    total[...] = x_ref[...].astype(WIDE)
    begin = 0
    started = []
    for bit in range(bits):
        half = length >> (bit + 1)
        upper = (me // (1 << bit)) % 2
        kept = pl.multiple_of(begin + upper * half, 128)
        given = pl.multiple_of(begin + (1 - upper) * half, 128)
        staged[:, half : 2 * half] = total[:, pl.ds(given, half)].astype(SIXTEEN)
        copy = pltpu.make_async_remote_copy(
            src_ref=staged.at[:, half : 2 * half], dst_ref=arrived.at[:, half : 2 * half],
            send_sem=send_sem.at[bit], recv_sem=recv_sem.at[bit],
            device_id=partners[bit], device_id_type=MESH,
        )
        copy.start()
        started.append(copy)
        copy.wait_recv()
        total[:, pl.ds(kept, half)] += arrived[:, half : 2 * half].astype(WIDE)
        begin = kept
    half = length >> bits
    out_ref[:, pl.ds(pl.multiple_of(begin, 128), half)] = total[
        :, pl.ds(pl.multiple_of(begin, 128), half)
    ].astype(SIXTEEN)
    for bit in range(bits - 1, -1, -1):
        half = length >> (bit + 1)
        here = out_ref.at[:, pl.ds(pl.multiple_of(begin, 128), half)]
        copy = pltpu.make_async_remote_copy(
            src_ref=here, dst_ref=here, send_sem=back_send.at[bit], recv_sem=back_recv.at[bit],
            device_id=partners[bit], device_id_type=MESH,
        )
        copy.start()
        started.append(copy)
        copy.wait_recv()
        begin = begin - ((me // (1 << bit)) % 2) * half
    for copy in started:
        copy.wait_send()


def seq_sum(values, collective_id, after=()):
    bits = bits_of(lax.axis_size("seq"))
    rows, length = values.shape
    sems = pltpu.SemaphoreType.DMA((bits,))
    return pl.pallas_call(
        functools.partial(seq_sum_kernel, bits, len(after)),
        out_shape=jax.ShapeDtypeStruct((rows, length), SIXTEEN),
        in_specs=[VMEM] + [ANY] * len(after),
        out_specs=VMEM,
        scratch_shapes=[
            pltpu.VMEM((rows, length), WIDE),
            pltpu.VMEM((rows, length), SIXTEEN),
            pltpu.VMEM((rows, length), SIXTEEN),
            sems, sems, sems, sems,
        ],
        compiler_params=pltpu.CompilerParams(
            collective_id=collective_id, has_side_effects=True, vmem_limit_bytes=48 * MIB
        ),
        cost_estimate=takes(30),
    )(values, *after)


def seq_sum_small_kernel(groups, x_ref, out_ref, arrived, staged, send_sem, recv_sem):
    row, me = lax.axis_index("row"), lax.axis_index("seq")
    phases = []
    for size, stride in groups:
        spot = (me // stride) % size
        phases.append(
            [(row, me + ((spot + far) % size - spot) * stride) for far in range(1, size)]
        )
    greet([peer for peers in phases for peer in peers])
    total = x_ref[...]
    copies, slot = [], 0
    for phase, peers in enumerate(phases):
        staged[phase] = total
        flights = []
        for peer in peers:
            copy = pltpu.make_async_remote_copy(
                src_ref=staged.at[phase], dst_ref=arrived.at[slot], send_sem=send_sem.at[slot],
                recv_sem=recv_sem.at[slot], device_id=peer, device_id_type=MESH,
            )
            copy.start()
            flights.append((copy, slot))
            slot += 1
        for copy, here in flights:
            copy.wait_recv()
            total = total + arrived[here]
        copies += flights
    out_ref[...] = total
    for copy, _ in copies:
        copy.wait_send()


def seq_sum_small(values, collective_id):
    bits = bits_of(lax.axis_size("seq"))
    low = 1 << (bits // 2)
    groups = ((low, 1), ((1 << bits) // low, low))
    count = sum(size - 1 for size, _ in groups)
    shape = values.shape
    tiles = values.reshape(-1, 128)
    sems = pltpu.SemaphoreType.DMA((count,))
    return pl.pallas_call(
        functools.partial(seq_sum_small_kernel, groups),
        out_shape=jax.ShapeDtypeStruct(tiles.shape, WIDE),
        in_specs=[VMEM],
        out_specs=VMEM,
        scratch_shapes=[
            pltpu.VMEM((count,) + tiles.shape, WIDE),
            pltpu.VMEM((len(groups),) + tiles.shape, WIDE),
            sems, sems,
        ],
        compiler_params=pltpu.CompilerParams(collective_id=collective_id, has_side_effects=True),
        cost_estimate=takes(12),
    )(tiles).reshape(shape)


def all_peers(rows, shards):
    me = lax.axis_index("row") * shards + lax.axis_index("seq")
    count = rows * shards
    ahead = [(me + far) % count for far in range(1, count)]
    return me, count, [(other, (other // shards, other % shards)) for other in ahead]


def push_gather_kernel(rows, shards, x_ref, out_ref, send_sem, recv_sem):
    me, count, peers = all_peers(rows, shards)
    greet([device for _, device in peers])
    copies = []
    for far, (_, device) in enumerate(peers):
        copy = pltpu.make_async_remote_copy(
            src_ref=x_ref, dst_ref=out_ref.at[me], send_sem=send_sem.at[far],
            recv_sem=recv_sem.at[far], device_id=device, device_id_type=MESH,
        )
        copy.start()
        copies.append(copy)
    out_ref[me] = x_ref[...]
    for copy in copies:
        copy.wait()


def push_gather(block, collective_id):
    rows, shards = lax.axis_size("row"), lax.axis_size("seq")
    sems = pltpu.SemaphoreType.DMA((rows * shards - 1,))
    return pl.pallas_call(
        functools.partial(push_gather_kernel, rows, shards),
        out_shape=jax.ShapeDtypeStruct((rows * shards,) + block.shape, block.dtype),
        in_specs=[VMEM],
        out_specs=VMEM,
        scratch_shapes=[sems, sems],
        compiler_params=pltpu.CompilerParams(collective_id=collective_id, has_side_effects=True),
        cost_estimate=takes(20),
    )(block)


def push_scatter_kernel(rows, shards, x_ref, out_ref, arrived, send_sem, recv_sem):
    me, count, peers = all_peers(rows, shards)
    greet([device for _, device in peers])
    copies = []
    for far, (other, device) in enumerate(peers):
        copy = pltpu.make_async_remote_copy(
            src_ref=x_ref.at[other], dst_ref=arrived.at[far], send_sem=send_sem.at[far],
            recv_sem=recv_sem.at[far], device_id=device, device_id_type=MESH,
        )
        copy.start()
        copies.append(copy)
    total = x_ref[me].astype(WIDE)
    for far, copy in enumerate(copies):
        copy.wait_recv()
        total = total + arrived[far].astype(WIDE)
    out_ref[...] = total
    for copy in copies:
        copy.wait_send()


def push_scatter(blocks, collective_id):
    rows, shards = lax.axis_size("row"), lax.axis_size("seq")
    count = rows * shards
    sems = pltpu.SemaphoreType.DMA((count - 1,))
    return pl.pallas_call(
        functools.partial(push_scatter_kernel, rows, shards),
        out_shape=jax.ShapeDtypeStruct(blocks.shape[1:], WIDE),
        in_specs=[VMEM],
        out_specs=VMEM,
        scratch_shapes=[pltpu.VMEM((count - 1,) + blocks.shape[1:], blocks.dtype), sems, sems],
        compiler_params=pltpu.CompilerParams(
            collective_id=collective_id, has_side_effects=True, vmem_limit_bytes=32 * MIB
        ),
        cost_estimate=takes(20),
    )(blocks)


def conv_piece(extended, conv_w, conv_b, lag_masks):
    length = extended.shape[0] - (CONV - 1)
    summed = conv_b
    for j in range(CONV):
        summed = (
            summed + conv_w[j] * extended[CONV - 1 - j : CONV - 1 - j + length] * lag_masks[j]
        )
    return silu_fn(summed)


def nt_dot(left, right):
    return lax.dot_general(left, right, (((1,), (1,)), ((), ())), preferred_element_type=WIDE)


def seen_keys(block, first_row):
    window = (REACH + 1) * BLOCK
    k_pos = (block - REACH) * BLOCK + lax.broadcasted_iota(jnp.int32, (window, BLOCK), 0)
    q_pos = block * BLOCK + lax.broadcasted_iota(jnp.int32, (window, BLOCK), 1)
    return (k_pos >= first_row) & (k_pos <= q_pos) & (k_pos > q_pos - REACH * BLOCK)


PER = 4


def attend_forward_kernel(heads, waits, *refs):
    first_ref, q_ref, kv_ref, turned_ref, meta_ref, meta_turned_ref = refs[:6]
    out_ref, total_ref = refs[6 + waits : 8 + waits]
    for sub in range(PER):
        block = pl.program_id(0) * PER + sub
        here = slice(sub * BLOCK, (sub + 1) * BLOCK)
        span = pl.ds(pl.multiple_of(block * BLOCK, BLOCK), (REACH + 1) * BLOCK)
        seen = seen_keys(block, first_ref[sub])
        outs, totals = [], []
        for h in range(heads):
            cut = slice(h * HEAD, (h + 1) * HEAD)
            v_cut = slice((heads + h) * HEAD, (heads + h + 1) * HEAD)
            query = q_ref[here, cut] * SIXTEEN(HEAD ** (-0.5))
            near = jnp.where(seen, nt_dot(kv_ref[span, cut], query), -1e30)
            meta = nt_dot(meta_ref[:, cut], query)
            top = jnp.maximum(
                jnp.max(near, axis=0, keepdims=True), jnp.max(meta, axis=0, keepdims=True)
            )
            near = jnp.exp(near - top)
            meta = jnp.exp(meta - top)
            total = jnp.sum(near, axis=0, keepdims=True) + jnp.sum(meta, axis=0, keepdims=True)
            out = jnp.dot(turned_ref[v_cut, span], near.astype(SIXTEEN), preferred_element_type=WIDE)
            out += jnp.dot(meta_turned_ref[v_cut, :], meta.astype(SIXTEEN), preferred_element_type=WIDE)
            outs.append(out / total)
            totals.append(top + jnp.log(total))
        out_ref[here, :] = jnp.concatenate(outs, axis=0).T
        total_ref[sub] = jnp.concatenate(totals, axis=0)


def attend_backward_kernel(heads, waits, *refs):
    first_ref, q_ref, kv_ref, turned_ref, meta_ref, meta_turned_ref = refs[:6]
    out_ref, total_ref, do_ref = refs[6:9]
    dq_ref, dkv_ref, dmeta_ref = refs[9 + waits : 12 + waits]
    block = pl.program_id(0)

    @pl.when(block == 0)
    def _():
        dkv_ref[...] = jnp.zeros_like(dkv_ref)
        dmeta_ref[...] = jnp.zeros_like(dmeta_ref)

    span = pl.ds(pl.multiple_of(block * BLOCK, BLOCK), (REACH + 1) * BLOCK)
    seen = seen_keys(block, first_ref[0])
    d_out = do_ref[...]
    row_sums = (d_out * out_ref[...]).T
    d_half = d_out.astype(SIXTEEN)
    d_queries, near_k, near_v, meta_k, meta_v = [], [], [], [], []
    for h in range(heads):
        cut = slice(h * HEAD, (h + 1) * HEAD)
        v_cut = slice((heads + h) * HEAD, (heads + h + 1) * HEAD)
        query = q_ref[:, cut] * SIXTEEN(HEAD ** (-0.5))
        do = d_half[:, cut]
        total = total_ref[0, h : h + 1, :]
        mean = jnp.sum(row_sums[cut], axis=0, keepdims=True)
        near = jnp.where(seen, jnp.exp(nt_dot(kv_ref[span, cut], query) - total), 0.0)
        meta = jnp.exp(nt_dot(meta_ref[:, cut], query) - total)
        d_near = (near * (nt_dot(kv_ref[span, v_cut], do) - mean)).astype(SIXTEEN)
        d_meta = (meta * (nt_dot(meta_ref[:, v_cut], do) - mean)).astype(SIXTEEN)
        near_v.append(jnp.dot(near.astype(SIXTEEN), do, preferred_element_type=WIDE))
        meta_v.append(jnp.dot(meta.astype(SIXTEEN), do, preferred_element_type=WIDE))
        near_k.append(jnp.dot(d_near, query, preferred_element_type=WIDE))
        meta_k.append(jnp.dot(d_meta, query, preferred_element_type=WIDE))
        d_query = jnp.dot(turned_ref[cut, span], d_near, preferred_element_type=WIDE)
        d_query += jnp.dot(meta_turned_ref[cut, :], d_meta, preferred_element_type=WIDE)
        d_queries.append(d_query * HEAD ** (-0.5))
    dq_ref[...] = jnp.concatenate(d_queries, axis=0).T.astype(SIXTEEN)
    dkv_ref[span, :] += jnp.concatenate(near_k + near_v, axis=1)
    dmeta_ref[...] += jnp.concatenate(meta_k + meta_v, axis=1)


def attend_operands(queries, kv_rows, doc_first):
    length = doc_first.shape[0]
    count = length // BLOCK
    near = jnp.pad(kv_rows[:length], ((REACH * BLOCK, 0), (0, 0)))
    meta = kv_rows[length:]
    arrays = (doc_first.reshape(count, 1, BLOCK), queries, near, near.T, meta, meta.T)
    width = queries.shape[1]

    def whole(array):
        return pl.BlockSpec(array.shape, lambda i: (0,) * array.ndim)

    specs = [
        pl.BlockSpec((1, 1, BLOCK), lambda i: (i, 0, 0)),
        pl.BlockSpec((BLOCK, width), lambda i: (i, 0)),
    ] + [whole(a) for a in arrays[2:]]
    return arrays, specs, count, width


def attend_forward(queries, kv_rows, doc_first, through=()):
    arrays, specs, count, width = attend_operands(queries, kv_rows, doc_first)
    heads = width // HEAD
    specs = [
        pl.BlockSpec((PER, 1, BLOCK), lambda i: (i, 0, 0)),
        pl.BlockSpec((PER * BLOCK, width), lambda i: (i, 0)),
    ] + specs[2:]
    return pl.pallas_call(
        lambda *refs: attend_forward_kernel(heads, len(through), *refs),
        grid=(count // PER,),
        in_specs=specs + [ANY] * len(through),
        out_specs=[
            pl.BlockSpec((PER * BLOCK, width), lambda i: (i, 0)),
            pl.BlockSpec((PER, heads, BLOCK), lambda i: (i, 0, 0)),
        ]
        + [ANY] * len(through),
        out_shape=[
            jax.ShapeDtypeStruct(queries.shape, WIDE),
            jax.ShapeDtypeStruct((count, heads, BLOCK), WIDE),
        ]
        + [jax.ShapeDtypeStruct(x.shape, x.dtype) for x in through],
        input_output_aliases={6 + i: 2 + i for i in range(len(through))},
        compiler_params=pltpu.CompilerParams(vmem_limit_bytes=48 * MIB),
        cost_estimate=takes(24),
    )(*arrays, *through)


def attend_backward(queries, kv_rows, doc_first, out, log_total, d_out, through=()):
    arrays, specs, count, width = attend_operands(queries, kv_rows, doc_first)
    heads = width // HEAD
    near, meta = arrays[2], arrays[4]
    row_spec = pl.BlockSpec((BLOCK, width), lambda i: (i, 0))
    d_queries, d_near, d_meta, *through = pl.pallas_call(
        lambda *refs: attend_backward_kernel(heads, len(through), *refs),
        grid=(count,),
        in_specs=specs
        + [row_spec, pl.BlockSpec((1, heads, BLOCK), lambda i: (i, 0, 0)), row_spec]
        + [ANY] * len(through),
        out_specs=[
            row_spec,
            pl.BlockSpec(near.shape, lambda i: (0, 0)),
            pl.BlockSpec(meta.shape, lambda i: (0, 0)),
        ]
        + [ANY] * len(through),
        out_shape=[
            jax.ShapeDtypeStruct(queries.shape, SIXTEEN),
            jax.ShapeDtypeStruct(near.shape, WIDE),
            jax.ShapeDtypeStruct(meta.shape, WIDE),
        ]
        + [jax.ShapeDtypeStruct(x.shape, x.dtype) for x in through],
        input_output_aliases={9 + i: 3 + i for i in range(len(through))},
        compiler_params=pltpu.CompilerParams(vmem_limit_bytes=48 * MIB),
        cost_estimate=takes(24),
    )(*arrays, out, log_total, d_out, *through)
    return d_queries, d_near[REACH * BLOCK :].astype(SIXTEEN), d_meta.astype(SIXTEEN), *through


def step_sum():
    rows = lax.broadcasted_iota(jnp.int32, (SUB, SUB * STATE), 0)
    cols = lax.broadcasted_iota(jnp.int32, (SUB, SUB * STATE), 1)
    return (cols // STATE == rows).astype(SIXTEEN)


def lanes_from(tile, group):
    return pltpu.roll(tile, (SPAN - group * SUB) % SPAN, axis=1)


def scan_forward_kernel(waits, *refs):
    keep_ref, conv_ref, delta_ref, bc_ref, a_ref = refs[:5]
    y_ref, start_ref, kept_ref = refs[5 + waits : 8 + waits]
    state_ref = refs[-1]
    block = pl.program_id(0)

    @pl.when(block == 0)
    def _():
        state_ref[...] = jnp.zeros_like(state_ref)

    start_ref[0] = state_ref[...]
    decay_rate = a_ref[...]
    fold = step_sum()
    b_span = bc_ref[:STATE, :].astype(WIDE)
    c_span = bc_ref[STATE:, :].astype(WIDE)

    def body(group, state):
        rows = pl.ds(pl.multiple_of(group * SUB, SUB), SUB)
        delta = delta_ref[rows, :]
        drive = delta * conv_ref[rows, :]
        b_tile = lanes_from(b_span, group)
        c_tile = lanes_from(c_span, group)
        reads = []
        for i in range(SUB):
            keep = keep_ref[block * SPAN + group * SUB + i]
            decay = jnp.exp(delta[i : i + 1, :] * decay_rate) * keep
            state = decay * state + drive[i : i + 1, :] * b_tile[:, i : i + 1]
            kept_ref[group * SUB + i] = state.astype(SIXTEEN)
            reads.append((state * c_tile[:, i : i + 1]).astype(SIXTEEN))
        y_ref[rows, :] = jnp.dot(
            fold, jnp.concatenate(reads, axis=0), preferred_element_type=WIDE
        )
        return state

    state_ref[...] = lax.fori_loop(0, SPAN // SUB, body, state_ref[...], unroll=8)


def scan_forward(keep, conv_out, delta, bc_rows, decay_rate, after=(), through=()):
    length, lanes = conv_out.shape
    waits = len(after) + len(through)
    blocks = length // SPAN
    span_spec = pl.BlockSpec((SPAN, lanes), lambda i: (i, 0))
    return pl.pallas_call(
        functools.partial(scan_forward_kernel, waits),
        grid=(blocks,),
        in_specs=[
            pl.BlockSpec(memory_space=pltpu.SMEM),
            span_spec,
            span_spec,
            pl.BlockSpec((2 * STATE, SPAN), lambda i: (0, i)),
            pl.BlockSpec((STATE, lanes), lambda i: (0, 0)),
        ]
        + [ANY] * waits,
        out_specs=[
            span_spec,
            pl.BlockSpec((1, STATE, lanes), lambda i: (i, 0, 0)),
            pl.BlockSpec((SPAN, STATE, lanes), lambda i: (i, 0, 0)),
        ]
        + [ANY] * len(through),
        out_shape=[
            jax.ShapeDtypeStruct((length, lanes), WIDE),
            jax.ShapeDtypeStruct((blocks, STATE, lanes), WIDE),
            jax.ShapeDtypeStruct((length, STATE, lanes), SIXTEEN),
        ]
        + [jax.ShapeDtypeStruct(x.shape, x.dtype) for x in through],
        input_output_aliases={5 + len(after) + i: 3 + i for i in range(len(through))},
        scratch_shapes=[pltpu.VMEM((STATE, lanes), WIDE)],
        cost_estimate=takes(24),
    )(keep, conv_out, delta, bc_rows, decay_rate, *after, *through)


def scan_backward_kernel(waits, *refs):
    keep_ref, conv_ref, delta_ref, bc_ref, a_ref, start_ref, kept_ref, dy_ref = refs[:8]
    dconv_ref, ddelta_ref, dbc_ref, da_ref, adjoint_ref = refs[8 + waits :]
    turn = pl.program_id(0)
    block = pl.num_programs(0) - 1 - turn

    @pl.when(turn == 0)
    def _():
        adjoint_ref[...] = jnp.zeros_like(adjoint_ref)
        da_ref[...] = jnp.zeros_like(da_ref)

    decay_rate = a_ref[...]
    fold = step_sum()
    lanes = decay_rate.shape[1]
    ones = jnp.ones((lanes, SPAN), SIXTEEN)
    spot = lax.broadcasted_iota(jnp.int32, (STATE, SPAN), 1)
    b_span = bc_ref[:STATE, :].astype(WIDE)
    c_span = bc_ref[STATE:, :].astype(WIDE)
    def back(step, carry):
        adjoint, da, db, dc = carry
        group = SPAN // SUB - 1 - step
        rows = pl.ds(pl.multiple_of(group * SUB, SUB), SUB)
        delta = delta_ref[rows, :]
        conv = conv_ref[rows, :]
        drive = delta * conv
        dy = dy_ref[rows, :]
        b_tile = lanes_from(b_span, group)
        c_tile = lanes_from(c_span, group)
        before = kept_ref[jnp.maximum(group * SUB - 1, 0)].astype(WIDE)
        before = jnp.where(group == 0, start_ref[0], before)
        states = [before] + [kept_ref[group * SUB + i].astype(WIDE) for i in range(SUB)]
        by_c, by_b, by_drive, by_delta = ([None] * SUB for _ in range(4))
        for i in range(SUB - 1, -1, -1):
            keep = keep_ref[block * SPAN + group * SUB + i]
            decay = jnp.exp(delta[i : i + 1, :] * decay_rate) * keep
            dy_row = dy[i : i + 1, :]
            total = adjoint + dy_row * c_tile[:, i : i + 1]
            by_c[i] = (dy_row * states[i + 1]).astype(SIXTEEN)
            by_b[i] = (total * drive[i : i + 1, :]).astype(SIXTEEN)
            by_drive[i] = (total * b_tile[:, i : i + 1]).astype(SIXTEEN)
            adjoint = total * decay
            rate = adjoint * states[i]
            by_delta[i] = (rate * decay_rate).astype(SIXTEEN)
            da = da + rate * delta[i : i + 1, :]

        def over_state(parts):
            return jnp.dot(fold, jnp.concatenate(parts, axis=0), preferred_element_type=WIDE)

        def over_lanes(parts, tile):
            sums = jnp.dot(jnp.concatenate(parts, axis=0), ones, preferred_element_type=WIDE)
            for i in range(SUB):
                here = spot == group * SUB + i
                tile = jnp.where(here, sums[i * STATE : (i + 1) * STATE, :], tile)
            return tile

        d_drive = over_state(by_drive)
        dconv_ref[rows, :] = d_drive * delta
        ddelta_ref[rows, :] = over_state(by_delta) + d_drive * conv
        return adjoint, da, over_lanes(by_b, db), over_lanes(by_c, dc)

    none = jnp.zeros((STATE, SPAN), WIDE)
    adjoint, da, db, dc = lax.fori_loop(
        0, SPAN // SUB, back, (adjoint_ref[...], da_ref[...], none, none), unroll=16
    )
    adjoint_ref[...] = adjoint
    da_ref[...] = da
    dbc_ref[...] = jnp.concatenate([db, dc], axis=0)


def scan_backward(keep, conv_out, delta, bc_rows, decay_rate, starts, kept, dy, after=()):
    length, lanes = conv_out.shape
    blocks = length // SPAN
    span_spec = pl.BlockSpec((SPAN, lanes), lambda i: (blocks - 1 - i, 0))
    rows_spec = pl.BlockSpec((2 * STATE, SPAN), lambda i: (0, blocks - 1 - i))
    whole = pl.BlockSpec((STATE, lanes), lambda i: (0, 0))
    return pl.pallas_call(
        functools.partial(scan_backward_kernel, len(after)),
        grid=(blocks,),
        in_specs=[
            pl.BlockSpec(memory_space=pltpu.SMEM),
            span_spec,
            span_spec,
            rows_spec,
            whole,
            pl.BlockSpec((1, STATE, lanes), lambda i: (blocks - 1 - i, 0, 0)),
            pl.BlockSpec((SPAN, STATE, lanes), lambda i: (blocks - 1 - i, 0, 0)),
            span_spec,
        ]
        + [ANY] * len(after),
        out_specs=[span_spec, span_spec, rows_spec, whole],
        out_shape=[
            jax.ShapeDtypeStruct((length, lanes), WIDE),
            jax.ShapeDtypeStruct((length, lanes), WIDE),
            jax.ShapeDtypeStruct((2 * STATE, length), WIDE),
            jax.ShapeDtypeStruct((STATE, lanes), WIDE),
        ],
        scratch_shapes=[
            pltpu.VMEM((STATE, lanes), WIDE),
        ],
        compiler_params=pltpu.CompilerParams(vmem_limit_bytes=32 * MIB),
        cost_estimate=takes(40),
    )(keep, conv_out, delta, bc_rows, decay_rate, starts, kept, dy, *after)


def padded_lanes(array, lanes):
    return jnp.pad(array, ((0, 0), (0, lanes - array.shape[1])))


def rms_pull(values, scale, gain, d_normed, mean):
    d_values = scale * gain * d_normed - values * (scale * scale * scale) * mean
    return d_values, jnp.sum(d_normed * values * scale, axis=0)


def per_device(tokens, doc_ids, meta_tokens, mixer_params, small_params, ffn_params, cotangent):
    tokens, cotangent = tokens[0], cotangent[0]
    small_whole, ids, meta_whole = start_blocks(small_params, doc_ids[0], meta_tokens)
    g_one = small_shards(small_whole)[0]
    rows, shards = lax.axis_size("row"), lax.axis_size("seq")
    staged = weights_fit(mixer_params.shape[0], ffn_params.shape[0], rows, shards)
    if staged:
        columns, pull_columns = jax.vjp(partial(to_columns, width=view_width()), mixer_params)
    length = ids.shape[0]
    positions = jnp.arange(length, dtype=jnp.int32)
    starts = jnp.concatenate([jnp.ones((1,), bool), ids[1:] != ids[:-1]])
    doc_first = lax.cummax(jnp.where(starts, positions, 0), axis=0)
    keep_mask = (positions != doc_first).astype(WIDE)
    lag_masks = jnp.stack(
        [(positions - j >= doc_first).astype(WIDE)[:, None] for j in range(CONV)]
    )

    tokens_f = tokens.astype(WIDE)
    normed_f, norm_pull = jax.vjp(rms_norm, tokens_f, g_one)
    meta_own = meta_tokens.astype(WIDE)
    meta_unit = rms_norm(meta_whole.astype(WIDE), 1.0)
    normed_own = normed_f.astype(SIXTEEN)
    if staged:
        normed_own, columns = tie(normed_own, columns)
        both, pull_both = jax.vjp(both_halves, columns)
    normed = ring_seq_gather(normed_own, 1)
    cotangent_later = cotangent
    if staged:
        normed, both, cotangent_later = tie(normed, both, cotangent)
        (w_in, w_dt, q_rows, out_rows), pull_parts = jax.vjp(mixer_parts, both)
        (by_heads, w_x), pull_rows = jax.vjp(heads_cut, q_rows)
    else:
        (w_qkv, w_in, w_x, w_dt, w_out), pull_mixer = jax.vjp(mixer_shards_whole, mixer_params)
        (w_gate, w_up, w_down), pull_ffn = jax.vjp(ffn_shards_whole, ffn_params)
    normed, small_later = tie(normed, small_whole)
    (_, g_two, g_attn, channel_part), small_pull = jax.vjp(small_shards, small_later)
    channels = channel_part.shape[0]
    lanes = -(-channels // 128) * 128
    g_ssm = channel_part[:, 0]
    conv_w = channel_part[:, 1 : 1 + CONV].T
    conv_b = channel_part[:, 1 + CONV]
    dt_bias = channel_part[:, 2 + CONV]
    a_log = channel_part[:, 3 + CONV : 3 + CONV + STATE]
    d_skip = channel_part[:, 3 + CONV + STATE]
    meta_normed = (meta_unit * g_one).astype(SIXTEEN)
    every = jnp.concatenate([normed, meta_normed], axis=0)
    cotangent_all = gather_seq(cotangent_later)

    xz = dot_last(normed, w_in).astype(SIXTEEN)
    extended = jnp.pad(xz[:, :channels], ((CONV - 1, 0), (0, 0))).astype(WIDE)
    conv_fn = partial(conv_piece, lag_masks=lag_masks)
    conv_out, conv_pull = jax.vjp(conv_fn, extended, conv_w, conv_b)
    conv_half = conv_out.astype(SIXTEEN)
    if staged:
        conv_half, by_heads, w_x, ffn_later = tie(conv_half, by_heads, w_x, ffn_params)
        w_qkv, pull_heads = jax.vjp(heads_from, by_heads)
        ffn_cut, pull_ffn_cut = jax.vjp(ffn_blocks, ffn_later)
    conv_f = conv_half.astype(WIDE)
    w_x_rows = jnp.pad(w_x.T, ((0, -w_x.shape[1] % 16), (0, 0)))
    projected = seq_sum(jnp.einsum("nc,tc->nt", w_x_rows, conv_half, preferred_element_type=WIDE), 2)
    rank_half = projected[:DT_RANK]
    pre_dt = jnp.einsum("rt,rc->tc", rank_half, w_dt, preferred_element_type=WIDE)
    delta, delta_pull = jax.vjp(lambda p, b: softplus_fn(p + b), pre_dt, dt_bias)
    a_neg, a_pull = jax.vjp(lambda a: -jnp.exp(a), a_log)
    if staged:
        after, through = (w_qkv, cotangent_all), (ffn_cut,)
    else:
        after, through = (), ()
    scan_in = (
        keep_mask,
        padded_lanes(conv_f, lanes),
        padded_lanes(delta, lanes),
        projected[DT_RANK : DT_RANK + 2 * STATE],
        padded_lanes(a_neg.T, lanes),
    )
    y_scan, scan_starts, scan_states, *through = scan_forward(*scan_in, after, through)
    if staged:
        (ffn_cut,) = through
        ffn_columns, pull_ffn_columns = jax.vjp(exchange, ffn_cut)
        ffn_both, pull_ffn_both = jax.vjp(both_halves, ffn_columns)
        (w_gate, w_up, down_rows), pull_ffn_parts = jax.vjp(ffn_parts, ffn_both)
        down_received, pull_down_exchange = jax.vjp(exchange, down_rows)
        w_down, pull_down = jax.vjp(down_from, down_received)

    def gate_piece(y, c, skip, z):
        return (y + skip * c) * silu_fn(z)

    z_in = xz[:, channels:].astype(WIDE)
    ssm_out, gate_pull = jax.vjp(gate_piece, y_scan[:, :channels], conv_f, d_skip, z_in)

    own_heads = g_attn.shape[0]
    queries = dot_last(normed, w_qkv[:, :own_heads]).astype(SIXTEEN)
    kv_rows = dot_last(every, w_qkv[:, own_heads:]).astype(SIXTEEN)
    through = (out_rows.transpose(0, 2, 1),) if staged else ()
    attn_out, log_total, *through = attend_forward(queries, kv_rows, doc_first, through)
    if staged:
        out_received, pull_out_exchange = jax.vjp(exchange, through[0].transpose(0, 2, 1))

    squares = jnp.stack([jnp.sum(attn_out * attn_out, axis=1), jnp.sum(ssm_out * ssm_out, axis=1)])
    squares = seq_sum_small(squares, 3)
    if staged:
        out_received = hand_on(out_received.transpose(0, 2, 1), squares).transpose(0, 2, 1)
        w_out, pull_out = jax.vjp(out_from, out_received)
    scale_a = lax.rsqrt(squares[0] / (HEADS * HEAD) + norm_eps)[:, None]
    scale_m = lax.rsqrt(squares[1] / INNER + norm_eps)[:, None]
    mixed = 0.5 * jnp.concatenate(
        [attn_out * scale_a * g_attn, ssm_out * scale_m * g_ssm], axis=1
    )
    mixed = mixed.astype(SIXTEEN)
    hidden = tokens_f + product_scatter([(mixed, w_out, False)], 4)

    second_f, second_pull = jax.vjp(rms_norm, hidden, g_two)
    second, act, d_gate, d_up = gather_ffn(
        second_f.astype(SIXTEEN), cotangent_all, w_gate, w_up, w_down, 5
    )
    d_second = product_scatter([(d_gate, w_gate, True), (d_up, w_up, True)], 6)
    d_hidden, grad_g_two = second_pull(d_second)
    d_hidden = d_hidden + cotangent.astype(WIDE)

    _, grad_gate, grad_up, grad_down, down_product, d_mixed, grad_out = gather_beside_ffn(
        d_hidden.astype(SIXTEEN), second, cotangent_all, act, d_gate, d_up, w_down, mixed, w_out, 7
    )
    grads_ffn = (grad_gate, grad_up, grad_down)
    block_out = (hidden + scatter_seq(down_product)).astype(SIXTEEN)
    d_mixed = 0.5 * d_mixed
    d_mix_a, d_mix_m = d_mixed[:, :own_heads], d_mixed[:, own_heads:]
    means = jnp.stack(
        [jnp.sum(attn_out * g_attn * d_mix_a, axis=1), jnp.sum(ssm_out * g_ssm * d_mix_m, axis=1)]
    )
    means = seq_sum_small(means, 8)
    d_attn, grad_g_attn = rms_pull(
        attn_out, scale_a, g_attn, d_mix_a, means[0][:, None] / (HEADS * HEAD)
    )
    d_ssm, grad_g_ssm = rms_pull(ssm_out, scale_m, g_ssm, d_mix_m, means[1][:, None] / INNER)

    through = ()
    if staged:
        d_down_cut = hand_on(pull_down(grad_down)[0], means)
        (d_down_rows,) = pull_down_exchange(d_down_cut)
        through = (pull_out(grad_out)[0].transpose(0, 2, 1),)
    d_queries, d_kv, d_meta_kv, *through = attend_backward(
        queries, kv_rows, doc_first, attn_out, log_total, d_attn, through
    )

    if staged:
        (d_ffn_both,) = pull_ffn_parts((grad_gate, grad_up, d_down_rows))
        d_ffn_own, d_ffn_other = row_parts(d_ffn_both)
        (d_out_rows,) = pull_out_exchange(through[0].transpose(0, 2, 1))
    grad_kv = dot_weight(normed, d_kv) + dot_weight(meta_normed, d_meta_kv)
    grad_qkv = jnp.concatenate([dot_weight(normed, d_queries), grad_kv], axis=1)
    grad_qkv = hold(grad_qkv.astype(SIXTEEN))

    d_y, d_conv, grad_d_skip, d_z = gate_pull(d_ssm)
    if staged:
        d_y, grad_qkv = tie(d_y, grad_qkv)
    after = (d_ffn_other,) if staged else ()
    d_conv_scan, d_delta, d_bc, d_rate = scan_backward(
        *scan_in, scan_starts, scan_states, padded_lanes(d_y, lanes), after
    )
    if staged:
        d_ffn_columns = d_ffn_own + other_row(d_ffn_other)
        d_out_rows = hand_on(d_out_rows.transpose(0, 2, 1), d_delta).transpose(0, 2, 1)
    d_conv = d_conv + d_conv_scan[:, :channels]
    d_pre, grad_dt_bias = delta_pull(d_delta[:, :channels])
    (grad_a_log,) = a_pull(d_rate[:, :channels].T)
    d_pre = d_pre.astype(SIXTEEN)
    grad_dt = jnp.einsum("rt,tc->rc", rank_half, d_pre, preferred_element_type=WIDE)
    d_rank = jnp.einsum("rc,tc->rt", w_dt, d_pre, preferred_element_type=WIDE)
    d_proj = jnp.concatenate([d_rank, d_bc], axis=0)
    d_proj = seq_sum(jnp.pad(d_proj, ((0, -d_proj.shape[0] % 16), (0, 0))), 10, (block_out,))
    if staged:
        d_proj = hand_on(d_proj, d_ffn_columns)
        (d_by_heads,) = pull_heads(hand_on(grad_qkv, d_proj))
        (grad_ffn,) = pull_ffn_cut(pull_ffn_columns(d_ffn_columns)[0])
    d_proj = d_proj[: DT_RANK + 2 * STATE].T
    grad_x = hold(dot_weight(conv_half, d_proj).astype(SIXTEEN))
    if staged:
        (d_q_rows,) = pull_rows((d_by_heads, grad_x))
    d_extended, grad_conv_w, grad_conv_b = conv_pull(d_conv + dot_back(d_proj, w_x))
    d_xz = jnp.concatenate([d_extended[CONV - 1 :], d_z], axis=1).astype(SIXTEEN)
    grad_in = hold(dot_weight(normed, d_xz).astype(SIXTEEN))
    grad_dt = grad_dt.astype(SIXTEEN)
    if staged:
        (d_both,) = pull_parts((grad_in, grad_dt, d_q_rows, d_out_rows))
        d_xz, d_both = tie(d_xz, d_both)
        (d_columns,) = pull_both(d_both)
    w_q, w_kv = w_qkv[:, :own_heads], w_qkv[:, own_heads:]
    d_meta = dot_back(d_meta_kv, w_kv)
    d_normed = product_scatter(
        [(d_xz, w_in, True), (d_queries, w_q, True), (d_kv, w_kv, True)], 11
    )
    if staged:
        d_normed, d_columns = tie(d_normed, d_columns)
        (grad_mixer,) = pull_columns(d_columns)
    else:
        (grad_mixer,) = pull_mixer((grad_qkv, grad_in, grad_x, grad_dt, grad_out))
        (grad_ffn,) = pull_ffn(grads_ffn)
    grad_from_norm, grad_g_one = norm_pull(d_normed)
    grad_tokens = d_hidden + grad_from_norm
    grad_g_meta = jnp.sum(d_meta * meta_unit, axis=0)
    grad_channels = jnp.concatenate(
        [
            grad_g_ssm[:, None],
            grad_conv_w.T,
            grad_conv_b[:, None],
            grad_dt_bias[:, None],
            grad_a_log,
            grad_d_skip[:, None],
        ],
        axis=1,
    )
    (grad_small,) = small_pull((grad_g_one + grad_g_meta, grad_g_two, grad_g_attn, grad_channels))
    grad_small, d_meta = end_blocks(grad_small, d_meta)
    _, meta_pull = jax.vjp(lambda v: rms_norm(v, g_one), meta_own)
    (grad_meta,) = meta_pull(d_meta)
    return (
        block_out[None],
        grad_tokens[None],
        grad_meta,
        hold(grad_mixer).astype(WIDE),
        grad_small,
        hold(grad_ffn).astype(WIDE),
    )


def solution(mesh):
    in_specs = (
        P("row", "seq", None),
        P("row", "seq"),
        P(("row", "seq"), None),
        P(("row", "seq")),
        P(("row", "seq")),
        P(("row", "seq")),
        P("row", "seq", None),
    )
    out_specs = (
        P("row", "seq", None),
        P("row", "seq", None),
        P(("row", "seq"), None),
        P(("row", "seq")),
        P(("row", "seq")),
        P(("row", "seq")),
    )
    return jax.shard_map(
        per_device, mesh=mesh, in_specs=in_specs, out_specs=out_specs, check_vma=False
    )
```
